32 devices in a mesh: section: 2 (over core), dp: 4 (over z), seq: 4 (over y, x).
Axes of the slice: x: 2, y: 2, z: 4, core: 2. Of those that a mesh axis runs over, the one named last changes fastest.
Arguments:
- layer_in: bfloat16 [2, 4, 1024, 767], P(None, 'dp', 'seq'), may hold values from -12 to 12
- cotangent: bfloat16 [2, 4, 1024, 767], P(None, 'dp', 'seq'), may hold values from -6 to 6
- lengths: int32 [2, 4, 4], P(None, 'dp'), may hold values from 1 to 896, 1024 in all within a row
- w_qkv: bfloat16 [2, 767, 2304], P('section'), may hold values from -0.21875 to 0.21875
- bias_qv: float32 [2, 1536], P('section'), may hold values from -3 to 3
- w_out: bfloat16 [2, 768, 767], P('section'), may hold values from -1.5 to 1.5
- bias_out: float32 [2, 767], P('section'), may hold values from -2 to 2
- gain_attn: float32 [2, 767], P('section'), may hold values from 0.5 to 1.5
- gain_mlp: float32 [2, 767], P('section'), may hold values from 0.5 to 1.5
- w_up: bfloat16 [2, 767, 3072], P('section'), may hold values from -0.21875 to 0.21875
- bias_up: float32 [2, 3072], P('section'), may hold values from -3 to 3
- w_down: bfloat16 [2, 3072, 767], P('section'), may hold values from -0.109375 to 0.109375
- bias_down: float32 [2, 767], P('section'), may hold values from -2 to 2
Outputs:
- layer_out: bfloat16 [2, 2, 4, 1024, 767], P('section', None, 'dp', 'seq')
- input_grad: bfloat16 [2, 2, 4, 1024, 767], P('section', None, 'dp', 'seq')
- grad_w_qkv: float32 [2, 767, 2304], P('section')
- grad_bias_qv: float32 [2, 1536], P('section')
- grad_w_out: float32 [2, 768, 767], P('section')
- grad_bias_out: float32 [2, 767], P('section')
- grad_gain_attn: float32 [2, 767], P('section')
- grad_gain_mlp: float32 [2, 767], P('section')
- grad_w_up: float32 [2, 767, 3072], P('section')
- grad_bias_up: float32 [2, 3072], P('section')
- grad_w_down: float32 [2, 3072, 767], P('section')
- grad_bias_down: float32 [2, 767], P('section')
- rms_log: float32 [2], P('section')
The draws below stay inside these ranges and needn't reach their ends.
Inputs may be any that keep to these rules, and one draw needn't show every extreme that they name: The lengths of each row sum to 1024, and the longest in every row is 896.
All inputs are finite; a program needn't handle non-finite values.
Results may differ from the reference program's by a relative error of at most 0.015.
Values may be sent and summed in bfloat16 or wider, within the bound.
No kernel may reach another device: no remote copies, remote signals or barrier semaphores. Data moves between devices by JAX's collectives and lax.ppermute only.
A program may use at most 320 MiB of HBM per device.

```python
import math
import jax
import jax.numpy as jnp
import numpy as np
from jax import lax

D = 768
HEADS = 12
FF = 3072
C = 767
SEQ_LEN = 1024
DOCS = 4
MOST = 896
ROWS = 4
MICRO = 2
LAYERS = 2


def draw_layer_in(key, part):
    key = jax.random.fold_in(key, 11)
    first_key = jax.random.fold_in(key, 0)
    full_shape = (MICRO, ROWS, SEQ_LEN, C)
    row_frac = jnp.arange(ROWS, dtype=jnp.float32) / ROWS
    pos_frac = jnp.arange(SEQ_LEN, dtype=jnp.float32) / SEQ_LEN
    level = 0.4 * jnp.exp(0.5 * jnp.log(5.0) * (row_frac[None, :, None, None] + pos_frac[None, None, :, None]))
    values = jnp.clip(jax.random.normal(first_key, full_shape, jnp.float32), -6.0, 6.0) * level
    return values.astype(jnp.bfloat16)


def block_scale(stream_key, extent, pieces, smallest, high):
    def one(axis_at, parts):
        heights = jax.random.uniform(jax.random.fold_in(jax.random.fold_in(stream_key, 6), axis_at), (parts,), jnp.float32, smallest / len(pieces), high / len(pieces))
        return jnp.repeat(jnp.exp(heights), extent[axis_at] // parts).reshape((-1,) + (1,) * (len(extent) - axis_at - 1))

    factor_of = one(*pieces[0])
    for cut in pieces[1:]:
        factor_of = factor_of * one(*cut)
    return factor_of


def profile(count, total, limit, skew):
    portions = [(1 << 20) // math.isqrt(standing ** skew) + 1 for standing in range(2, count + 1)]
    surplus, given = total - limit - (count - 1), [1] * (count - 1)
    while surplus > 0:
        movable = [i for i in range(count - 1) if given[i] < limit]
        whole, left = sum([portions[i] for i in movable]), surplus
        for i in movable:
            addition = min(limit - given[i], max(1, left * portions[i] // whole), surplus)
            given[i] = given[i] + addition
            surplus = surplus - addition
    return np.array([limit] + given)


def ragged_sizes(own_key, amount, total, bound, slope):
    if amount == 2:
        one = jax.random.randint(own_key, (), max(1, total - bound), min(bound, total - 1) + 1)
        return jnp.stack([one, total - one])
    sizes = jnp.asarray(profile(amount, total, bound, slope), jnp.int32)
    pairs = (amount - 1) // 2
    giver, sink = sizes[1:1 + 2 * pairs:2], sizes[2:2 + 2 * pairs:2]
    slack = jnp.minimum(giver - 1, bound - sink)
    moved = jax.random.randint(jax.random.fold_in(own_key, 1), (pairs,), 0, 1 << 20) % (slack + 1)
    sizes = sizes.at[1:1 + 2 * pairs:2].set(giver - moved).at[2:2 + 2 * pairs:2].set(sink + moved)
    return sizes[jax.random.permutation(jax.random.fold_in(own_key, 2), amount)]


def bell_draw(key, dims, spread, bound, pieces=(), held_as=jnp.bfloat16):
    values = spread * jax.random.normal(key, dims, jnp.float32)
    if pieces:
        values = values * block_scale(key, dims, pieces, -0.22, 0.18)
    return jnp.clip(values, -bound, bound).astype(held_as)


def setup_inputs(seed: int = 0) -> dict:
    streams_of = jax.random.split(jax.random.key(seed), 14)
    layer_in = draw_layer_in(jax.random.fold_in(streams_of[13], 71), 0)
    cotangent = bell_draw(streams_of[1], (MICRO, ROWS, SEQ_LEN, C), 1.0, 6.0, ((1, 4), (2, 4)))
    lengths = jax.vmap(lambda own: ragged_sizes(own, DOCS, SEQ_LEN, MOST, 2))(jax.random.split(streams_of[2], MICRO * ROWS)).reshape((MICRO, ROWS, DOCS)).astype(jnp.int32)
    w_qkv = bell_draw(streams_of[3], (LAYERS, C, 3 * D), C ** -0.5, 0.21875, ((0, 2),))
    bias_qv = bell_draw(streams_of[4], (LAYERS, 2 * D), 0.5, 3.0, ((0, 2),), jnp.float32)
    w_out = bell_draw(streams_of[5], (LAYERS, D, C), (max(D // 48, 4)) ** -0.5, 1.5, ((0, 2),))
    bias_out = bell_draw(streams_of[6], (LAYERS, C), 0.3, 2.0, ((0, 2),), jnp.float32)
    gain_attn = jnp.clip(1.0 + 0.1 * jax.random.normal(streams_of[7], (LAYERS, C), jnp.float32), 0.5, 1.5)
    gain_mlp = jnp.clip(1.0 + 0.1 * jax.random.normal(streams_of[8], (LAYERS, C), jnp.float32), 0.5, 1.5)
    w_up = bell_draw(streams_of[9], (LAYERS, C, FF), C ** -0.5, 0.21875, ((0, 2),))
    bias_up = bell_draw(streams_of[10], (LAYERS, FF), 0.5, 3.0, ((0, 2),), jnp.float32)
    w_down = bell_draw(streams_of[11], (LAYERS, FF, C), FF ** -0.5, 0.109375, ((0, 2),))
    bias_down = bell_draw(streams_of[12], (LAYERS, C), 0.3, 2.0, ((0, 2),), jnp.float32)
    return dict(layer_in=layer_in, cotangent=cotangent, lengths=lengths, w_qkv=w_qkv, bias_qv=bias_qv, w_out=w_out, bias_out=bias_out, gain_attn=gain_attn, gain_mlp=gain_mlp, w_up=w_up, bias_up=bias_up, w_down=w_down, bias_down=bias_down)


epsilon = 1e-06
masked_fill = -1e+30
per_group = 4

@jax.custom_vjp
def low(v):
    return lax.optimization_barrier(v.astype(jnp.bfloat16)).astype(jnp.float32)

@jax.custom_vjp
def low_back(v):
    return v

def low_keep(v):
    return (low(v), None)

def low_pass(kept, grad):
    return (grad,)

def back_keep(v):
    return (v, None)

def back_low(kept, grad):
    return (low(grad),)
low.defvjp(low_keep, low_pass)
low_back.defvjp(back_keep, back_low)

def crms_norm(values, gain_vec):
    full_width = values.shape[-1] + 1
    squares = lax.optimization_barrier(jnp.sum(values * values, axis=-1, keepdims=True))
    column_sum = lax.optimization_barrier(jnp.sum(values, axis=-1, keepdims=True))
    scale_inv = lax.rsqrt((squares + column_sum * column_sum) / full_width + epsilon)
    return values * scale_inv * gain_vec

def mean_square(values):
    full_width = values.shape[-1] + 1
    column_sum = lax.optimization_barrier(jnp.sum(values, axis=-1))
    return (lax.optimization_barrier(jnp.sum(values * values, axis=-1)) + column_sum * column_sum) / full_width

def segments(doc_lengths, positions):
    doc_ends = jnp.cumsum(doc_lengths, axis=-1)
    return lax.optimization_barrier(jnp.sum((doc_ends[..., None, :] <= positions[:, None]).astype(jnp.int32), axis=-1)).astype(jnp.int32)

def einsum_high(form, left_side, right_side):
    return jnp.einsum(form, left_side, right_side, precision=lax.Precision.HIGHEST)

def layer(layer_input, params, visible):
    w_qkv, bias_qv, w_out, bias_out, gain_attn, gain_mlp, w_up, bias_up, w_down, bias_down = params
    model_width = w_out.shape[0]
    head_size = model_width // HEADS
    score_scale = head_size ** (-0.5)
    seq_count, token_count = (layer_input.shape[0], layer_input.shape[1])
    normed = low(crms_norm(layer_input, gain_attn))
    bias_full = jnp.concatenate([bias_qv[:model_width], jnp.zeros((model_width,), jnp.float32), bias_qv[model_width:]])
    qkv = low(low_back(einsum_high('stc,cf->stf', normed, w_qkv) + bias_full))
    heads_shape = (seq_count, token_count, HEADS, head_size)
    queries = qkv[..., :model_width].reshape(heads_shape)
    key_heads = qkv[..., model_width:2 * model_width].reshape(heads_shape)
    value_heads = qkv[..., 2 * model_width:].reshape(heads_shape)
    raw_scores = einsum_high('sqhd,skhd->shqk', queries, key_heads)
    scores = low_back(jnp.where(visible[:, None], raw_scores * score_scale, masked_fill))
    attn_probs = low(jax.nn.softmax(scores, axis=-1))
    attended = einsum_high('shqk,skhd->sqhd', attn_probs, value_heads).reshape(seq_count, token_count, model_width)
    attended = low(low_back(attended))
    middle = layer_input + low_back(einsum_high('std,dc->stc', attended, w_out) + bias_out)
    normed_mlp = low(crms_norm(middle, gain_mlp))
    up_proj = low_back(einsum_high('stc,cf->stf', normed_mlp, w_up) + bias_up)
    activated = low(jax.nn.gelu(up_proj))
    return middle + low_back(einsum_high('stf,fc->stc', activated, w_down) + bias_down)

def reference(layer_in, cotangent, lengths, w_qkv, bias_qv, w_out, bias_out, gain_attn, gain_mlp, w_up, bias_up, w_down, bias_down):
    micro_count, row_count, seq_len, compact = layer_in.shape
    block_count = micro_count * row_count // per_group
    positions = jnp.arange(seq_len, dtype=jnp.int32)
    weights = (w_qkv, bias_qv, w_out, bias_out, gain_attn, gain_mlp, w_up, bias_up, w_down, bias_down)
    first_params = tuple((weight_item[0].astype(jnp.float32) for weight_item in weights))
    second_params = tuple((weight_item[1].astype(jnp.float32) for weight_item in weights))

    def blocked(stacked):
        return stacked.reshape((block_count, per_group) + stacked.shape[2:])
    inputs = (blocked(layer_in), blocked(cotangent), blocked(lengths))

    def one_block(totals, block_item):
        block_in, block_cot, block_lengths = block_item
        seg_ids = segments(block_lengths, positions)
        visible = (seg_ids[:, :, None] == seg_ids[:, None, :]) & (positions[None, None, :] <= positions[None, :, None])

        def whole(start_in, params_one, params_two, probe_zero):
            first_out = layer(start_in, params_one, visible)
            handed = low(low_back(first_out)) + probe_zero
            second_out = layer(handed, params_two, visible)
            return (low(low_back(second_out)), (handed, jnp.sum(mean_square(first_out)), jnp.sum(mean_square(second_out))))
        probe_zero = jnp.zeros(block_in.shape, jnp.float32)
        result, pullback, extras = jax.vjp(whole, block_in.astype(jnp.float32), first_params, second_params, probe_zero, has_aux=True)
        grad_in, grad_one, grad_two, grad_handed = pullback(block_cot.astype(jnp.float32))
        totals = jax.tree.map(jnp.add, totals, (grad_one, grad_two, extras[1], extras[2]))
        return (totals, (extras[0].astype(jnp.bfloat16), result.astype(jnp.bfloat16), grad_in.astype(jnp.bfloat16), grad_handed.astype(jnp.bfloat16)))
    zero_params = tuple((jnp.zeros(weight_item.shape, jnp.float32) for weight_item in first_params))
    initial = (zero_params, zero_params, jnp.zeros((), jnp.float32), jnp.zeros((), jnp.float32))
    totals, stacked_outs = lax.scan(one_block, initial, inputs)
    full_shape = (micro_count, row_count, seq_len, compact)
    handed_all, result_all, grad_in_all, grad_handed_all = [piece.reshape(full_shape) for piece in stacked_outs]
    layer_out = jnp.stack([handed_all, result_all])
    input_grad = jnp.stack([grad_in_all, grad_handed_all])
    grads_one, grads_two, square_one, square_two = totals
    stacked_grads = [jnp.stack([grads_one[index], grads_two[index]]) for index in range(10)]
    rms_log = jnp.sqrt(jnp.stack([square_one, square_two]) / (micro_count * row_count * seq_len))
    return (layer_out, input_grad, stacked_grads[0], stacked_grads[1], stacked_grads[2], stacked_grads[3], stacked_grads[4], stacked_grads[5], stacked_grads[6], stacked_grads[7], stacked_grads[8], stacked_grads[9], rms_log)
```

```python
import functools

import jax
import jax.numpy as jnp
from jax import lax
from jax.experimental import pallas as pl
from jax.experimental.pallas import tpu as pltpu
from jax.sharding import PartitionSpec as P

HEADS = 12
EPS = 1e-6
NEG = -1e30
F32 = jnp.float32
BF16 = jnp.bfloat16
MIB = 1 << 20
QUAD = 4


def nn(a, b):
    return lax.dot_general(a, b, (((1,), (0,)), ((), ())), preferred_element_type=F32)


def nt(a, b):
    return lax.dot_general(a, b, (((1,), (1,)), ((), ())), preferred_element_type=F32)


def tn(a, b):
    return lax.dot_general(a, b, (((0,), (0,)), ((), ())), preferred_element_type=F32)


def order(core, k):
    if isinstance(k, int):
        return jnp.where(core == 1, k, ((k & 1) << 1) | (k >> 1))
    return jnp.where(core == 1, k, ((k & 1) << 1) | (k >> 1))


def crms_scale(v):
    sq = jnp.sum(v * v, axis=-1, keepdims=True)
    su = jnp.sum(v, axis=-1, keepdims=True)
    full = v.shape[-1] + 1
    return lax.rsqrt((sq + su * su) / full + EPS), su, (sq + su * su) / full


def crms_back(v, gain, grad):
    r, su, _ = crms_scale(v)
    gd = grad * gain
    w = jnp.sum(gd * v, axis=-1, keepdims=True)
    unit = v * r
    dv = gd * r - (w * r * r * r / (v.shape[-1] + 1)) * (v + su)
    return dv, grad * unit, unit * gain


GC = 0.7978845608028654


def gelu_parts(u):
    inner = GC * (u + 0.044715 * (u * u * u))
    th = jnp.tanh(inner)
    return th


def params(mib, **kw):
    return pltpu.CompilerParams(vmem_limit_bytes=mib * MIB, **kw)


def cost(flops, nbytes, trans=0):
    return pl.CostEstimate(flops=int(flops), bytes_accessed=int(nbytes), transcendentals=int(trans))


SMEM = pl.BlockSpec(memory_space=pltpu.SMEM)
VMEM = pl.BlockSpec(memory_space=pltpu.VMEM)
ANY = pl.BlockSpec(memory_space=pl.ANY)


def norm_kernel(x_ref, pv_ref, o_ref):
    x = x_ref[...].astype(F32)
    r, _, _ = crms_scale(x)
    o_ref[...] = (x * r * pv_ref[3:4, : x.shape[-1]]).astype(BF16)


def first_norm(x, pv):
    return pl.pallas_call(
        norm_kernel,
        in_specs=[VMEM, VMEM],
        out_specs=VMEM,
        out_shape=jax.ShapeDtypeStruct(x.shape, BF16),
        compiler_params=params(8),
        cost_estimate=cost(0, x.size * 4),
    )(x, pv)


def visible_bias(ids, n, t, span):
    i = t * span + lax.broadcasted_iota(jnp.int32, (1, span), 1)
    start = jnp.zeros((1, span), jnp.int32)
    for d in range(4):
        end = ids[2 + d]
        start = jnp.maximum(start, jnp.where(i >= end, end, 0))
    j = lax.broadcasted_iota(jnp.int32, (n, span), 0)
    return jnp.where((j >= start) & (j <= i), 0.0, NEG)


def attn_fwd_kernel(
    ids, n0, n1, n2, n3, w_ref, pv_ref, qh, kh, vh, lse, a0, a1, a2, a3, at, bias_scr
):
    c, s = ids[0], ids[1]
    heads, _, hd = qh.shape
    span = n0.shape[0]
    width = heads * hd
    bias = pv_ref[5:6, : 3 * width]
    for p, nb in enumerate((n0, n1, n2, n3)):
        t = jnp.bitwise_xor(order(c, p), s)
        row = pl.multiple_of(t * span, span)
        y = nn(nb[...], w_ref[...]) + bias
        for h in range(heads):
            lo = h * hd
            qh[h, pl.ds(row, span), :] = (y[:, lo : lo + hd] * (hd**-0.5)).astype(BF16)
            kh[h, pl.ds(row, span), :] = y[:, width + lo : width + lo + hd].astype(BF16)
            vh[h, pl.ds(row, span), :] = y[:, 2 * width + lo : 2 * width + lo + hd].astype(BF16)
    for t in range(QUAD):
        n = span * (t + 1)
        bias_scr[:n, :] = visible_bias(ids, n, t, span)

        def head(h, carry, t=t, n=n):
            q = qh[h, t * span : (t + 1) * span, :]
            sc = nt(kh[h, :n, :], q) + bias_scr[:n, :]
            m = jnp.max(sc, axis=0, keepdims=True)
            e = jnp.exp(sc - m)
            tot = jnp.sum(e, axis=0, keepdims=True)
            pr = (e * (1.0 / tot)).astype(BF16)
            o = tn(vh[h, :n, :], pr)
            at[t, pl.ds(pl.multiple_of(h * hd, hd), hd), :] = o.astype(BF16)
            lse[h, t : t + 1, :] = m + jnp.log(tot)
            return carry

        lax.fori_loop(0, heads, head, 0)
    for k, a in enumerate((a0, a1, a2, a3)):
        a[...] = at[jnp.bitwise_xor(s, k)]


def attn_fwd(ids, blocks, w3, pv, heads, hd):
    span, width = blocks[0].shape
    full = span * QUAD
    hh = jax.ShapeDtypeStruct((heads, full, hd), BF16)
    aa = jax.ShapeDtypeStruct((heads * hd, span), BF16)
    return pl.pallas_call(
        attn_fwd_kernel,
        in_specs=[SMEM] + [VMEM] * 6,
        out_specs=[VMEM] * 8,
        out_shape=[hh, hh, hh, jax.ShapeDtypeStruct((heads, QUAD, span), F32), aa, aa, aa, aa],
        scratch_shapes=[
            pltpu.VMEM((QUAD, heads * hd, span), BF16),
            pltpu.VMEM((full, span), F32),
        ],
        compiler_params=params(40),
        cost_estimate=cost(
            2 * full * width * 3 * heads * hd + 3 * 4 * full * full * hd * heads,
            4 * full * width,
            heads * full * full,
        ),
    )(ids, *blocks, w3, pv)


def mlp_fwd_kernel(
    layer, ids, x, a0, a1, a2, a3, wo, pv, pvn, pvb, upo, upr, dno, dnr,
    mid, u, xout, nnext, sq, astk, nm, acc,
):
    j = pl.program_id(0)
    c, s = ids[0], ids[1]
    cc = x.shape[-1]
    own = c == layer

    @pl.when(j == 0)
    def _():
        rows = a0.shape[0]
        m = x[...].astype(F32) + pv[1:2, :cc]
        for k, a in enumerate((a0, a1, a2, a3)):
            row = pl.multiple_of(jnp.bitwise_xor(s, k) * rows, rows)
            m = m + tn(a[...], wo[pl.ds(row, rows), :])
            astk[k] = a[...]
        mid[...] = m
        r, _, _ = crms_scale(m)
        nm[...] = (m * r * pv[4:5, :cc]).astype(BF16)
        acc[...] = m + pv[2:3, :cc]

    wu = lax.select(own, upo[0], upr[0])
    wd = lax.select(own, dno[0], dnr[0])
    ub = nn(nm[...], wu) + pvb[0:1, :]
    u[...] = ub
    act = (0.5 * ub * (1.0 + gelu_parts(ub))).astype(BF16)
    acc[...] += nn(act, wd)

    @pl.when(j == pl.num_programs(0) - 1)
    def _():
        fin = acc[...]
        _, _, ms = crms_scale(fin)
        sq[...] = jnp.broadcast_to(jnp.sum(ms, axis=0, keepdims=True), sq.shape)
        low = fin.astype(BF16)
        xout[...] = low
        lf = low.astype(F32)
        r, _, _ = crms_scale(lf)
        nnext[...] = (lf * r * pvn[3:4, :cc]).astype(BF16)


def mlp_fwd(layer, ids, x, att, wo, pv, pvn, up, dn):
    span, cc = x.shape
    ff = up[0].shape[-1]
    fb = ff // 8
    rows = att[0].shape[0]

    def whole(shape):
        return pl.BlockSpec(shape, lambda j, ids: (0,) * len(shape))

    def pick(mine):
        return lambda j, ids: jnp.where((ids[0] == layer) == mine, j, 0)

    mine, other = pick(True), pick(False)
    grid = pltpu.PrefetchScalarGridSpec(
        num_scalar_prefetch=1,
        grid=(8,),
        in_specs=[whole((span, cc))]
        + [whole((rows, span))] * 4
        + [whole(wo.shape), whole(pv.shape), whole(pvn.shape)]
        + [
            pl.BlockSpec((8, fb), lambda j, ids: (0, j)),
            pl.BlockSpec((1, cc, fb), lambda j, ids: (0, 0, mine(j, ids))),
            pl.BlockSpec((1, cc, fb), lambda j, ids: (0, 0, other(j, ids))),
            pl.BlockSpec((1, fb, cc), lambda j, ids: (0, mine(j, ids), 0)),
            pl.BlockSpec((1, fb, cc), lambda j, ids: (0, other(j, ids), 0)),
        ],
        out_specs=[
            whole((span, cc)),
            pl.BlockSpec((span, fb), lambda j, ids: (0, j)),
            whole((span, cc)),
            whole((span, cc)),
            whole((8, 128)),
            whole((QUAD, rows, span)),
        ],
        scratch_shapes=[pltpu.VMEM((span, cc), BF16), pltpu.VMEM((span, cc), F32)],
    )
    return pl.pallas_call(
        functools.partial(mlp_fwd_kernel, layer),
        grid_spec=grid,
        out_shape=[
            jax.ShapeDtypeStruct((span, cc), F32),
            jax.ShapeDtypeStruct((span, ff), F32),
            jax.ShapeDtypeStruct((span, cc), BF16),
            jax.ShapeDtypeStruct((span, cc), BF16),
            jax.ShapeDtypeStruct((8, 128), F32),
            jax.ShapeDtypeStruct((QUAD, rows, span), BF16),
        ],
        compiler_params=params(40, dimension_semantics=("arbitrary",)),
        cost_estimate=cost(6 * span * cc * ff, 4 * cc * ff + 4 * span * ff, span * ff),
    )(ids, x, *att, wo, pv, pvn, pv, up[0], up[1], dn[0], dn[1])


def mlp_bwd_kernel(
    layer, ids, df, u, mid, wo, pv, upo, upr, dno, dnr,
    lr, rr, dmid, dmlow, g, d0, d1, d2, d3, acc,
):
    j = pl.program_id(0)
    c, s = ids[0], ids[1]
    cc = df.shape[-1]
    fb = u.shape[-1]
    own = c == layer

    @pl.when(j == 0)
    def _():
        acc[...] = jnp.zeros_like(acc)
        g[...] = jnp.zeros_like(g)

    wu = lax.select(own, upo[0], upr[0])
    wd = lax.select(own, dno[0], dnr[0])
    da = nt(df[...], wd)
    ub = u[...]
    th = gelu_parts(ub)
    half = 0.5 * (1.0 + th)
    lr[0] = (ub * half).astype(BF16)
    slope = half + 0.5 * ub * (1.0 - th * th) * (GC * (1.0 + 3 * 0.044715 * (ub * ub)))
    du = (slope * da).astype(BF16)
    lr[1] = du
    g[0:1, pl.ds(pl.multiple_of(j * fb, 128), fb)] = jnp.sum(du.astype(F32), axis=0, keepdims=True)
    acc[...] += nt(du, wu)

    @pl.when(j == pl.num_programs(0) - 1)
    def _():
        dff = df[...].astype(F32)
        dv, gg, nm = crms_back(mid[...], pv[4:5, :cc], acc[...])
        dm = dff + dv
        low = dm.astype(BF16)
        rr[0] = df[...]
        rr[1] = nm.astype(BF16)
        dmid[...] = dm
        dmlow[...] = low
        g[1:2, :cc] = jnp.sum(low.astype(F32), axis=0, keepdims=True)
        g[2:3, :cc] = jnp.sum(dff, axis=0, keepdims=True)
        g[4:5, :cc] = jnp.sum(gg, axis=0, keepdims=True)
        rows = d0.shape[0]
        for k, d in enumerate((d0, d1, d2, d3)):
            row = pl.multiple_of(jnp.bitwise_xor(s, k) * rows, rows)
            d[...] = nt(wo[pl.ds(row, rows), :], low).astype(BF16)


def mlp_bwd(layer, ids, df, u, mid, wo, pv, up, dn):
    span, cc = df.shape
    ff = u.shape[-1]
    fb = ff // 8
    rows = wo.shape[0] // QUAD

    def whole(shape):
        return pl.BlockSpec(shape, lambda j, ids: (0,) * len(shape))

    def pick(mine):
        return lambda j, ids: jnp.where((ids[0] == layer) == mine, j, 0)

    mine, other = pick(True), pick(False)
    grid = pltpu.PrefetchScalarGridSpec(
        num_scalar_prefetch=1,
        grid=(8,),
        in_specs=[
            whole((span, cc)),
            pl.BlockSpec((span, fb), lambda j, ids: (0, j)),
            whole((span, cc)),
            whole(wo.shape),
            whole(pv.shape),
            pl.BlockSpec((1, cc, fb), lambda j, ids: (0, 0, mine(j, ids))),
            pl.BlockSpec((1, cc, fb), lambda j, ids: (0, 0, other(j, ids))),
            pl.BlockSpec((1, fb, cc), lambda j, ids: (0, mine(j, ids), 0)),
            pl.BlockSpec((1, fb, cc), lambda j, ids: (0, other(j, ids), 0)),
        ],
        out_specs=[
            pl.BlockSpec((2, span, fb), lambda j, ids: (0, 0, j)),
            whole((2, span, cc)),
            whole((span, cc)),
            whole((span, cc)),
            whole((8, ff)),
        ]
        + [whole((rows, span))] * 4,
        scratch_shapes=[pltpu.VMEM((span, cc), F32)],
    )
    dd = jax.ShapeDtypeStruct((rows, span), BF16)
    return pl.pallas_call(
        functools.partial(mlp_bwd_kernel, layer),
        grid_spec=grid,
        out_shape=[
            jax.ShapeDtypeStruct((2, span, ff), BF16),
            jax.ShapeDtypeStruct((2, span, cc), BF16),
            jax.ShapeDtypeStruct((span, cc), F32),
            jax.ShapeDtypeStruct((span, cc), BF16),
            jax.ShapeDtypeStruct((8, ff), F32),
            dd, dd, dd, dd,
        ],
        compiler_params=params(40, dimension_semantics=("arbitrary",)),
        cost_estimate=cost(6 * span * cc * ff, 4 * cc * ff + 8 * span * ff, span * ff),
    )(ids, df, u, mid, wo, pv, up[0], up[1], dn[0], dn[1])


def product_kernel(send, ids, lr, rr, att, dmlow, *rest):
    out = rest[-1]
    core = 1 - ids[0] if send else ids[0]
    block = lr.shape[-1]
    part = att.shape[1] // 2
    main = tn(lr[0], rr[0])
    row = pl.multiple_of(core * part, part)
    side = nn(att[0, pl.ds(row, part), :], dmlow[...])
    if send:
        out[:block, :] = main.astype(BF16)
        out[block:, :] = side.astype(BF16)
    else:
        got = rest[0]
        out[:block, :] = (main + got[:block, :].astype(F32)).astype(BF16)
        out[block:, :] = (side + got[block:, :].astype(F32)).astype(BF16)


def product(send, place, ids, lr, rr, att, dmlow, got=None):
    span, cc = dmlow.shape
    block = lr.shape[-1] // QUAD
    rows = att.shape[1]
    total = block + rows // 2

    def core(ids):
        return 1 - ids[0] if send else ids[0]

    def offset(ids):
        return order(core(ids), place)

    in_specs = [
        pl.BlockSpec((1, span, block), lambda i, ids: (core(ids), 0, offset(ids) ^ ids[1])),
        pl.BlockSpec((1, span, cc), lambda i, ids: (core(ids), 0, 0)),
        pl.BlockSpec((1, rows, span), lambda i, ids: (offset(ids), 0, 0)),
        pl.BlockSpec((span, cc), lambda i, ids: (0, 0)),
    ]
    operands = [lr, rr, att, dmlow]
    if not send:
        in_specs.append(pl.BlockSpec((total, cc), lambda i, ids: (0, 0)))
        operands.append(got)
    return pl.pallas_call(
        functools.partial(product_kernel, send),
        grid_spec=pltpu.PrefetchScalarGridSpec(
            num_scalar_prefetch=1,
            grid=(1,),
            in_specs=in_specs,
            out_specs=pl.BlockSpec((total, cc), lambda i, ids: (0, 0)),
        ),
        out_shape=jax.ShapeDtypeStruct((total, cc), BF16),
        compiler_params=params(24, dimension_semantics=("arbitrary",)),
        cost_estimate=cost(2 * span * total * cc, 2 * total * cc * 2),
    )(ids, *operands)


def attn_bwd_kernel(
    ids, n0, n1, n2, n3, w_ref, qh, kh, vh, lse, d0, d1, d2, d3,
    p0, p1, p2, p3, gs, gk, gb, do, dk, dv, dy, acc, bias_scr,
):
    c, s = ids[0], ids[1]
    heads, _, hd = qh.shape
    span = n0.shape[0]
    width = heads * hd
    for k, d in enumerate((d0, d1, d2, d3)):
        do[jnp.bitwise_xor(s, k)] = d[...]
    for t in reversed(range(QUAD)):
        n = span * (t + 1)
        bias_scr[:n, :] = visible_bias(ids, n, t, span)
        for h in range(heads):
            q = qh[h, t * span : (t + 1) * span, :]
            kk = kh[h, :n, :]
            sc = nt(kk, q) + (bias_scr[:n, :] - lse[h, t : t + 1, :])
            pr = jnp.exp(sc)
            dot = do[t, h * hd : (h + 1) * hd, :]
            dp = nn(vh[h, :n, :], dot)
            inner = jnp.sum(pr * dp, axis=0, keepdims=True)
            ds = (pr * (dp - inner)).astype(BF16)
            newk = nn(ds, q)
            newv = nt(pr.astype(BF16), dot)
            if t == QUAD - 1:
                dk[h, :n, :] = newk
                dv[h, :n, :] = newv
            else:
                dk[h, :n, :] += newk
                dv[h, :n, :] += newv
            dq = tn(kk, ds) * (hd**-0.5)
            dy[t * span : (t + 1) * span, h * hd : (h + 1) * hd] = dq.T.astype(BF16)
    for h in range(heads):
        dy[:, width + h * hd : width + (h + 1) * hd] = dk[h].astype(BF16)
        dy[:, 2 * width + h * hd : 2 * width + (h + 1) * hd] = dv[h].astype(BF16)
    total = jnp.zeros((1, 3 * width), F32)
    for p, (nb, out) in enumerate(((n0, p0), (n1, p1), (n2, p2), (n3, p3))):
        row = pl.multiple_of(jnp.bitwise_xor(order(c, p), s) * span, span)
        y = dy[pl.ds(row, span), :]
        out[...] = nt(y, w_ref[...]).astype(BF16)
        total = total + jnp.sum(y.astype(F32), axis=0, keepdims=True)
        g = tn(y, nb[...])
        if p == 0:
            acc[...] = g
        else:
            acc[...] += g
    gb[...] = jnp.broadcast_to(total, gb.shape)
    part = gs.shape[0]

    @pl.when(c == 0)
    def _():
        gk[...] = acc[:part, :].astype(BF16)
        gs[...] = acc[part:, :].astype(BF16)

    @pl.when(c == 1)
    def _():
        gs[...] = acc[:part, :].astype(BF16)
        gk[...] = acc[part:, :].astype(BF16)


def attn_bwd(ids, blocks, w3, qkvl, douts):
    span, cc = blocks[0].shape
    heads, full, hd = qkvl[0].shape
    width = heads * hd
    part = 3 * width // 2
    pp = jax.ShapeDtypeStruct((span, cc), BF16)
    gg = jax.ShapeDtypeStruct((part, cc), BF16)
    return pl.pallas_call(
        attn_bwd_kernel,
        in_specs=[SMEM] + [VMEM] * 13,
        out_specs=[VMEM] * 7,
        out_shape=[pp, pp, pp, pp, gg, gg, jax.ShapeDtypeStruct((8, 3 * width), F32)],
        scratch_shapes=[
            pltpu.VMEM((QUAD, width, span), BF16),
            pltpu.VMEM((heads, full, hd), F32),
            pltpu.VMEM((heads, full, hd), F32),
            pltpu.VMEM((full, 3 * width), BF16),
            pltpu.VMEM((3 * width, cc), F32),
            pltpu.VMEM((full, span), F32),
        ],
        compiler_params=params(48),
        cost_estimate=cost(
            4 * full * cc * 3 * width + 3 * 10 * full * full * hd * heads,
            8 * full * cc,
            heads * full * full,
        ),
    )(ids, *blocks, w3, *qkvl, *douts)


def input_kernel(part, r0, r1, dmid, x, pv, dx, gg):
    cc = x.shape[-1]
    dn = part[...].astype(F32) + r0[...].astype(F32) + r1[...].astype(F32)
    dv, g, _ = crms_back(x[...].astype(F32), pv[3:4, :cc], dn)
    dx[...] = (dmid[...] + dv).astype(BF16)
    gg[...] = jnp.broadcast_to(jnp.sum(g, axis=0, keepdims=True), gg.shape)


def input_grad_of(part, r0, r1, dmid, x, pv):
    return pl.pallas_call(
        input_kernel,
        in_specs=[VMEM] * 6,
        out_specs=[VMEM] * 2,
        out_shape=[
            jax.ShapeDtypeStruct(x.shape, BF16),
            jax.ShapeDtypeStruct((8, x.shape[-1]), F32),
        ],
        compiler_params=params(16),
        cost_estimate=cost(0, x.size * 14),
    )(part, r0, r1, dmid, x, pv)


def place_kernel(place, first, ids, *refs):
    srcs = refs[:4]
    outs = refs[4:7] if first else refs[7:10]
    x0, x1, od, ou, ow, sem = refs[7:] if first else refs[10:]
    c, s = ids[0], ids[1]
    down, up, wout = outs
    f0, r1, r0, f1 = srcs

    @pl.when(c == 0)
    def _():
        a = pltpu.make_async_copy(f0, x0, sem.at[0])
        b = pltpu.make_async_copy(r0, x1, sem.at[1])
        a.start()
        b.start()
        a.wait()
        b.wait()

    @pl.when(c != 0)
    def _():
        a = pltpu.make_async_copy(r1, x0, sem.at[0])
        b = pltpu.make_async_copy(f1, x1, sem.at[1])
        a.start()
        b.start()
        a.wait()
        b.wait()

    block = od.shape[0]
    part = ow.shape[1]
    t0 = jnp.bitwise_xor(((place & 1) << 1) | (place >> 1), s)
    t1 = jnp.bitwise_xor(place, s)
    od[...] = x0[:block, :].astype(F32)
    ow[0] = x0[block:, :].astype(F32)
    ow[1] = x1[block:, :].astype(F32)
    ca = pltpu.make_async_copy(od, down.at[pl.ds(pl.multiple_of(t0 * block, block), block), :], sem.at[0])
    cb = pltpu.make_async_copy(
        ow.at[0], wout.at[pl.ds(pl.multiple_of(t0 * 2 * part, part), part), :], sem.at[1]
    )
    cd = pltpu.make_async_copy(
        ow.at[1], wout.at[pl.ds(pl.multiple_of((t1 * 2 + 1) * part, part), part), :], sem.at[2]
    )
    ca.start()
    cb.start()
    cd.start()
    ou[...] = x1[:block, :].astype(F32).T
    ce = pltpu.make_async_copy(ou, up.at[:, pl.ds(pl.multiple_of(t1 * block, block), block)], sem.at[3])
    ce.start()
    ca.wait()
    cb.wait()
    cd.wait()
    ce.wait()


def place_rows(place, ids, srcs, outs, shapes):
    total, cc = srcs[0].shape
    block = shapes[0][0] // QUAD
    part = total - block
    first = outs is None
    operands = [ids, *srcs] + ([] if first else list(outs))
    return pl.pallas_call(
        functools.partial(place_kernel, place, first),
        in_specs=[SMEM] + [ANY] * (len(operands) - 1),
        out_specs=[ANY] * 3,
        out_shape=[jax.ShapeDtypeStruct(s, F32) for s in shapes],
        input_output_aliases={} if first else {5: 0, 6: 1, 7: 2},
        scratch_shapes=[
            pltpu.VMEM((total, cc), BF16),
            pltpu.VMEM((total, cc), BF16),
            pltpu.VMEM((block, cc), F32),
            pltpu.VMEM((cc, block), F32),
            pltpu.VMEM((2, part, cc), F32),
            pltpu.SemaphoreType.DMA((4,)),
        ],
        compiler_params=params(24),
        cost_estimate=cost(0, 12 * total * cc),
    )(*operands)


def qkv_out_kernel(width, ids, *refs):
    srcs, out, rows, sem = refs[:16], refs[16], refs[17], refs[18]
    c, s = ids[0], ids[1]
    part = 3 * width // 2
    group = QUAD * width

    def copies(place, head, tail):
        t0 = jnp.bitwise_xor(((place & 1) << 1) | (place >> 1), s) * width
        t1 = jnp.bitwise_xor(place, s) * width
        spans = (
            (head, 0, width, t0),
            (head, width, part - width, group + t0),
            (tail, 0, 2 * width - part, group + t1 + (part - width)),
            (tail, 2 * width - part, width, 2 * group + t1),
        )
        return [
            pltpu.make_async_copy(
                src.at[pl.ds(lo, size), :],
                rows.at[pl.ds(pl.multiple_of(dst, width // 2), size), :],
                sem.at[place, i],
            )
            for i, (src, lo, size, dst) in enumerate(spans)
        ]

    def run(pick):
        todo = []
        for p in range(QUAD):
            f0, r1, r0, f1 = srcs[4 * p : 4 * p + 4]
            todo += copies(p, *pick(f0, r1, r0, f1))
        for one in todo:
            one.start()
        for one in todo:
            one.wait()

    @pl.when(c == 0)
    def _():
        run(lambda f0, r1, r0, f1: (f0, r0))

    @pl.when(c != 0)
    def _():
        run(lambda f0, r1, r0, f1: (r1, f1))

    for i in range(3):
        out[:, i * group : (i + 1) * group] = rows[i * group : (i + 1) * group, :].astype(F32).T


def qkv_out(ids, srcs, width, shape):
    cc = srcs[0].shape[-1]
    return pl.pallas_call(
        functools.partial(qkv_out_kernel, width),
        in_specs=[SMEM] + [ANY] * 16,
        out_specs=VMEM,
        out_shape=jax.ShapeDtypeStruct(shape, F32),
        scratch_shapes=[
            pltpu.VMEM((3 * QUAD * width, cc), BF16),
            pltpu.SemaphoreType.DMA((QUAD, 4)),
        ],
        compiler_params=params(32),
        cost_estimate=cost(0, 6 * shape[0] * shape[1]),
    )(ids, *srcs)


def to_first(v):
    pairs = [(i, i ^ 1) for i in range(QUAD)] + [(QUAD + i, QUAD + (i ^ 2)) for i in range(QUAD)]
    return lax.ppermute(v, ("section", "seq"), pairs)


def to_second(v):
    pairs = [(i, i ^ 2) for i in range(QUAD)] + [(QUAD + i, QUAD + (i ^ 1)) for i in range(QUAD)]
    return lax.ppermute(v, ("section", "seq"), pairs)


def to_quad(v, k):
    return lax.ppermute(v, "seq", [(i, i ^ k) for i in range(QUAD)])


def to_core(v):
    return lax.ppermute(v, "section", [(0, 1), (1, 0)])


def dp_partner(v, step):
    n = lax.axis_size("dp")
    return lax.ppermute(v, "dp", [(i, i ^ step) for i in range(n)])


def dp_sum(v):
    n = lax.axis_size("dp")
    z = lax.axis_index("dp")
    rows, cc = v.shape
    piece = rows // n
    steps = []
    cur = v.reshape(n, piece, cc)
    step = 1
    while step < n:
        cur = cur.reshape(cur.shape[0] // 2, 2, piece, cc)
        low = (z & step) == 0
        away = jnp.where(low, cur[:, 1], cur[:, 0])
        keep = jnp.where(low, cur[:, 0], cur[:, 1])
        cur = (keep.astype(F32) + dp_partner(away, step).astype(F32)).astype(BF16)
        steps.append(step)
        step *= 2
    for step in reversed(steps):
        low = (z & step) == 0
        got = dp_partner(cur, step)
        cur = jnp.where(low, jnp.stack([cur, got], 1), jnp.stack([got, cur], 1))
        cur = cur.reshape(-1, piece, cc)
    return cur.reshape(rows, cc)


def add_low(a, b):
    return (a.astype(F32) + b.astype(F32)).astype(BF16)


def quad_gather(own):
    one = to_second(own)
    two = to_first(own)
    three = to_first(one)
    return [own, one, two, three]


def on_device(
    layer_in, cotangent, lengths, w_qkv, bias_qv, w_out, bias_out,
    gain_attn, gain_mlp, w_up, bias_up, w_down, bias_down,
):
    micro, _, span, cc = layer_in.shape
    model = w_out.shape[1]
    ff = w_up.shape[-1]
    hd = model // HEADS
    width = model // QUAD
    heads = width // hd
    c = lax.axis_index("section")
    s = lax.axis_index("seq")
    dp_count = lax.axis_size("dp")
    mine = c == 0

    x0 = lax.dynamic_index_in_dim(layer_in, c, 0, keepdims=False)[0]
    cot = lax.dynamic_index_in_dim(cotangent, c, 0, keepdims=False)[0]
    lens = lax.dynamic_index_in_dim(lengths, c, 0, keepdims=False)[0]
    e0 = lens[0]
    e1 = e0 + lens[1]
    e2 = e1 + lens[2]
    e3 = e2 + lens[3]
    ids = jnp.stack([c, s, e0, e1, e2, e3, c, s]).astype(jnp.int32)

    def row(v, n=ff):
        return jnp.pad(v, ((0, 0), (0, n - v.shape[-1])))

    qb = lax.dynamic_slice_in_dim(bias_qv, s * width, width, 1)
    vb = lax.dynamic_slice_in_dim(bias_qv, model + s * width, width, 1)
    heads_bias = jnp.concatenate([qb, jnp.zeros((1, width), F32), vb], 1)
    pv_own = jnp.concatenate(
        [row(v) for v in (bias_up, bias_out, bias_down, gain_attn, gain_mlp, heads_bias)]
        + [jnp.zeros((2, ff), F32)]
    )
    w3_own = jnp.concatenate(
        [lax.dynamic_slice_in_dim(w_qkv[0], i * model + s * width, width, 1) for i in range(3)], 1
    )
    pv_got = to_core(pv_own)
    w3_got = to_core(w3_own)
    wo_got = to_core(w_out[0])
    up = (w_up, to_core(w_up))
    dn = (w_down, to_core(w_down))
    pv = [jnp.where(mine, pv_own, pv_got), jnp.where(mine, pv_got, pv_own)]
    w3 = [jnp.where(mine, w3_own, w3_got), jnp.where(mine, w3_got, w3_own)]
    wo = [jnp.where(mine, w_out[0], wo_got), jnp.where(mine, wo_got, w_out[0])]

    x = x0
    normed = first_norm(x0, pv[0])
    saved = []
    squares = []
    for l in range(2):
        blocks = quad_gather(normed)
        qh, kh, vh, lse, *att = attn_fwd(ids, blocks, w3[l], pv[l], heads, hd)
        att = [att[0]] + [to_quad(att[k], k) for k in (1, 2, 3)]
        mid, u, xout, normed, sq, astk = mlp_fwd(
            l, ids, x, att, wo[l], pv[l], pv[min(l + 1, 1)], up, dn
        )
        saved.append((x, blocks, (qh, kh, vh, lse), astk, mid, u))
        squares.append(sq[0, 0])
        x = xout
    outs = [saved[1][0], x]

    df = cot
    grads = [None, None]
    smalls = [None, None]
    in_grads = [None, None]
    for l in (1, 0):
        xl, blocks, qkvl, astk, mid, u = saved[l]
        lr, rr, dmid, dmlow, g, *douts = mlp_bwd(l, ids, df, u, mid, wo[l], pv[l], up, dn)
        douts = [douts[0]] + [to_quad(douts[k], k) for k in (1, 2, 3)]
        got = [None] * QUAD
        for p in (3, 1, 2, 0):
            got[p] = to_core(product(True, p, ids, lr, rr, astk, dmlow))
        tot = [None] * QUAD
        for p in (3, 1, 2, 0):
            tot[p] = product(False, p, ids, lr, rr, astk, dmlow, got[p])
        half1 = add_low(tot[1], to_first(tot[3]))
        half0 = add_low(tot[0], to_first(tot[2]))
        quarter = add_low(half0, to_second(half1))

        p0, p1, p2, p3, gs, gk, gb = attn_bwd(ids, blocks, w3[l], qkvl, douts)
        q1 = add_low(p1, to_first(p3))
        dx, gg = input_grad_of(p0, to_first(p2), to_second(q1), dmid, xl, pv[l])
        tq = add_low(gk, to_core(gs))
        grads[l] = (quad_gather(dp_sum(quarter)), quad_gather(dp_sum(tq)))

        spot = jnp.arange(QUAD)[:, None] == s
        qs = jnp.where(spot, gb[0:1, :width], 0.0).reshape(model)
        vs = jnp.where(spot, gb[0:1, 2 * width :], 0.0).reshape(model)
        pad = jnp.zeros((1,), F32)
        smalls[l] = jnp.concatenate(
            [g[0], g[1, :cc], pad, g[2, :cc], pad, gg[0, :cc], pad, g[4, :cc], pad, qs, vs]
            + [jnp.broadcast_to(squares[l], (128,))]
        ).reshape(-1, 128)
        in_grads[l] = dx
        df = dx

    small = jnp.where(mine, smalls[0], smalls[1]) + to_core(jnp.where(mine, smalls[1], smalls[0]))
    for k in (1, 2):
        small = small + to_quad(small, k)
    step = 1
    while step < dp_count:
        small = small + dp_partner(small, step)
        step *= 2
    small = small.reshape(-1)

    def handed(l, i):
        pairs = [(1, 0)] if l == 0 else [(0, 1)]
        return [lax.ppermute(f, "section", pairs) for f in grads[l][i]]

    shapes = [(ff, cc), (cc, ff), (model, cc)]
    outs_w = None
    r1m, r0m = handed(1, 0), handed(0, 0)
    r1q, r0q = handed(1, 1), handed(0, 1)
    srcs = []
    for p in range(QUAD):
        srcs += [grads[0][1][p], r1q[p], r0q[p], grads[1][1][p]]
    grad_qkv = qkv_out(ids, srcs, width, (cc, 3 * model))
    for p in range(QUAD):
        outs_w = place_rows(
            p, ids, [grads[0][0][p], r1m[p], r0m[p], grads[1][0][p]], outs_w, shapes
        )
    grad_down, grad_up, grad_out = outs_w

    def both(pair):
        own = jnp.where(mine, pair[0], pair[1])
        got = to_core(jnp.where(mine, pair[1], pair[0]))
        return jnp.where(mine, jnp.stack([own, got]), jnp.stack([got, own]))[None, :, None]

    layer_out = both(outs)
    input_grad = both(in_grads)

    def take(lo, n):
        return small[lo : lo + n][None]

    d = cc + 1
    at = ff
    total = micro * dp_count * span * QUAD
    base = ff + 4 * d
    rms = jnp.sqrt(small[base + 2 * model] / total).reshape(1)
    return (
        layer_out,
        input_grad,
        grad_qkv[None],
        take(base, 2 * model),
        grad_out[None],
        take(at, cc),
        take(at + 2 * d, cc),
        take(at + 3 * d, cc),
        grad_up[None],
        take(0, ff),
        grad_down[None],
        take(at + d, cc),
        rms,
    )


def solution(mesh):
    two = P("section", None)
    three = P("section", None, None)
    tokens = P(None, "dp", "seq", None)
    stacked = P("section", None, "dp", "seq", None)
    return jax.shard_map(
        on_device,
        mesh=mesh,
        in_specs=(
            tokens, tokens, P(None, "dp", None), three, two, three, two, two, two, three, two, three, two,
        ),
        out_specs=(
            stacked, stacked, three, two, three, two, two, two, three, two, three, two, P("section"),
        ),
        check_vma=False,
    )
```

```python
import functools

import jax
import jax.numpy as jnp
from jax import lax
from jax.experimental import pallas as pl
from jax.experimental.pallas import tpu as pltpu
from jax.sharding import PartitionSpec as P

HEADS = 12
EPS = 1e-6
NEG = -1e30
F32 = jnp.float32
BF16 = jnp.bfloat16
MIB = 1 << 20
QUAD = 4


def nn(a, b):
    return lax.dot_general(a, b, (((1,), (0,)), ((), ())), preferred_element_type=F32)


def nt(a, b):
    return lax.dot_general(a, b, (((1,), (1,)), ((), ())), preferred_element_type=F32)


def tn(a, b):
    return lax.dot_general(a, b, (((0,), (0,)), ((), ())), preferred_element_type=F32)


def order(core, k):
    return jnp.where(core == 1, k, ((k & 1) << 1) | (k >> 1))


def crms_scale(v):
    sq = jnp.sum(v * v, axis=-1, keepdims=True)
    su = jnp.sum(v, axis=-1, keepdims=True)
    full = v.shape[-1] + 1
    return lax.rsqrt((sq + su * su) / full + EPS), su, (sq + su * su) / full


def crms_back(v, gain, grad):
    r, su, _ = crms_scale(v)
    gd = grad * gain
    w = jnp.sum(gd * v, axis=-1, keepdims=True)
    unit = v * r
    dv = gd * r - (w * r * r * r / (v.shape[-1] + 1)) * (v + su)
    return dv, grad * unit, unit * gain


GC = 0.7978845608028654


def gelu_parts(u):
    inner = GC * (u + 0.044715 * (u * u * u))
    th = jnp.tanh(inner)
    return th


def params(mib, **kw):
    return pltpu.CompilerParams(vmem_limit_bytes=mib * MIB, **kw)


def cost(flops, nbytes, trans=0):
    return pl.CostEstimate(flops=int(flops), bytes_accessed=int(nbytes), transcendentals=int(trans))


SMEM = pl.BlockSpec(memory_space=pltpu.SMEM)
VMEM = pl.BlockSpec(memory_space=pltpu.VMEM)
HBM = pl.BlockSpec(memory_space=pltpu.HBM)


def rows_in_kernel(ids, v, o):
    @pl.when(ids[0] == 0)
    def _():
        o[...] = v[:, 0, :].T

    @pl.when(ids[0] != 0)
    def _():
        o[...] = v[:, 1, :].T


def rows_in(ids, v):
    micro, _, span, cc = v.shape
    return pl.pallas_call(
        rows_in_kernel,
        in_specs=[SMEM, VMEM],
        out_specs=VMEM,
        out_shape=jax.ShapeDtypeStruct((span, cc), BF16),
        compiler_params=params(16),
        cost_estimate=cost(0, 6 * span * cc),
    )(ids, jnp.transpose(v[:, 0], (2, 0, 1)))


def rows_out_kernel(ids, own, got, o):
    @pl.when(ids[0] == 0)
    def _():
        o[:, 0, :] = own[...].T
        o[:, 1, :] = got[...].T

    @pl.when(ids[0] != 0)
    def _():
        o[:, 0, :] = got[...].T
        o[:, 1, :] = own[...].T


def rows_out(ids, own, got):
    span, cc = own.shape
    o = pl.pallas_call(
        rows_out_kernel,
        in_specs=[SMEM, VMEM, VMEM],
        out_specs=VMEM,
        out_shape=jax.ShapeDtypeStruct((cc, 2, span), BF16),
        compiler_params=params(16),
        cost_estimate=cost(0, 8 * span * cc),
    )(ids, own, got)
    return jnp.transpose(o, (1, 2, 0))[None, :, None]


def visible_bias(ids, n, t, span):
    i = t * span + lax.broadcasted_iota(jnp.int32, (1, span), 1)
    start = jnp.zeros((1, span), jnp.int32)
    for d in range(4):
        end = ids[2 + d]
        start = jnp.maximum(start, jnp.where(i >= end, end, 0))
    j = lax.broadcasted_iota(jnp.int32, (n, span), 0)
    return jnp.where((j >= start) & (j <= i), 0.0, NEG)


def attn_fwd_kernel(
    raw, ids, n0, n1, n2, n3, w_ref, pv_ref, qh, kh, vh, lse, a0, a1, a2, a3, *rest
):
    c, s = ids[0], ids[1]
    heads, _, hd = qh.shape
    span, cc = n0.shape
    width = heads * hd
    at, bias_scr = rest[-2:]
    bias = pv_ref[5:6, : 3 * width]
    for p, nb in enumerate((n0, n1, n2, n3)):
        t = jnp.bitwise_xor(order(c, p), s)
        row = pl.multiple_of(t * span, span)
        rows = nb[...]
        if raw:
            v = rows.astype(F32)
            rows = (v * crms_scale(v)[0] * pv_ref[3:4, :cc]).astype(BF16)
            rest[p][...] = rows
        y = nn(rows, w_ref[...]) + bias
        for h in range(heads):
            lo = h * hd
            qh[h, pl.ds(row, span), :] = (y[:, lo : lo + hd] * (hd**-0.5)).astype(BF16)
            kh[h, pl.ds(row, span), :] = y[:, width + lo : width + lo + hd].astype(BF16)
            vh[h, pl.ds(row, span), :] = y[:, 2 * width + lo : 2 * width + lo + hd].astype(BF16)
    for t in range(QUAD):
        n = span * (t + 1)
        bias_scr[:n, :] = visible_bias(ids, n, t, span)

        def head(h, carry, t=t, n=n):
            q = qh[h, t * span : (t + 1) * span, :]
            sc = nt(kh[h, :n, :], q) + bias_scr[:n, :]
            m = jnp.max(sc, axis=0, keepdims=True)
            e = jnp.exp(sc - m)
            tot = jnp.sum(e, axis=0, keepdims=True)
            pr = (e * (1.0 / tot)).astype(BF16)
            o = tn(vh[h, :n, :], pr)
            at[t, pl.ds(pl.multiple_of(h * hd, hd), hd), :] = o.astype(BF16)
            lse[h, t : t + 1, :] = m + jnp.log(tot)
            return carry

        lax.fori_loop(0, heads, head, 0)
    for k, a in enumerate((a0, a1, a2, a3)):
        a[...] = at[jnp.bitwise_xor(s, k)]


def attn_fwd(raw, ids, blocks, w3, pv, heads, hd):
    span, width = blocks[0].shape
    full = span * QUAD
    hh = jax.ShapeDtypeStruct((heads, full, hd), BF16)
    aa = jax.ShapeDtypeStruct((heads * hd, span), BF16)
    normed = [jax.ShapeDtypeStruct((span, width), BF16)] * (QUAD if raw else 0)
    return pl.pallas_call(
        functools.partial(attn_fwd_kernel, raw),
        in_specs=[SMEM] + [VMEM] * 6,
        out_specs=[VMEM] * (8 + len(normed)),
        out_shape=[hh, hh, hh, jax.ShapeDtypeStruct((heads, QUAD, span), F32), aa, aa, aa, aa] + normed,
        scratch_shapes=[
            pltpu.VMEM((QUAD, heads * hd, span), BF16),
            pltpu.VMEM((full, span), F32),
        ],
        compiler_params=params(40),
        cost_estimate=cost(
            2 * full * width * 3 * heads * hd + 3 * 4 * full * full * hd * heads,
            4 * full * width,
            heads * full * full,
        ),
    )(ids, *blocks, w3, pv)


def mlp_fwd_kernel(
    layer, ids, x, a0, a1, a2, a3, wo, pv, pvn, pvb, upo, upr, dno, dnr,
    mid, u, xout, nnext, sq, astk, nm, acc,
):
    j = pl.program_id(0)
    c, s = ids[0], ids[1]
    cc = x.shape[-1]
    own = c == layer

    @pl.when(j == 0)
    def _():
        rows = a0.shape[0]
        m = x[...].astype(F32) + pv[1:2, :cc]
        for k, a in enumerate((a0, a1, a2, a3)):
            row = pl.multiple_of(jnp.bitwise_xor(s, k) * rows, rows)
            m = m + tn(a[...], wo[pl.ds(row, rows), :])
            astk[jnp.bitwise_xor(s, k)] = a[...].T
        mid[...] = m
        r, _, _ = crms_scale(m)
        nm[...] = (m * r * pv[4:5, :cc]).astype(BF16)
        acc[...] = m + pv[2:3, :cc]

    wu = lax.select(own, upo[0], upr[0])
    wd = lax.select(own, dno[0], dnr[0])
    ub = nn(nm[...], wu) + pvb[0:1, :]
    u[...] = ub
    act = (0.5 * ub * (1.0 + gelu_parts(ub))).astype(BF16)
    acc[...] += nn(act, wd)

    @pl.when(j == pl.num_programs(0) - 1)
    def _():
        fin = acc[...]
        _, _, ms = crms_scale(fin)
        sq[...] = jnp.broadcast_to(jnp.sum(ms, axis=0, keepdims=True), sq.shape)
        low = fin.astype(BF16)
        xout[...] = low
        lf = low.astype(F32)
        r, _, _ = crms_scale(lf)
        nnext[...] = (lf * r * pvn[3:4, :cc]).astype(BF16)


def mlp_fwd(layer, ids, x, att, wo, pv, pvn, up, dn):
    span, cc = x.shape
    ff = up[0].shape[-1]
    fb = ff // 8
    rows = att[0].shape[0]

    def whole(shape):
        return pl.BlockSpec(shape, lambda j, ids: (0,) * len(shape))

    def pick(mine):
        return lambda j, ids: jnp.where((ids[0] == layer) == mine, j, 0)

    mine, other = pick(True), pick(False)
    grid = pltpu.PrefetchScalarGridSpec(
        num_scalar_prefetch=1,
        grid=(8,),
        in_specs=[whole((span, cc))]
        + [whole((rows, span))] * 4
        + [whole(wo.shape), whole(pv.shape), whole(pvn.shape)]
        + [
            pl.BlockSpec((8, fb), lambda j, ids: (0, j)),
            pl.BlockSpec((1, cc, fb), lambda j, ids: (0, 0, mine(j, ids))),
            pl.BlockSpec((1, cc, fb), lambda j, ids: (0, 0, other(j, ids))),
            pl.BlockSpec((1, fb, cc), lambda j, ids: (0, mine(j, ids), 0)),
            pl.BlockSpec((1, fb, cc), lambda j, ids: (0, other(j, ids), 0)),
        ],
        out_specs=[
            whole((span, cc)),
            pl.BlockSpec((span, fb), lambda j, ids: (0, j)),
            whole((span, cc)),
            whole((span, cc)),
            whole((8, 128)),
            whole((QUAD, span, rows)),
        ],
        scratch_shapes=[pltpu.VMEM((span, cc), BF16), pltpu.VMEM((span, cc), F32)],
    )
    return pl.pallas_call(
        functools.partial(mlp_fwd_kernel, layer),
        grid_spec=grid,
        out_shape=[
            jax.ShapeDtypeStruct((span, cc), F32),
            jax.ShapeDtypeStruct((span, ff), F32),
            jax.ShapeDtypeStruct((span, cc), BF16),
            jax.ShapeDtypeStruct((span, cc), BF16),
            jax.ShapeDtypeStruct((8, 128), F32),
            jax.ShapeDtypeStruct((QUAD, span, rows), BF16),
        ],
        compiler_params=params(40, dimension_semantics=("arbitrary",)),
        cost_estimate=cost(6 * span * cc * ff, 4 * cc * ff + 4 * span * ff, span * ff),
    )(ids, x, *att, wo, pv, pvn, pv, up[0], up[1], dn[0], dn[1])


def mlp_bwd_kernel(
    layer, ids, df, u, mid, wo, pv, upo, upr, dno, dnr,
    lr, rr, dmid, g, d0, d1, d2, d3, acc, wide,
):
    j = pl.program_id(0)
    c, s = ids[0], ids[1]
    cc = df.shape[-1]
    fb = u.shape[-1]
    own = c == layer

    @pl.when(j == 0)
    def _():
        acc[...] = jnp.zeros_like(acc)
        g[...] = jnp.zeros_like(g)

    wu = lax.select(own, upo[0], upr[0])
    wd = lax.select(own, dno[0], dnr[0])
    da = nt(df[...], wd)
    ub = u[...]
    th = gelu_parts(ub)
    half = 0.5 * (1.0 + th)
    lr[0] = (ub * half).astype(BF16)
    slope = half + 0.5 * ub * (1.0 - th * th) * (GC * (1.0 + 3 * 0.044715 * (ub * ub)))
    du = (slope * da).astype(BF16)
    lr[1] = du
    g[0:1, pl.ds(pl.multiple_of(j * fb, 128), fb)] = jnp.sum(du.astype(F32), axis=0, keepdims=True)
    acc[...] += nt(du, wu)

    @pl.when(j == pl.num_programs(0) - 1)
    def _():
        dff = df[...].astype(F32)
        dv, gg, nm = crms_back(mid[...], pv[4:5, :cc], acc[...])
        dm = dff + dv
        low = dm.astype(BF16)
        dmid[...] = dm
        quarter = rr.shape[-1]
        wide[:, cc:] = jnp.zeros((wide.shape[0], wide.shape[1] - cc), BF16)
        for i, v in enumerate((df[...], nm.astype(BF16), low)):
            wide[:, :cc] = v
            for t in range(QUAD):
                rr[i, t] = wide[:, t * quarter : (t + 1) * quarter]
        g[1:2, :cc] = jnp.sum(low.astype(F32), axis=0, keepdims=True)
        g[2:3, :cc] = jnp.sum(dff, axis=0, keepdims=True)
        g[4:5, :cc] = jnp.sum(gg, axis=0, keepdims=True)
        rows = d0.shape[0]
        for k, d in enumerate((d0, d1, d2, d3)):
            row = pl.multiple_of(jnp.bitwise_xor(s, k) * rows, rows)
            d[...] = nt(wo[pl.ds(row, rows), :], low).astype(BF16)


def mlp_bwd(layer, ids, df, u, mid, wo, pv, up, dn):
    span, cc = df.shape
    ff = u.shape[-1]
    fb = ff // 8
    rows = wo.shape[0] // QUAD

    def whole(shape):
        return pl.BlockSpec(shape, lambda j, ids: (0,) * len(shape))

    def pick(mine):
        return lambda j, ids: jnp.where((ids[0] == layer) == mine, j, 0)

    mine, other = pick(True), pick(False)
    grid = pltpu.PrefetchScalarGridSpec(
        num_scalar_prefetch=1,
        grid=(8,),
        in_specs=[
            whole((span, cc)),
            pl.BlockSpec((span, fb), lambda j, ids: (0, j)),
            whole((span, cc)),
            whole(wo.shape),
            whole(pv.shape),
            pl.BlockSpec((1, cc, fb), lambda j, ids: (0, 0, mine(j, ids))),
            pl.BlockSpec((1, cc, fb), lambda j, ids: (0, 0, other(j, ids))),
            pl.BlockSpec((1, fb, cc), lambda j, ids: (0, mine(j, ids), 0)),
            pl.BlockSpec((1, fb, cc), lambda j, ids: (0, other(j, ids), 0)),
        ],
        out_specs=[
            pl.BlockSpec((2, span, fb), lambda j, ids: (0, 0, j)),
            whole((3, QUAD, span, (cc + 1) // QUAD)),
            whole((span, cc)),
            whole((8, ff)),
        ]
        + [whole((rows, span))] * 4,
        scratch_shapes=[pltpu.VMEM((span, cc), F32), pltpu.VMEM((span, cc + 1), BF16)],
    )
    dd = jax.ShapeDtypeStruct((rows, span), BF16)
    return pl.pallas_call(
        functools.partial(mlp_bwd_kernel, layer),
        grid_spec=grid,
        out_shape=[
            jax.ShapeDtypeStruct((2, span, ff), BF16),
            jax.ShapeDtypeStruct((3, QUAD, span, (cc + 1) // QUAD), BF16),
            jax.ShapeDtypeStruct((span, cc), F32),
            jax.ShapeDtypeStruct((8, ff), F32),
            dd, dd, dd, dd,
        ],
        compiler_params=params(40, dimension_semantics=("arbitrary",)),
        cost_estimate=cost(6 * span * cc * ff, 4 * cc * ff + 8 * span * ff, span * ff),
    )(ids, df, u, mid, wo, pv, up[0], up[1], dn[0], dn[1])


def product_kernel(send, places, ids, lr, rr, att, *rest):
    outs = rest[-len(places) :]
    core = 1 - ids[0] if send else ids[0]
    ff = lr.shape[-1]
    part = att.shape[-1]
    for i, place in enumerate(places):
        t = jnp.bitwise_xor(order(core, place), ids[1])
        out = outs[i]
        main = tn(rr[core, t], lr[core])
        low = rr[2, t]
        sides = [tn(low, att[2 * core + h]) for h in range(2)]
        if not send:
            got = rest[i]
            main = main + got[:, :ff].astype(F32)
            sides = [v + got[:, ff + h * part : ff + (h + 1) * part].astype(F32) for h, v in enumerate(sides)]
        out[:, :ff] = main.astype(BF16)
        for h, v in enumerate(sides):
            out[:, ff + h * part : ff + (h + 1) * part] = v.astype(BF16)


def product(send, places, ids, lr, rr, att, got=()):
    span, quarter = rr.shape[2:]
    cols = lr.shape[-1] + 2 * att.shape[-1]
    return pl.pallas_call(
        functools.partial(product_kernel, send, places),
        in_specs=[SMEM] + [VMEM] * (3 + len(got)),
        out_specs=[VMEM] * len(places),
        out_shape=[jax.ShapeDtypeStruct((quarter, cols), BF16)] * len(places),
        compiler_params=params(32),
        cost_estimate=cost(2 * span * quarter * cols * len(places), 2 * 4 * quarter * cols * len(places)),
    )(ids, lr, rr, att, *got)


def attn_bwd_kernel(
    ids, n0, n1, n2, n3, w_ref, qh, kh, vh, lse, d0, d1, d2, d3,
    p0, p1, p2, p3, gs, gk, gb, do, dk, dv, dy, acc, bias_scr,
):
    c, s = ids[0], ids[1]
    heads, _, hd = qh.shape
    span, cc = n0.shape
    width = heads * hd
    for k, d in enumerate((d0, d1, d2, d3)):
        do[jnp.bitwise_xor(s, k)] = d[...]
    for t in reversed(range(QUAD)):
        n = span * (t + 1)
        bias_scr[:n, :] = visible_bias(ids, n, t, span)
        for h in range(heads):
            q = qh[h, t * span : (t + 1) * span, :]
            kk = kh[h, :n, :]
            sc = nt(kk, q) + (bias_scr[:n, :] - lse[h, t : t + 1, :])
            pr = jnp.exp(sc)
            dot = do[t, h * hd : (h + 1) * hd, :]
            dp = nn(vh[h, :n, :], dot)
            inner = jnp.sum(pr * dp, axis=0, keepdims=True)
            ds = (pr * (dp - inner)).astype(BF16)
            newk = nn(ds, q)
            newv = nt(pr.astype(BF16), dot)
            if t == QUAD - 1:
                dk[h, :n, :] = newk
                dv[h, :n, :] = newv
            else:
                dk[h, :n, :] += newk
                dv[h, :n, :] += newv
            dq = tn(kk, ds) * (hd**-0.5)
            dy[t * span : (t + 1) * span, h * hd : (h + 1) * hd] = dq.T.astype(BF16)
    for h in range(heads):
        dy[:, width + h * hd : width + (h + 1) * hd] = dk[h].astype(BF16)
        dy[:, 2 * width + h * hd : 2 * width + (h + 1) * hd] = dv[h].astype(BF16)
    total = jnp.zeros((1, 3 * width), F32)
    for p, (nb, out) in enumerate(((n0, p0), (n1, p1), (n2, p2), (n3, p3))):
        row = pl.multiple_of(jnp.bitwise_xor(order(c, p), s) * span, span)
        y = dy[pl.ds(row, span), :]
        out[...] = nt(y, w_ref[...]).astype(BF16)
        total = total + jnp.sum(y.astype(F32), axis=0, keepdims=True)
        g = tn(nb[...], y)
        if p == 0:
            acc[:cc, :] = g
        else:
            acc[:cc, :] += g
    gb[...] = jnp.broadcast_to(total, gb.shape)
    part = gs.shape[0]
    acc[cc:, :] = jnp.zeros((acc.shape[0] - cc, acc.shape[1]), F32)
    gk[...] = acc[pl.ds(pl.multiple_of(c * part, part), part), :].astype(BF16)
    gs[...] = acc[pl.ds(pl.multiple_of((1 - c) * part, part), part), :].astype(BF16)


def attn_bwd(ids, blocks, w3, qkvl, douts):
    span, cc = blocks[0].shape
    heads, full, hd = qkvl[0].shape
    width = heads * hd
    pp = jax.ShapeDtypeStruct((span, cc), BF16)
    gg = jax.ShapeDtypeStruct(((cc + 1) // 2, 3 * width), BF16)
    return pl.pallas_call(
        attn_bwd_kernel,
        in_specs=[SMEM] + [VMEM] * 13,
        out_specs=[VMEM] * 7,
        out_shape=[pp, pp, pp, pp, gg, gg, jax.ShapeDtypeStruct((8, 3 * width), F32)],
        scratch_shapes=[
            pltpu.VMEM((QUAD, width, span), BF16),
            pltpu.VMEM((heads, full, hd), F32),
            pltpu.VMEM((heads, full, hd), F32),
            pltpu.VMEM((full, 3 * width), BF16),
            pltpu.VMEM((cc + 1, 3 * width), F32),
            pltpu.VMEM((full, span), F32),
        ],
        compiler_params=params(48),
        cost_estimate=cost(
            4 * full * cc * 3 * width + 3 * 10 * full * full * hd * heads,
            8 * full * cc,
            heads * full * full,
        ),
    )(ids, *blocks, w3, *qkvl, *douts)


def input_kernel(part, r0, r1, dmid, x, pv, dx, gg):
    cc = x.shape[-1]
    dn = part[...].astype(F32) + r0[...].astype(F32) + r1[...].astype(F32)
    dv, g, _ = crms_back(x[...].astype(F32), pv[3:4, :cc], dn)
    dx[...] = (dmid[...] + dv).astype(BF16)
    gg[...] = jnp.broadcast_to(jnp.sum(g, axis=0, keepdims=True), gg.shape)


def input_grad_of(part, r0, r1, dmid, x, pv):
    return pl.pallas_call(
        input_kernel,
        in_specs=[VMEM] * 6,
        out_specs=[VMEM] * 2,
        out_shape=[
            jax.ShapeDtypeStruct(x.shape, BF16),
            jax.ShapeDtypeStruct((8, x.shape[-1]), F32),
        ],
        compiler_params=params(16),
        cost_estimate=cost(0, x.size * 14),
    )(part, r0, r1, dmid, x, pv)


def both_lengths(t, rows, start):
    @pl.when(t < QUAD - 1)
    def _():
        start(rows)

    @pl.when(t == QUAD - 1)
    def _():
        start(rows - 1)


def place_kernel(place, first, ids, *refs):
    srcs = refs[:4]
    outs = refs[4:7] if first else refs[7:10]
    x0, x1, od, ou, ow, sem = refs[7:] if first else refs[10:]
    c, s = ids[0], ids[1]
    down, up, wout = outs
    rows, _, ff = od.shape
    part = ow.shape[-1]

    def load(a, b):
        moves = [pltpu.make_async_copy(a, x0, sem.at[0]), pltpu.make_async_copy(b, x1, sem.at[1])]
        for m in moves:
            m.start()
        for m in moves:
            m.wait()

    @pl.when(c == 0)
    def _():
        load(srcs[0], srcs[1])

    @pl.when(c != 0)
    def _():
        load(srcs[2], srcs[3])

    t0 = jnp.bitwise_xor(((place & 1) << 1) | (place >> 1), s)
    t1 = jnp.bitwise_xor(place, s)

    def moves(n, t, i, src, dst, lo, cols):
        return [
            pltpu.make_async_copy(src.at[pl.ds(0, n)], dst.at[pl.ds(t * rows, n)], sem.at[2 * i]),
            pltpu.make_async_copy(
                ow.at[i, pl.ds(0, n)], wout.at[pl.ds(t * rows, n), :, pl.ds(lo, cols)], sem.at[2 * i + 1]
            ),
        ]

    jobs = ((t0, 0, x0, od, down, 0), (t1, 1, x1, ou, up, part))
    for t, i, x, o, dst, lo in jobs:
        o[:, 0, :] = x[:, :ff].astype(F32)
        ow[i, :, 0, :] = x[:, ff:].astype(F32)
        both_lengths(t, rows, lambda n: [m.start() for m in moves(n, t, i, o, dst, lo, part)])
    for t, i, x, o, dst, lo in jobs:
        both_lengths(t, rows, lambda n: [m.wait() for m in moves(n, t, i, o, dst, lo, part)])


def place_rows(place, ids, srcs, outs, cc, ff, model):
    rows, cols = srcs[0].shape
    first = outs is None
    operands = [ids, *srcs] + ([] if first else list(outs))
    return pl.pallas_call(
        functools.partial(place_kernel, place, first),
        in_specs=[SMEM] + [HBM] * (len(operands) - 1),
        out_specs=[HBM] * 3,
        out_shape=[jax.ShapeDtypeStruct((cc, 1, n), F32) for n in (ff, ff, model)],
        input_output_aliases={} if first else {5: 0, 6: 1, 7: 2},
        scratch_shapes=[
            pltpu.VMEM((rows, cols), BF16),
            pltpu.VMEM((rows, cols), BF16),
            pltpu.VMEM((rows, 1, ff), F32),
            pltpu.VMEM((rows, 1, ff), F32),
            pltpu.VMEM((2, rows, 1, cols - ff), F32),
            pltpu.SemaphoreType.DMA((4,)),
        ],
        compiler_params=params(32),
        cost_estimate=cost(0, 12 * rows * cols),
    )(*operands)


def qkv_out_kernel(ids, *refs):
    srcs, out, rows, wide, od, sem = refs[:8], *refs[8:]
    c, s = ids[0], ids[1]
    width = rows.shape[-1] // 3

    def load(four):
        todo = [
            pltpu.make_async_copy(src, rows.at[jnp.bitwise_xor(s, k)], sem.at[k])
            for k, src in enumerate(four)
        ]
        for m in todo:
            m.start()
        for m in todo:
            m.wait()

    @pl.when(c == 0)
    def _():
        load(srcs[:4])

    @pl.when(c != 0)
    def _():
        load(srcs[4:])

    step = rows.shape[1] // QUAD
    moves = []
    for b in range(QUAD):
        if b >= 2:
            moves[b - 2].wait()
        for t in range(QUAD):
            v = rows[t, b * step : (b + 1) * step, :].astype(F32)
            for i in range(3):
                lo = (i * QUAD + t) * width
                wide[:, lo : lo + width] = v[:, i * width : (i + 1) * width]
        od[b % 2, :, 0, :] = wide[...]
        n = step - (b == QUAD - 1)
        m = pltpu.make_async_copy(
            od.at[b % 2, pl.ds(0, n)], out.at[pl.ds(b * step, n)], sem.at[QUAD + b % 2]
        )
        m.start()
        moves.append(m)
    for m in moves[-2:]:
        m.wait()


def qkv_out(ids, srcs, cc):
    _, half, cols = srcs[0].shape
    full = 2 * half
    return pl.pallas_call(
        qkv_out_kernel,
        in_specs=[SMEM] + [HBM] * 8,
        out_specs=HBM,
        out_shape=jax.ShapeDtypeStruct((cc, 1, QUAD * cols), F32),
        scratch_shapes=[
            pltpu.VMEM((QUAD, full, cols), BF16),
            pltpu.VMEM((full // QUAD, QUAD * cols), F32),
            pltpu.VMEM((2, full // QUAD, 1, QUAD * cols), F32),
            pltpu.SemaphoreType.DMA((QUAD + 2,)),
        ],
        compiler_params=params(32),
        cost_estimate=cost(0, 6 * cc * QUAD * cols),
    )(ids, *[v.reshape(full, cols) for v in srcs])


def to_first(v):
    pairs = [(i, i ^ 1) for i in range(QUAD)] + [(QUAD + i, QUAD + (i ^ 2)) for i in range(QUAD)]
    return lax.ppermute(v, ("section", "seq"), pairs)


def to_second(v):
    pairs = [(i, i ^ 2) for i in range(QUAD)] + [(QUAD + i, QUAD + (i ^ 1)) for i in range(QUAD)]
    return lax.ppermute(v, ("section", "seq"), pairs)


def to_quad(v, k):
    return lax.ppermute(v, "seq", [(i, i ^ k) for i in range(QUAD)])


def to_core(v):
    return lax.ppermute(v, "section", [(0, 1), (1, 0)])


def dp_partner(v, step):
    n = lax.axis_size("dp")
    return lax.ppermute(v, "dp", [(i, i ^ step) for i in range(n)])


def dp_scatter(v):
    n = lax.axis_size("dp")
    z = lax.axis_index("dp")
    rows, cols = v.shape
    piece = rows // n
    cur = v.reshape(n, piece, cols)
    step = 1
    while step < n:
        cur = cur.reshape(cur.shape[0] // 2, 2, piece, cols)
        low = (z & step) == 0
        away = jnp.where(low, cur[:, 1], cur[:, 0])
        keep = jnp.where(low, cur[:, 0], cur[:, 1])
        cur = add_low(keep, dp_partner(away, step))
        step *= 2
    return cur[0]


def owner_gather(l, v):
    n = lax.axis_size("dp")
    z = lax.axis_index("dp")
    piece, cols = v.shape
    got = lax.ppermute(v, "section", [(1 - l, l)])
    cur = jnp.stack([v, got] if l == 0 else [got, v])[:, None]
    step = n // 2
    while step:
        low = (z & step) == 0
        got = lax.ppermute(cur, ("section", "dp"), [(l * n + i, l * n + (i ^ step)) for i in range(n)])
        pairs = [
            jnp.where(low, jnp.stack([a, b], 1), jnp.stack([b, a], 1)).reshape(-1, piece, cols)
            for a, b in ((cur[0], got[0]), (cur[1], got[1]))
        ]
        step //= 2
        if step:
            cur = jnp.stack(pairs)
    return [w.reshape(n * piece, cols) for w in pairs]


def owner_quad(l, v, k):
    return lax.ppermute(
        v, ("section", "seq"), [(l * QUAD + i, l * QUAD + (i ^ k)) for i in range(QUAD)]
    )


def add_low(a, b):
    return (a.astype(F32) + b.astype(F32)).astype(BF16)


def quad_gather(own):
    one = to_second(own)
    two = to_first(own)
    three = to_first(one)
    return [own, one, two, three]


def on_device(
    layer_in, cotangent, lengths, w_qkv, bias_qv, w_out, bias_out,
    gain_attn, gain_mlp, w_up, bias_up, w_down, bias_down,
):
    micro, _, span, cc = layer_in.shape
    model = w_out.shape[1]
    ff = w_up.shape[-1]
    hd = model // HEADS
    width = model // QUAD
    heads = width // hd
    c = lax.axis_index("section")
    s = lax.axis_index("seq")
    dp_count = lax.axis_size("dp")
    mine = c == 0

    lens = lax.dynamic_index_in_dim(lengths, c, 0, keepdims=False)[0]
    e0 = lens[0]
    e1 = e0 + lens[1]
    e2 = e1 + lens[2]
    e3 = e2 + lens[3]
    ids = jnp.stack([c, s, e0, e1, e2, e3, c, s]).astype(jnp.int32)
    x = rows_in(ids, layer_in)

    def row(v, n=ff):
        return jnp.pad(v, ((0, 0), (0, n - v.shape[-1])))

    qb = lax.dynamic_slice_in_dim(bias_qv, s * width, width, 1)
    vb = lax.dynamic_slice_in_dim(bias_qv, model + s * width, width, 1)
    heads_bias = jnp.concatenate([qb, jnp.zeros((1, width), F32), vb], 1)
    pv_own = jnp.concatenate(
        [row(v) for v in (bias_up, bias_out, bias_down, gain_attn, gain_mlp, heads_bias)]
        + [jnp.zeros((2, ff), F32)]
    )
    w3_own = jnp.concatenate(
        [lax.dynamic_slice_in_dim(w_qkv[0], i * model + s * width, width, 1) for i in range(3)], 1
    )
    pv_got = to_core(pv_own)
    w3_got = to_core(w3_own)
    wo_got = to_core(w_out[0])
    up = (w_up, to_core(w_up))
    dn = (w_down, to_core(w_down))
    pv = [jnp.where(mine, pv_own, pv_got), jnp.where(mine, pv_got, pv_own)]
    w3 = [jnp.where(mine, w3_own, w3_got), jnp.where(mine, w3_got, w3_own)]
    wo = [jnp.where(mine, w_out[0], wo_got), jnp.where(mine, wo_got, w_out[0])]

    normed = x
    saved = []
    squares = []
    for l in range(2):
        blocks = quad_gather(normed)
        qh, kh, vh, lse, *att = attn_fwd(l == 0, ids, blocks, w3[l], pv[l], heads, hd)
        if l == 0:
            att, blocks = att[:QUAD], att[QUAD:]
        att = [att[0]] + [to_quad(att[k], k) for k in (1, 2, 3)]
        mid, u, xout, normed, sq, astk = mlp_fwd(
            l, ids, x, att, wo[l], pv[l], pv[min(l + 1, 1)], up, dn
        )
        saved.append((x, blocks, (qh, kh, vh, lse), astk, mid, u))
        squares.append(sq[0, 0])
        x = xout
    outs = [saved[1][0], x]

    df = rows_in(ids, cotangent)
    rows_of = [None, None]
    qkv_of = [None, None]
    smalls = [None, None]
    in_grads = [None, None]
    for l in (1, 0):
        xl, blocks, qkvl, astk, mid, u = saved[l]
        lr, rr, dmid, g, *douts = mlp_bwd(l, ids, df, u, mid, wo[l], pv[l], up, dn)
        douts = [douts[0]] + [to_quad(douts[k], k) for k in (1, 2, 3)]
        far = [to_core(v) for v in product(True, (3, 2), ids, lr, rr, astk)]
        near = [to_core(v) for v in product(True, (1, 0), ids, lr, rr, astk)]
        far = product(False, (3, 2), ids, lr, rr, astk, far)
        far, douts = lax.optimization_barrier((far, douts))
        near = product(False, (1, 0), ids, lr, rr, astk, near)
        half1 = add_low(near[0], to_first(far[0]))
        half0 = add_low(near[1], to_first(far[1]))
        quarter = add_low(half0, to_second(half1))

        p0, p1, p2, p3, gs, gk, gb = attn_bwd(ids, blocks, w3[l], qkvl, douts)
        q1 = add_low(p1, to_first(p3))
        dx, gg = input_grad_of(p0, to_first(p2), to_second(q1), dmid, xl, pv[l])

        f0, g0 = owner_gather(l, dp_scatter(quarter))
        f1, g1 = owner_quad(l, f0, 2), owner_quad(l, g0, 1)
        f2, g2 = owner_quad(l, f0, 1), owner_quad(l, g0, 2)
        f3, g3 = owner_quad(l, f1, 1), owner_quad(l, g1, 2)
        rows_of[l] = ((f0, g0), (f1, g1), (f2, g2), (f3, g3))

        tq = add_low(gk, to_core(gs))
        q0 = jnp.stack(owner_gather(l, dp_scatter(tq)))
        if l == 1:
            k1, k2 = owner_quad(l, q0, 1), owner_quad(l, q0, 2)
            k3 = owner_quad(l, k1, 2)
        else:
            k1, k2 = owner_quad(l, q0, 1), owner_quad(l, q0, 2)
            k3 = owner_quad(l, k2, 1)
        qkv_of[l] = [q0, k1, k2, k3]

        spot = jnp.arange(QUAD)[:, None] == s
        qs = jnp.where(spot, gb[0:1, :width], 0.0).reshape(model)
        vs = jnp.where(spot, gb[0:1, 2 * width :], 0.0).reshape(model)
        pad = jnp.zeros((1,), F32)
        smalls[l] = jnp.concatenate(
            [g[0], g[1, :cc], pad, g[2, :cc], pad, gg[0, :cc], pad, g[4, :cc], pad, qs, vs]
            + [jnp.broadcast_to(squares[l], (128,))]
        ).reshape(-1, 128)
        in_grads[l] = dx
        df = dx

    small = jnp.where(mine, smalls[0], smalls[1]) + to_core(jnp.where(mine, smalls[1], smalls[0]))
    for k in (1, 2):
        small = small + to_quad(small, k)
    step = 1
    while step < dp_count:
        small = small + dp_partner(small, step)
        step *= 2
    small = small.reshape(-1)

    grad_qkv = qkv_out(ids, [*qkv_of[0], *qkv_of[1]], cc)
    outs_w = None
    for p in range(QUAD):
        outs_w = place_rows(p, ids, [*rows_of[0][p], *rows_of[1][p]], outs_w, cc, ff, model)
    grad_down, grad_up, grad_out = outs_w

    def both(pair):
        own = jnp.where(mine, pair[0], pair[1])
        got = to_core(jnp.where(mine, pair[1], pair[0]))
        return rows_out(ids, own, got)

    layer_out = both(outs)
    input_grad = both(in_grads)

    def take(lo, n):
        return small[lo : lo + n][None]

    d = cc + 1
    at = ff
    total = micro * dp_count * span * QUAD
    base = ff + 4 * d
    rms = jnp.sqrt(small[base + 2 * model] / total).reshape(1)
    return (
        layer_out,
        input_grad,
        jnp.transpose(grad_qkv, (1, 0, 2)),
        take(base, 2 * model),
        jnp.transpose(grad_out, (1, 2, 0)),
        take(at, cc),
        take(at + 2 * d, cc),
        take(at + 3 * d, cc),
        jnp.transpose(grad_up, (1, 0, 2)),
        take(0, ff),
        jnp.transpose(grad_down, (1, 2, 0)),
        take(at + d, cc),
        rms,
    )


def solution(mesh):
    two = P("section", None)
    three = P("section", None, None)
    tokens = P(None, "dp", "seq", None)
    stacked = P("section", None, "dp", "seq", None)
    return jax.shard_map(
        on_device,
        mesh=mesh,
        in_specs=(
            tokens, tokens, P(None, "dp", None), three, two, three, two, two, two, three, two, three, two,
        ),
        out_specs=(
            stacked, stacked, three, two, three, two, two, two, three, two, three, two, P("section"),
        ),
        check_vma=False,
    )
```

```python
import functools

import jax
import jax.numpy as jnp
from jax import lax
from jax.experimental import pallas as pl
from jax.experimental.pallas import tpu as pltpu
from jax.sharding import PartitionSpec as P

HEADS = 12
EPS = 1e-6
NEG = -1e30
F32 = jnp.float32
BF16 = jnp.bfloat16
MIB = 1 << 20
QUAD = 4


def nn(a, b):
    return lax.dot_general(a, b, (((1,), (0,)), ((), ())), preferred_element_type=F32)


def nt(a, b):
    return lax.dot_general(a, b, (((1,), (1,)), ((), ())), preferred_element_type=F32)


def tn(a, b):
    return lax.dot_general(a, b, (((0,), (0,)), ((), ())), preferred_element_type=F32)


def order(core, k):
    return jnp.where(core == 1, k, ((k & 1) << 1) | (k >> 1))


def crms_scale(v):
    sq = jnp.sum(v * v, axis=-1, keepdims=True)
    su = jnp.sum(v, axis=-1, keepdims=True)
    full = v.shape[-1] + 1
    return lax.rsqrt((sq + su * su) / full + EPS), su, (sq + su * su) / full


def crms_back(v, gain, grad):
    r, su, _ = crms_scale(v)
    gd = grad * gain
    w = jnp.sum(gd * v, axis=-1, keepdims=True)
    unit = v * r
    dv = gd * r - (w * r * r * r / (v.shape[-1] + 1)) * (v + su)
    return dv, grad * unit, unit * gain


GC = 0.7978845608028654


def gelu_parts(u):
    inner = GC * (u + 0.044715 * (u * u * u))
    th = jnp.tanh(inner)
    return th


def params(mib, **kw):
    return pltpu.CompilerParams(vmem_limit_bytes=mib * MIB, **kw)


def cost(flops, nbytes, trans=0):
    return pl.CostEstimate(flops=int(flops), bytes_accessed=int(nbytes), transcendentals=int(trans))


SMEM = pl.BlockSpec(memory_space=pltpu.SMEM)
VMEM = pl.BlockSpec(memory_space=pltpu.VMEM)
HBM = pl.BlockSpec(memory_space=pltpu.HBM)


def rows_in_kernel(ids, v, o):
    @pl.when(ids[0] == 0)
    def _():
        o[...] = v[:, 0, :].T

    @pl.when(ids[0] != 0)
    def _():
        o[...] = v[:, 1, :].T


def rows_in(ids, v):
    micro, _, span, cc = v.shape
    return pl.pallas_call(
        rows_in_kernel,
        in_specs=[SMEM, VMEM],
        out_specs=VMEM,
        out_shape=jax.ShapeDtypeStruct((span, cc), BF16),
        compiler_params=params(16),
        cost_estimate=cost(0, 6 * span * cc),
    )(ids, jnp.transpose(v[:, 0], (2, 0, 1)))


def rows_out_kernel(ids, own, got, o):
    @pl.when(ids[0] == 0)
    def _():
        o[:, 0, :] = own[...].T
        o[:, 1, :] = got[...].T

    @pl.when(ids[0] != 0)
    def _():
        o[:, 0, :] = got[...].T
        o[:, 1, :] = own[...].T


def rows_out(ids, own, got):
    span, cc = own.shape
    o = pl.pallas_call(
        rows_out_kernel,
        in_specs=[SMEM, VMEM, VMEM],
        out_specs=VMEM,
        out_shape=jax.ShapeDtypeStruct((cc, 2, span), BF16),
        compiler_params=params(16),
        cost_estimate=cost(0, 8 * span * cc),
    )(ids, own, got)
    return jnp.transpose(o, (1, 2, 0))[None, :, None]


def visible_bias(ids, n, t, span):
    i = t * span + lax.broadcasted_iota(jnp.int32, (1, span), 1)
    start = jnp.zeros((1, span), jnp.int32)
    for d in range(4):
        end = ids[2 + d]
        start = jnp.maximum(start, jnp.where(i >= end, end, 0))
    j = lax.broadcasted_iota(jnp.int32, (n, span), 0)
    return jnp.where((j >= start) & (j <= i), 0.0, NEG)


def attn_fwd_kernel(
    raw, ids, n0, n1, n2, n3, w_ref, pv_ref, qh, kh, vh, lse, a0, a1, a2, a3, *rest
):
    c, s = ids[0], ids[1]
    heads, _, hd = qh.shape
    span, cc = n0.shape
    width = heads * hd
    at, bias_scr = rest[-2:]
    bias = pv_ref[5:6, : 3 * width]
    for p, nb in enumerate((n0, n1, n2, n3)):
        t = jnp.bitwise_xor(order(c, p), s)
        row = pl.multiple_of(t * span, span)
        rows = nb[...]
        if raw:
            v = rows.astype(F32)
            rows = (v * crms_scale(v)[0] * pv_ref[3:4, :cc]).astype(BF16)
            rest[p][...] = rows
        y = nn(rows, w_ref[...]) + bias
        for h in range(heads):
            lo = h * hd
            qh[h, pl.ds(row, span), :] = (y[:, lo : lo + hd] * (hd**-0.5)).astype(BF16)
            kh[h, pl.ds(row, span), :] = y[:, width + lo : width + lo + hd].astype(BF16)
            vh[h, pl.ds(row, span), :] = y[:, 2 * width + lo : 2 * width + lo + hd].astype(BF16)
    for t in range(QUAD):
        n = span * (t + 1)
        bias_scr[:n, :] = visible_bias(ids, n, t, span)

        def head(h, carry, t=t, n=n):
            q = qh[h, t * span : (t + 1) * span, :]
            sc = nt(kh[h, :n, :], q) + bias_scr[:n, :]
            m = jnp.max(sc, axis=0, keepdims=True)
            e = jnp.exp(sc - m)
            tot = jnp.sum(e, axis=0, keepdims=True)
            pr = (e * (1.0 / tot)).astype(BF16)
            o = tn(vh[h, :n, :], pr)
            at[t, pl.ds(pl.multiple_of(h * hd, hd), hd), :] = o.astype(BF16)
            lse[h, t : t + 1, :] = m + jnp.log(tot)
            return carry

        lax.fori_loop(0, heads, head, 0)
    for k, a in enumerate((a0, a1, a2, a3)):
        a[...] = at[jnp.bitwise_xor(s, k)]


def attn_fwd(raw, ids, blocks, w3, pv, heads, hd):
    span, width = blocks[0].shape
    full = span * QUAD
    hh = jax.ShapeDtypeStruct((heads, full, hd), BF16)
    aa = jax.ShapeDtypeStruct((heads * hd, span), BF16)
    normed = [jax.ShapeDtypeStruct((span, width), BF16)] * (QUAD if raw else 0)
    return pl.pallas_call(
        functools.partial(attn_fwd_kernel, raw),
        in_specs=[SMEM] + [VMEM] * 6,
        out_specs=[VMEM] * (8 + len(normed)),
        out_shape=[hh, hh, hh, jax.ShapeDtypeStruct((heads, QUAD, span), F32), aa, aa, aa, aa] + normed,
        scratch_shapes=[
            pltpu.VMEM((QUAD, heads * hd, span), BF16),
            pltpu.VMEM((full, span), F32),
        ],
        compiler_params=params(40),
        cost_estimate=cost(
            2 * full * width * 3 * heads * hd + 3 * 4 * full * full * hd * heads,
            4 * full * width,
            heads * full * full,
        ),
    )(ids, *blocks, w3, pv)


def mlp_fwd_kernel(
    layer, ids, x, a0, a1, a2, a3, wo, pv, pvn, pvb, upo, upr, dno, dnr,
    mid, u, xout, nnext, sq, astk, nm, acc,
):
    j = pl.program_id(0)
    c, s = ids[0], ids[1]
    cc = x.shape[-1]
    own = c == layer

    @pl.when(j == 0)
    def _():
        rows = a0.shape[0]
        m = x[...].astype(F32) + pv[1:2, :cc]
        for k, a in enumerate((a0, a1, a2, a3)):
            row = pl.multiple_of(jnp.bitwise_xor(s, k) * rows, rows)
            m = m + tn(a[...], wo[pl.ds(row, rows), :])
            astk[jnp.bitwise_xor(s, k)] = a[...].T
        mid[...] = m
        r, _, _ = crms_scale(m)
        nm[...] = (m * r * pv[4:5, :cc]).astype(BF16)
        acc[...] = m + pv[2:3, :cc]

    wu = lax.select(own, upo[0], upr[0])
    wd = lax.select(own, dno[0], dnr[0])
    ub = nn(nm[...], wu) + pvb[0:1, :]
    u[...] = ub
    act = (0.5 * ub * (1.0 + gelu_parts(ub))).astype(BF16)
    acc[...] += nn(act, wd)

    @pl.when(j == pl.num_programs(0) - 1)
    def _():
        fin = acc[...]
        _, _, ms = crms_scale(fin)
        sq[...] = jnp.broadcast_to(jnp.sum(ms, axis=0, keepdims=True), sq.shape)
        low = fin.astype(BF16)
        xout[...] = low
        lf = low.astype(F32)
        r, _, _ = crms_scale(lf)
        nnext[...] = (lf * r * pvn[3:4, :cc]).astype(BF16)


def mlp_fwd(layer, ids, x, att, wo, pv, pvn, up, dn):
    span, cc = x.shape
    ff = up[0].shape[-1]
    fb = ff // 8
    rows = att[0].shape[0]

    def whole(shape):
        return pl.BlockSpec(shape, lambda j, ids: (0,) * len(shape))

    def pick(mine):
        return lambda j, ids: jnp.where((ids[0] == layer) == mine, j, 0)

    mine, other = pick(True), pick(False)
    grid = pltpu.PrefetchScalarGridSpec(
        num_scalar_prefetch=1,
        grid=(8,),
        in_specs=[whole((span, cc))]
        + [whole((rows, span))] * 4
        + [whole(wo.shape), whole(pv.shape), whole(pvn.shape)]
        + [
            pl.BlockSpec((8, fb), lambda j, ids: (0, j)),
            pl.BlockSpec((1, cc, fb), lambda j, ids: (0, 0, mine(j, ids))),
            pl.BlockSpec((1, cc, fb), lambda j, ids: (0, 0, other(j, ids))),
            pl.BlockSpec((1, fb, cc), lambda j, ids: (0, mine(j, ids), 0)),
            pl.BlockSpec((1, fb, cc), lambda j, ids: (0, other(j, ids), 0)),
        ],
        out_specs=[
            whole((span, cc)),
            pl.BlockSpec((span, fb), lambda j, ids: (0, j)),
            whole((span, cc)),
            whole((span, cc)),
            whole((8, 128)),
            whole((QUAD, span, rows)),
        ],
        scratch_shapes=[pltpu.VMEM((span, cc), BF16), pltpu.VMEM((span, cc), F32)],
    )
    return pl.pallas_call(
        functools.partial(mlp_fwd_kernel, layer),
        grid_spec=grid,
        out_shape=[
            jax.ShapeDtypeStruct((span, cc), F32),
            jax.ShapeDtypeStruct((span, ff), F32),
            jax.ShapeDtypeStruct((span, cc), BF16),
            jax.ShapeDtypeStruct((span, cc), BF16),
            jax.ShapeDtypeStruct((8, 128), F32),
            jax.ShapeDtypeStruct((QUAD, span, rows), BF16),
        ],
        compiler_params=params(40, dimension_semantics=("arbitrary",)),
        cost_estimate=cost(6 * span * cc * ff, 4 * cc * ff + 4 * span * ff, span * ff),
    )(ids, x, *att, wo, pv, pvn, pv, up[0], up[1], dn[0], dn[1])


def mlp_bwd_kernel(
    layer, ids, df, u, mid, wo, pv, upo, upr, dno, dnr,
    lr, rr, dmid, g, d0, d1, d2, d3, acc, wide,
):
    j = pl.program_id(0)
    c, s = ids[0], ids[1]
    cc = df.shape[-1]
    fb = u.shape[-1]
    own = c == layer

    @pl.when(j == 0)
    def _():
        acc[...] = jnp.zeros_like(acc)
        g[...] = jnp.zeros_like(g)

    wu = lax.select(own, upo[0], upr[0])
    wd = lax.select(own, dno[0], dnr[0])
    da = nt(df[...], wd)
    ub = u[...]
    th = gelu_parts(ub)
    half = 0.5 * (1.0 + th)
    lr[0] = (ub * half).astype(BF16)
    slope = half + 0.5 * ub * (1.0 - th * th) * (GC * (1.0 + 3 * 0.044715 * (ub * ub)))
    du = (slope * da).astype(BF16)
    lr[1] = du
    g[0:1, pl.ds(pl.multiple_of(j * fb, 128), fb)] = jnp.sum(du.astype(F32), axis=0, keepdims=True)
    acc[...] += nt(du, wu)

    @pl.when(j == pl.num_programs(0) - 1)
    def _():
        dff = df[...].astype(F32)
        dv, gg, nm = crms_back(mid[...], pv[4:5, :cc], acc[...])
        dm = dff + dv
        low = dm.astype(BF16)
        dmid[...] = dm
        quarter = rr.shape[-1]
        wide[:, cc:] = jnp.zeros((wide.shape[0], wide.shape[1] - cc), BF16)
        for i, v in enumerate((df[...], nm.astype(BF16), low)):
            wide[:, :cc] = v
            for t in range(QUAD):
                rr[i, t] = wide[:, t * quarter : (t + 1) * quarter]
        g[1:2, :cc] = jnp.sum(low.astype(F32), axis=0, keepdims=True)
        g[2:3, :cc] = jnp.sum(dff, axis=0, keepdims=True)
        g[4:5, :cc] = jnp.sum(gg, axis=0, keepdims=True)
        rows = d0.shape[0]
        for k, d in enumerate((d0, d1, d2, d3)):
            row = pl.multiple_of(jnp.bitwise_xor(s, k) * rows, rows)
            d[...] = nt(wo[pl.ds(row, rows), :], low).astype(BF16)


def mlp_bwd(layer, ids, df, u, mid, wo, pv, up, dn):
    span, cc = df.shape
    ff = u.shape[-1]
    fb = ff // 8
    rows = wo.shape[0] // QUAD

    def whole(shape):
        return pl.BlockSpec(shape, lambda j, ids: (0,) * len(shape))

    def pick(mine):
        return lambda j, ids: jnp.where((ids[0] == layer) == mine, j, 0)

    mine, other = pick(True), pick(False)
    grid = pltpu.PrefetchScalarGridSpec(
        num_scalar_prefetch=1,
        grid=(8,),
        in_specs=[
            whole((span, cc)),
            pl.BlockSpec((span, fb), lambda j, ids: (0, j)),
            whole((span, cc)),
            whole(wo.shape),
            whole(pv.shape),
            pl.BlockSpec((1, cc, fb), lambda j, ids: (0, 0, mine(j, ids))),
            pl.BlockSpec((1, cc, fb), lambda j, ids: (0, 0, other(j, ids))),
            pl.BlockSpec((1, fb, cc), lambda j, ids: (0, mine(j, ids), 0)),
            pl.BlockSpec((1, fb, cc), lambda j, ids: (0, other(j, ids), 0)),
        ],
        out_specs=[
            pl.BlockSpec((2, span, fb), lambda j, ids: (0, 0, j)),
            whole((3, QUAD, span, (cc + 1) // QUAD)),
            whole((span, cc)),
            whole((8, ff)),
        ]
        + [whole((rows, span))] * 4,
        scratch_shapes=[pltpu.VMEM((span, cc), F32), pltpu.VMEM((span, cc + 1), BF16)],
    )
    dd = jax.ShapeDtypeStruct((rows, span), BF16)
    return pl.pallas_call(
        functools.partial(mlp_bwd_kernel, layer),
        grid_spec=grid,
        out_shape=[
            jax.ShapeDtypeStruct((2, span, ff), BF16),
            jax.ShapeDtypeStruct((3, QUAD, span, (cc + 1) // QUAD), BF16),
            jax.ShapeDtypeStruct((span, cc), F32),
            jax.ShapeDtypeStruct((8, ff), F32),
            dd, dd, dd, dd,
        ],
        compiler_params=params(40, dimension_semantics=("arbitrary",)),
        cost_estimate=cost(6 * span * cc * ff, 4 * cc * ff + 8 * span * ff, span * ff),
    )(ids, df, u, mid, wo, pv, up[0], up[1], dn[0], dn[1])


def product_kernel(send, places, ids, lr, rr, att, *rest):
    outs = [rest[0].at[i] for i in range(len(places))] if send else rest[1:]
    core = 1 - ids[0] if send else ids[0]
    ff = lr.shape[-1]
    part = att.shape[-1]
    for i, place in enumerate(places):
        t = jnp.bitwise_xor(order(core, place), ids[1])
        out = outs[i]
        main = tn(rr[core, t], lr[core])
        low = rr[2, t]
        sides = [tn(low, att[2 * core + h]) for h in range(2)]
        if not send:
            got = rest[0].at[i]
            main = main + got[:, :ff].astype(F32)
            sides = [v + got[:, ff + h * part : ff + (h + 1) * part].astype(F32) for h, v in enumerate(sides)]
        out[:, :ff] = main.astype(BF16)
        for h, v in enumerate(sides):
            out[:, ff + h * part : ff + (h + 1) * part] = v.astype(BF16)


def product(send, places, ids, lr, rr, att, *got):
    span, quarter = rr.shape[2:]
    cols = lr.shape[-1] + 2 * att.shape[-1]
    return pl.pallas_call(
        functools.partial(product_kernel, send, places),
        in_specs=[SMEM] + [VMEM] * (3 + len(got)),
        out_specs=VMEM if send else [VMEM] * len(places),
        out_shape=jax.ShapeDtypeStruct((len(places), quarter, cols), BF16)
        if send
        else [jax.ShapeDtypeStruct((quarter, cols), BF16)] * len(places),
        compiler_params=params(32),
        cost_estimate=cost(2 * span * quarter * cols * len(places), 2 * 4 * quarter * cols * len(places)),
    )(ids, lr, rr, att, *got)


def attn_bwd_kernel(
    ids, n0, n1, n2, n3, w_ref, qh, kh, vh, lse, d0, d1, d2, d3,
    p0, p1, far, gs, gk, gb, do, dk, dv, dy, acc, bias_scr,
):
    c, s = ids[0], ids[1]
    heads, _, hd = qh.shape
    span, cc = n0.shape
    width = heads * hd
    for k, d in enumerate((d0, d1, d2, d3)):
        do[jnp.bitwise_xor(s, k)] = d[...]
    for t in reversed(range(QUAD)):
        n = span * (t + 1)
        bias_scr[:n, :] = visible_bias(ids, n, t, span)
        for h in range(heads):
            q = qh[h, t * span : (t + 1) * span, :]
            kk = kh[h, :n, :]
            sc = nt(kk, q) + (bias_scr[:n, :] - lse[h, t : t + 1, :])
            pr = jnp.exp(sc)
            dot = do[t, h * hd : (h + 1) * hd, :]
            dp = nn(vh[h, :n, :], dot)
            inner = jnp.sum(pr * dp, axis=0, keepdims=True)
            ds = (pr * (dp - inner)).astype(BF16)
            newk = nn(ds, q)
            newv = nt(pr.astype(BF16), dot)
            if t == QUAD - 1:
                dk[h, :n, :] = newk
                dv[h, :n, :] = newv
            else:
                dk[h, :n, :] += newk
                dv[h, :n, :] += newv
            dq = tn(kk, ds) * (hd**-0.5)
            dy[t * span : (t + 1) * span, h * hd : (h + 1) * hd] = dq.T.astype(BF16)
    for h in range(heads):
        dy[:, width + h * hd : width + (h + 1) * hd] = dk[h].astype(BF16)
        dy[:, 2 * width + h * hd : 2 * width + (h + 1) * hd] = dv[h].astype(BF16)
    total = jnp.zeros((1, 3 * width), F32)
    outs = (p0, p1, far.at[span:], far.at[:span])
    for p, (nb, out) in enumerate(zip((n0, n1, n2, n3), outs)):
        row = pl.multiple_of(jnp.bitwise_xor(order(c, p), s) * span, span)
        y = dy[pl.ds(row, span), :]
        out[...] = nt(y, w_ref[...]).astype(BF16)
        total = total + jnp.sum(y.astype(F32), axis=0, keepdims=True)
        g = tn(nb[...], y)
        if p == 0:
            acc[:cc, :] = g
        else:
            acc[:cc, :] += g
    gb[...] = jnp.broadcast_to(total, gb.shape)
    part = gs.shape[0]
    acc[cc:, :] = jnp.zeros((acc.shape[0] - cc, acc.shape[1]), F32)
    gk[...] = acc[pl.ds(pl.multiple_of(c * part, part), part), :].astype(BF16)
    gs[...] = acc[pl.ds(pl.multiple_of((1 - c) * part, part), part), :].astype(BF16)


def attn_bwd(ids, blocks, w3, qkvl, douts):
    span, cc = blocks[0].shape
    heads, full, hd = qkvl[0].shape
    width = heads * hd
    pp = jax.ShapeDtypeStruct((span, cc), BF16)
    gg = jax.ShapeDtypeStruct(((cc + 1) // 2, 3 * width), BF16)
    return pl.pallas_call(
        attn_bwd_kernel,
        in_specs=[SMEM] + [VMEM] * 13,
        out_specs=[VMEM] * 6,
        out_shape=[pp, pp, jax.ShapeDtypeStruct((2 * span, cc), BF16), gg, gg, jax.ShapeDtypeStruct((8, 3 * width), F32)],
        scratch_shapes=[
            pltpu.VMEM((QUAD, width, span), BF16),
            pltpu.VMEM((heads, full, hd), F32),
            pltpu.VMEM((heads, full, hd), F32),
            pltpu.VMEM((full, 3 * width), BF16),
            pltpu.VMEM((cc + 1, 3 * width), F32),
            pltpu.VMEM((full, span), F32),
        ],
        compiler_params=params(48),
        cost_estimate=cost(
            4 * full * cc * 3 * width + 3 * 10 * full * full * hd * heads,
            8 * full * cc,
            heads * full * full,
        ),
    )(ids, *blocks, w3, *qkvl, *douts)


def input_kernel(part, r0, r1, dmid, x, pv, dx, gg):
    cc = x.shape[-1]
    dn = part[...].astype(F32) + r0[part.shape[0] :, :].astype(F32) + r1[...].astype(F32)
    dv, g, _ = crms_back(x[...].astype(F32), pv[3:4, :cc], dn)
    dx[...] = (dmid[...] + dv).astype(BF16)
    gg[...] = jnp.broadcast_to(jnp.sum(g, axis=0, keepdims=True), gg.shape)


def input_grad_of(part, r0, r1, dmid, x, pv):
    return pl.pallas_call(
        input_kernel,
        in_specs=[VMEM] * 6,
        out_specs=[VMEM] * 2,
        out_shape=[
            jax.ShapeDtypeStruct(x.shape, BF16),
            jax.ShapeDtypeStruct((8, x.shape[-1]), F32),
        ],
        compiler_params=params(16),
        cost_estimate=cost(0, x.size * 14),
    )(part, r0, r1, dmid, x, pv)


def both_lengths(t, rows, start):
    @pl.when(t < QUAD - 1)
    def _():
        start(rows)

    @pl.when(t == QUAD - 1)
    def _():
        start(rows - 1)


def place_kernel(pair, first, ids, *refs):
    srcs = refs[:4]
    outs = refs[4:7] if first else refs[7:10]
    x0, x1, od, ou, ow, sem = refs[7:] if first else refs[10:]
    c, s = ids[0], ids[1]
    down, up, wout = outs
    _, rows, _, ff = od.shape
    part = ow.shape[-1]

    def reads(i, a, b):
        return [
            pltpu.make_async_copy(a.at[i], x0.at[i], sem.at[0, i]),
            pltpu.make_async_copy(b.at[i], x1.at[i], sem.at[1, i]),
        ]

    def load(a, b):
        for i in range(2):
            for m in reads(i, a, b):
                m.start()

    @pl.when(c == 0)
    def _():
        load(srcs[0], srcs[1])

    @pl.when(c != 0)
    def _():
        load(srcs[2], srcs[3])

    def writes(n, i, side, t):
        o, dst = ((od, down), (ou, up))[side]
        return [
            pltpu.make_async_copy(
                o.at[i, pl.ds(0, n)], dst.at[pl.ds(t * rows, n)], sem.at[2 + side, i]
            ),
            pltpu.make_async_copy(
                ow.at[side, i, pl.ds(0, n)],
                wout.at[pl.ds(t * rows, n), :, pl.ds(side * part, part)],
                sem.at[4 + side, i],
            ),
        ]

    jobs = []
    for i in range(2):
        place = 2 * pair + i
        for m in reads(i, srcs[0], srcs[1]):
            m.wait()
        swapped = ((place & 1) << 1) | (place >> 1)
        for side, (x, o, k) in enumerate(((x0, od, swapped), (x1, ou, place))):
            t = jnp.bitwise_xor(k, s)
            o[i, :, 0, :] = x[i, :, :ff].astype(F32)
            ow[side, i, :, 0, :] = x[i, :, ff:].astype(F32)
            both_lengths(t, rows, lambda n: [m.start() for m in writes(n, i, side, t)])
            jobs.append((i, side, t))
    for i, side, t in jobs:
        both_lengths(t, rows, lambda n: [m.wait() for m in writes(n, i, side, t)])


def place_rows(pair, ids, srcs, outs, cc, ff, model):
    _, rows, cols = srcs[0].shape
    first = outs is None
    operands = [ids, *srcs] + ([] if first else list(outs))
    return pl.pallas_call(
        functools.partial(place_kernel, pair, first),
        in_specs=[SMEM] + [HBM] * (len(operands) - 1),
        out_specs=[HBM] * 3,
        out_shape=[jax.ShapeDtypeStruct((cc, 1, n), F32) for n in (ff, ff, model)],
        input_output_aliases={} if first else {5: 0, 6: 1, 7: 2},
        scratch_shapes=[
            pltpu.VMEM((2, rows, cols), BF16),
            pltpu.VMEM((2, rows, cols), BF16),
            pltpu.VMEM((2, rows, 1, ff), F32),
            pltpu.VMEM((2, rows, 1, ff), F32),
            pltpu.VMEM((2, 2, rows, 1, cols - ff), F32),
            pltpu.SemaphoreType.DMA((6, 2)),
        ],
        compiler_params=params(40),
        cost_estimate=cost(0, 24 * rows * cols),
    )(*operands)


def qkv_out_kernel(ids, *refs):
    srcs, out, rows, wide, od, sem = refs[:4], *refs[4:]
    c, s = ids[0], ids[1]
    _, _, half, cols = rows.shape
    width = cols // 3

    def reads(a, b):
        return [
            pltpu.make_async_copy(
                src.at[p, pl.ds(0, half), :],
                rows.at[i, jnp.bitwise_xor(p if i else ((p & 1) << 1) | (p >> 1), s)],
                sem.at[0, i * QUAD + p],
            )
            for i, src in enumerate((a, b))
            for p in range(QUAD)
        ]

    @pl.when(c == 0)
    def _():
        for m in reads(srcs[0], srcs[1]):
            m.start()

    @pl.when(c != 0)
    def _():
        for m in reads(srcs[2], srcs[3]):
            m.start()

    for m in reads(srcs[0], srcs[1]):
        m.wait()
    step = half // 2
    moves = []
    for b in range(4):
        if b >= 2:
            moves[b - 2].wait()
        for t in range(QUAD):
            v = rows[b // 2, t, (b % 2) * step : (b % 2 + 1) * step, :].astype(F32)
            for i in range(3):
                lo = (i * QUAD + t) * width
                wide[:, lo : lo + width] = v[:, i * width : (i + 1) * width]
        od[b % 2, :, 0, :] = wide[...]
        n = step - (b == 3)
        m = pltpu.make_async_copy(
            od.at[b % 2, pl.ds(0, n)], out.at[pl.ds(b * step, n)], sem.at[1, b % 2]
        )
        m.start()
        moves.append(m)
    for m in moves[-2:]:
        m.wait()


def qkv_out(ids, srcs, cc):
    cols = srcs[0].shape[-1]
    half = (cc + 1) // 2
    return pl.pallas_call(
        qkv_out_kernel,
        in_specs=[SMEM] + [HBM] * 4,
        out_specs=HBM,
        out_shape=jax.ShapeDtypeStruct((cc, 1, QUAD * cols), F32),
        scratch_shapes=[
            pltpu.VMEM((2, QUAD, half, cols), BF16),
            pltpu.VMEM((half // 2, QUAD * cols), F32),
            pltpu.VMEM((2, half // 2, 1, QUAD * cols), F32),
            pltpu.SemaphoreType.DMA((2, 2 * QUAD)),
        ],
        compiler_params=params(32),
        cost_estimate=cost(0, 6 * cc * QUAD * cols),
    )(ids, *srcs)


def to_first(v):
    pairs = [(i, i ^ 1) for i in range(QUAD)] + [(QUAD + i, QUAD + (i ^ 2)) for i in range(QUAD)]
    return lax.ppermute(v, ("section", "seq"), pairs)


def to_second(v):
    pairs = [(i, i ^ 2) for i in range(QUAD)] + [(QUAD + i, QUAD + (i ^ 1)) for i in range(QUAD)]
    return lax.ppermute(v, ("section", "seq"), pairs)


def to_quad(v, k):
    return lax.ppermute(v, "seq", [(i, i ^ k) for i in range(QUAD)])


def to_core(v):
    return lax.ppermute(v, "section", [(0, 1), (1, 0)])


def dp_partner(v, step):
    n = lax.axis_size("dp")
    return lax.ppermute(v, "dp", [(i, i ^ step) for i in range(n)])


def to_owner(l, v):
    return lax.ppermute(v, "section", [(1 - l, l)])


def tied(*v):
    return lax.optimization_barrier(v)


class Order:
    def __init__(self, token):
        self.token = token

    def wait(self, *v):
        *v, self.token = lax.optimization_barrier((*v, self.token))
        return v

    def run(self, step, *operands):
        out = step(*self.wait(*operands))
        out, self.token = lax.optimization_barrier((out, self.token))
        return out


class DpSum:
    def __init__(self, order_of, make, *operands):
        self.value = None
        self.steps = self.work(order_of, make, operands)

    def go(self):
        next(self.steps, None)

    def finish(self):
        for _ in self.steps:
            pass
        return self.value

    def work(self, order_of, make, operands):
        n = lax.axis_size("dp")
        z = lax.axis_index("dp")

        def split(v, step):
            left = v.shape[0] // n * step if v.ndim == 2 else v.shape[1]
            v = v.reshape(n // (2 * step), 2, left, v.shape[-1])
            low = (z & step) == 0
            return jnp.where(low, v[:, 1], v[:, 0]), jnp.where(low, v[:, 0], v[:, 1])

        def join(v, got, step):
            low = (z & step) == 0
            both = jnp.where(low, jnp.stack([v, got], 1), jnp.stack([got, v], 1))
            return both.reshape(-1, *v.shape[1:])

        away, keep = order_of.run(lambda *v: split(make(*v), 1), *operands)
        step = 1
        while step < n:
            got = dp_partner(away, step)
            yield
            step *= 2
            if step < n:
                away, keep = order_of.run(lambda a, b, s=step: split(add_low(a, b), s), keep, got)
            else:
                v = order_of.run(add_low, keep, got)
        while step > 1:
            step //= 2
            got = dp_partner(v, step)
            yield
            v = order_of.run(functools.partial(join, step=step), v, got)
        self.value = v.reshape(-1, v.shape[-1])


def add_low(a, b):
    return (a.astype(F32) + b.astype(F32)).astype(BF16)


def quad_gather(own):
    one = to_second(own)
    two = to_first(own)
    three = to_first(one)
    return [own, one, two, three]


def on_device(
    layer_in, cotangent, lengths, w_qkv, bias_qv, w_out, bias_out,
    gain_attn, gain_mlp, w_up, bias_up, w_down, bias_down,
):
    micro, _, span, cc = layer_in.shape
    model = w_out.shape[1]
    ff = w_up.shape[-1]
    hd = model // HEADS
    width = model // QUAD
    heads = width // hd
    c = lax.axis_index("section")
    s = lax.axis_index("seq")
    dp_count = lax.axis_size("dp")
    mine = c == 0

    lens = lax.dynamic_index_in_dim(lengths, c, 0, keepdims=False)[0]
    e0 = lens[0]
    e1 = e0 + lens[1]
    e2 = e1 + lens[2]
    e3 = e2 + lens[3]
    ids = jnp.stack([c, s, e0, e1, e2, e3, c, s]).astype(jnp.int32)
    x = rows_in(ids, layer_in)
    x, w_qkv = tied(x, w_qkv)

    def row(v, n=ff):
        return jnp.pad(v, ((0, 0), (0, n - v.shape[-1])))

    qb = lax.dynamic_slice_in_dim(bias_qv, s * width, width, 1)
    vb = lax.dynamic_slice_in_dim(bias_qv, model + s * width, width, 1)
    heads_bias = jnp.concatenate([qb, jnp.zeros((1, width), F32), vb], 1)
    pv_own = jnp.concatenate(
        [row(v) for v in (bias_up, bias_out, bias_down, gain_attn, gain_mlp, heads_bias)]
        + [jnp.zeros((2, ff), F32)]
    )
    w3_own = jnp.concatenate(
        [lax.dynamic_slice_in_dim(w_qkv[0], i * model + s * width, width, 1) for i in range(3)], 1
    )
    pv_got = to_core(pv_own)
    w3_got = to_core(w3_own)
    wo_got = to_core(w_out[0])
    up = (w_up, to_core(w_up))
    dn = (w_down, to_core(w_down))
    pv = [jnp.where(mine, pv_own, pv_got), jnp.where(mine, pv_got, pv_own)]
    w3 = [jnp.where(mine, w3_own, w3_got), jnp.where(mine, w3_got, w3_own)]
    wo = [jnp.where(mine, w_out[0], wo_got), jnp.where(mine, wo_got, w_out[0])]

    normed = x
    saved = []
    squares = []
    for l in range(2):
        blocks = quad_gather(normed)
        qh, kh, vh, lse, *att = attn_fwd(l == 0, ids, blocks, w3[l], pv[l], heads, hd)
        if l == 0:
            att, blocks = att[:QUAD], att[QUAD:]
        att = [att[0]] + [to_quad(att[k], k) for k in (1, 2, 3)]
        mid, u, xout, normed, sq, astk = mlp_fwd(
            l, ids, x, att, wo[l], pv[l], pv[min(l + 1, 1)], up, dn
        )
        saved.append((x, blocks, (qh, kh, vh, lse), astk, mid, u))
        squares.append(sq[0, 0])
        x = xout
    outs = [saved[1][0], x]

    order_of = Order(ids)
    run = order_of.run

    def first_part(l, df):
        lr, rr, dmid, g, *douts = run(
            lambda v: mlp_bwd(l, ids, v, saved[l][5], saved[l][4], wo[l], pv[l], up, dn), df
        )
        return lr, rr, dmid, g, [douts[0]] + [to_quad(douts[k], k) for k in (1, 2, 3)]

    def send(l, places, lr, rr):
        return run(lambda a, b: product(True, places, ids, a, b, saved[l][3]), lr, rr)

    def keep(l, places, lr, rr, got):
        return run(lambda a, b, v: product(False, places, ids, a, b, saved[l][3], v), lr, rr, got)

    def attention(l, douts):
        outs = run(lambda *v: attn_bwd(ids, saved[l][1], w3[l], saved[l][2], v), *douts)
        return (*outs, to_first(outs[2]), to_core(outs[3]))

    def input_part(l, p0, pr, q, dmid):
        return run(lambda *v: input_grad_of(*v, saved[l][0], pv[l]), p0, pr, q, dmid)

    def projection(l, gk, gs_got, g, gb, gg):
        pad = jnp.zeros((1,), F32)
        heads_sum = jnp.concatenate([gb[0, :width], gb[0, 2 * width :]])
        v = jnp.concatenate(
            [g[0], g[1, :cc], pad, g[2, :cc], pad, gg[0, :cc], pad, g[4, :cc], pad]
            + [jnp.broadcast_to(squares[l], (128,)), heads_sum]
        )
        v = jnp.pad(v, (0, 32 * 3 * width - v.shape[0])).reshape(32, 3 * width).astype(BF16)
        return jnp.concatenate([add_low(gk, gs_got), v])

    def wait(*v):
        out = order_of.wait(*v)
        return out[0] if len(out) == 1 else out

    def pair_up(a, b):
        return jnp.stack([a, b])

    def add_first(a, b):
        return add_low(a, b[:span])

    df = rows_in(ids, cotangent)
    out_got = to_core(jnp.where(mine, outs[1], outs[0]))
    lr1, rr1, dmid1, g1, douts1 = first_part(1, df)
    out_got = wait(out_got)

    far1 = to_core(send(1, (3, 2), lr1, rr1))
    near1 = send(1, (1, 0), lr1, rr1)
    far1, *douts1 = wait(far1, *douts1)

    far1 = keep(1, (3, 2), lr1, rr1, far1)
    x1a, near1 = to_first(far1[0]), to_core(near1)
    p0, p1, _, _, gk1, gb1, pr, gs_got = attention(1, douts1)
    x1a, near1 = wait(x1a, near1)

    near1 = keep(1, (1, 0), lr1, rr1, near1)
    half1 = run(add_low, near1[0], x1a)
    pr, gs_got = wait(pr, gs_got)

    q = to_second(run(add_first, p1, pr))
    q = wait(q)

    x1b, half1 = wait(far1[1], half1)
    x1b, x2 = to_first(x1b), to_second(half1)
    dx1, gg1 = input_part(1, p0, pr, q, dmid1)
    qkv_sum1 = DpSum(order_of, functools.partial(projection, 1), gk1, gs_got, g1, gb1, gg1)
    lr0, rr0, dmid0, g0, douts0 = first_part(0, dx1)
    x1b, x2 = wait(x1b, x2)

    far0 = to_core(send(0, (3, 2), lr0, rr0))
    near0 = send(0, (1, 0), lr0, rr0)
    far0, *douts0 = wait(far0, *douts0)

    far0 = keep(0, (3, 2), lr0, rr0, far0)
    x1a, near0 = to_first(far0[0]), to_core(near0)
    sum1 = DpSum(order_of, lambda a, b, d: add_low(add_low(a, b), d), near1[1], x1b, x2)
    sum1.go()
    p0, p1, _, _, gk0, gb0, pr, gs_got = attention(0, douts0)
    x1a, near0 = wait(x1a, near0)
    sum1.go()

    near0 = keep(0, (1, 0), lr0, rr0, near0)
    half1 = run(add_low, near0[0], x1a)
    qkv_sum1.go()
    pr, gs_got = wait(pr, gs_got)

    q = to_second(run(add_first, p1, pr))
    q = wait(q)

    x1b, half1 = wait(far0[1], half1)
    x1b, x2 = to_first(x1b), to_second(half1)
    dx0, gg0 = input_part(0, p0, pr, q, dmid0)
    qkv_sum1.go()
    sum1.go()
    qkv_sum0 = DpSum(order_of, functools.partial(projection, 0), gk0, gs_got, g0, gb0, gg0)
    qkv_sum0.go()
    qkv_sum1.go()
    sum1.go()
    qkv_sum0.go()
    qkv_sum1.go()
    x1b, x2 = wait(x1b, x2)

    own1 = sum1.finish()
    sum0 = DpSum(order_of, lambda a, b, d: add_low(add_low(a, b), d), near0[1], x1b, x2)
    next1 = to_second(own1)
    sum0.go()
    qkv_own1 = qkv_sum1.finish()
    qkv_next1 = to_second(qkv_own1)
    in_got = to_core(run(lambda a, b: jnp.where(mine, a, b), dx1, dx0))
    qkv_sum0.go()
    next1, qkv_next1, in_got = wait(next1, qkv_next1, in_got)

    pair1 = run(pair_up, own1, next1)
    rest1 = to_first(pair1)
    sum0.go()
    qkv_pair1 = run(pair_up, qkv_own1, qkv_next1)
    qkv_rest1 = to_first(qkv_pair1)
    qkv_sum0.go()

    sum0.go()
    qkv_own0 = qkv_sum0.finish()
    qkv_next0 = to_second(qkv_own0)
    rest1, qkv_rest1 = wait(rest1, qkv_rest1)
    pair1_got = to_owner(1, pair1)
    qkv1 = run(lambda a, b: jnp.concatenate([a, b]), qkv_pair1, qkv_rest1)
    qkv_next0, pair1_got = wait(qkv_next0, pair1_got)

    qkv_pair0 = run(pair_up, qkv_own0, qkv_next0)
    qkv_rest0 = to_first(qkv_pair0)
    rest1_got = to_owner(1, rest1)
    sum0.go()
    rest1_got, qkv_rest0 = wait(rest1_got, qkv_rest0)

    own0 = sum0.finish()
    next0, qkv1_got = to_second(own0), to_owner(1, qkv1)
    qkv0 = run(lambda a, b: jnp.concatenate([a, b]), qkv_pair0, qkv_rest0)
    next0, qkv1_got = wait(next0, qkv1_got)

    pair0 = run(pair_up, own0, next0)
    rest0, pair0_got = to_first(pair0), to_owner(0, pair0)
    qkv0_got = to_owner(0, qkv0)
    layer_out = run(
        lambda a, b, d: rows_out(ids, jnp.where(mine, a, b), d), outs[0], outs[1], out_got
    )
    input_grad = run(lambda a, b, d: rows_out(ids, jnp.where(mine, a, b), d), dx0, dx1, in_got)
    pair0_got = wait(pair0_got)
    outs_w = run(
        lambda *v: place_rows(0, ids, v, None, cc, ff, model), pair0, pair0_got, pair1_got, pair1
    )
    qkv0_got = wait(qkv0_got)
    grad_qkv = run(lambda *v: qkv_out(ids, v, cc), qkv0, qkv0_got, qkv1_got, qkv1)
    rest0 = wait(rest0)
    rest0_got = wait(to_owner(0, rest0))
    grad_down, grad_up, grad_out = place_rows(
        1, order_of.token, [rest0, rest0_got, rest1_got, rest1], outs_w, cc, ff, model
    )

    half = (cc + 1) // 2
    tails = [v[:, half:].astype(F32).reshape(QUAD, -1) for v in (qkv0, qkv0_got, qkv1_got, qkv1)]
    tails = [jnp.where(mine, tails[0], tails[2]), jnp.where(mine, tails[1], tails[3])]
    small = jnp.sum(tails[0] + tails[1], 0)

    def take(lo, n):
        return small[lo : lo + n][None]

    d = cc + 1
    at = ff
    total = micro * dp_count * span * QUAD
    base = ff + 4 * d
    rms = jnp.sqrt(small[base] / total).reshape(1)
    seq_of = jnp.arange(QUAD)
    heads_of = jnp.zeros((QUAD, 2 * width), F32)
    for chain in range(2):
        for p in range(QUAD):
            here = seq_of == jnp.bitwise_xor(order(chain, p), s)
            row_of = tails[chain][p, base + 128 : base + 128 + 2 * width]
            heads_of = heads_of + jnp.where(here[:, None], row_of, 0.0)
    grad_bqv = jnp.concatenate(
        [heads_of[:, i * width : (i + 1) * width].reshape(model) for i in range(2)]
    )
    return (
        layer_out,
        input_grad,
        jnp.transpose(grad_qkv, (1, 0, 2)),
        grad_bqv[None],
        jnp.transpose(grad_out, (1, 2, 0)),
        take(at, cc),
        take(at + 2 * d, cc),
        take(at + 3 * d, cc),
        jnp.transpose(grad_up, (1, 0, 2)),
        take(0, ff),
        jnp.transpose(grad_down, (1, 2, 0)),
        take(at + d, cc),
        rms,
    )


def solution(mesh):
    two = P("section", None)
    three = P("section", None, None)
    tokens = P(None, "dp", "seq", None)
    stacked = P("section", None, "dp", "seq", None)
    return jax.shard_map(
        on_device,
        mesh=mesh,
        in_specs=(
            tokens, tokens, P(None, "dp", None), three, two, three, two, two, two, three, two, three, two,
        ),
        out_specs=(
            stacked, stacked, three, two, three, two, two, two, three, two, three, two, P("section"),
        ),
        check_vma=False,
    )
```

```python
import functools

import jax
import jax.numpy as jnp
from jax import lax
from jax.experimental import pallas as pl
from jax.experimental.pallas import tpu as pltpu
from jax.sharding import PartitionSpec as P

HEADS = 12
EPS = 1e-6
NEG = -1e30
F32 = jnp.float32
BF16 = jnp.bfloat16
MIB = 1 << 20
QUAD = 4


def nn(a, b):
    return lax.dot_general(a, b, (((1,), (0,)), ((), ())), preferred_element_type=F32)


def nt(a, b):
    return lax.dot_general(a, b, (((1,), (1,)), ((), ())), preferred_element_type=F32)


def tn(a, b):
    return lax.dot_general(a, b, (((0,), (0,)), ((), ())), preferred_element_type=F32)


def order(core, k):
    return jnp.where(core == 1, k, ((k & 1) << 1) | (k >> 1))


def crms_scale(v):
    sq = jnp.sum(v * v, axis=-1, keepdims=True)
    su = jnp.sum(v, axis=-1, keepdims=True)
    full = v.shape[-1] + 1
    return lax.rsqrt((sq + su * su) / full + EPS), su, (sq + su * su) / full


def crms_back(v, gain, grad):
    r, su, _ = crms_scale(v)
    gd = grad * gain
    w = jnp.sum(gd * v, axis=-1, keepdims=True)
    unit = v * r
    dv = gd * r - (w * r * r * r / (v.shape[-1] + 1)) * (v + su)
    return dv, grad * unit, unit * gain


GC = 0.7978845608028654


def gelu_parts(u):
    inner = GC * (u + 0.044715 * (u * u * u))
    th = jnp.tanh(inner)
    return th


def params(mib, **kw):
    return pltpu.CompilerParams(vmem_limit_bytes=mib * MIB, **kw)


def cost(flops, nbytes, trans=0):
    return pl.CostEstimate(flops=int(flops), bytes_accessed=int(nbytes), transcendentals=int(trans))


SMEM = pl.BlockSpec(memory_space=pltpu.SMEM)
VMEM = pl.BlockSpec(memory_space=pltpu.VMEM)
HBM = pl.BlockSpec(memory_space=pltpu.HBM)


def rows_in_kernel(ids, v, o):
    @pl.when(ids[0] == 0)
    def _():
        o[...] = v[:, 0, :].T

    @pl.when(ids[0] != 0)
    def _():
        o[...] = v[:, 1, :].T


def rows_in(ids, v):
    micro, _, span, cc = v.shape
    return pl.pallas_call(
        rows_in_kernel,
        in_specs=[SMEM, VMEM],
        out_specs=VMEM,
        out_shape=jax.ShapeDtypeStruct((span, cc), BF16),
        compiler_params=params(16),
        cost_estimate=cost(0, 6 * span * cc),
    )(ids, jnp.transpose(v[:, 0], (2, 0, 1)))


def rows_out_kernel(ids, own, got, o):
    @pl.when(ids[0] == 0)
    def _():
        o[:, 0, :] = own[...].T
        o[:, 1, :] = got[...].T

    @pl.when(ids[0] != 0)
    def _():
        o[:, 0, :] = got[...].T
        o[:, 1, :] = own[...].T


def rows_out(ids, own, got):
    span, cc = own.shape
    o = pl.pallas_call(
        rows_out_kernel,
        in_specs=[SMEM, VMEM, VMEM],
        out_specs=VMEM,
        out_shape=jax.ShapeDtypeStruct((cc, 2, span), BF16),
        compiler_params=params(16),
        cost_estimate=cost(0, 8 * span * cc),
    )(ids, own, got)
    return jnp.transpose(o, (1, 2, 0))[None, :, None]


def visible_bias(ids, n, t, span):
    i = t * span + lax.broadcasted_iota(jnp.int32, (1, span), 1)
    start = jnp.zeros((1, span), jnp.int32)
    for d in range(4):
        end = ids[2 + d]
        start = jnp.maximum(start, jnp.where(i >= end, end, 0))
    j = lax.broadcasted_iota(jnp.int32, (n, span), 0)
    return jnp.where((j >= start) & (j <= i), 0.0, NEG)


def attn_fwd_kernel(
    raw, ids, n0, n1, n2, n3, w_ref, pv_ref, qh, kh, vh, lse, a0, a1, a2, a3, *rest
):
    c, s = ids[0], ids[1]
    heads, _, hd = qh.shape
    span, cc = n0.shape
    width = heads * hd
    at, bias_scr = rest[-2:]
    bias = pv_ref[5:6, : 3 * width]
    for p, nb in enumerate((n0, n1, n2, n3)):
        t = jnp.bitwise_xor(order(c, p), s)
        row = pl.multiple_of(t * span, span)
        rows = nb[...]
        if raw:
            v = rows.astype(F32)
            rows = (v * crms_scale(v)[0] * pv_ref[3:4, :cc]).astype(BF16)
            rest[p][...] = rows
        y = nn(rows, w_ref[...]) + bias
        for h in range(heads):
            lo = h * hd
            qh[h, pl.ds(row, span), :] = (y[:, lo : lo + hd] * (hd**-0.5)).astype(BF16)
            kh[h, pl.ds(row, span), :] = y[:, width + lo : width + lo + hd].astype(BF16)
            vh[h, pl.ds(row, span), :] = y[:, 2 * width + lo : 2 * width + lo + hd].astype(BF16)
    for t in range(QUAD):
        n = span * (t + 1)
        bias_scr[:n, :] = visible_bias(ids, n, t, span)

        def head(h, carry, t=t, n=n):
            q = qh[h, t * span : (t + 1) * span, :]
            sc = nt(kh[h, :n, :], q) + bias_scr[:n, :]
            m = jnp.max(sc, axis=0, keepdims=True)
            e = jnp.exp(sc - m)
            tot = jnp.sum(e, axis=0, keepdims=True)
            pr = (e * (1.0 / tot)).astype(BF16)
            o = tn(vh[h, :n, :], pr)
            at[t, pl.ds(pl.multiple_of(h * hd, hd), hd), :] = o.astype(BF16)
            lse[h, t : t + 1, :] = m + jnp.log(tot)
            return carry

        lax.fori_loop(0, heads, head, 0)
    for k, a in enumerate((a0, a1, a2, a3)):
        a[...] = at[jnp.bitwise_xor(s, k)]


def attn_fwd(raw, ids, blocks, w3, pv, heads, hd):
    span, width = blocks[0].shape
    full = span * QUAD
    hh = jax.ShapeDtypeStruct((heads, full, hd), BF16)
    aa = jax.ShapeDtypeStruct((heads * hd, span), BF16)
    normed = [jax.ShapeDtypeStruct((span, width), BF16)] * (QUAD if raw else 0)
    return pl.pallas_call(
        functools.partial(attn_fwd_kernel, raw),
        in_specs=[SMEM] + [VMEM] * 6,
        out_specs=[VMEM] * (8 + len(normed)),
        out_shape=[hh, hh, hh, jax.ShapeDtypeStruct((heads, QUAD, span), F32), aa, aa, aa, aa] + normed,
        scratch_shapes=[
            pltpu.VMEM((QUAD, heads * hd, span), BF16),
            pltpu.VMEM((full, span), F32),
        ],
        compiler_params=params(40),
        cost_estimate=cost(
            2 * full * width * 3 * heads * hd + 3 * 4 * full * full * hd * heads,
            4 * full * width,
            heads * full * full,
        ),
    )(ids, *blocks, w3, pv)


def mlp_fwd_kernel(
    layer, ids, x, a0, a1, a2, a3, wo, pv, pvn, pvb, upo, upr, dno, dnr,
    mid, u, xout, nnext, sq, astk, nm, acc,
):
    j = pl.program_id(0)
    c, s = ids[0], ids[1]
    cc = x.shape[-1]
    own = c == layer

    @pl.when(j == 0)
    def _():
        rows = a0.shape[0]
        m = x[...].astype(F32) + pv[1:2, :cc]
        for k, a in enumerate((a0, a1, a2, a3)):
            row = pl.multiple_of(jnp.bitwise_xor(s, k) * rows, rows)
            m = m + tn(a[...], wo[pl.ds(row, rows), :])
            astk[jnp.bitwise_xor(s, k)] = a[...].T
        mid[...] = m
        r, _, _ = crms_scale(m)
        nm[...] = (m * r * pv[4:5, :cc]).astype(BF16)
        acc[...] = m + pv[2:3, :cc]

    wu = lax.select(own, upo[0], upr[0])
    wd = lax.select(own, dno[0], dnr[0])
    ub = nn(nm[...], wu) + pvb[0:1, :]
    u[...] = ub
    act = (0.5 * ub * (1.0 + gelu_parts(ub))).astype(BF16)
    acc[...] += nn(act, wd)

    @pl.when(j == pl.num_programs(0) - 1)
    def _():
        fin = acc[...]
        _, _, ms = crms_scale(fin)
        sq[...] = jnp.broadcast_to(jnp.sum(ms, axis=0, keepdims=True), sq.shape)
        low = fin.astype(BF16)
        xout[...] = low
        lf = low.astype(F32)
        r, _, _ = crms_scale(lf)
        nnext[...] = (lf * r * pvn[3:4, :cc]).astype(BF16)


def mlp_fwd(layer, ids, x, att, wo, pv, pvn, up, dn):
    span, cc = x.shape
    ff = up[0].shape[-1]
    fb = ff // 8
    rows = att[0].shape[0]

    def whole(shape):
        return pl.BlockSpec(shape, lambda j, ids: (0,) * len(shape))

    def pick(mine):
        return lambda j, ids: jnp.where((ids[0] == layer) == mine, j, 0)

    mine, other = pick(True), pick(False)
    grid = pltpu.PrefetchScalarGridSpec(
        num_scalar_prefetch=1,
        grid=(8,),
        in_specs=[whole((span, cc))]
        + [whole((rows, span))] * 4
        + [whole(wo.shape), whole(pv.shape), whole(pvn.shape)]
        + [
            pl.BlockSpec((8, fb), lambda j, ids: (0, j)),
            pl.BlockSpec((1, cc, fb), lambda j, ids: (0, 0, mine(j, ids))),
            pl.BlockSpec((1, cc, fb), lambda j, ids: (0, 0, other(j, ids))),
            pl.BlockSpec((1, fb, cc), lambda j, ids: (0, mine(j, ids), 0)),
            pl.BlockSpec((1, fb, cc), lambda j, ids: (0, other(j, ids), 0)),
        ],
        out_specs=[
            whole((span, cc)),
            pl.BlockSpec((span, fb), lambda j, ids: (0, j)),
            whole((span, cc)),
            whole((span, cc)),
            whole((8, 128)),
            whole((QUAD, span, rows)),
        ],
        scratch_shapes=[pltpu.VMEM((span, cc), BF16), pltpu.VMEM((span, cc), F32)],
    )
    return pl.pallas_call(
        functools.partial(mlp_fwd_kernel, layer),
        grid_spec=grid,
        out_shape=[
            jax.ShapeDtypeStruct((span, cc), F32),
            jax.ShapeDtypeStruct((span, ff), F32),
            jax.ShapeDtypeStruct((span, cc), BF16),
            jax.ShapeDtypeStruct((span, cc), BF16),
            jax.ShapeDtypeStruct((8, 128), F32),
            jax.ShapeDtypeStruct((QUAD, span, rows), BF16),
        ],
        compiler_params=params(40, dimension_semantics=("arbitrary",)),
        cost_estimate=cost(6 * span * cc * ff, 4 * cc * ff + 4 * span * ff, span * ff),
    )(ids, x, *att, wo, pv, pvn, pv, up[0], up[1], dn[0], dn[1])


def mlp_bwd_kernel(
    layer, ids, df, u, mid, wo, pv, upo, upr, dno, dnr,
    lr, rr, dmid, g, d0, d1, d2, d3, acc, wide,
):
    j = pl.program_id(0)
    c, s = ids[0], ids[1]
    cc = df.shape[-1]
    fb = u.shape[-1]
    own = c == layer

    @pl.when(j == 0)
    def _():
        acc[...] = jnp.zeros_like(acc)
        g[...] = jnp.zeros_like(g)

    wu = lax.select(own, upo[0], upr[0])
    wd = lax.select(own, dno[0], dnr[0])
    da = nt(df[...], wd)
    ub = u[...]
    th = gelu_parts(ub)
    half = 0.5 * (1.0 + th)
    lr[0] = (ub * half).astype(BF16)
    slope = half + 0.5 * ub * (1.0 - th * th) * (GC * (1.0 + 3 * 0.044715 * (ub * ub)))
    du = (slope * da).astype(BF16)
    lr[1] = du
    g[0:1, pl.ds(pl.multiple_of(j * fb, 128), fb)] = jnp.sum(du.astype(F32), axis=0, keepdims=True)
    acc[...] += nt(du, wu)

    @pl.when(j == pl.num_programs(0) - 1)
    def _():
        dff = df[...].astype(F32)
        dv, gg, nm = crms_back(mid[...], pv[4:5, :cc], acc[...])
        dm = dff + dv
        low = dm.astype(BF16)
        dmid[...] = dm
        quarter = rr.shape[-1]
        wide[:, cc:] = jnp.zeros((wide.shape[0], wide.shape[1] - cc), BF16)
        for i, v in enumerate((df[...], nm.astype(BF16), low)):
            wide[:, :cc] = v
            for t in range(QUAD):
                rr[i, t] = wide[:, t * quarter : (t + 1) * quarter]
        g[1:2, :cc] = jnp.sum(low.astype(F32), axis=0, keepdims=True)
        g[2:3, :cc] = jnp.sum(dff, axis=0, keepdims=True)
        g[4:5, :cc] = jnp.sum(gg, axis=0, keepdims=True)
        rows = d0.shape[0]
        for k, d in enumerate((d0, d1, d2, d3)):
            row = pl.multiple_of(jnp.bitwise_xor(s, k) * rows, rows)
            d[...] = nt(wo[pl.ds(row, rows), :], low).astype(BF16)


def mlp_bwd(layer, ids, df, u, mid, wo, pv, up, dn):
    span, cc = df.shape
    ff = u.shape[-1]
    fb = ff // 8
    rows = wo.shape[0] // QUAD

    def whole(shape):
        return pl.BlockSpec(shape, lambda j, ids: (0,) * len(shape))

    def pick(mine):
        return lambda j, ids: jnp.where((ids[0] == layer) == mine, j, 0)

    mine, other = pick(True), pick(False)
    grid = pltpu.PrefetchScalarGridSpec(
        num_scalar_prefetch=1,
        grid=(8,),
        in_specs=[
            whole((span, cc)),
            pl.BlockSpec((span, fb), lambda j, ids: (0, j)),
            whole((span, cc)),
            whole(wo.shape),
            whole(pv.shape),
            pl.BlockSpec((1, cc, fb), lambda j, ids: (0, 0, mine(j, ids))),
            pl.BlockSpec((1, cc, fb), lambda j, ids: (0, 0, other(j, ids))),
            pl.BlockSpec((1, fb, cc), lambda j, ids: (0, mine(j, ids), 0)),
            pl.BlockSpec((1, fb, cc), lambda j, ids: (0, other(j, ids), 0)),
        ],
        out_specs=[
            pl.BlockSpec((2, span, fb), lambda j, ids: (0, 0, j)),
            whole((3, QUAD, span, (cc + 1) // QUAD)),
            whole((span, cc)),
            whole((8, ff)),
        ]
        + [whole((rows, span))] * 4,
        scratch_shapes=[pltpu.VMEM((span, cc), F32), pltpu.VMEM((span, cc + 1), BF16)],
    )
    dd = jax.ShapeDtypeStruct((rows, span), BF16)
    return pl.pallas_call(
        functools.partial(mlp_bwd_kernel, layer),
        grid_spec=grid,
        out_shape=[
            jax.ShapeDtypeStruct((2, span, ff), BF16),
            jax.ShapeDtypeStruct((3, QUAD, span, (cc + 1) // QUAD), BF16),
            jax.ShapeDtypeStruct((span, cc), F32),
            jax.ShapeDtypeStruct((8, ff), F32),
            dd, dd, dd, dd,
        ],
        compiler_params=params(40, dimension_semantics=("arbitrary",)),
        cost_estimate=cost(6 * span * cc * ff, 4 * cc * ff + 8 * span * ff, span * ff),
    )(ids, df, u, mid, wo, pv, up[0], up[1], dn[0], dn[1])


def product_kernel(send, places, ids, lr, rr, att, *rest):
    outs = [rest[0].at[i] for i in range(len(places))] if send else rest[1:]
    core = 1 - ids[0] if send else ids[0]
    ff = lr.shape[-1]
    part = att.shape[-1]
    for i, place in enumerate(places):
        t = jnp.bitwise_xor(order(core, place), ids[1])
        out = outs[i]
        main = tn(rr[core, t], lr[core])
        low = rr[2, t]
        sides = [tn(low, att[2 * core + h]) for h in range(2)]
        if not send:
            got = rest[0].at[i]
            main = main + got[:, :ff].astype(F32)
            sides = [v + got[:, ff + h * part : ff + (h + 1) * part].astype(F32) for h, v in enumerate(sides)]
        out[:, :ff] = main.astype(BF16)
        for h, v in enumerate(sides):
            out[:, ff + h * part : ff + (h + 1) * part] = v.astype(BF16)


def product(send, places, ids, lr, rr, att, *got):
    span, quarter = rr.shape[2:]
    cols = lr.shape[-1] + 2 * att.shape[-1]
    return pl.pallas_call(
        functools.partial(product_kernel, send, places),
        in_specs=[SMEM] + [VMEM] * (3 + len(got)),
        out_specs=VMEM if send else [VMEM] * len(places),
        out_shape=jax.ShapeDtypeStruct((len(places), quarter, cols), BF16)
        if send
        else [jax.ShapeDtypeStruct((quarter, cols), BF16)] * len(places),
        compiler_params=params(32),
        cost_estimate=cost(2 * span * quarter * cols * len(places), 2 * 4 * quarter * cols * len(places)),
    )(ids, lr, rr, att, *got)


def attn_bwd_kernel(
    ids, n0, n1, n2, n3, w_hbm, q_hbm, k_hbm, v_hbm, l_hbm, d0, d1, d2, d3,
    p0, p1, far, gs, gk, gb, do, dk, dv, dy, acc, bias_scr,
    nb, w_ref, qh, kh, vh, lse, sem,
):
    c, s = ids[0], ids[1]
    heads, _, hd = qh.shape
    span, cc = n0.shape
    width = heads * hd
    moves = [
        pltpu.make_async_copy(src, dst, sem.at[i])
        for i, (src, dst) in enumerate(
            [(q_hbm, qh), (k_hbm, kh), (v_hbm, vh), (l_hbm, lse), (w_hbm, w_ref)]
            + [(n, nb.at[i]) for i, n in enumerate((n0, n1, n2, n3))]
        )
    ]
    for m in moves:
        m.start()
    for k, d in enumerate((d0, d1, d2, d3)):
        do[jnp.bitwise_xor(s, k)] = d[...]
    for m in moves[:4]:
        m.wait()
    for t in reversed(range(QUAD)):
        n = span * (t + 1)
        bias_scr[:n, :] = visible_bias(ids, n, t, span)
        for h in range(heads):
            q = qh[h, t * span : (t + 1) * span, :]
            kk = kh[h, :n, :]
            sc = nt(kk, q) + (bias_scr[:n, :] - lse[h, t : t + 1, :])
            pr = jnp.exp(sc)
            dot = do[t, h * hd : (h + 1) * hd, :]
            dp = nn(vh[h, :n, :], dot)
            inner = jnp.sum(pr * dp, axis=0, keepdims=True)
            ds = (pr * (dp - inner)).astype(BF16)
            newk = nn(ds, q)
            newv = nt(pr.astype(BF16), dot)
            if t == QUAD - 1:
                dk[h, :n, :] = newk
                dv[h, :n, :] = newv
            else:
                dk[h, :n, :] += newk
                dv[h, :n, :] += newv
            dq = tn(kk, ds) * (hd**-0.5)
            dy[t * span : (t + 1) * span, h * hd : (h + 1) * hd] = dq.T.astype(BF16)
    for h in range(heads):
        dy[:, width + h * hd : width + (h + 1) * hd] = dk[h].astype(BF16)
        dy[:, 2 * width + h * hd : 2 * width + (h + 1) * hd] = dv[h].astype(BF16)
    for m in moves[4:]:
        m.wait()
    total = jnp.zeros((1, 3 * width), F32)
    for p, out in enumerate((p0, p1, far.at[span:], far.at[:span])):
        row = pl.multiple_of(jnp.bitwise_xor(order(c, p), s) * span, span)
        y = dy[pl.ds(row, span), :]
        out[...] = nt(y, w_ref[...]).astype(BF16)
        total = total + jnp.sum(y.astype(F32), axis=0, keepdims=True)
        g = tn(nb[p], y)
        if p == 0:
            acc[:cc, :] = g
        else:
            acc[:cc, :] += g
    gb[...] = jnp.broadcast_to(total, gb.shape)
    part = gs.shape[0]
    acc[cc:, :] = jnp.zeros((acc.shape[0] - cc, acc.shape[1]), F32)
    gk[...] = acc[pl.ds(pl.multiple_of(c * part, part), part), :].astype(BF16)
    gs[...] = acc[pl.ds(pl.multiple_of((1 - c) * part, part), part), :].astype(BF16)


def attn_bwd(ids, blocks, w3, qkvl, douts):
    span, cc = blocks[0].shape
    heads, full, hd = qkvl[0].shape
    width = heads * hd
    pp = jax.ShapeDtypeStruct((span, cc), BF16)
    gg = jax.ShapeDtypeStruct(((cc + 1) // 2, 3 * width), BF16)
    return pl.pallas_call(
        attn_bwd_kernel,
        in_specs=[SMEM] + [HBM] * 9 + [VMEM] * 4,
        out_specs=[VMEM] * 6,
        out_shape=[pp, pp, jax.ShapeDtypeStruct((2 * span, cc), BF16), gg, gg, jax.ShapeDtypeStruct((8, 3 * width), F32)],
        scratch_shapes=[
            pltpu.VMEM((QUAD, width, span), BF16),
            pltpu.VMEM((heads, full, hd), F32),
            pltpu.VMEM((heads, full, hd), F32),
            pltpu.VMEM((full, 3 * width), BF16),
            pltpu.VMEM((cc + 1, 3 * width), F32),
            pltpu.VMEM((full, span), F32),
            pltpu.VMEM((QUAD, span, cc), BF16),
            pltpu.VMEM(w3.shape, BF16),
            pltpu.VMEM((heads, full, hd), BF16),
            pltpu.VMEM((heads, full, hd), BF16),
            pltpu.VMEM((heads, full, hd), BF16),
            pltpu.VMEM((heads, QUAD, span), F32),
            pltpu.SemaphoreType.DMA((9,)),
        ],
        compiler_params=params(48),
        cost_estimate=cost(
            4 * full * cc * 3 * width + 3 * 10 * full * full * hd * heads,
            8 * full * cc,
            heads * full * full,
        ),
    )(ids, *blocks, w3, *qkvl, *douts)


def input_kernel(part, r0, r1, dmid, x, pv, dx, gg):
    cc = x.shape[-1]
    dn = part[...].astype(F32) + r0[part.shape[0] :, :].astype(F32) + r1[...].astype(F32)
    dv, g, _ = crms_back(x[...].astype(F32), pv[3:4, :cc], dn)
    dx[...] = (dmid[...] + dv).astype(BF16)
    gg[...] = jnp.broadcast_to(jnp.sum(g, axis=0, keepdims=True), gg.shape)


def input_grad_of(part, r0, r1, dmid, x, pv):
    return pl.pallas_call(
        input_kernel,
        in_specs=[VMEM] * 6,
        out_specs=[VMEM] * 2,
        out_shape=[
            jax.ShapeDtypeStruct(x.shape, BF16),
            jax.ShapeDtypeStruct((8, x.shape[-1]), F32),
        ],
        compiler_params=params(16),
        cost_estimate=cost(0, x.size * 14),
    )(part, r0, r1, dmid, x, pv)


def both_lengths(t, rows, start):
    @pl.when(t < QUAD - 1)
    def _():
        start(rows)

    @pl.when(t == QUAD - 1)
    def _():
        start(rows - 1)


def place_kernel(places, first, ids, *refs):
    n = len(places)
    srcs = refs[: 4 * n]
    refs = refs[4 * n :]
    outs = refs[:3] if first else refs[3:6]
    x0, x1, od, ou, ow, sem = refs[3:] if first else refs[6:]
    c, s = ids[0], ids[1]
    down, up, wout = outs
    _, rows, _, ff = od.shape
    part = ow.shape[-1]

    def reads(i, j):
        return [
            pltpu.make_async_copy(srcs[4 * i + j], x0.at[i], sem.at[0, i]),
            pltpu.make_async_copy(srcs[4 * i + j + 1], x1.at[i], sem.at[1, i]),
        ]

    for core in range(2):

        @pl.when(c == core)
        def _():
            for i in range(n):
                for m in reads(i, 2 * core):
                    m.start()

    def writes(length, i, side, t):
        o, dst = ((od, down), (ou, up))[side]
        return [
            pltpu.make_async_copy(
                o.at[i, pl.ds(0, length)], dst.at[pl.ds(t * rows, length)], sem.at[2 + side, i]
            ),
            pltpu.make_async_copy(
                ow.at[side, i, pl.ds(0, length)],
                wout.at[pl.ds(t * rows, length), :, pl.ds(side * part, part)],
                sem.at[4 + side, i],
            ),
        ]

    jobs = []
    for i, place in enumerate(places):
        for m in reads(i, 0):
            m.wait()
        swapped = ((place & 1) << 1) | (place >> 1)
        for side, (x, o, k) in enumerate(((x0, od, swapped), (x1, ou, place))):
            t = jnp.bitwise_xor(k, s)
            o[i, :, 0, :] = x[i, :, :ff].astype(F32)
            ow[side, i, :, 0, :] = x[i, :, ff:].astype(F32)
            both_lengths(t, rows, lambda length: [m.start() for m in writes(length, i, side, t)])
            jobs.append((i, side, t))
    for i, side, t in jobs:
        both_lengths(t, rows, lambda length: [m.wait() for m in writes(length, i, side, t)])


def place_rows(places, ids, srcs, outs, cc, ff, model):
    rows, cols = srcs[0].shape
    n = len(places)
    first = outs is None
    operands = [ids, *srcs] + ([] if first else list(outs))
    return pl.pallas_call(
        functools.partial(place_kernel, places, first),
        in_specs=[SMEM] + [HBM] * (len(operands) - 1),
        out_specs=[HBM] * 3,
        out_shape=[jax.ShapeDtypeStruct((cc, 1, m), F32) for m in (ff, ff, model)],
        input_output_aliases={} if first else {4 * n + 1 + i: i for i in range(3)},
        scratch_shapes=[
            pltpu.VMEM((n, rows, cols), BF16),
            pltpu.VMEM((n, rows, cols), BF16),
            pltpu.VMEM((n, rows, 1, ff), F32),
            pltpu.VMEM((n, rows, 1, ff), F32),
            pltpu.VMEM((2, n, rows, 1, cols - ff), F32),
            pltpu.SemaphoreType.DMA((6, n)),
        ],
        compiler_params=params(40),
        cost_estimate=cost(0, 12 * n * rows * cols),
    )(*operands)


def qkv_out_kernel(ids, *refs):
    srcs, out, rows, wide, od, sem = refs[:4], *refs[4:]
    c, s = ids[0], ids[1]
    _, _, half, cols = rows.shape
    width = cols // 3

    def reads(a, b):
        return [
            pltpu.make_async_copy(
                src.at[p, pl.ds(0, half), :],
                rows.at[i, jnp.bitwise_xor(p if i else ((p & 1) << 1) | (p >> 1), s)],
                sem.at[0, i * QUAD + p],
            )
            for i, src in enumerate((a, b))
            for p in range(QUAD)
        ]

    @pl.when(c == 0)
    def _():
        for m in reads(srcs[0], srcs[1]):
            m.start()

    @pl.when(c != 0)
    def _():
        for m in reads(srcs[2], srcs[3]):
            m.start()

    for m in reads(srcs[0], srcs[1]):
        m.wait()
    step = half // 2
    moves = []
    for b in range(4):
        if b >= 2:
            moves[b - 2].wait()
        for t in range(QUAD):
            v = rows[b // 2, t, (b % 2) * step : (b % 2 + 1) * step, :].astype(F32)
            for i in range(3):
                lo = (i * QUAD + t) * width
                wide[:, lo : lo + width] = v[:, i * width : (i + 1) * width]
        od[b % 2, :, 0, :] = wide[...]
        n = step - (b == 3)
        m = pltpu.make_async_copy(
            od.at[b % 2, pl.ds(0, n)], out.at[pl.ds(b * step, n)], sem.at[1, b % 2]
        )
        m.start()
        moves.append(m)
    for m in moves[-2:]:
        m.wait()


def qkv_out(ids, srcs, cc):
    cols = srcs[0].shape[-1]
    half = (cc + 1) // 2
    return pl.pallas_call(
        qkv_out_kernel,
        in_specs=[SMEM] + [HBM] * 4,
        out_specs=HBM,
        out_shape=jax.ShapeDtypeStruct((cc, 1, QUAD * cols), F32),
        scratch_shapes=[
            pltpu.VMEM((2, QUAD, half, cols), BF16),
            pltpu.VMEM((half // 2, QUAD * cols), F32),
            pltpu.VMEM((2, half // 2, 1, QUAD * cols), F32),
            pltpu.SemaphoreType.DMA((2, 2 * QUAD)),
        ],
        compiler_params=params(32),
        cost_estimate=cost(0, 6 * cc * QUAD * cols),
    )(ids, *srcs)


def to_first(v):
    pairs = [(i, i ^ 1) for i in range(QUAD)] + [(QUAD + i, QUAD + (i ^ 2)) for i in range(QUAD)]
    return lax.ppermute(v, ("section", "seq"), pairs)


def to_second(v):
    pairs = [(i, i ^ 2) for i in range(QUAD)] + [(QUAD + i, QUAD + (i ^ 1)) for i in range(QUAD)]
    return lax.ppermute(v, ("section", "seq"), pairs)


def to_quad(v, k):
    return lax.ppermute(v, "seq", [(i, i ^ k) for i in range(QUAD)])


def to_core(v):
    return lax.ppermute(v, "section", [(0, 1), (1, 0)])


def dp_partner(v, step):
    n = lax.axis_size("dp")
    return lax.ppermute(v, "dp", [(i, i ^ step) for i in range(n)])


def to_owner(l, v):
    return lax.ppermute(v, "section", [(1 - l, l)])


def tied(*v):
    return lax.optimization_barrier(v)


class Order:
    def __init__(self, token):
        self.token = token

    def wait(self, *v):
        *v, self.token = lax.optimization_barrier((*v, self.token))
        return v

    def run(self, step, *operands):
        out = step(*self.wait(*operands))
        out, self.token = lax.optimization_barrier((out, self.token))
        return out


class DpSum:
    def __init__(self, order_of, make, *operands):
        self.value = None
        self.steps = self.work(order_of, make, operands)

    def go(self):
        next(self.steps, None)

    def finish(self):
        for _ in self.steps:
            pass
        return self.value

    def work(self, order_of, make, operands):
        n = lax.axis_size("dp")
        z = lax.axis_index("dp")

        def split(v, step):
            left = v.shape[0] // n * step if v.ndim == 2 else v.shape[1]
            v = v.reshape(n // (2 * step), 2, left, v.shape[-1])
            low = (z & step) == 0
            return jnp.where(low, v[:, 1], v[:, 0]), jnp.where(low, v[:, 0], v[:, 1])

        def join(v, got, step):
            low = (z & step) == 0
            both = jnp.where(low, jnp.stack([v, got], 1), jnp.stack([got, v], 1))
            return both.reshape(-1, *v.shape[1:])

        away, keep = order_of.run(lambda *v: split(make(*v), 1), *operands)
        step = 1
        while step < n:
            got = dp_partner(away, step)
            yield
            step *= 2
            if step < n:
                away, keep = order_of.run(lambda a, b, s=step: split(add_low(a, b), s), keep, got)
            else:
                v = order_of.run(add_low, keep, got)
        while step > 1:
            step //= 2
            got = dp_partner(v, step)
            yield
            v = order_of.run(functools.partial(join, step=step), v, got)
        self.value = v.reshape(-1, v.shape[-1])


def add_low(a, b):
    return (a.astype(F32) + b.astype(F32)).astype(BF16)


def quad_gather(own):
    one = to_second(own)
    two = to_first(own)
    three = to_first(one)
    return [own, one, two, three]


def on_device(
    layer_in, cotangent, lengths, w_qkv, bias_qv, w_out, bias_out,
    gain_attn, gain_mlp, w_up, bias_up, w_down, bias_down,
):
    micro, _, span, cc = layer_in.shape
    model = w_out.shape[1]
    ff = w_up.shape[-1]
    hd = model // HEADS
    width = model // QUAD
    heads = width // hd
    c = lax.axis_index("section")
    s = lax.axis_index("seq")
    dp_count = lax.axis_size("dp")
    mine = c == 0

    lens = lax.dynamic_index_in_dim(lengths, c, 0, keepdims=False)[0]
    e0 = lens[0]
    e1 = e0 + lens[1]
    e2 = e1 + lens[2]
    e3 = e2 + lens[3]
    ids = jnp.stack([c, s, e0, e1, e2, e3, c, s]).astype(jnp.int32)
    x = rows_in(ids, layer_in)
    x, w_qkv = tied(x, w_qkv)

    def row(v, n=ff):
        return jnp.pad(v, ((0, 0), (0, n - v.shape[-1])))

    qb = lax.dynamic_slice_in_dim(bias_qv, s * width, width, 1)
    vb = lax.dynamic_slice_in_dim(bias_qv, model + s * width, width, 1)
    heads_bias = jnp.concatenate([qb, jnp.zeros((1, width), F32), vb], 1)
    pv_own = jnp.concatenate(
        [row(v) for v in (bias_up, bias_out, bias_down, gain_attn, gain_mlp, heads_bias)]
        + [jnp.zeros((2, ff), F32)]
    )
    w3_own = jnp.concatenate(
        [lax.dynamic_slice_in_dim(w_qkv[0], i * model + s * width, width, 1) for i in range(3)], 1
    )
    pv_got = to_core(pv_own)
    w3_got = to_core(w3_own)
    wo_got = to_core(w_out[0])
    up = (w_up, to_core(w_up))
    dn = (w_down, to_core(w_down))
    pv = [jnp.where(mine, pv_own, pv_got), jnp.where(mine, pv_got, pv_own)]
    w3 = [jnp.where(mine, w3_own, w3_got), jnp.where(mine, w3_got, w3_own)]
    wo = [jnp.where(mine, w_out[0], wo_got), jnp.where(mine, wo_got, w_out[0])]

    normed = x
    saved = []
    squares = []
    for l in range(2):
        blocks = quad_gather(normed)
        qh, kh, vh, lse, *att = attn_fwd(l == 0, ids, blocks, w3[l], pv[l], heads, hd)
        if l == 0:
            att, blocks = att[:QUAD], att[QUAD:]
        att = [att[0]] + [to_quad(att[k], k) for k in (1, 2, 3)]
        mid, u, xout, normed, sq, astk = mlp_fwd(
            l, ids, x, att, wo[l], pv[l], pv[min(l + 1, 1)], up, dn
        )
        saved.append((x, blocks, (qh, kh, vh, lse), astk, mid, u))
        squares.append(sq[0, 0])
        x = xout
    outs = [saved[1][0], x]

    order_of = Order(ids)
    run = order_of.run

    def first_part(l, df):
        lr, rr, dmid, g, *douts = run(
            lambda v: mlp_bwd(l, ids, v, saved[l][5], saved[l][4], wo[l], pv[l], up, dn), df
        )
        return lr, rr, dmid, g, [douts[0]] + [to_quad(douts[k], k) for k in (1, 2, 3)]

    def send(l, places, lr, rr):
        return run(lambda a, b: product(True, places, ids, a, b, saved[l][3]), lr, rr)

    def keep(l, places, lr, rr, got):
        return run(lambda a, b, v: product(False, places, ids, a, b, saved[l][3], v), lr, rr, got)

    def attention(l, douts):
        outs = run(lambda *v: attn_bwd(ids, saved[l][1], w3[l], saved[l][2], v), *douts)
        return (*outs, to_first(outs[2]), to_core(outs[3]))

    def input_part(l, p0, pr, q, dmid):
        return run(lambda *v: input_grad_of(*v, saved[l][0], pv[l]), p0, pr, q, dmid)

    def projection(l, gk, gs_got, g, gb, gg):
        pad = jnp.zeros((1,), F32)
        heads_sum = jnp.concatenate([gb[0, :width], gb[0, 2 * width :]])
        v = jnp.concatenate(
            [g[0], g[1, :cc], pad, g[2, :cc], pad, gg[0, :cc], pad, g[4, :cc], pad]
            + [jnp.broadcast_to(squares[l], (128,)), heads_sum]
        )
        v = jnp.pad(v, (0, 32 * 3 * width - v.shape[0])).reshape(32, 3 * width).astype(BF16)
        return jnp.concatenate([add_low(gk, gs_got), v])

    def wait(*v):
        out = order_of.wait(*v)
        return out[0] if len(out) == 1 else out

    def pair_up(a, b):
        return jnp.stack([a, b])

    def add_first(a, b):
        return add_low(a, b[:span])

    df = rows_in(ids, cotangent)
    out_got = to_core(jnp.where(mine, outs[1], outs[0]))
    lr1, rr1, dmid1, g1, douts1 = first_part(1, df)
    out_got = wait(out_got)

    far1 = to_core(send(1, (3, 2), lr1, rr1))
    douts1 = wait(*douts1)
    near1 = send(1, (1, 0), lr1, rr1)
    far1 = wait(far1)

    far1 = keep(1, (3, 2), lr1, rr1, far1)
    x1a, near1 = to_first(far1[0]), to_core(near1)
    p0, p1, _, _, gk1, gb1, pr, gs_got = attention(1, douts1)
    x1a, near1 = wait(x1a, near1)

    near1 = keep(1, (1, 0), lr1, rr1, near1)
    half1 = run(add_low, near1[0], x1a)
    pr, gs_got = wait(pr, gs_got)

    q = to_second(run(add_first, p1, pr))
    q = wait(q)

    x1b, half1 = wait(far1[1], half1)
    x1b, x2 = to_first(x1b), to_second(half1)
    dx1, gg1 = input_part(1, p0, pr, q, dmid1)
    qkv_sum1 = DpSum(order_of, functools.partial(projection, 1), gk1, gs_got, g1, gb1, gg1)
    lr0, rr0, dmid0, g0, douts0 = first_part(0, dx1)
    far0 = to_core(send(0, (3, 2), lr0, rr0))
    near0 = send(0, (1, 0), lr0, rr0)
    x1b, x2 = wait(x1b, x2)

    sum1 = DpSum(order_of, lambda a, b, d: add_low(add_low(a, b), d), near1[1], x1b, x2)
    sum1.go()
    far0, *douts0 = wait(far0, *douts0)

    far0 = keep(0, (3, 2), lr0, rr0, far0)
    x1a, near0 = to_first(far0[0]), to_core(near0)
    p0, p1, _, _, gk0, gb0, pr, gs_got = attention(0, douts0)
    x1a, near0 = wait(x1a, near0)

    sum1.go()
    near0 = keep(0, (1, 0), lr0, rr0, near0)
    half1 = run(add_low, near0[0], x1a)
    qkv_sum1.go()
    pr, gs_got = wait(pr, gs_got)

    q = to_second(run(add_first, p1, pr))
    q = wait(q)

    x1b = to_first(wait(far0[1]))
    dx0, gg0 = input_part(0, p0, pr, q, dmid0)
    qkv_sum1.go()
    sum1.go()
    x1b, half1 = wait(x1b, half1)

    x2 = to_second(half1)
    sum1.go()
    half0 = run(add_low, near0[1], x1b)
    qkv_sum0 = DpSum(order_of, functools.partial(projection, 0), gk0, gs_got, g0, gb0, gg0)
    qkv_sum0.go()
    qkv_sum1.go()
    x2 = wait(x2)
    own1 = sum1.finish()

    have1 = [own1, to_second(own1), to_first(own1)]
    sum0 = DpSum(order_of, add_low, half0, x2)
    sum0.go()
    qkv_sum1.go()
    qkv_sum0.go()
    sum0.go()
    have1[1], have1[2] = wait(have1[1], have1[2])

    have1.append(to_first(have1[1]))
    qkv_own1 = qkv_sum1.finish()
    qkv_sum0.go()
    got1 = [to_owner(1, own1)]
    sum0.go()
    have1[3], got1[0] = wait(have1[3], got1[0])

    qkv_next1 = to_second(qkv_own1)
    got1.append(to_owner(1, have1[1]))
    qkv_sum0.go()
    qkv_next1, got1[1] = wait(qkv_next1, got1[1])
    qkv_pair1 = run(pair_up, qkv_own1, qkv_next1)
    sum0.go()

    qkv_rest1 = to_first(qkv_pair1)
    got1.append(to_owner(1, have1[2]))
    qkv_own0 = qkv_sum0.finish()
    qkv_next0 = to_second(qkv_own0)
    qkv_rest1, got1[2], qkv_next0 = wait(qkv_rest1, got1[2], qkv_next0)

    own0 = sum0.finish()
    have0 = [own0, to_second(own0), to_first(own0)]
    got1.append(to_owner(1, have1[3]))
    qkv_pair0 = run(pair_up, qkv_own0, qkv_next0)
    qkv_rest0 = to_first(qkv_pair0)
    got1[3] = wait(got1[3])
    got0 = [to_owner(0, own0)]
    in_got = to_core(run(lambda a, b: jnp.where(mine, a, b), dx1, dx0))
    qkv1 = run(lambda a, b: jnp.concatenate([a, b]), qkv_pair1, qkv_rest1)
    layer_out = run(
        lambda a, b, d: rows_out(ids, jnp.where(mine, a, b), d), outs[0], outs[1], out_got
    )
    got0[0], in_got = wait(got0[0], in_got)

    def place(places, outs_w):
        srcs = [v[p] for p in places for v in (have0, got0, got1, have1)]
        n = len(srcs)
        return run(
            lambda *v: place_rows(places, ids, v[:n], v[n:] or None, cc, ff, model), *srcs, *outs_w
        )

    outs_w = place((0,), ())
    input_grad = run(lambda a, b, d: rows_out(ids, jnp.where(mine, a, b), d), dx0, dx1, in_got)
    have0[1], have0[2], qkv_rest0 = wait(have0[1], have0[2], qkv_rest0)

    have0.append(to_first(have0[1]))
    got0 += [to_owner(0, have0[1]), to_owner(0, have0[2])]
    qkv0 = run(lambda a, b: jnp.concatenate([a, b]), qkv_pair0, qkv_rest0)
    got0[1], got0[2] = wait(got0[1], got0[2])
    qkv0_got, qkv1_got = to_owner(0, qkv0), to_owner(1, qkv1)
    outs_w = place((1,), outs_w)
    qkv0_got, qkv1_got = wait(qkv0_got, qkv1_got)
    outs_w = place((2,), outs_w)
    have0[3] = wait(have0[3])

    got0.append(to_owner(0, have0[3]))
    grad_qkv = run(lambda *v: qkv_out(ids, v, cc), qkv0, qkv0_got, qkv1_got, qkv1)
    got0[3] = wait(got0[3])
    grad_down, grad_up, grad_out = place_rows(
        (3,), order_of.token, [v[3] for v in (have0, got0, got1, have1)], outs_w, cc, ff, model
    )

    half = (cc + 1) // 2
    tails = [v[:, half:].astype(F32).reshape(QUAD, -1) for v in (qkv0, qkv0_got, qkv1_got, qkv1)]
    tails = [jnp.where(mine, tails[0], tails[2]), jnp.where(mine, tails[1], tails[3])]
    small = jnp.sum(tails[0] + tails[1], 0)

    def take(lo, n):
        return small[lo : lo + n][None]

    d = cc + 1
    at = ff
    total = micro * dp_count * span * QUAD
    base = ff + 4 * d
    rms = jnp.sqrt(small[base] / total).reshape(1)
    seq_of = jnp.arange(QUAD)
    heads_of = jnp.zeros((QUAD, 2 * width), F32)
    for chain in range(2):
        for p in range(QUAD):
            here = seq_of == jnp.bitwise_xor(order(chain, p), s)
            row_of = tails[chain][p, base + 128 : base + 128 + 2 * width]
            heads_of = heads_of + jnp.where(here[:, None], row_of, 0.0)
    grad_bqv = jnp.concatenate(
        [heads_of[:, i * width : (i + 1) * width].reshape(model) for i in range(2)]
    )
    return (
        layer_out,
        input_grad,
        jnp.transpose(grad_qkv, (1, 0, 2)),
        grad_bqv[None],
        jnp.transpose(grad_out, (1, 2, 0)),
        take(at, cc),
        take(at + 2 * d, cc),
        take(at + 3 * d, cc),
        jnp.transpose(grad_up, (1, 0, 2)),
        take(0, ff),
        jnp.transpose(grad_down, (1, 2, 0)),
        take(at + d, cc),
        rms,
    )


def solution(mesh):
    two = P("section", None)
    three = P("section", None, None)
    tokens = P(None, "dp", "seq", None)
    stacked = P("section", None, "dp", "seq", None)
    return jax.shard_map(
        on_device,
        mesh=mesh,
        in_specs=(
            tokens, tokens, P(None, "dp", None), three, two, three, two, two, two, three, two, three, two,
        ),
        out_specs=(
            stacked, stacked, three, two, three, two, two, two, three, two, three, two, P("section"),
        ),
        check_vma=False,
    )
```

```python
import functools

import jax
import jax.numpy as jnp
from jax import lax
from jax.experimental import pallas as pl
from jax.experimental.pallas import tpu as pltpu
from jax.sharding import PartitionSpec as P

HEADS = 12
EPS = 1e-6
NEG = -1e30
F32 = jnp.float32
BF16 = jnp.bfloat16
MIB = 1 << 20
QUAD = 4


def nn(a, b):
    return lax.dot_general(a, b, (((1,), (0,)), ((), ())), preferred_element_type=F32)


def nt(a, b):
    return lax.dot_general(a, b, (((1,), (1,)), ((), ())), preferred_element_type=F32)


def tn(a, b):
    return lax.dot_general(a, b, (((0,), (0,)), ((), ())), preferred_element_type=F32)


def order(core, k):
    return jnp.where(core == 1, k, ((k & 1) << 1) | (k >> 1))


def crms_scale(v):
    sq = jnp.sum(v * v, axis=-1, keepdims=True)
    su = jnp.sum(v, axis=-1, keepdims=True)
    full = v.shape[-1] + 1
    return lax.rsqrt((sq + su * su) / full + EPS), su, (sq + su * su) / full


def crms_back(v, gain, grad):
    r, su, _ = crms_scale(v)
    gd = grad * gain
    w = jnp.sum(gd * v, axis=-1, keepdims=True)
    unit = v * r
    dv = gd * r - (w * r * r * r / (v.shape[-1] + 1)) * (v + su)
    return dv, grad * unit, unit * gain


GC = 0.7978845608028654


def gelu_parts(u):
    inner = GC * (u + 0.044715 * (u * u * u))
    th = jnp.tanh(inner)
    return th


def params(mib, **kw):
    return pltpu.CompilerParams(vmem_limit_bytes=mib * MIB, **kw)


def cost(flops, nbytes, trans=0):
    return pl.CostEstimate(flops=int(flops), bytes_accessed=int(nbytes), transcendentals=int(trans))


SMEM = pl.BlockSpec(memory_space=pltpu.SMEM)
VMEM = pl.BlockSpec(memory_space=pltpu.VMEM)
HBM = pl.BlockSpec(memory_space=pltpu.HBM)


def rows_in_kernel(ids, v, o):
    @pl.when(ids[0] == 0)
    def _():
        o[...] = v[:, 0, :].T

    @pl.when(ids[0] != 0)
    def _():
        o[...] = v[:, 1, :].T


def rows_in(ids, v):
    micro, _, span, cc = v.shape
    return pl.pallas_call(
        rows_in_kernel,
        in_specs=[SMEM, VMEM],
        out_specs=VMEM,
        out_shape=jax.ShapeDtypeStruct((span, cc), BF16),
        compiler_params=params(16),
        cost_estimate=cost(0, 6 * span * cc),
    )(ids, jnp.transpose(v[:, 0], (2, 0, 1)))


def rows_out_kernel(ids, own, got, o):
    @pl.when(ids[0] == 0)
    def _():
        o[:, 0, :] = own[...].T
        o[:, 1, :] = got[...].T

    @pl.when(ids[0] != 0)
    def _():
        o[:, 0, :] = got[...].T
        o[:, 1, :] = own[...].T


def rows_out(ids, own, got):
    span, cc = own.shape
    o = pl.pallas_call(
        rows_out_kernel,
        in_specs=[SMEM, VMEM, VMEM],
        out_specs=VMEM,
        out_shape=jax.ShapeDtypeStruct((cc, 2, span), BF16),
        compiler_params=params(16),
        cost_estimate=cost(0, 8 * span * cc),
    )(ids, own, got)
    return jnp.transpose(o, (1, 2, 0))[None, :, None]


def visible_bias(ids, n, t, span):
    i = t * span + lax.broadcasted_iota(jnp.int32, (1, span), 1)
    start = jnp.zeros((1, span), jnp.int32)
    for d in range(4):
        end = ids[2 + d]
        start = jnp.maximum(start, jnp.where(i >= end, end, 0))
    j = lax.broadcasted_iota(jnp.int32, (n, span), 0)
    return jnp.where((j >= start) & (j <= i), 0.0, NEG)


def attn_fwd_kernel(
    raw, ids, n0, n1, n2, n3, w_ref, pv_ref, qh, kh, vh, lse, a0, a1, a2, a3, *rest
):
    c, s = ids[0], ids[1]
    heads, _, hd = qh.shape
    span, cc = n0.shape
    width = heads * hd
    at, bias_scr = rest[-2:]
    bias = pv_ref[5:6, : 3 * width]
    for p, nb in enumerate((n0, n1, n2, n3)):
        t = jnp.bitwise_xor(order(c, p), s)
        row = pl.multiple_of(t * span, span)
        rows = nb[...]
        if raw:
            v = rows.astype(F32)
            rows = (v * crms_scale(v)[0] * pv_ref[3:4, :cc]).astype(BF16)
            rest[p][...] = rows
        y = nn(rows, w_ref[...]) + bias
        for h in range(heads):
            lo = h * hd
            qh[h, pl.ds(row, span), :] = (y[:, lo : lo + hd] * (hd**-0.5)).astype(BF16)
            kh[h, pl.ds(row, span), :] = y[:, width + lo : width + lo + hd].astype(BF16)
            vh[h, pl.ds(row, span), :] = y[:, 2 * width + lo : 2 * width + lo + hd].astype(BF16)
    for t in range(QUAD):
        n = span * (t + 1)
        bias_scr[:n, :] = visible_bias(ids, n, t, span)

        def head(h, carry, t=t, n=n):
            q = qh[h, t * span : (t + 1) * span, :]
            sc = nt(kh[h, :n, :], q) + bias_scr[:n, :]
            m = jnp.max(sc, axis=0, keepdims=True)
            e = jnp.exp(sc - m)
            tot = jnp.sum(e, axis=0, keepdims=True)
            pr = (e * (1.0 / tot)).astype(BF16)
            o = tn(vh[h, :n, :], pr)
            at[t, pl.ds(pl.multiple_of(h * hd, hd), hd), :] = o.astype(BF16)
            lse[h, t : t + 1, :] = m + jnp.log(tot)
            return carry

        lax.fori_loop(0, heads, head, 0)
    for k, a in enumerate((a0, a1, a2, a3)):
        a[...] = at[jnp.bitwise_xor(s, k)]


def attn_fwd(raw, ids, blocks, w3, pv, heads, hd):
    span, width = blocks[0].shape
    full = span * QUAD
    hh = jax.ShapeDtypeStruct((heads, full, hd), BF16)
    aa = jax.ShapeDtypeStruct((heads * hd, span), BF16)
    normed = [jax.ShapeDtypeStruct((span, width), BF16)] * (QUAD if raw else 0)
    return pl.pallas_call(
        functools.partial(attn_fwd_kernel, raw),
        in_specs=[SMEM] + [VMEM] * 6,
        out_specs=[VMEM] * (8 + len(normed)),
        out_shape=[hh, hh, hh, jax.ShapeDtypeStruct((heads, QUAD, span), F32), aa, aa, aa, aa] + normed,
        scratch_shapes=[
            pltpu.VMEM((QUAD, heads * hd, span), BF16),
            pltpu.VMEM((full, span), F32),
        ],
        compiler_params=params(22),
        cost_estimate=cost(
            2 * full * width * 3 * heads * hd + 3 * 4 * full * full * hd * heads,
            4 * full * width,
            heads * full * full,
        ),
    )(ids, *blocks, w3, pv)


def mlp_fwd_kernel(
    layer, ids, x, a0, a1, a2, a3, wo, pv, pvn, pvb, upo, upr, dno, dnr,
    mid, u, xout, nnext, sq, astk, nm, acc,
):
    j = pl.program_id(0)
    c, s = ids[0], ids[1]
    cc = x.shape[-1]
    own = c == layer

    @pl.when(j == 0)
    def _():
        rows = a0.shape[0]
        m = x[...].astype(F32) + pv[1:2, :cc]
        for k, a in enumerate((a0, a1, a2, a3)):
            row = pl.multiple_of(jnp.bitwise_xor(s, k) * rows, rows)
            m = m + tn(a[...], wo[pl.ds(row, rows), :])
            astk[jnp.bitwise_xor(s, k)] = a[...].T
        mid[...] = m
        r, _, _ = crms_scale(m)
        nm[...] = (m * r * pv[4:5, :cc]).astype(BF16)
        acc[...] = m + pv[2:3, :cc]

    wu = lax.select(own, upo[0], upr[0])
    wd = lax.select(own, dno[0], dnr[0])
    ub = nn(nm[...], wu) + pvb[0:1, :]
    u[...] = ub
    act = (0.5 * ub * (1.0 + gelu_parts(ub))).astype(BF16)
    acc[...] += nn(act, wd)

    @pl.when(j == pl.num_programs(0) - 1)
    def _():
        fin = acc[...]
        _, _, ms = crms_scale(fin)
        sq[...] = jnp.broadcast_to(jnp.sum(ms, axis=0, keepdims=True), sq.shape)
        low = fin.astype(BF16)
        xout[...] = low
        lf = low.astype(F32)
        r, _, _ = crms_scale(lf)
        nnext[...] = (lf * r * pvn[3:4, :cc]).astype(BF16)


def mlp_fwd(layer, ids, x, att, wo, pv, pvn, up, dn):
    span, cc = x.shape
    ff = up[0].shape[-1]
    fb = ff // 8
    rows = att[0].shape[0]

    def whole(shape):
        return pl.BlockSpec(shape, lambda j, ids: (0,) * len(shape))

    def pick(mine):
        return lambda j, ids: jnp.where((ids[0] == layer) == mine, j, 0)

    mine, other = pick(True), pick(False)
    grid = pltpu.PrefetchScalarGridSpec(
        num_scalar_prefetch=1,
        grid=(8,),
        in_specs=[whole((span, cc))]
        + [whole((rows, span))] * 4
        + [whole(wo.shape), whole(pv.shape), whole(pvn.shape)]
        + [
            pl.BlockSpec((8, fb), lambda j, ids: (0, j)),
            pl.BlockSpec((1, cc, fb), lambda j, ids: (0, 0, mine(j, ids))),
            pl.BlockSpec((1, cc, fb), lambda j, ids: (0, 0, other(j, ids))),
            pl.BlockSpec((1, fb, cc), lambda j, ids: (0, mine(j, ids), 0)),
            pl.BlockSpec((1, fb, cc), lambda j, ids: (0, other(j, ids), 0)),
        ],
        out_specs=[
            whole((span, cc)),
            pl.BlockSpec((span, fb), lambda j, ids: (0, j)),
            whole((span, cc)),
            whole((span, cc)),
            whole((8, 128)),
            whole((QUAD, span, rows)),
        ],
        scratch_shapes=[pltpu.VMEM((span, cc), BF16), pltpu.VMEM((span, cc), F32)],
    )
    return pl.pallas_call(
        functools.partial(mlp_fwd_kernel, layer),
        grid_spec=grid,
        out_shape=[
            jax.ShapeDtypeStruct((span, cc), F32),
            jax.ShapeDtypeStruct((span, ff), F32),
            jax.ShapeDtypeStruct((span, cc), BF16),
            jax.ShapeDtypeStruct((span, cc), BF16),
            jax.ShapeDtypeStruct((8, 128), F32),
            jax.ShapeDtypeStruct((QUAD, span, rows), BF16),
        ],
        compiler_params=params(22, dimension_semantics=("arbitrary",)),
        cost_estimate=cost(6 * span * cc * ff, 4 * cc * ff + 4 * span * ff, span * ff),
    )(ids, x, *att, wo, pv, pvn, pv, up[0], up[1], dn[0], dn[1])


def mlp_bwd_kernel(
    layer, ids, df, u, mid, wo, pv, upo, upr, dno, dnr,
    lr, rr, dmid, g, d0, d1, d2, d3, acc, wide,
):
    j = pl.program_id(0)
    c, s = ids[0], ids[1]
    cc = df.shape[-1]
    fb = u.shape[-1]
    own = c == layer

    @pl.when(j == 0)
    def _():
        acc[...] = jnp.zeros_like(acc)
        g[...] = jnp.zeros_like(g)

    wu = lax.select(own, upo[0], upr[0])
    wd = lax.select(own, dno[0], dnr[0])
    da = nt(df[...], wd)
    ub = u[...]
    th = gelu_parts(ub)
    half = 0.5 * (1.0 + th)
    lr[0] = (ub * half).astype(BF16)
    slope = half + 0.5 * ub * (1.0 - th * th) * (GC * (1.0 + 3 * 0.044715 * (ub * ub)))
    du = (slope * da).astype(BF16)
    lr[1] = du
    g[0:1, pl.ds(pl.multiple_of(j * fb, 128), fb)] = jnp.sum(du.astype(F32), axis=0, keepdims=True)
    acc[...] += nt(du, wu)

    @pl.when(j == pl.num_programs(0) - 1)
    def _():
        dff = df[...].astype(F32)
        dv, gg, nm = crms_back(mid[...], pv[4:5, :cc], acc[...])
        dm = dff + dv
        low = dm.astype(BF16)
        dmid[...] = dm
        quarter = rr.shape[-1]
        wide[:, cc:] = jnp.zeros((wide.shape[0], wide.shape[1] - cc), BF16)
        for i, v in enumerate((df[...], nm.astype(BF16), low)):
            wide[:, :cc] = v
            for t in range(QUAD):
                rr[i, t] = wide[:, t * quarter : (t + 1) * quarter]
        g[1:2, :cc] = jnp.sum(low.astype(F32), axis=0, keepdims=True)
        g[2:3, :cc] = jnp.sum(dff, axis=0, keepdims=True)
        g[4:5, :cc] = jnp.sum(gg, axis=0, keepdims=True)
        rows = d0.shape[0]
        for k, d in enumerate((d0, d1, d2, d3)):
            row = pl.multiple_of(jnp.bitwise_xor(s, k) * rows, rows)
            d[...] = nt(wo[pl.ds(row, rows), :], low).astype(BF16)


def mlp_bwd(layer, ids, df, u, mid, wo, pv, up, dn):
    span, cc = df.shape
    ff = u.shape[-1]
    fb = ff // 8
    rows = wo.shape[0] // QUAD

    def whole(shape):
        return pl.BlockSpec(shape, lambda j, ids: (0,) * len(shape))

    def pick(mine):
        return lambda j, ids: jnp.where((ids[0] == layer) == mine, j, 0)

    mine, other = pick(True), pick(False)
    grid = pltpu.PrefetchScalarGridSpec(
        num_scalar_prefetch=1,
        grid=(8,),
        in_specs=[
            whole((span, cc)),
            pl.BlockSpec((span, fb), lambda j, ids: (0, j)),
            whole((span, cc)),
            whole(wo.shape),
            whole(pv.shape),
            pl.BlockSpec((1, cc, fb), lambda j, ids: (0, 0, mine(j, ids))),
            pl.BlockSpec((1, cc, fb), lambda j, ids: (0, 0, other(j, ids))),
            pl.BlockSpec((1, fb, cc), lambda j, ids: (0, mine(j, ids), 0)),
            pl.BlockSpec((1, fb, cc), lambda j, ids: (0, other(j, ids), 0)),
        ],
        out_specs=[
            pl.BlockSpec((2, span, fb), lambda j, ids: (0, 0, j)),
            whole((3, QUAD, span, (cc + 1) // QUAD)),
            whole((span, cc)),
            whole((8, ff)),
        ]
        + [whole((rows, span))] * 4,
        scratch_shapes=[pltpu.VMEM((span, cc), F32), pltpu.VMEM((span, cc + 1), BF16)],
    )
    dd = jax.ShapeDtypeStruct((rows, span), BF16)
    return pl.pallas_call(
        functools.partial(mlp_bwd_kernel, layer),
        grid_spec=grid,
        out_shape=[
            jax.ShapeDtypeStruct((2, span, ff), BF16),
            jax.ShapeDtypeStruct((3, QUAD, span, (cc + 1) // QUAD), BF16),
            jax.ShapeDtypeStruct((span, cc), F32),
            jax.ShapeDtypeStruct((8, ff), F32),
            dd, dd, dd, dd,
        ],
        compiler_params=params(24, dimension_semantics=("arbitrary",)),
        cost_estimate=cost(6 * span * cc * ff, 4 * cc * ff + 8 * span * ff, span * ff),
    )(ids, df, u, mid, wo, pv, up[0], up[1], dn[0], dn[1])


def product_kernel(send, places, ids, lr, rr, att, *rest):
    outs = [rest[0].at[i] for i in range(len(places))] if send else rest[1:]
    core = 1 - ids[0] if send else ids[0]
    ff = lr.shape[-1]
    part = att.shape[-1]
    for i, place in enumerate(places):
        t = jnp.bitwise_xor(order(core, place), ids[1])
        out = outs[i]
        main = tn(rr[core, t], lr[core])
        low = rr[2, t]
        sides = [tn(low, att[2 * core + h]) for h in range(2)]
        if not send:
            got = rest[0].at[i]
            main = main + got[:, :ff].astype(F32)
            sides = [v + got[:, ff + h * part : ff + (h + 1) * part].astype(F32) for h, v in enumerate(sides)]
        out[:, :ff] = main.astype(BF16)
        for h, v in enumerate(sides):
            out[:, ff + h * part : ff + (h + 1) * part] = v.astype(BF16)


def product(send, places, ids, lr, rr, att, *got):
    span, quarter = rr.shape[2:]
    cols = lr.shape[-1] + 2 * att.shape[-1]
    return pl.pallas_call(
        functools.partial(product_kernel, send, places),
        in_specs=[SMEM] + [VMEM] * (3 + len(got)),
        out_specs=VMEM if send else [VMEM] * len(places),
        out_shape=jax.ShapeDtypeStruct((len(places), quarter, cols), BF16)
        if send
        else [jax.ShapeDtypeStruct((quarter, cols), BF16)] * len(places),
        compiler_params=params(22),
        cost_estimate=cost(2 * span * quarter * cols * len(places), 2 * 4 * quarter * cols * len(places)),
    )(ids, lr, rr, att, *got)


def attn_bwd_kernel(
    ids, n0, n1, n2, n3, w_hbm, q_hbm, k_hbm, v_hbm, l_hbm, d0, d1, d2, d3,
    p0, p1, far, gs, gk, gb, do, dk, dv, dy, acc, bias_scr,
    nb, w_ref, qh, kh, vh, lse, sem,
):
    c, s = ids[0], ids[1]
    heads, _, hd = qh.shape
    span, cc = n0.shape
    width = heads * hd
    moves = [
        pltpu.make_async_copy(src, dst, sem.at[i])
        for i, (src, dst) in enumerate(
            [(q_hbm, qh), (k_hbm, kh), (v_hbm, vh), (l_hbm, lse), (w_hbm, w_ref)]
            + [(n, nb.at[i]) for i, n in enumerate((n0, n1, n2, n3))]
        )
    ]
    for m in moves:
        m.start()
    for k, d in enumerate((d0, d1, d2, d3)):
        do[jnp.bitwise_xor(s, k)] = d[...]
    for m in moves[:4]:
        m.wait()
    for t in reversed(range(QUAD)):
        n = span * (t + 1)
        bias_scr[:n, :] = visible_bias(ids, n, t, span)
        for h in range(heads):
            q = qh[h, t * span : (t + 1) * span, :]
            kk = kh[h, :n, :]
            sc = nt(kk, q) + (bias_scr[:n, :] - lse[h, t : t + 1, :])
            pr = jnp.exp(sc)
            dot = do[t, h * hd : (h + 1) * hd, :]
            dp = nn(vh[h, :n, :], dot)
            inner = jnp.sum(pr * dp, axis=0, keepdims=True)
            ds = (pr * (dp - inner)).astype(BF16)
            newk = nn(ds, q)
            newv = nt(pr.astype(BF16), dot)
            if t == QUAD - 1:
                dk[h, :n, :] = newk
                dv[h, :n, :] = newv
            else:
                dk[h, :n, :] += newk
                dv[h, :n, :] += newv
            dq = tn(kk, ds) * (hd**-0.5)
            dy[t * span : (t + 1) * span, h * hd : (h + 1) * hd] = dq.T.astype(BF16)
    for h in range(heads):
        dy[:, width + h * hd : width + (h + 1) * hd] = dk[h].astype(BF16)
        dy[:, 2 * width + h * hd : 2 * width + (h + 1) * hd] = dv[h].astype(BF16)
    for m in moves[4:]:
        m.wait()
    total = jnp.zeros((1, 3 * width), F32)
    for p, out in enumerate((p0, p1, far.at[span:], far.at[:span])):
        row = pl.multiple_of(jnp.bitwise_xor(order(c, p), s) * span, span)
        y = dy[pl.ds(row, span), :]
        out[...] = nt(y, w_ref[...]).astype(BF16)
        total = total + jnp.sum(y.astype(F32), axis=0, keepdims=True)
        g = tn(nb[p], y)
        if p == 0:
            acc[:cc, :] = g
        else:
            acc[:cc, :] += g
    gb[...] = jnp.broadcast_to(total, gb.shape)
    part = gs.shape[0]
    acc[cc:, :] = jnp.zeros((acc.shape[0] - cc, acc.shape[1]), F32)
    gk[...] = acc[pl.ds(pl.multiple_of(c * part, part), part), :].astype(BF16)
    gs[...] = acc[pl.ds(pl.multiple_of((1 - c) * part, part), part), :].astype(BF16)


def attn_bwd(ids, blocks, w3, qkvl, douts):
    span, cc = blocks[0].shape
    heads, full, hd = qkvl[0].shape
    width = heads * hd
    pp = jax.ShapeDtypeStruct((span, cc), BF16)
    gg = jax.ShapeDtypeStruct(((cc + 1) // 2, 3 * width), BF16)
    return pl.pallas_call(
        attn_bwd_kernel,
        in_specs=[SMEM] + [HBM] * 9 + [VMEM] * 4,
        out_specs=[VMEM] * 6,
        out_shape=[pp, pp, jax.ShapeDtypeStruct((2 * span, cc), BF16), gg, gg, jax.ShapeDtypeStruct((8, 3 * width), F32)],
        scratch_shapes=[
            pltpu.VMEM((QUAD, width, span), BF16),
            pltpu.VMEM((heads, full, hd), F32),
            pltpu.VMEM((heads, full, hd), F32),
            pltpu.VMEM((full, 3 * width), BF16),
            pltpu.VMEM((cc + 1, 3 * width), F32),
            pltpu.VMEM((full, span), F32),
            pltpu.VMEM((QUAD, span, cc), BF16),
            pltpu.VMEM(w3.shape, BF16),
            pltpu.VMEM((heads, full, hd), BF16),
            pltpu.VMEM((heads, full, hd), BF16),
            pltpu.VMEM((heads, full, hd), BF16),
            pltpu.VMEM((heads, QUAD, span), F32),
            pltpu.SemaphoreType.DMA((9,)),
        ],
        compiler_params=params(30),
        cost_estimate=cost(
            4 * full * cc * 3 * width + 3 * 10 * full * full * hd * heads,
            8 * full * cc,
            heads * full * full,
        ),
    )(ids, *blocks, w3, *qkvl, *douts)


def input_kernel(part, r0, r1, dmid, x, pv, dx, gg):
    cc = x.shape[-1]
    dn = part[...].astype(F32) + r0[part.shape[0] :, :].astype(F32) + r1[...].astype(F32)
    dv, g, _ = crms_back(x[...].astype(F32), pv[3:4, :cc], dn)
    dx[...] = (dmid[...] + dv).astype(BF16)
    gg[...] = jnp.broadcast_to(jnp.sum(g, axis=0, keepdims=True), gg.shape)


def input_grad_of(part, r0, r1, dmid, x, pv):
    return pl.pallas_call(
        input_kernel,
        in_specs=[VMEM] * 6,
        out_specs=[VMEM] * 2,
        out_shape=[
            jax.ShapeDtypeStruct(x.shape, BF16),
            jax.ShapeDtypeStruct((8, x.shape[-1]), F32),
        ],
        compiler_params=params(16),
        cost_estimate=cost(0, x.size * 14),
    )(part, r0, r1, dmid, x, pv)


def both_lengths(t, rows, start):
    @pl.when(t < QUAD - 1)
    def _():
        start(rows)

    @pl.when(t == QUAD - 1)
    def _():
        start(rows - 1)


def place_kernel(places, first, ids, *refs):
    n = len(places)
    srcs = refs[: 4 * n]
    refs = refs[4 * n :]
    outs = refs[:3] if first else refs[3:6]
    x0, x1, od, ou, ow, sem = refs[3:] if first else refs[6:]
    c, s = ids[0], ids[1]
    down, up, wout = outs
    _, rows, _, ff = od.shape
    part = ow.shape[-1]

    def reads(i, j):
        return [
            pltpu.make_async_copy(srcs[4 * i + j], x0.at[i], sem.at[0, i]),
            pltpu.make_async_copy(srcs[4 * i + j + 1], x1.at[i], sem.at[1, i]),
        ]

    for core in range(2):

        @pl.when(c == core)
        def _():
            for i in range(n):
                for m in reads(i, 2 * core):
                    m.start()

    def writes(length, i, side, t):
        o, dst = ((od, down), (ou, up))[side]
        return [
            pltpu.make_async_copy(
                o.at[i, pl.ds(0, length)], dst.at[pl.ds(t * rows, length)], sem.at[2 + side, i]
            ),
            pltpu.make_async_copy(
                ow.at[side, i, pl.ds(0, length)],
                wout.at[pl.ds(t * rows, length), :, pl.ds(side * part, part)],
                sem.at[4 + side, i],
            ),
        ]

    jobs = []
    for i, place in enumerate(places):
        for m in reads(i, 0):
            m.wait()
        swapped = ((place & 1) << 1) | (place >> 1)
        for side, (x, o, k) in enumerate(((x0, od, swapped), (x1, ou, place))):
            t = jnp.bitwise_xor(k, s)
            o[i, :, 0, :] = x[i, :, :ff].astype(F32)
            ow[side, i, :, 0, :] = x[i, :, ff:].astype(F32)
            both_lengths(t, rows, lambda length: [m.start() for m in writes(length, i, side, t)])
            jobs.append((i, side, t))
    for i, side, t in jobs:
        both_lengths(t, rows, lambda length: [m.wait() for m in writes(length, i, side, t)])


def place_rows(places, ids, srcs, outs, cc, ff, model):
    rows, cols = srcs[0].shape
    n = len(places)
    first = outs is None
    operands = [ids, *srcs] + ([] if first else list(outs))
    return pl.pallas_call(
        functools.partial(place_kernel, places, first),
        in_specs=[SMEM] + [HBM] * (len(operands) - 1),
        out_specs=[HBM] * 3,
        out_shape=[jax.ShapeDtypeStruct((cc, 1, m), F32) for m in (ff, ff, model)],
        input_output_aliases={} if first else {4 * n + 1 + i: i for i in range(3)},
        scratch_shapes=[
            pltpu.VMEM((n, rows, cols), BF16),
            pltpu.VMEM((n, rows, cols), BF16),
            pltpu.VMEM((n, rows, 1, ff), F32),
            pltpu.VMEM((n, rows, 1, ff), F32),
            pltpu.VMEM((2, n, rows, 1, cols - ff), F32),
            pltpu.SemaphoreType.DMA((6, n)),
        ],
        compiler_params=params(16),
        cost_estimate=cost(0, 12 * n * rows * cols),
    )(*operands)


def qkv_out_kernel(ids, *refs):
    srcs, out, rows, wide, od, sem = refs[:4], *refs[4:]
    c, s = ids[0], ids[1]
    _, _, half, cols = rows.shape
    width = cols // 3

    def reads(a, b):
        return [
            pltpu.make_async_copy(
                src.at[p, pl.ds(0, half), :],
                rows.at[i, jnp.bitwise_xor(p if i else ((p & 1) << 1) | (p >> 1), s)],
                sem.at[0, i * QUAD + p],
            )
            for i, src in enumerate((a, b))
            for p in range(QUAD)
        ]

    @pl.when(c == 0)
    def _():
        for m in reads(srcs[0], srcs[1]):
            m.start()

    @pl.when(c != 0)
    def _():
        for m in reads(srcs[2], srcs[3]):
            m.start()

    for m in reads(srcs[0], srcs[1]):
        m.wait()
    step = half // 2
    moves = []
    for b in range(4):
        if b >= 2:
            moves[b - 2].wait()
        for t in range(QUAD):
            v = rows[b // 2, t, (b % 2) * step : (b % 2 + 1) * step, :].astype(F32)
            for i in range(3):
                lo = (i * QUAD + t) * width
                wide[:, lo : lo + width] = v[:, i * width : (i + 1) * width]
        od[b % 2, :, 0, :] = wide[...]
        n = step - (b == 3)
        m = pltpu.make_async_copy(
            od.at[b % 2, pl.ds(0, n)], out.at[pl.ds(b * step, n)], sem.at[1, b % 2]
        )
        m.start()
        moves.append(m)
    for m in moves[-2:]:
        m.wait()


def qkv_out(ids, srcs, cc):
    cols = srcs[0].shape[-1]
    half = (cc + 1) // 2
    return pl.pallas_call(
        qkv_out_kernel,
        in_specs=[SMEM] + [HBM] * 4,
        out_specs=HBM,
        out_shape=jax.ShapeDtypeStruct((cc, 1, QUAD * cols), F32),
        scratch_shapes=[
            pltpu.VMEM((2, QUAD, half, cols), BF16),
            pltpu.VMEM((half // 2, QUAD * cols), F32),
            pltpu.VMEM((2, half // 2, 1, QUAD * cols), F32),
            pltpu.SemaphoreType.DMA((2, 2 * QUAD)),
        ],
        compiler_params=params(18),
        cost_estimate=cost(0, 6 * cc * QUAD * cols),
    )(ids, *srcs)


def vectors_kernel(count, ids, *refs):
    srcs, outs, (rows, heads, sem) = refs[:4], refs[4:-3], refs[-3:]
    c, s = ids[0], ids[1]
    _, _, tall, row_len = rows.shape
    top = srcs[0].shape[1] - tall

    def reads(pair):
        return [
            pltpu.make_async_copy(v.at[p, pl.ds(top, tall), :], rows.at[i, p], sem.at[i * QUAD + p])
            for i, v in enumerate(pair)
            for p in range(QUAD)
        ]

    for core in range(2):

        @pl.when(c == core)
        def _():
            for m in reads(srcs[2 * core : 2 * core + 2]):
                m.start()

    for m in reads(srcs[:2]):
        m.wait()
    total = jnp.zeros((tall, row_len), F32)
    for i in range(2):
        for p in range(QUAD):
            total = total + rows[i, p].astype(F32)
    at = 0
    for o in outs[:5]:
        n = o.shape[1]
        for lo in range(0, n, row_len):
            size = min(row_len, n - lo)
            o[0:1, lo : lo + size] = total[at : at + 1, :size]
            at += 1
    heads[...] = jnp.zeros_like(heads)
    for i in range(2):
        for p in range(QUAD):
            k = p if i else ((p & 1) << 1) | (p >> 1)
            heads[jnp.bitwise_xor(k, s)] += rows[i, p, at : at + 8, :].astype(F32)
    width = row_len // 3
    for part in range(2):
        for t in range(QUAD):
            lo = (part * QUAD + t) * width
            outs[5][0:1, lo : lo + width] = heads[t, 0:1, part * width : (part + 1) * width]
    outs[6][0:1, :] = jnp.sqrt(total[at + 1 : at + 2, : outs[6].shape[1]] / count)


def vectors_out(ids, srcs, count, cc, ff, model):
    row_len = srcs[0].shape[-1]
    shapes = [ff, cc, cc, cc, cc, 2 * model, 128]
    return pl.pallas_call(
        functools.partial(vectors_kernel, count),
        in_specs=[SMEM] + [HBM] * 4,
        out_specs=[VMEM] * 7,
        out_shape=[jax.ShapeDtypeStruct((1, n), F32) for n in shapes],
        scratch_shapes=[
            pltpu.VMEM((2, QUAD, 32, row_len), BF16),
            pltpu.VMEM((QUAD, 8, row_len), F32),
            pltpu.SemaphoreType.DMA((2 * QUAD,)),
        ],
        compiler_params=params(8),
        cost_estimate=cost(0, 1 << 19),
    )(ids, *srcs)


def to_first(v):
    pairs = [(i, i ^ 1) for i in range(QUAD)] + [(QUAD + i, QUAD + (i ^ 2)) for i in range(QUAD)]
    return lax.ppermute(v, ("section", "seq"), pairs)


def to_second(v):
    pairs = [(i, i ^ 2) for i in range(QUAD)] + [(QUAD + i, QUAD + (i ^ 1)) for i in range(QUAD)]
    return lax.ppermute(v, ("section", "seq"), pairs)


def to_quad(v, k):
    return lax.ppermute(v, "seq", [(i, i ^ k) for i in range(QUAD)])


def to_core(v):
    return lax.ppermute(v, "section", [(0, 1), (1, 0)])


def dp_partner(v, step):
    n = lax.axis_size("dp")
    return lax.ppermute(v, "dp", [(i, i ^ step) for i in range(n)])


def to_owner(l, v):
    return lax.ppermute(v, "section", [(1 - l, l)])


def tied(*v):
    return lax.optimization_barrier(v)


class Order:
    def __init__(self, token):
        self.token = token

    def wait(self, *v):
        *v, self.token = lax.optimization_barrier((*v, self.token))
        return v

    def run(self, step, *operands):
        out = step(*self.wait(*operands))
        out, self.token = lax.optimization_barrier((out, self.token))
        return out


class DpSum:
    def __init__(self, order_of, make, *operands):
        self.value = None
        self.steps = self.work(order_of, make, operands)

    def go(self):
        next(self.steps, None)

    def finish(self):
        for _ in self.steps:
            pass
        return self.value

    def work(self, order_of, make, operands):
        n = lax.axis_size("dp")
        z = lax.axis_index("dp")

        def split(v, step):
            left = v.shape[0] // n * step if v.ndim == 2 else v.shape[1]
            v = v.reshape(n // (2 * step), 2, left, v.shape[-1])
            low = (z & step) == 0
            return jnp.where(low, v[:, 1], v[:, 0]), jnp.where(low, v[:, 0], v[:, 1])

        def join(v, got, step):
            low = (z & step) == 0
            both = jnp.where(low, jnp.stack([v, got], 1), jnp.stack([got, v], 1))
            return both.reshape(-1, *v.shape[1:])

        away, keep = order_of.run(lambda *v: split(make(*v), 1), *operands)
        step = 1
        while step < n:
            got = dp_partner(away, step)
            yield
            step *= 2
            if step < n:
                away, keep = order_of.run(lambda a, b, s=step: split(add_low(a, b), s), keep, got)
            else:
                v = order_of.run(add_low, keep, got)
        while step > 1:
            step //= 2
            got = dp_partner(v, step)
            yield
            v = order_of.run(functools.partial(join, step=step), v, got)
        self.value = v.reshape(-1, v.shape[-1])


def add_low(a, b):
    return (a.astype(F32) + b.astype(F32)).astype(BF16)


def quad_gather(own):
    one = to_second(own)
    two = to_first(own)
    three = to_first(one)
    return [own, one, two, three]


def on_device(
    layer_in, cotangent, lengths, w_qkv, bias_qv, w_out, bias_out,
    gain_attn, gain_mlp, w_up, bias_up, w_down, bias_down,
):
    micro, _, span, cc = layer_in.shape
    model = w_out.shape[1]
    ff = w_up.shape[-1]
    hd = model // HEADS
    width = model // QUAD
    heads = width // hd
    c = lax.axis_index("section")
    s = lax.axis_index("seq")
    dp_count = lax.axis_size("dp")
    mine = c == 0

    lens = lax.dynamic_index_in_dim(lengths, c, 0, keepdims=False)[0]
    e0 = lens[0]
    e1 = e0 + lens[1]
    e2 = e1 + lens[2]
    e3 = e2 + lens[3]
    ids = jnp.stack([c, s, e0, e1, e2, e3, c, s]).astype(jnp.int32)
    x = rows_in(ids, layer_in)
    x, w_qkv = tied(x, w_qkv)

    def row(v, n=ff):
        return jnp.pad(v, ((0, 0), (0, n - v.shape[-1])))

    qb = lax.dynamic_slice_in_dim(bias_qv, s * width, width, 1)
    vb = lax.dynamic_slice_in_dim(bias_qv, model + s * width, width, 1)
    heads_bias = jnp.concatenate([qb, jnp.zeros((1, width), F32), vb], 1)
    pv_own = jnp.concatenate(
        [row(v) for v in (bias_up, bias_out, bias_down, gain_attn, gain_mlp, heads_bias)]
        + [jnp.zeros((2, ff), F32)]
    )
    w3_own = jnp.concatenate(
        [lax.dynamic_slice_in_dim(w_qkv[0], i * model + s * width, width, 1) for i in range(3)], 1
    )
    pv_got = to_core(pv_own)
    w3_got = to_core(w3_own)
    wo_got = to_core(w_out[0])
    up = (w_up, to_core(w_up))
    dn = (w_down, to_core(w_down))
    pv = [jnp.where(mine, pv_own, pv_got), jnp.where(mine, pv_got, pv_own)]
    w3 = [jnp.where(mine, w3_own, w3_got), jnp.where(mine, w3_got, w3_own)]
    wo = [jnp.where(mine, w_out[0], wo_got), jnp.where(mine, wo_got, w_out[0])]

    normed = x
    saved = []
    squares = []
    for l in range(2):
        blocks = quad_gather(normed)
        qh, kh, vh, lse, *att = attn_fwd(l == 0, ids, blocks, w3[l], pv[l], heads, hd)
        if l == 0:
            att, blocks = att[:QUAD], att[QUAD:]
        att = [att[0]] + [to_quad(att[k], k) for k in (1, 2, 3)]
        mid, u, xout, normed, sq, astk = mlp_fwd(
            l, ids, x, att, wo[l], pv[l], pv[min(l + 1, 1)], up, dn
        )
        saved.append((x, blocks, (qh, kh, vh, lse), astk, mid, u))
        squares.append(sq[0, 0])
        x = xout
    outs = [saved[1][0], x]

    order_of = Order(ids)
    run = order_of.run

    def first_part(l, df):
        lr, rr, dmid, g, *douts = run(
            lambda v: mlp_bwd(l, ids, v, saved[l][5], saved[l][4], wo[l], pv[l], up, dn), df
        )
        return lr, rr, dmid, g, [douts[0]] + [to_quad(douts[k], k) for k in (1, 2, 3)]

    def send(l, places, lr, rr):
        return run(lambda a, b: product(True, places, ids, a, b, saved[l][3]), lr, rr)

    def keep(l, places, lr, rr, got):
        return run(lambda a, b, v: product(False, places, ids, a, b, saved[l][3], v), lr, rr, got)

    def attention(l, douts):
        outs = run(lambda *v: attn_bwd(ids, saved[l][1], w3[l], saved[l][2], v), *douts)
        return (*outs, to_first(outs[2]), to_core(outs[3]))

    def input_part(l, p0, pr, q, dmid):
        return run(lambda *v: input_grad_of(*v, saved[l][0], pv[l]), p0, pr, q, dmid)

    def projection(l, gk, gs_got, g, gb, gg):
        heads_sum = jnp.concatenate([gb[0, :width], gb[0, 2 * width :]])
        row_len = 3 * width
        vectors = [
            g[0], g[1, :cc], g[2, :cc], gg[0, :cc], g[4, :cc], heads_sum,
            jnp.broadcast_to(squares[l], (row_len,)),
        ]
        v = [jnp.pad(x, (0, -x.shape[0] % row_len)) for x in vectors]
        v = jnp.concatenate(v).reshape(-1, row_len)
        v = jnp.pad(v, ((0, 32 - v.shape[0]), (0, 0))).astype(BF16)
        return jnp.concatenate([add_low(gk, gs_got), v])

    def wait(*v):
        out = order_of.wait(*v)
        return out[0] if len(out) == 1 else out

    def pair_up(a, b):
        return jnp.stack([a, b])

    def add_first(a, b):
        return add_low(a, b[:span])

    df = rows_in(ids, cotangent)
    out_got = to_core(jnp.where(mine, outs[1], outs[0]))
    lr1, rr1, dmid1, g1, douts1 = first_part(1, df)
    out_got = wait(out_got)

    far1 = to_core(send(1, (3, 2), lr1, rr1))
    douts1 = wait(*douts1)
    near1 = send(1, (1, 0), lr1, rr1)
    far1 = wait(far1)

    far1 = keep(1, (3, 2), lr1, rr1, far1)
    x1a, near1 = to_first(far1[0]), to_core(near1)
    p0, p1, _, _, gk1, gb1, pr, gs_got = attention(1, douts1)
    x1a, near1 = wait(x1a, near1)

    near1 = keep(1, (1, 0), lr1, rr1, near1)
    half1 = run(add_low, near1[0], x1a)
    pr, gs_got = wait(pr, gs_got)

    q = to_second(run(add_first, p1, pr))
    q = wait(q)

    x1b, half1 = wait(far1[1], half1)
    x1b, x2 = to_first(x1b), to_second(half1)
    dx1, gg1 = input_part(1, p0, pr, q, dmid1)
    qkv_sum1 = DpSum(order_of, functools.partial(projection, 1), gk1, gs_got, g1, gb1, gg1)
    lr0, rr0, dmid0, g0, douts0 = first_part(0, dx1)
    far0 = to_core(send(0, (3, 2), lr0, rr0))
    near0 = send(0, (1, 0), lr0, rr0)
    x1b, x2 = wait(x1b, x2)

    sum1 = DpSum(order_of, lambda a, b, d: add_low(add_low(a, b), d), near1[1], x1b, x2)
    sum1.go()
    far0, *douts0 = wait(far0, *douts0)

    far0 = keep(0, (3, 2), lr0, rr0, far0)
    x1a, near0 = to_first(far0[0]), to_core(near0)
    p0, p1, _, _, gk0, gb0, pr, gs_got = attention(0, douts0)
    x1a, near0 = wait(x1a, near0)

    sum1.go()
    near0 = keep(0, (1, 0), lr0, rr0, near0)
    half1 = run(add_low, near0[0], x1a)
    qkv_sum1.go()
    pr, gs_got = wait(pr, gs_got)

    q = to_second(run(add_first, p1, pr))
    q = wait(q)

    x1b = to_first(wait(far0[1]))
    dx0, gg0 = input_part(0, p0, pr, q, dmid0)
    qkv_sum1.go()
    sum1.go()
    x1b, half1 = wait(x1b, half1)

    x2 = to_second(half1)
    sum1.go()
    half0 = run(add_low, near0[1], x1b)
    qkv_sum0 = DpSum(order_of, functools.partial(projection, 0), gk0, gs_got, g0, gb0, gg0)
    qkv_sum0.go()
    qkv_sum1.go()
    x2 = wait(x2)
    own1 = sum1.finish()

    have1 = [own1, to_second(own1), to_first(own1)]
    sum0 = DpSum(order_of, add_low, half0, x2)
    sum0.go()
    qkv_sum1.go()
    qkv_sum0.go()
    sum0.go()
    have1[1], have1[2] = wait(have1[1], have1[2])

    have1.append(to_first(have1[1]))
    qkv_own1 = qkv_sum1.finish()
    qkv_sum0.go()
    got1 = [to_owner(1, own1)]
    sum0.go()
    have1[3], got1[0] = wait(have1[3], got1[0])

    qkv_next1 = to_second(qkv_own1)
    got1.append(to_owner(1, have1[1]))
    qkv_sum0.go()
    qkv_next1, got1[1] = wait(qkv_next1, got1[1])
    qkv_pair1 = run(pair_up, qkv_own1, qkv_next1)
    sum0.go()

    qkv_rest1 = to_first(qkv_pair1)
    got1.append(to_owner(1, have1[2]))
    qkv_own0 = qkv_sum0.finish()
    qkv_next0 = to_second(qkv_own0)
    qkv_rest1, got1[2], qkv_next0 = wait(qkv_rest1, got1[2], qkv_next0)

    own0 = sum0.finish()
    have0 = [own0, to_second(own0), to_first(own0)]
    got1.append(to_owner(1, have1[3]))
    qkv_pair0 = run(pair_up, qkv_own0, qkv_next0)
    qkv_rest0 = to_first(qkv_pair0)
    got1[3] = wait(got1[3])
    got0 = [to_owner(0, own0)]
    in_got = to_core(run(lambda a, b: jnp.where(mine, a, b), dx1, dx0))
    qkv1 = run(lambda a, b: jnp.concatenate([a, b]), qkv_pair1, qkv_rest1)
    layer_out = run(
        lambda a, b, d: rows_out(ids, jnp.where(mine, a, b), d), outs[0], outs[1], out_got
    )
    got0[0], in_got = wait(got0[0], in_got)

    def place(places, outs_w):
        srcs = [v[p] for p in places for v in (have0, got0, got1, have1)]
        n = len(srcs)
        return run(
            lambda *v: place_rows(places, ids, v[:n], v[n:] or None, cc, ff, model), *srcs, *outs_w
        )

    outs_w = place((0,), ())
    input_grad = run(lambda a, b, d: rows_out(ids, jnp.where(mine, a, b), d), dx0, dx1, in_got)
    have0[1], have0[2], qkv_rest0 = wait(have0[1], have0[2], qkv_rest0)

    have0.append(to_first(have0[1]))
    got0 += [to_owner(0, have0[1]), to_owner(0, have0[2])]
    qkv0 = run(lambda a, b: jnp.concatenate([a, b]), qkv_pair0, qkv_rest0)
    got0[1], got0[2] = wait(got0[1], got0[2])
    qkv0_got, qkv1_got = to_owner(0, qkv0), to_owner(1, qkv1)
    outs_w = place((1,), outs_w)
    qkv0_got, qkv1_got = wait(qkv0_got, qkv1_got)
    outs_w = place((2,), outs_w)
    count = micro * dp_count * span * QUAD
    vectors = run(
        lambda *v: vectors_out(ids, v, count, cc, ff, model), qkv0, qkv0_got, qkv1_got, qkv1
    )
    have0[3] = wait(have0[3])

    got0.append(to_owner(0, have0[3]))
    grad_qkv = run(lambda *v: qkv_out(ids, v, cc), qkv0, qkv0_got, qkv1_got, qkv1)
    got0[3] = wait(got0[3])
    grad_down, grad_up, grad_out = place_rows(
        (3,), order_of.token, [v[3] for v in (have0, got0, got1, have1)], outs_w, cc, ff, model
    )

    grad_bup, grad_bout, grad_bdown, grad_ga, grad_gm, grad_bqv, rms = vectors
    return (
        layer_out,
        input_grad,
        jnp.transpose(grad_qkv, (1, 0, 2)),
        grad_bqv,
        jnp.transpose(grad_out, (1, 2, 0)),
        grad_bout,
        grad_ga,
        grad_gm,
        jnp.transpose(grad_up, (1, 0, 2)),
        grad_bup,
        jnp.transpose(grad_down, (1, 2, 0)),
        grad_bdown,
        rms[0, :1],
    )


def solution(mesh):
    two = P("section", None)
    three = P("section", None, None)
    tokens = P(None, "dp", "seq", None)
    stacked = P("section", None, "dp", "seq", None)
    return jax.shard_map(
        on_device,
        mesh=mesh,
        in_specs=(
            tokens, tokens, P(None, "dp", None), three, two, three, two, two, two, three, two, three, two,
        ),
        out_specs=(
            stacked, stacked, three, two, three, two, two, two, three, two, three, two, P("section"),
        ),
        check_vma=False,
    )
```

```python
import functools

import jax
import jax.numpy as jnp
from jax import lax
from jax.experimental import pallas as pl
from jax.experimental.pallas import tpu as pltpu
from jax.sharding import PartitionSpec as P

HEADS = 12
EPS = 1e-6
NEG = -1e30
F32 = jnp.float32
BF16 = jnp.bfloat16
MIB = 1 << 20
QUAD = 4


def nn(a, b):
    return lax.dot_general(a, b, (((1,), (0,)), ((), ())), preferred_element_type=F32)


def nt(a, b):
    return lax.dot_general(a, b, (((1,), (1,)), ((), ())), preferred_element_type=F32)


def tn(a, b):
    return lax.dot_general(a, b, (((0,), (0,)), ((), ())), preferred_element_type=F32)


def order(core, k):
    return jnp.where(core == 1, k, ((k & 1) << 1) | (k >> 1))


def crms_scale(v):
    sq = jnp.sum(v * v, axis=-1, keepdims=True)
    su = jnp.sum(v, axis=-1, keepdims=True)
    full = v.shape[-1] + 1
    return lax.rsqrt((sq + su * su) / full + EPS), su, (sq + su * su) / full


def crms_back(v, gain, grad):
    r, su, _ = crms_scale(v)
    gd = grad * gain
    w = jnp.sum(gd * v, axis=-1, keepdims=True)
    unit = v * r
    dv = gd * r - (w * r * r * r / (v.shape[-1] + 1)) * (v + su)
    return dv, grad * unit, unit * gain


GC = 0.7978845608028654


def gelu_parts(u):
    inner = GC * (u + 0.044715 * (u * u * u))
    th = jnp.tanh(inner)
    return th


def params(mib, **kw):
    return pltpu.CompilerParams(vmem_limit_bytes=mib * MIB, **kw)


def cost(flops, nbytes, trans=0):
    return pl.CostEstimate(flops=int(flops), bytes_accessed=int(nbytes), transcendentals=int(trans))


SMEM = pl.BlockSpec(memory_space=pltpu.SMEM)
VMEM = pl.BlockSpec(memory_space=pltpu.VMEM)
HBM = pl.BlockSpec(memory_space=pltpu.HBM)


def rows_in_kernel(ids, v, o):
    @pl.when(ids[0] == 0)
    def _():
        o[...] = v[:, 0, :].T

    @pl.when(ids[0] != 0)
    def _():
        o[...] = v[:, 1, :].T


def rows_in(ids, v):
    micro, _, span, cc = v.shape
    return pl.pallas_call(
        rows_in_kernel,
        in_specs=[SMEM, VMEM],
        out_specs=VMEM,
        out_shape=jax.ShapeDtypeStruct((span, cc), BF16),
        compiler_params=params(16),
        cost_estimate=cost(0, 6 * span * cc),
    )(ids, jnp.transpose(v[:, 0], (2, 0, 1)))


def rows_out_kernel(ids, own, got, o):
    @pl.when(ids[0] == 0)
    def _():
        o[:, 0, :] = own[...].T
        o[:, 1, :] = got[...].T

    @pl.when(ids[0] != 0)
    def _():
        o[:, 0, :] = got[...].T
        o[:, 1, :] = own[...].T


def rows_out(ids, own, got):
    span, cc = own.shape
    o = pl.pallas_call(
        rows_out_kernel,
        in_specs=[SMEM, VMEM, VMEM],
        out_specs=VMEM,
        out_shape=jax.ShapeDtypeStruct((cc, 2, span), BF16),
        compiler_params=params(16),
        cost_estimate=cost(0, 8 * span * cc),
    )(ids, own, got)
    return jnp.transpose(o, (1, 2, 0))[None, :, None]


def visible_bias(ids, n, t, span):
    i = t * span + lax.broadcasted_iota(jnp.int32, (1, span), 1)
    start = jnp.zeros((1, span), jnp.int32)
    for d in range(4):
        end = ids[2 + d]
        start = jnp.maximum(start, jnp.where(i >= end, end, 0))
    j = lax.broadcasted_iota(jnp.int32, (n, span), 0)
    return jnp.where((j >= start) & (j <= i), 0.0, NEG)


def attn_fwd_kernel(
    raw, ids, n0, n1, n2, n3, w_ref, pv_ref, q_hbm, k_hbm, v_hbm, l_hbm, n_hbm,
    a0, a1, a2, a3, qh, kh, vh, lse, nb_scr, at, bias_scr, sem,
):
    c, s = ids[0], ids[1]
    heads, _, hd = qh.shape
    span, cc = n0.shape
    width = heads * hd
    bias = pv_ref[5:6, : 3 * width]
    for p, nb in enumerate((n0, n1, n2, n3)):
        t = jnp.bitwise_xor(order(c, p), s)
        row = pl.multiple_of(t * span, span)
        rows = nb[...]
        if raw:
            v = rows.astype(F32)
            rows = (v * crms_scale(v)[0] * pv_ref[3:4, :cc]).astype(BF16)
            nb_scr[p] = rows
        y = nn(rows, w_ref[...]) + bias
        for h in range(heads):
            lo = h * hd
            qh[h, pl.ds(row, span), :] = (y[:, lo : lo + hd] * (hd**-0.5)).astype(BF16)
            kh[h, pl.ds(row, span), :] = y[:, width + lo : width + lo + hd].astype(BF16)
            vh[h, pl.ds(row, span), :] = y[:, 2 * width + lo : 2 * width + lo + hd].astype(BF16)
    moves = [
        pltpu.make_async_copy(src, dst, sem.at[i])
        for i, (src, dst) in enumerate(
            [(qh, q_hbm), (kh, k_hbm), (vh, v_hbm), (lse, l_hbm)]
            + [(nb_scr.at[p] if raw else nb, n_hbm.at[p]) for p, nb in enumerate((n0, n1, n2, n3))]
        )
    ]
    for i, m in enumerate(moves):
        if i != 3:
            m.start()
    for t in range(QUAD):
        n = span * (t + 1)
        bias_scr[:n, :] = visible_bias(ids, n, t, span)

        def head(h, carry, t=t, n=n):
            q = qh[h, t * span : (t + 1) * span, :]
            sc = nt(kh[h, :n, :], q) + bias_scr[:n, :]
            m = jnp.max(sc, axis=0, keepdims=True)
            e = jnp.exp(sc - m)
            tot = jnp.sum(e, axis=0, keepdims=True)
            pr = (e * (1.0 / tot)).astype(BF16)
            o = tn(vh[h, :n, :], pr)
            at[t, pl.ds(pl.multiple_of(h * hd, hd), hd), :] = o.astype(BF16)
            lse[h, t : t + 1, :] = m + jnp.log(tot)
            return carry

        lax.fori_loop(0, heads, head, 0)
    moves[3].start()
    for k, a in enumerate((a0, a1, a2, a3)):
        a[...] = at[jnp.bitwise_xor(s, k)]
    for m in moves:
        m.wait()


def attn_fwd(raw, ids, blocks, w3, pv, heads, hd):
    span, width = blocks[0].shape
    full = span * QUAD
    hh = jax.ShapeDtypeStruct((heads, full, hd), BF16)
    aa = jax.ShapeDtypeStruct((heads * hd, span), BF16)
    saved = [hh, hh, hh, jax.ShapeDtypeStruct((heads, QUAD, span), F32)]
    nb = jax.ShapeDtypeStruct((QUAD, span, width), BF16)
    return pl.pallas_call(
        functools.partial(attn_fwd_kernel, raw),
        in_specs=[SMEM] + [VMEM] * 6,
        out_specs=[HBM] * 5 + [VMEM] * 4,
        out_shape=[*saved, nb, aa, aa, aa, aa],
        scratch_shapes=[pltpu.VMEM(v.shape, v.dtype) for v in saved]
        + [
            pltpu.VMEM(nb.shape if raw else (1, 8, 128), BF16),
            pltpu.VMEM((QUAD, heads * hd, span), BF16),
            pltpu.VMEM((full, span), F32),
            pltpu.SemaphoreType.DMA((8,)),
        ],
        compiler_params=params(22),
        cost_estimate=cost(
            2 * full * width * 3 * heads * hd + 3 * 4 * full * full * hd * heads,
            4 * full * width,
            heads * full * full,
        ),
    )(ids, *blocks, w3, pv)


def mlp_fwd_kernel(
    layer, ids, x, a0, a1, a2, a3, wo, pv, pvn, pvb, upo, upr, dno, dnr,
    mid, u, xout, nnext, sq, astk, nm, acc,
):
    j = pl.program_id(0)
    c, s = ids[0], ids[1]
    cc = x.shape[-1]
    own = c == layer

    @pl.when(j == 0)
    def _():
        rows = a0.shape[0]
        m = x[...].astype(F32) + pv[1:2, :cc]
        for k, a in enumerate((a0, a1, a2, a3)):
            row = pl.multiple_of(jnp.bitwise_xor(s, k) * rows, rows)
            m = m + tn(a[...], wo[pl.ds(row, rows), :])
            astk[jnp.bitwise_xor(s, k)] = a[...].T
        mid[...] = m
        r, _, _ = crms_scale(m)
        nm[...] = (m * r * pv[4:5, :cc]).astype(BF16)
        acc[...] = m + pv[2:3, :cc]

    wu = lax.select(own, upo[0], upr[0])
    wd = lax.select(own, dno[0], dnr[0])
    ub = nn(nm[...], wu) + pvb[0:1, :]
    u[...] = ub
    act = (0.5 * ub * (1.0 + gelu_parts(ub))).astype(BF16)
    acc[...] += nn(act, wd)

    @pl.when(j == pl.num_programs(0) - 1)
    def _():
        fin = acc[...]
        _, _, ms = crms_scale(fin)
        sq[...] = jnp.broadcast_to(jnp.sum(ms, axis=0, keepdims=True), sq.shape)
        low = fin.astype(BF16)
        xout[...] = low
        lf = low.astype(F32)
        r, _, _ = crms_scale(lf)
        nnext[...] = (lf * r * pvn[3:4, :cc]).astype(BF16)


def mlp_fwd(layer, ids, x, att, wo, pv, pvn, up, dn):
    span, cc = x.shape
    ff = up[0].shape[-1]
    fb = ff // 4
    rows = att[0].shape[0]

    def whole(shape):
        return pl.BlockSpec(shape, lambda j, ids: (0,) * len(shape))

    def pick(mine):
        return lambda j, ids: jnp.where((ids[0] == layer) == mine, j, 0)

    mine, other = pick(True), pick(False)
    grid = pltpu.PrefetchScalarGridSpec(
        num_scalar_prefetch=1,
        grid=(4,),
        in_specs=[whole((span, cc))]
        + [whole((rows, span))] * 4
        + [whole(wo.shape), whole(pv.shape), whole(pvn.shape)]
        + [
            pl.BlockSpec((8, fb), lambda j, ids: (0, j)),
            pl.BlockSpec((1, cc, fb), lambda j, ids: (0, 0, mine(j, ids))),
            pl.BlockSpec((1, cc, fb), lambda j, ids: (0, 0, other(j, ids))),
            pl.BlockSpec((1, fb, cc), lambda j, ids: (0, mine(j, ids), 0)),
            pl.BlockSpec((1, fb, cc), lambda j, ids: (0, other(j, ids), 0)),
        ],
        out_specs=[
            whole((span, cc)),
            pl.BlockSpec((span, fb), lambda j, ids: (0, j)),
            whole((span, cc)),
            whole((span, cc)),
            whole((8, 128)),
            whole((QUAD, span, rows)),
        ],
        scratch_shapes=[pltpu.VMEM((span, cc), BF16), pltpu.VMEM((span, cc), F32)],
    )
    return pl.pallas_call(
        functools.partial(mlp_fwd_kernel, layer),
        grid_spec=grid,
        out_shape=[
            jax.ShapeDtypeStruct((span, cc), F32),
            jax.ShapeDtypeStruct((span, ff), F32),
            jax.ShapeDtypeStruct((span, cc), BF16),
            jax.ShapeDtypeStruct((span, cc), BF16),
            jax.ShapeDtypeStruct((8, 128), F32),
            jax.ShapeDtypeStruct((QUAD, span, rows), BF16),
        ],
        compiler_params=params(32, dimension_semantics=("arbitrary",)),
        cost_estimate=cost(6 * span * cc * ff, 4 * cc * ff + 4 * span * ff, span * ff),
    )(ids, x, *att, wo, pv, pvn, pv, up[0], up[1], dn[0], dn[1])


def mlp_bwd_kernel(
    layer, ids, df, u, mid, wo, pv, upo, upr, dno, dnr,
    lr, rr, dmid, g, d0, d1, d2, d3, acc, wide,
):
    j = pl.program_id(0)
    c, s = ids[0], ids[1]
    cc = df.shape[-1]
    fb = u.shape[-1]
    own = c == layer

    @pl.when(j == 0)
    def _():
        acc[...] = jnp.zeros_like(acc)
        g[...] = jnp.zeros_like(g)

    wu = lax.select(own, upo[0], upr[0])
    wd = lax.select(own, dno[0], dnr[0])
    da = nt(df[...], wd)
    ub = u[...]
    th = gelu_parts(ub)
    half = 0.5 * (1.0 + th)
    lr[0] = (ub * half).astype(BF16)
    slope = half + 0.5 * ub * (1.0 - th * th) * (GC * (1.0 + 3 * 0.044715 * (ub * ub)))
    du = (slope * da).astype(BF16)
    lr[1] = du
    g[0:1, pl.ds(pl.multiple_of(j * fb, 128), fb)] = jnp.sum(du.astype(F32), axis=0, keepdims=True)
    acc[...] += nt(du, wu)

    @pl.when(j == pl.num_programs(0) - 1)
    def _():
        dff = df[...].astype(F32)
        dv, gg, nm = crms_back(mid[...], pv[4:5, :cc], acc[...])
        dm = dff + dv
        low = dm.astype(BF16)
        dmid[...] = dm
        quarter = rr.shape[-1]
        wide[:, cc:] = jnp.zeros((wide.shape[0], wide.shape[1] - cc), BF16)
        for i, v in enumerate((df[...], nm.astype(BF16), low)):
            wide[:, :cc] = v
            for t in range(QUAD):
                rr[i, t] = wide[:, t * quarter : (t + 1) * quarter]
        g[1:2, :cc] = jnp.sum(low.astype(F32), axis=0, keepdims=True)
        g[2:3, :cc] = jnp.sum(dff, axis=0, keepdims=True)
        g[4:5, :cc] = jnp.sum(gg, axis=0, keepdims=True)
        rows = d0.shape[0]
        for k, d in enumerate((d0, d1, d2, d3)):
            row = pl.multiple_of(jnp.bitwise_xor(s, k) * rows, rows)
            d[...] = nt(wo[pl.ds(row, rows), :], low).astype(BF16)


def mlp_bwd(layer, ids, df, u, mid, wo, pv, up, dn):
    span, cc = df.shape
    ff = u.shape[-1]
    fb = ff // 4
    rows = wo.shape[0] // QUAD

    def whole(shape):
        return pl.BlockSpec(shape, lambda j, ids: (0,) * len(shape))

    def pick(mine):
        return lambda j, ids: jnp.where((ids[0] == layer) == mine, j, 0)

    mine, other = pick(True), pick(False)
    grid = pltpu.PrefetchScalarGridSpec(
        num_scalar_prefetch=1,
        grid=(4,),
        in_specs=[
            whole((span, cc)),
            pl.BlockSpec((span, fb), lambda j, ids: (0, j)),
            whole((span, cc)),
            whole(wo.shape),
            whole(pv.shape),
            pl.BlockSpec((1, cc, fb), lambda j, ids: (0, 0, mine(j, ids))),
            pl.BlockSpec((1, cc, fb), lambda j, ids: (0, 0, other(j, ids))),
            pl.BlockSpec((1, fb, cc), lambda j, ids: (0, mine(j, ids), 0)),
            pl.BlockSpec((1, fb, cc), lambda j, ids: (0, other(j, ids), 0)),
        ],
        out_specs=[
            pl.BlockSpec((2, span, fb), lambda j, ids: (0, 0, j)),
            whole((3, QUAD, span, (cc + 1) // QUAD)),
            whole((span, cc)),
            whole((8, ff)),
        ]
        + [whole((rows, span))] * 4,
        scratch_shapes=[pltpu.VMEM((span, cc), F32), pltpu.VMEM((span, cc + 1), BF16)],
    )
    dd = jax.ShapeDtypeStruct((rows, span), BF16)
    return pl.pallas_call(
        functools.partial(mlp_bwd_kernel, layer),
        grid_spec=grid,
        out_shape=[
            jax.ShapeDtypeStruct((2, span, ff), BF16),
            jax.ShapeDtypeStruct((3, QUAD, span, (cc + 1) // QUAD), BF16),
            jax.ShapeDtypeStruct((span, cc), F32),
            jax.ShapeDtypeStruct((8, ff), F32),
            dd, dd, dd, dd,
        ],
        compiler_params=params(32, dimension_semantics=("arbitrary",)),
        cost_estimate=cost(6 * span * cc * ff, 4 * cc * ff + 8 * span * ff, span * ff),
    )(ids, df, u, mid, wo, pv, up[0], up[1], dn[0], dn[1])


def product_kernel(send, places, ids, lr, rr, att, *rest):
    outs = [rest[0].at[i] for i in range(len(places))] if send else rest[1:]
    core = 1 - ids[0] if send else ids[0]
    ff = lr.shape[-1]
    part = att.shape[-1]
    for i, place in enumerate(places):
        t = jnp.bitwise_xor(order(core, place), ids[1])
        out = outs[i]
        main = tn(rr[core, t], lr[core])
        low = rr[2, t]
        sides = [tn(low, att[2 * core + h]) for h in range(2)]
        if not send:
            got = rest[0].at[i]
            main = main + got[:, :ff].astype(F32)
            sides = [v + got[:, ff + h * part : ff + (h + 1) * part].astype(F32) for h, v in enumerate(sides)]
        out[:, :ff] = main.astype(BF16)
        for h, v in enumerate(sides):
            out[:, ff + h * part : ff + (h + 1) * part] = v.astype(BF16)


def product(send, places, ids, lr, rr, att, *got):
    span, quarter = rr.shape[2:]
    cols = lr.shape[-1] + 2 * att.shape[-1]
    return pl.pallas_call(
        functools.partial(product_kernel, send, places),
        in_specs=[SMEM] + [VMEM] * (3 + len(got)),
        out_specs=VMEM if send else [VMEM] * len(places),
        out_shape=jax.ShapeDtypeStruct((len(places), quarter, cols), BF16)
        if send
        else [jax.ShapeDtypeStruct((quarter, cols), BF16)] * len(places),
        compiler_params=params(22),
        cost_estimate=cost(2 * span * quarter * cols * len(places), 2 * 4 * quarter * cols * len(places)),
    )(ids, lr, rr, att, *got)


def attn_bwd_kernel(
    ids, n_hbm, w_hbm, q_hbm, k_hbm, v_hbm, l_hbm, d0, d1, d2, d3,
    p0, p1, far, gs, gk, gb, do, dk, dv, dy, acc, bias_scr,
    nb, w_ref, qh, kh, vh, lse, sem,
):
    c, s = ids[0], ids[1]
    heads, _, hd = qh.shape
    _, span, cc = nb.shape
    width = heads * hd
    moves = [
        pltpu.make_async_copy(src, dst, sem.at[i])
        for i, (src, dst) in enumerate(
            [(q_hbm, qh), (k_hbm, kh), (v_hbm, vh), (l_hbm, lse), (w_hbm, w_ref), (n_hbm, nb)]
        )
    ]
    for m in moves:
        m.start()
    for k, d in enumerate((d0, d1, d2, d3)):
        do[jnp.bitwise_xor(s, k)] = d[...]
    for m in moves[:4]:
        m.wait()
    for t in reversed(range(QUAD)):
        n = span * (t + 1)
        bias_scr[:n, :] = visible_bias(ids, n, t, span)
        for h in range(heads):
            q = qh[h, t * span : (t + 1) * span, :]
            kk = kh[h, :n, :]
            sc = nt(kk, q) + (bias_scr[:n, :] - lse[h, t : t + 1, :])
            pr = jnp.exp(sc)
            dot = do[t, h * hd : (h + 1) * hd, :]
            dp = nn(vh[h, :n, :], dot)
            inner = jnp.sum(pr * dp, axis=0, keepdims=True)
            ds = (pr * (dp - inner)).astype(BF16)
            newk = nn(ds, q)
            newv = nt(pr.astype(BF16), dot)
            if t == QUAD - 1:
                dk[h, :n, :] = newk
                dv[h, :n, :] = newv
            else:
                dk[h, :n, :] += newk
                dv[h, :n, :] += newv
            dq = tn(kk, ds) * (hd**-0.5)
            dy[t * span : (t + 1) * span, h * hd : (h + 1) * hd] = dq.T.astype(BF16)
    for h in range(heads):
        dy[:, width + h * hd : width + (h + 1) * hd] = dk[h].astype(BF16)
        dy[:, 2 * width + h * hd : 2 * width + (h + 1) * hd] = dv[h].astype(BF16)
    for m in moves[4:]:
        m.wait()
    total = jnp.zeros((1, 3 * width), F32)
    for p, out in enumerate((p0, p1, far.at[span:], far.at[:span])):
        row = pl.multiple_of(jnp.bitwise_xor(order(c, p), s) * span, span)
        y = dy[pl.ds(row, span), :]
        out[...] = nt(y, w_ref[...]).astype(BF16)
        total = total + jnp.sum(y.astype(F32), axis=0, keepdims=True)
        g = tn(nb[p], y)
        if p == 0:
            acc[:cc, :] = g
        else:
            acc[:cc, :] += g
    gb[...] = jnp.broadcast_to(total, gb.shape)
    part = gs.shape[0]
    acc[cc:, :] = jnp.zeros((acc.shape[0] - cc, acc.shape[1]), F32)
    gk[...] = acc[pl.ds(pl.multiple_of(c * part, part), part), :].astype(BF16)
    gs[...] = acc[pl.ds(pl.multiple_of((1 - c) * part, part), part), :].astype(BF16)


def attn_bwd(ids, blocks, w3, qkvl, douts):
    _, span, cc = blocks.shape
    heads, full, hd = qkvl[0].shape
    width = heads * hd
    pp = jax.ShapeDtypeStruct((span, cc), BF16)
    gg = jax.ShapeDtypeStruct(((cc + 1) // 2, 3 * width), BF16)
    return pl.pallas_call(
        attn_bwd_kernel,
        in_specs=[SMEM] + [HBM] * 6 + [VMEM] * 4,
        out_specs=[VMEM] * 6,
        out_shape=[pp, pp, jax.ShapeDtypeStruct((2 * span, cc), BF16), gg, gg, jax.ShapeDtypeStruct((8, 3 * width), F32)],
        scratch_shapes=[
            pltpu.VMEM((QUAD, width, span), BF16),
            pltpu.VMEM((heads, full, hd), F32),
            pltpu.VMEM((heads, full, hd), F32),
            pltpu.VMEM((full, 3 * width), BF16),
            pltpu.VMEM((cc + 1, 3 * width), F32),
            pltpu.VMEM((full, span), F32),
            pltpu.VMEM((QUAD, span, cc), BF16),
            pltpu.VMEM(w3.shape, BF16),
            pltpu.VMEM((heads, full, hd), BF16),
            pltpu.VMEM((heads, full, hd), BF16),
            pltpu.VMEM((heads, full, hd), BF16),
            pltpu.VMEM((heads, QUAD, span), F32),
            pltpu.SemaphoreType.DMA((6,)),
        ],
        compiler_params=params(30),
        cost_estimate=cost(
            4 * full * cc * 3 * width + 3 * 10 * full * full * hd * heads,
            8 * full * cc,
            heads * full * full,
        ),
    )(ids, blocks, w3, *qkvl, *douts)


def input_kernel(part, r0, r1, dmid, x, pv, dx, gg):
    cc = x.shape[-1]
    dn = part[...].astype(F32) + r0[part.shape[0] :, :].astype(F32) + r1[...].astype(F32)
    dv, g, _ = crms_back(x[...].astype(F32), pv[3:4, :cc], dn)
    dx[...] = (dmid[...] + dv).astype(BF16)
    gg[...] = jnp.broadcast_to(jnp.sum(g, axis=0, keepdims=True), gg.shape)


def input_grad_of(part, r0, r1, dmid, x, pv):
    return pl.pallas_call(
        input_kernel,
        in_specs=[VMEM] * 6,
        out_specs=[VMEM] * 2,
        out_shape=[
            jax.ShapeDtypeStruct(x.shape, BF16),
            jax.ShapeDtypeStruct((8, x.shape[-1]), F32),
        ],
        compiler_params=params(16),
        cost_estimate=cost(0, x.size * 14),
    )(part, r0, r1, dmid, x, pv)


def both_lengths(t, rows, start):
    @pl.when(t < QUAD - 1)
    def _():
        start(rows)

    @pl.when(t == QUAD - 1)
    def _():
        start(rows - 1)


def place_kernel(places, first, ids, *refs):
    n = len(places)
    srcs = refs[: 4 * n]
    refs = refs[4 * n :]
    outs = refs[:3] if first else refs[3:6]
    x0, x1, od, ou, ow, sem = refs[3:] if first else refs[6:]
    c, s = ids[0], ids[1]
    down, up, wout = outs
    _, rows, _, ff = od.shape
    part = ow.shape[-1]

    def reads(i, j):
        return [
            pltpu.make_async_copy(srcs[4 * i + j], x0.at[i], sem.at[0, i]),
            pltpu.make_async_copy(srcs[4 * i + j + 1], x1.at[i], sem.at[1, i]),
        ]

    for core in range(2):

        @pl.when(c == core)
        def _():
            for i in range(n):
                for m in reads(i, 2 * core):
                    m.start()

    def writes(length, i, side, t):
        o, dst = ((od, down), (ou, up))[side]
        return [
            pltpu.make_async_copy(
                o.at[i, pl.ds(0, length)], dst.at[pl.ds(t * rows, length)], sem.at[2 + side, i]
            ),
            pltpu.make_async_copy(
                ow.at[side, i, pl.ds(0, length)],
                wout.at[pl.ds(t * rows, length), :, pl.ds(side * part, part)],
                sem.at[4 + side, i],
            ),
        ]

    jobs = []
    for i, place in enumerate(places):
        for m in reads(i, 0):
            m.wait()
        swapped = ((place & 1) << 1) | (place >> 1)
        for side, (x, o, k) in enumerate(((x0, od, swapped), (x1, ou, place))):
            t = jnp.bitwise_xor(k, s)
            o[i, :, 0, :] = x[i, :, :ff].astype(F32)
            ow[side, i, :, 0, :] = x[i, :, ff:].astype(F32)
            both_lengths(t, rows, lambda length: [m.start() for m in writes(length, i, side, t)])
            jobs.append((i, side, t))
    for i, side, t in jobs:
        both_lengths(t, rows, lambda length: [m.wait() for m in writes(length, i, side, t)])


def place_rows(places, ids, srcs, outs, cc, ff, model):
    rows, cols = srcs[0].shape
    n = len(places)
    first = outs is None
    operands = [ids, *srcs] + ([] if first else list(outs))
    return pl.pallas_call(
        functools.partial(place_kernel, places, first),
        in_specs=[SMEM] + [HBM] * (len(operands) - 1),
        out_specs=[HBM] * 3,
        out_shape=[jax.ShapeDtypeStruct((cc, 1, m), F32) for m in (ff, ff, model)],
        input_output_aliases={} if first else {4 * n + 1 + i: i for i in range(3)},
        scratch_shapes=[
            pltpu.VMEM((n, rows, cols), BF16),
            pltpu.VMEM((n, rows, cols), BF16),
            pltpu.VMEM((n, rows, 1, ff), F32),
            pltpu.VMEM((n, rows, 1, ff), F32),
            pltpu.VMEM((2, n, rows, 1, cols - ff), F32),
            pltpu.SemaphoreType.DMA((6, n)),
        ],
        compiler_params=params(16),
        cost_estimate=cost(0, 12 * n * rows * cols),
    )(*operands)


def qkv_out_kernel(ids, *refs):
    srcs, out, rows, wide, od, sem = refs[:4], *refs[4:]
    c, s = ids[0], ids[1]
    _, _, half, cols = rows.shape
    width = cols // 3

    def reads(a, b):
        return [
            pltpu.make_async_copy(
                src.at[p, pl.ds(0, half), :],
                rows.at[i, jnp.bitwise_xor(p if i else ((p & 1) << 1) | (p >> 1), s)],
                sem.at[0, i * QUAD + p],
            )
            for i, src in enumerate((a, b))
            for p in range(QUAD)
        ]

    @pl.when(c == 0)
    def _():
        for m in reads(srcs[0], srcs[1]):
            m.start()

    @pl.when(c != 0)
    def _():
        for m in reads(srcs[2], srcs[3]):
            m.start()

    for m in reads(srcs[0], srcs[1]):
        m.wait()
    step = half // 2
    moves = []
    for b in range(4):
        if b >= 2:
            moves[b - 2].wait()
        for t in range(QUAD):
            v = rows[b // 2, t, (b % 2) * step : (b % 2 + 1) * step, :].astype(F32)
            for i in range(3):
                lo = (i * QUAD + t) * width
                wide[:, lo : lo + width] = v[:, i * width : (i + 1) * width]
        od[b % 2, :, 0, :] = wide[...]
        n = step - (b == 3)
        m = pltpu.make_async_copy(
            od.at[b % 2, pl.ds(0, n)], out.at[pl.ds(b * step, n)], sem.at[1, b % 2]
        )
        m.start()
        moves.append(m)
    for m in moves[-2:]:
        m.wait()


def qkv_out(ids, srcs, cc):
    cols = srcs[0].shape[-1]
    half = (cc + 1) // 2
    return pl.pallas_call(
        qkv_out_kernel,
        in_specs=[SMEM] + [HBM] * 4,
        out_specs=HBM,
        out_shape=jax.ShapeDtypeStruct((cc, 1, QUAD * cols), F32),
        scratch_shapes=[
            pltpu.VMEM((2, QUAD, half, cols), BF16),
            pltpu.VMEM((half // 2, QUAD * cols), F32),
            pltpu.VMEM((2, half // 2, 1, QUAD * cols), F32),
            pltpu.SemaphoreType.DMA((2, 2 * QUAD)),
        ],
        compiler_params=params(18),
        cost_estimate=cost(0, 6 * cc * QUAD * cols),
    )(ids, *srcs)


def vectors_kernel(count, ids, *refs):
    srcs, outs, (rows, heads, sem) = refs[:4], refs[4:-3], refs[-3:]
    c, s = ids[0], ids[1]
    _, _, tall, row_len = rows.shape
    top = srcs[0].shape[1] - tall

    def reads(pair):
        return [
            pltpu.make_async_copy(v.at[p, pl.ds(top, tall), :], rows.at[i, p], sem.at[i * QUAD + p])
            for i, v in enumerate(pair)
            for p in range(QUAD)
        ]

    for core in range(2):

        @pl.when(c == core)
        def _():
            for m in reads(srcs[2 * core : 2 * core + 2]):
                m.start()

    for m in reads(srcs[:2]):
        m.wait()
    total = jnp.zeros((tall, row_len), F32)
    for i in range(2):
        for p in range(QUAD):
            total = total + rows[i, p].astype(F32)
    at = 0
    for o in outs[:5]:
        n = o.shape[1]
        for lo in range(0, n, row_len):
            size = min(row_len, n - lo)
            o[0:1, lo : lo + size] = total[at : at + 1, :size]
            at += 1
    heads[...] = jnp.zeros_like(heads)
    for i in range(2):
        for p in range(QUAD):
            k = p if i else ((p & 1) << 1) | (p >> 1)
            heads[jnp.bitwise_xor(k, s)] += rows[i, p, at : at + 8, :].astype(F32)
    width = row_len // 3
    for part in range(2):
        for t in range(QUAD):
            lo = (part * QUAD + t) * width
            outs[5][0:1, lo : lo + width] = heads[t, 0:1, part * width : (part + 1) * width]
    outs[6][0:1, :] = jnp.sqrt(total[at + 1 : at + 2, : outs[6].shape[1]] / count)


def vectors_out(ids, srcs, count, cc, ff, model):
    row_len = srcs[0].shape[-1]
    shapes = [ff, cc, cc, cc, cc, 2 * model, 128]
    return pl.pallas_call(
        functools.partial(vectors_kernel, count),
        in_specs=[SMEM] + [HBM] * 4,
        out_specs=[VMEM] * 7,
        out_shape=[jax.ShapeDtypeStruct((1, n), F32) for n in shapes],
        scratch_shapes=[
            pltpu.VMEM((2, QUAD, 32, row_len), BF16),
            pltpu.VMEM((QUAD, 8, row_len), F32),
            pltpu.SemaphoreType.DMA((2 * QUAD,)),
        ],
        compiler_params=params(8),
        cost_estimate=cost(0, 1 << 19),
    )(ids, *srcs)


def to_first(v):
    pairs = [(i, i ^ 1) for i in range(QUAD)] + [(QUAD + i, QUAD + (i ^ 2)) for i in range(QUAD)]
    return lax.ppermute(v, ("section", "seq"), pairs)


def to_second(v):
    pairs = [(i, i ^ 2) for i in range(QUAD)] + [(QUAD + i, QUAD + (i ^ 1)) for i in range(QUAD)]
    return lax.ppermute(v, ("section", "seq"), pairs)


def to_quad(v, k):
    return lax.ppermute(v, "seq", [(i, i ^ k) for i in range(QUAD)])


def to_core(v):
    return lax.ppermute(v, "section", [(0, 1), (1, 0)])


def dp_partner(v, step):
    n = lax.axis_size("dp")
    return lax.ppermute(v, "dp", [(i, i ^ step) for i in range(n)])


def to_owner(l, v):
    return lax.ppermute(v, "section", [(1 - l, l)])


def tied(*v):
    return lax.optimization_barrier(v)


class Order:
    def __init__(self, token):
        self.token = token

    def wait(self, *v):
        *v, self.token = lax.optimization_barrier((*v, self.token))
        return v

    def run(self, step, *operands):
        out = step(*self.wait(*operands))
        out, self.token = lax.optimization_barrier((out, self.token))
        return out


class DpSum:
    def __init__(self, order_of, make, *operands):
        self.value = None
        self.steps = self.work(order_of, make, operands)

    def go(self):
        next(self.steps, None)

    def finish(self):
        for _ in self.steps:
            pass
        return self.value

    def work(self, order_of, make, operands):
        n = lax.axis_size("dp")
        z = lax.axis_index("dp")

        def split(v, step):
            left = v.shape[0] // n * step if v.ndim == 2 else v.shape[1]
            v = v.reshape(n // (2 * step), 2, left, v.shape[-1])
            low = (z & step) == 0
            return jnp.where(low, v[:, 1], v[:, 0]), jnp.where(low, v[:, 0], v[:, 1])

        def join(v, got, step):
            low = (z & step) == 0
            both = jnp.where(low, jnp.stack([v, got], 1), jnp.stack([got, v], 1))
            return both.reshape(-1, *v.shape[1:])

        away, keep = order_of.run(lambda *v: split(make(*v), 1), *operands)
        step = 1
        while step < n:
            got = dp_partner(away, step)
            yield
            step *= 2
            if step < n:
                away, keep = order_of.run(lambda a, b, s=step: split(add_low(a, b), s), keep, got)
            else:
                v = order_of.run(add_low, keep, got)
        while step > 1:
            step //= 2
            got = dp_partner(v, step)
            yield
            v = order_of.run(functools.partial(join, step=step), v, got)
        self.value = v.reshape(-1, v.shape[-1])


def add_low(a, b):
    return (a.astype(F32) + b.astype(F32)).astype(BF16)


def quad_gather(own):
    one = to_second(own)
    two = to_first(own)
    three = to_first(one)
    return [own, one, two, three]


def on_device(
    layer_in, cotangent, lengths, w_qkv, bias_qv, w_out, bias_out,
    gain_attn, gain_mlp, w_up, bias_up, w_down, bias_down,
):
    micro, _, span, cc = layer_in.shape
    model = w_out.shape[1]
    ff = w_up.shape[-1]
    hd = model // HEADS
    width = model // QUAD
    heads = width // hd
    c = lax.axis_index("section")
    s = lax.axis_index("seq")
    dp_count = lax.axis_size("dp")
    mine = c == 0

    lens = lax.dynamic_index_in_dim(lengths, c, 0, keepdims=False)[0]
    e0 = lens[0]
    e1 = e0 + lens[1]
    e2 = e1 + lens[2]
    e3 = e2 + lens[3]
    ids = jnp.stack([c, s, e0, e1, e2, e3, c, s]).astype(jnp.int32)
    cs = jnp.stack([c, s]).astype(jnp.int32)
    x = rows_in(cs, layer_in)

    def row(v, n=ff):
        return jnp.pad(v, ((0, 0), (0, n - v.shape[-1])))

    qb = lax.dynamic_slice_in_dim(bias_qv, s * width, width, 1)
    vb = lax.dynamic_slice_in_dim(bias_qv, model + s * width, width, 1)
    heads_bias = jnp.concatenate([qb, jnp.zeros((1, width), F32), vb], 1)
    pv_own = jnp.concatenate(
        [row(v) for v in (bias_up, bias_out, bias_down, gain_attn, gain_mlp, heads_bias)]
        + [jnp.zeros((2, ff), F32)]
    )
    w3_own = jnp.concatenate(
        [lax.dynamic_slice_in_dim(w_qkv[0], i * model + s * width, width, 1) for i in range(3)], 1
    )
    pv_got = to_core(pv_own)
    w3_got = to_core(w3_own)
    wo_got = to_core(w_out[0])
    up = (w_up, to_core(w_up))
    dn = (w_down, to_core(w_down))
    pv = [jnp.where(mine, pv_own, pv_got), jnp.where(mine, pv_got, pv_own)]
    w3 = [jnp.where(mine, w3_own, w3_got), jnp.where(mine, w3_got, w3_own)]
    wo = [jnp.where(mine, w_out[0], wo_got), jnp.where(mine, wo_got, w_out[0])]

    normed = x
    saved = []
    squares = []
    for l in range(2):
        blocks = quad_gather(normed)
        if l == 1:
            blocks, df = tied(blocks, rows_in(cs, cotangent))
        qh, kh, vh, lse, blocks, *att = attn_fwd(l == 0, ids, blocks, w3[l], pv[l], heads, hd)
        att = [att[0]] + [to_quad(att[k], k) for k in (1, 2, 3)]
        mid, u, xout, normed, sq, astk = mlp_fwd(
            l, ids, x, att, wo[l], pv[l], pv[min(l + 1, 1)], up, dn
        )
        saved.append((x, blocks, (qh, kh, vh, lse), astk, mid, u))
        squares.append(sq[0, 0])
        x = xout
    outs = [saved[1][0], x]

    order_of = Order(ids)
    run = order_of.run

    def first_part(l, df):
        lr, rr, dmid, g, *douts = run(
            lambda v: mlp_bwd(l, ids, v, saved[l][5], saved[l][4], wo[l], pv[l], up, dn), df
        )
        return lr, rr, dmid, g, [douts[0]] + [to_quad(douts[k], k) for k in (1, 2, 3)]

    def send(l, places, lr, rr):
        return run(lambda a, b: product(True, places, ids, a, b, saved[l][3]), lr, rr)

    def keep(l, places, lr, rr, got):
        return run(lambda a, b, v: product(False, places, ids, a, b, saved[l][3], v), lr, rr, got)

    def attention(l, douts):
        outs = run(lambda *v: attn_bwd(ids, saved[l][1], w3[l], saved[l][2], v), *douts)
        return (*outs, to_first(outs[2]), to_core(outs[3]))

    def input_part(l, p0, pr, q, dmid):
        return run(lambda *v: input_grad_of(*v, saved[l][0], pv[l]), p0, pr, q, dmid)

    def projection(l, gk, gs_got, g, gb, gg):
        heads_sum = jnp.concatenate([gb[0, :width], gb[0, 2 * width :]])
        row_len = 3 * width
        vectors = [
            g[0], g[1, :cc], g[2, :cc], gg[0, :cc], g[4, :cc], heads_sum,
            jnp.broadcast_to(squares[l], (row_len,)),
        ]
        v = [jnp.pad(x, (0, -x.shape[0] % row_len)) for x in vectors]
        v = jnp.concatenate(v).reshape(-1, row_len)
        v = jnp.pad(v, ((0, 32 - v.shape[0]), (0, 0))).astype(BF16)
        return jnp.concatenate([add_low(gk, gs_got), v])

    def wait(*v):
        out = order_of.wait(*v)
        return out[0] if len(out) == 1 else out

    def pair_up(a, b):
        return jnp.stack([a, b])

    def add_first(a, b):
        return add_low(a, b[:span])

    lr1, rr1, dmid1, g1, douts1 = first_part(1, df)

    far1 = to_core(send(1, (3, 2), lr1, rr1))
    douts1 = wait(*douts1)
    near1 = send(1, (1, 0), lr1, rr1)
    far1 = wait(far1)

    far1 = keep(1, (3, 2), lr1, rr1, far1)
    x1a, near1 = to_first(far1[0]), to_core(near1)
    p0, p1, _, _, gk1, gb1, pr, gs_got = attention(1, douts1)
    x1a, near1 = wait(x1a, near1)

    out_got = to_core(run(lambda a, b: jnp.where(mine, a, b), outs[1], outs[0]))
    near1 = keep(1, (1, 0), lr1, rr1, near1)
    half1 = run(add_low, near1[0], x1a)
    pr, gs_got, out_got = wait(pr, gs_got, out_got)

    q = to_second(run(add_first, p1, pr))
    q = wait(q)

    x1b, half1 = wait(far1[1], half1)
    x1b, x2 = to_first(x1b), to_second(half1)
    dx1, gg1 = input_part(1, p0, pr, q, dmid1)
    qkv_sum1 = DpSum(order_of, functools.partial(projection, 1), gk1, gs_got, g1, gb1, gg1)
    lr0, rr0, dmid0, g0, douts0 = first_part(0, dx1)
    far0 = to_core(send(0, (3, 2), lr0, rr0))
    near0 = send(0, (1, 0), lr0, rr0)
    x1b, x2 = wait(x1b, x2)

    sum1 = DpSum(order_of, lambda a, b, d: add_low(add_low(a, b), d), near1[1], x1b, x2)
    sum1.go()
    far0, *douts0 = wait(far0, *douts0)

    far0 = keep(0, (3, 2), lr0, rr0, far0)
    x1a, near0 = to_first(far0[0]), to_core(near0)
    p0, p1, _, _, gk0, gb0, pr, gs_got = attention(0, douts0)
    x1a, near0 = wait(x1a, near0)

    sum1.go()
    near0 = keep(0, (1, 0), lr0, rr0, near0)
    half1 = run(add_low, near0[0], x1a)
    qkv_sum1.go()
    pr, gs_got = wait(pr, gs_got)

    q = to_second(run(add_first, p1, pr))
    q = wait(q)

    x1b = to_first(wait(far0[1]))
    dx0, gg0 = input_part(0, p0, pr, q, dmid0)
    qkv_sum1.go()
    sum1.go()
    x1b, half1 = wait(x1b, half1)

    x2 = to_second(half1)
    sum1.go()
    half0 = run(add_low, near0[1], x1b)
    qkv_sum0 = DpSum(order_of, functools.partial(projection, 0), gk0, gs_got, g0, gb0, gg0)
    qkv_sum0.go()
    qkv_sum1.go()
    x2 = wait(x2)
    own1 = sum1.finish()

    have1 = [own1, to_second(own1), to_first(own1)]
    sum0 = DpSum(order_of, add_low, half0, x2)
    sum0.go()
    qkv_sum1.go()
    qkv_sum0.go()
    sum0.go()
    have1[1], have1[2] = wait(have1[1], have1[2])

    have1.append(to_first(have1[1]))
    qkv_own1 = qkv_sum1.finish()
    qkv_sum0.go()
    got1 = [to_owner(1, own1)]
    sum0.go()
    have1[3], got1[0] = wait(have1[3], got1[0])

    qkv_next1 = to_second(qkv_own1)
    got1.append(to_owner(1, have1[1]))
    qkv_sum0.go()
    qkv_next1, got1[1] = wait(qkv_next1, got1[1])
    qkv_pair1 = run(pair_up, qkv_own1, qkv_next1)
    sum0.go()

    qkv_rest1 = to_first(qkv_pair1)
    got1.append(to_owner(1, have1[2]))
    qkv_own0 = qkv_sum0.finish()
    qkv_next0 = to_second(qkv_own0)
    qkv_rest1, got1[2], qkv_next0 = wait(qkv_rest1, got1[2], qkv_next0)

    own0 = sum0.finish()
    have0 = [own0, to_second(own0), to_first(own0)]
    got1.append(to_owner(1, have1[3]))
    qkv_pair0 = run(pair_up, qkv_own0, qkv_next0)
    qkv_rest0 = to_first(qkv_pair0)
    got1[3] = wait(got1[3])
    got0 = [to_owner(0, own0)]
    in_got = to_core(run(lambda a, b: jnp.where(mine, a, b), dx1, dx0))
    qkv1 = run(lambda a, b: jnp.concatenate([a, b]), qkv_pair1, qkv_rest1)
    layer_out = run(
        lambda a, b, d: rows_out(ids, jnp.where(mine, a, b), d), outs[0], outs[1], out_got
    )
    got0[0], in_got = wait(got0[0], in_got)

    def place(places, outs_w):
        srcs = [v[p] for p in places for v in (have0, got0, got1, have1)]
        n = len(srcs)
        return run(
            lambda *v: place_rows(places, ids, v[:n], v[n:] or None, cc, ff, model), *srcs, *outs_w
        )

    outs_w = place((0,), ())
    input_grad = run(lambda a, b, d: rows_out(ids, jnp.where(mine, a, b), d), dx0, dx1, in_got)
    have0[1], have0[2], qkv_rest0 = wait(have0[1], have0[2], qkv_rest0)

    have0.append(to_first(have0[1]))
    qkv0 = run(lambda a, b: jnp.concatenate([a, b]), qkv_pair0, qkv_rest0)
    have0[1], have0[2] = wait(have0[1], have0[2])
    got0.append(to_owner(0, have0[1]))
    qkv0_got, qkv1_got = to_owner(0, qkv0), to_owner(1, qkv1)
    got0[1] = wait(got0[1])
    outs_w = place((1,), outs_w)
    got0.append(to_owner(0, wait(have0[2])))
    qkv0_got, qkv1_got = wait(qkv0_got, qkv1_got)
    grad_qkv = run(lambda *v: qkv_out(ids, v, cc), qkv0, qkv0_got, qkv1_got, qkv1)
    count = micro * dp_count * span * QUAD
    vectors = run(
        lambda *v: vectors_out(ids, v, count, cc, ff, model), qkv0, qkv0_got, qkv1_got, qkv1
    )
    have0[3], got0[2] = wait(have0[3], got0[2])

    got0.append(to_owner(0, have0[3]))
    outs_w = place((2,), outs_w)
    got0[3] = wait(got0[3])
    grad_down, grad_up, grad_out = place_rows(
        (3,), order_of.token, [v[3] for v in (have0, got0, got1, have1)], outs_w, cc, ff, model
    )

    grad_bup, grad_bout, grad_bdown, grad_ga, grad_gm, grad_bqv, rms = vectors
    return (
        layer_out,
        input_grad,
        jnp.transpose(grad_qkv, (1, 0, 2)),
        grad_bqv,
        jnp.transpose(grad_out, (1, 2, 0)),
        grad_bout,
        grad_ga,
        grad_gm,
        jnp.transpose(grad_up, (1, 0, 2)),
        grad_bup,
        jnp.transpose(grad_down, (1, 2, 0)),
        grad_bdown,
        rms[0, :1],
    )


def solution(mesh):
    two = P("section", None)
    three = P("section", None, None)
    tokens = P(None, "dp", "seq", None)
    stacked = P("section", None, "dp", "seq", None)
    return jax.shard_map(
        on_device,
        mesh=mesh,
        in_specs=(
            tokens, tokens, P(None, "dp", None), three, two, three, two, two, two, three, two, three, two,
        ),
        out_specs=(
            stacked, stacked, three, two, three, two, two, two, three, two, three, two, P("section"),
        ),
        check_vma=False,
    )
```

```python
import functools

import jax
import jax.numpy as jnp
from jax import lax
from jax.experimental import pallas as pl
from jax.experimental.pallas import tpu as pltpu
from jax.sharding import PartitionSpec as P

HEADS = 12
EPS = 1e-6
NEG = -1e30
F32 = jnp.float32
BF16 = jnp.bfloat16
MIB = 1 << 20
QUAD = 4


def nn(a, b):
    return lax.dot_general(a, b, (((1,), (0,)), ((), ())), preferred_element_type=F32)


def nt(a, b):
    return lax.dot_general(a, b, (((1,), (1,)), ((), ())), preferred_element_type=F32)


def tn(a, b):
    return lax.dot_general(a, b, (((0,), (0,)), ((), ())), preferred_element_type=F32)


def order(core, k):
    return jnp.where(core == 1, k, ((k & 1) << 1) | (k >> 1))


def crms_scale(v):
    sq = jnp.sum(v * v, axis=-1, keepdims=True)
    su = jnp.sum(v, axis=-1, keepdims=True)
    full = v.shape[-1] + 1
    return lax.rsqrt((sq + su * su) / full + EPS), su, (sq + su * su) / full


def crms_back(v, gain, grad):
    r, su, _ = crms_scale(v)
    gd = grad * gain
    w = jnp.sum(gd * v, axis=-1, keepdims=True)
    unit = v * r
    dv = gd * r - (w * r * r * r / (v.shape[-1] + 1)) * (v + su)
    return dv, grad * unit, unit * gain


GC = 0.7978845608028654


def gelu_parts(u):
    inner = GC * (u + 0.044715 * (u * u * u))
    th = jnp.tanh(inner)
    return th


def params(mib, **kw):
    return pltpu.CompilerParams(vmem_limit_bytes=mib * MIB, **kw)


def cost(flops, nbytes, trans=0):
    return pl.CostEstimate(
        flops=int(2 * flops), bytes_accessed=int(2 * nbytes), transcendentals=int(2 * trans)
    )


SMEM = pl.BlockSpec(memory_space=pltpu.SMEM)
VMEM = pl.BlockSpec(memory_space=pltpu.VMEM)
HBM = pl.BlockSpec(memory_space=pltpu.HBM)


def rows_in_kernel(ids, v, o):
    @pl.when(ids[0] == 0)
    def _():
        o[...] = v[:, 0, :].T

    @pl.when(ids[0] != 0)
    def _():
        o[...] = v[:, 1, :].T


def rows_in(ids, v):
    micro, _, span, cc = v.shape
    return pl.pallas_call(
        rows_in_kernel,
        in_specs=[SMEM, VMEM],
        out_specs=VMEM,
        out_shape=jax.ShapeDtypeStruct((span, cc), BF16),
        compiler_params=params(16),
        cost_estimate=cost(0, 6 * span * cc),
    )(ids, jnp.transpose(v[:, 0], (2, 0, 1)))


def rows_out_kernel(ids, own, got, o):
    @pl.when(ids[0] == 0)
    def _():
        o[:, 0, :] = own[...].T
        o[:, 1, :] = got[...].T

    @pl.when(ids[0] != 0)
    def _():
        o[:, 0, :] = got[...].T
        o[:, 1, :] = own[...].T


def rows_out(ids, own, got):
    span, cc = own.shape
    o = pl.pallas_call(
        rows_out_kernel,
        in_specs=[SMEM, VMEM, VMEM],
        out_specs=VMEM,
        out_shape=jax.ShapeDtypeStruct((cc, 2, span), BF16),
        compiler_params=params(16),
        cost_estimate=cost(0, 8 * span * cc),
    )(ids, own, got)
    return jnp.transpose(o, (1, 2, 0))[None, :, None]


def visible_bias(ids, n, t, span):
    i = t * span + lax.broadcasted_iota(jnp.int32, (1, span), 1)
    start = jnp.zeros((1, span), jnp.int32)
    for d in range(4):
        end = ids[2 + d]
        start = jnp.maximum(start, jnp.where(i >= end, end, 0))
    j = lax.broadcasted_iota(jnp.int32, (n, span), 0)
    return jnp.where((j >= start) & (j <= i), 0.0, NEG)


def attn_fwd_kernel(
    raw, ids, n0, n1, n2, n3, w_ref, pv_ref, q_hbm, k_hbm, v_hbm, l_hbm, n_hbm,
    a0, a1, a2, a3, qh, kh, vh, lse, nb_scr, at, bias_scr, sem,
):
    c, s = ids[0], ids[1]
    heads, _, hd = qh.shape
    span, cc = n0.shape
    width = heads * hd
    bias = pv_ref[5:6, : 3 * width]
    for p, nb in enumerate((n0, n1, n2, n3)):
        t = jnp.bitwise_xor(order(c, p), s)
        row = pl.multiple_of(t * span, span)
        rows = nb[...]
        if raw:
            v = rows.astype(F32)
            rows = (v * crms_scale(v)[0] * pv_ref[3:4, :cc]).astype(BF16)
            nb_scr[p] = rows
        y = nn(rows, w_ref[...]) + bias
        for h in range(heads):
            lo = h * hd
            qh[h, pl.ds(row, span), :] = (y[:, lo : lo + hd] * (hd**-0.5)).astype(BF16)
            kh[h, pl.ds(row, span), :] = y[:, width + lo : width + lo + hd].astype(BF16)
            vh[h, pl.ds(row, span), :] = y[:, 2 * width + lo : 2 * width + lo + hd].astype(BF16)
    moves = [
        pltpu.make_async_copy(src, dst, sem.at[i])
        for i, (src, dst) in enumerate(
            [(qh, q_hbm), (kh, k_hbm), (vh, v_hbm), (lse, l_hbm)]
            + [(nb_scr.at[p] if raw else nb, n_hbm.at[p]) for p, nb in enumerate((n0, n1, n2, n3))]
        )
    ]
    for i, m in enumerate(moves):
        if i != 3:
            m.start()
    for t in range(QUAD):
        n = span * (t + 1)
        bias_scr[:n, :] = visible_bias(ids, n, t, span)

        def head(h, carry, t=t, n=n):
            q = qh[h, t * span : (t + 1) * span, :]
            sc = nt(kh[h, :n, :], q) + bias_scr[:n, :]
            m = jnp.max(sc, axis=0, keepdims=True)
            e = jnp.exp(sc - m)
            tot = jnp.sum(e, axis=0, keepdims=True)
            pr = (e * (1.0 / tot)).astype(BF16)
            o = tn(vh[h, :n, :], pr)
            at[t, pl.ds(pl.multiple_of(h * hd, hd), hd), :] = o.astype(BF16)
            lse[h, t : t + 1, :] = m + jnp.log(tot)
            return carry

        lax.fori_loop(0, heads, head, 0)
    moves[3].start()
    for k, a in enumerate((a0, a1, a2, a3)):
        a[...] = at[jnp.bitwise_xor(s, k)]
    for m in moves:
        m.wait()


def attn_fwd(raw, ids, blocks, w3, pv, heads, hd):
    span, width = blocks[0].shape
    full = span * QUAD
    hh = jax.ShapeDtypeStruct((heads, full, hd), BF16)
    aa = jax.ShapeDtypeStruct((heads * hd, span), BF16)
    saved = [hh, hh, hh, jax.ShapeDtypeStruct((heads, QUAD, span), F32)]
    nb = jax.ShapeDtypeStruct((QUAD, span, width), BF16)
    return pl.pallas_call(
        functools.partial(attn_fwd_kernel, raw),
        in_specs=[SMEM] + [VMEM] * 6,
        out_specs=[HBM] * 5 + [VMEM] * 4,
        out_shape=[*saved, nb, aa, aa, aa, aa],
        scratch_shapes=[pltpu.VMEM(v.shape, v.dtype) for v in saved]
        + [
            pltpu.VMEM(nb.shape if raw else (1, 8, 128), BF16),
            pltpu.VMEM((QUAD, heads * hd, span), BF16),
            pltpu.VMEM((full, span), F32),
            pltpu.SemaphoreType.DMA((8,)),
        ],
        compiler_params=params(22),
        cost_estimate=cost(
            2 * full * width * 3 * heads * hd + 3 * 4 * full * full * hd * heads,
            4 * full * width,
            heads * full * full,
        ),
    )(ids, *blocks, w3, pv)


def mlp_fwd_kernel(
    layer, ids, x, a0, a1, a2, a3, wo, pv, pvn, pvb, upo, upr, dno, dnr,
    mid, u, xout, nnext, sq, astk, nm, acc,
):
    j = pl.program_id(0)
    c, s = ids[0], ids[1]
    cc = x.shape[-1]
    own = c == layer

    @pl.when(j == 0)
    def _():
        rows = a0.shape[0]
        m = x[...].astype(F32) + pv[1:2, :cc]
        for k, a in enumerate((a0, a1, a2, a3)):
            row = pl.multiple_of(jnp.bitwise_xor(s, k) * rows, rows)
            m = m + tn(a[...], wo[pl.ds(row, rows), :])
            astk[jnp.bitwise_xor(s, k)] = a[...].T
        mid[...] = m
        r, _, _ = crms_scale(m)
        nm[...] = (m * r * pv[4:5, :cc]).astype(BF16)
        acc[...] = m + pv[2:3, :cc]

    wu = lax.select(own, upo[0], upr[0])
    wd = lax.select(own, dno[0], dnr[0])
    ub = nn(nm[...], wu) + pvb[0:1, :]
    u[...] = ub
    act = (0.5 * ub * (1.0 + gelu_parts(ub))).astype(BF16)
    acc[...] += nn(act, wd)

    @pl.when(j == pl.num_programs(0) - 1)
    def _():
        fin = acc[...]
        _, _, ms = crms_scale(fin)
        sq[...] = jnp.broadcast_to(jnp.sum(ms, axis=0, keepdims=True), sq.shape)
        low = fin.astype(BF16)
        xout[...] = low
        lf = low.astype(F32)
        r, _, _ = crms_scale(lf)
        nnext[...] = (lf * r * pvn[3:4, :cc]).astype(BF16)


def mlp_fwd(layer, ids, x, att, wo, pv, pvn, up, dn):
    span, cc = x.shape
    ff = up[0].shape[-1]
    fb = ff // 4
    rows = att[0].shape[0]

    def whole(shape):
        return pl.BlockSpec(shape, lambda j, ids: (0,) * len(shape))

    def pick(mine):
        return lambda j, ids: jnp.where((ids[0] == layer) == mine, j, 0)

    mine, other = pick(True), pick(False)
    grid = pltpu.PrefetchScalarGridSpec(
        num_scalar_prefetch=1,
        grid=(4,),
        in_specs=[whole((span, cc))]
        + [whole((rows, span))] * 4
        + [whole(wo.shape), whole(pv.shape), whole(pvn.shape)]
        + [
            pl.BlockSpec((8, fb), lambda j, ids: (0, j)),
            pl.BlockSpec((1, cc, fb), lambda j, ids: (0, 0, mine(j, ids))),
            pl.BlockSpec((1, cc, fb), lambda j, ids: (0, 0, other(j, ids))),
            pl.BlockSpec((1, fb, cc), lambda j, ids: (0, mine(j, ids), 0)),
            pl.BlockSpec((1, fb, cc), lambda j, ids: (0, other(j, ids), 0)),
        ],
        out_specs=[
            whole((span, cc)),
            pl.BlockSpec((span, fb), lambda j, ids: (0, j)),
            whole((span, cc)),
            whole((span, cc)),
            whole((8, 128)),
            whole((QUAD, span, rows)),
        ],
        scratch_shapes=[pltpu.VMEM((span, cc), BF16), pltpu.VMEM((span, cc), F32)],
    )
    return pl.pallas_call(
        functools.partial(mlp_fwd_kernel, layer),
        grid_spec=grid,
        out_shape=[
            jax.ShapeDtypeStruct((span, cc), F32),
            jax.ShapeDtypeStruct((span, ff), F32),
            jax.ShapeDtypeStruct((span, cc), BF16),
            jax.ShapeDtypeStruct((span, cc), BF16),
            jax.ShapeDtypeStruct((8, 128), F32),
            jax.ShapeDtypeStruct((QUAD, span, rows), BF16),
        ],
        compiler_params=params(32, dimension_semantics=("arbitrary",)),
        cost_estimate=cost(6 * span * cc * ff, 4 * cc * ff + 4 * span * ff, span * ff),
    )(ids, x, *att, wo, pv, pvn, pv, up[0], up[1], dn[0], dn[1])


def mlp_bwd_kernel(
    layer, ids, df, u, mid, wo, pv, upo, upr, dno, dnr,
    lr, rr, dmid, g, d0, d1, d2, d3, acc, wide,
):
    j = pl.program_id(0)
    c, s = ids[0], ids[1]
    cc = df.shape[-1]
    fb = u.shape[-1]
    own = c == layer

    @pl.when(j == 0)
    def _():
        acc[...] = jnp.zeros_like(acc)
        g[...] = jnp.zeros_like(g)

    wu = lax.select(own, upo[0], upr[0])
    wd = lax.select(own, dno[0], dnr[0])
    da = nt(df[...], wd)
    ub = u[...]
    th = gelu_parts(ub)
    half = 0.5 * (1.0 + th)
    lr[0] = (ub * half).astype(BF16)
    slope = half + 0.5 * ub * (1.0 - th * th) * (GC * (1.0 + 3 * 0.044715 * (ub * ub)))
    du = (slope * da).astype(BF16)
    lr[1] = du
    g[0:1, pl.ds(pl.multiple_of(j * fb, 128), fb)] = jnp.sum(du.astype(F32), axis=0, keepdims=True)
    acc[...] += nt(du, wu)

    @pl.when(j == pl.num_programs(0) - 1)
    def _():
        dff = df[...].astype(F32)
        dv, gg, nm = crms_back(mid[...], pv[4:5, :cc], acc[...])
        dm = dff + dv
        low = dm.astype(BF16)
        dmid[...] = dm
        quarter = rr.shape[-1]
        wide[:, cc:] = jnp.zeros((wide.shape[0], wide.shape[1] - cc), BF16)
        for i, v in enumerate((df[...], nm.astype(BF16), low)):
            wide[:, :cc] = v
            for t in range(QUAD):
                rr[i, t] = wide[:, t * quarter : (t + 1) * quarter]
        g[1:2, :cc] = jnp.sum(low.astype(F32), axis=0, keepdims=True)
        g[2:3, :cc] = jnp.sum(dff, axis=0, keepdims=True)
        g[4:5, :cc] = jnp.sum(gg, axis=0, keepdims=True)
        rows = d0.shape[0]
        for k, d in enumerate((d0, d1, d2, d3)):
            row = pl.multiple_of(jnp.bitwise_xor(s, k) * rows, rows)
            d[...] = nt(wo[pl.ds(row, rows), :], low).astype(BF16)


def mlp_bwd(layer, ids, df, u, mid, wo, pv, up, dn):
    span, cc = df.shape
    ff = u.shape[-1]
    fb = ff // 4
    rows = wo.shape[0] // QUAD

    def whole(shape):
        return pl.BlockSpec(shape, lambda j, ids: (0,) * len(shape))

    def pick(mine):
        return lambda j, ids: jnp.where((ids[0] == layer) == mine, j, 0)

    mine, other = pick(True), pick(False)
    grid = pltpu.PrefetchScalarGridSpec(
        num_scalar_prefetch=1,
        grid=(4,),
        in_specs=[
            whole((span, cc)),
            pl.BlockSpec((span, fb), lambda j, ids: (0, j)),
            whole((span, cc)),
            whole(wo.shape),
            whole(pv.shape),
            pl.BlockSpec((1, cc, fb), lambda j, ids: (0, 0, mine(j, ids))),
            pl.BlockSpec((1, cc, fb), lambda j, ids: (0, 0, other(j, ids))),
            pl.BlockSpec((1, fb, cc), lambda j, ids: (0, mine(j, ids), 0)),
            pl.BlockSpec((1, fb, cc), lambda j, ids: (0, other(j, ids), 0)),
        ],
        out_specs=[
            pl.BlockSpec((2, span, fb), lambda j, ids: (0, 0, j)),
            whole((3, QUAD, span, (cc + 1) // QUAD)),
            whole((span, cc)),
            whole((8, ff)),
        ]
        + [whole((rows, span))] * 4,
        scratch_shapes=[pltpu.VMEM((span, cc), F32), pltpu.VMEM((span, cc + 1), BF16)],
    )
    dd = jax.ShapeDtypeStruct((rows, span), BF16)
    return pl.pallas_call(
        functools.partial(mlp_bwd_kernel, layer),
        grid_spec=grid,
        out_shape=[
            jax.ShapeDtypeStruct((2, span, ff), BF16),
            jax.ShapeDtypeStruct((3, QUAD, span, (cc + 1) // QUAD), BF16),
            jax.ShapeDtypeStruct((span, cc), F32),
            jax.ShapeDtypeStruct((8, ff), F32),
            dd, dd, dd, dd,
        ],
        compiler_params=params(32, dimension_semantics=("arbitrary",)),
        cost_estimate=cost(6 * span * cc * ff, 4 * cc * ff + 8 * span * ff, span * ff),
    )(ids, df, u, mid, wo, pv, up[0], up[1], dn[0], dn[1])


def product_kernel(send, places, ids, lr, rr, att, *rest):
    outs = [rest[0].at[i] for i in range(len(places))] if send else rest[1:]
    core = 1 - ids[0] if send else ids[0]
    ff = lr.shape[-1]
    part = att.shape[-1]
    for i, place in enumerate(places):
        t = jnp.bitwise_xor(order(core, place), ids[1])
        out = outs[i]
        main = tn(rr[core, t], lr[core])
        low = rr[2, t]
        sides = [tn(low, att[2 * core + h]) for h in range(2)]
        if not send:
            got = rest[0].at[i]
            main = main + got[:, :ff].astype(F32)
            sides = [v + got[:, ff + h * part : ff + (h + 1) * part].astype(F32) for h, v in enumerate(sides)]
        out[:, :ff] = main.astype(BF16)
        for h, v in enumerate(sides):
            out[:, ff + h * part : ff + (h + 1) * part] = v.astype(BF16)


def product(send, places, ids, lr, rr, att, *got):
    span, quarter = rr.shape[2:]
    cols = lr.shape[-1] + 2 * att.shape[-1]
    return pl.pallas_call(
        functools.partial(product_kernel, send, places),
        in_specs=[SMEM] + [VMEM] * (3 + len(got)),
        out_specs=VMEM if send else [VMEM] * len(places),
        out_shape=jax.ShapeDtypeStruct((len(places), quarter, cols), BF16)
        if send
        else [jax.ShapeDtypeStruct((quarter, cols), BF16)] * len(places),
        compiler_params=params(22),
        cost_estimate=cost(2 * span * quarter * cols * len(places), 2 * 4 * quarter * cols * len(places)),
    )(ids, lr, rr, att, *got)


def attn_bwd_kernel(
    ids, n_hbm, w_hbm, q_hbm, k_hbm, v_hbm, l_hbm, d0, d1, d2, d3,
    p0, p1, far, gs, gk, gb, do, dk, dv, dy, acc, bias_scr,
    nb, w_ref, qh, kh, vh, lse, sem,
):
    c, s = ids[0], ids[1]
    heads, _, hd = qh.shape
    _, span, cc = nb.shape
    width = heads * hd
    moves = [
        pltpu.make_async_copy(src, dst, sem.at[i])
        for i, (src, dst) in enumerate(
            [(q_hbm, qh), (k_hbm, kh), (v_hbm, vh), (l_hbm, lse), (w_hbm, w_ref), (n_hbm, nb)]
        )
    ]
    for m in moves:
        m.start()
    for k, d in enumerate((d0, d1, d2, d3)):
        do[jnp.bitwise_xor(s, k)] = d[...]
    for m in moves[:4]:
        m.wait()
    for t in reversed(range(QUAD)):
        n = span * (t + 1)
        bias_scr[:n, :] = visible_bias(ids, n, t, span)
        for h in range(heads):
            q = qh[h, t * span : (t + 1) * span, :]
            kk = kh[h, :n, :]
            sc = nt(kk, q) + (bias_scr[:n, :] - lse[h, t : t + 1, :])
            pr = jnp.exp(sc)
            dot = do[t, h * hd : (h + 1) * hd, :]
            dp = nn(vh[h, :n, :], dot)
            inner = jnp.sum(pr * dp, axis=0, keepdims=True)
            ds = (pr * (dp - inner)).astype(BF16)
            newk = nn(ds, q)
            newv = nt(pr.astype(BF16), dot)
            if t == QUAD - 1:
                dk[h, :n, :] = newk
                dv[h, :n, :] = newv
            else:
                dk[h, :n, :] += newk
                dv[h, :n, :] += newv
            dq = tn(kk, ds) * (hd**-0.5)
            dy[t * span : (t + 1) * span, h * hd : (h + 1) * hd] = dq.T.astype(BF16)
    for h in range(heads):
        dy[:, width + h * hd : width + (h + 1) * hd] = dk[h].astype(BF16)
        dy[:, 2 * width + h * hd : 2 * width + (h + 1) * hd] = dv[h].astype(BF16)
    for m in moves[4:]:
        m.wait()
    total = jnp.zeros((1, 3 * width), F32)
    for p, out in enumerate((p0, p1, far.at[span:], far.at[:span])):
        row = pl.multiple_of(jnp.bitwise_xor(order(c, p), s) * span, span)
        y = dy[pl.ds(row, span), :]
        out[...] = nt(y, w_ref[...]).astype(BF16)
        total = total + jnp.sum(y.astype(F32), axis=0, keepdims=True)
        g = tn(nb[p], y)
        if p == 0:
            acc[:cc, :] = g
        else:
            acc[:cc, :] += g
    gb[...] = jnp.broadcast_to(total, gb.shape)
    part = gs.shape[0]
    acc[cc:, :] = jnp.zeros((acc.shape[0] - cc, acc.shape[1]), F32)
    gk[...] = acc[pl.ds(pl.multiple_of(c * part, part), part), :].astype(BF16)
    gs[...] = acc[pl.ds(pl.multiple_of((1 - c) * part, part), part), :].astype(BF16)


def attn_bwd(ids, blocks, w3, qkvl, douts):
    _, span, cc = blocks.shape
    heads, full, hd = qkvl[0].shape
    width = heads * hd
    pp = jax.ShapeDtypeStruct((span, cc), BF16)
    gg = jax.ShapeDtypeStruct(((cc + 1) // 2, 3 * width), BF16)
    return pl.pallas_call(
        attn_bwd_kernel,
        in_specs=[SMEM] + [HBM] * 6 + [VMEM] * 4,
        out_specs=[VMEM] * 6,
        out_shape=[pp, pp, jax.ShapeDtypeStruct((2 * span, cc), BF16), gg, gg, jax.ShapeDtypeStruct((8, 3 * width), F32)],
        scratch_shapes=[
            pltpu.VMEM((QUAD, width, span), BF16),
            pltpu.VMEM((heads, full, hd), F32),
            pltpu.VMEM((heads, full, hd), F32),
            pltpu.VMEM((full, 3 * width), BF16),
            pltpu.VMEM((cc + 1, 3 * width), F32),
            pltpu.VMEM((full, span), F32),
            pltpu.VMEM((QUAD, span, cc), BF16),
            pltpu.VMEM(w3.shape, BF16),
            pltpu.VMEM((heads, full, hd), BF16),
            pltpu.VMEM((heads, full, hd), BF16),
            pltpu.VMEM((heads, full, hd), BF16),
            pltpu.VMEM((heads, QUAD, span), F32),
            pltpu.SemaphoreType.DMA((6,)),
        ],
        compiler_params=params(30),
        cost_estimate=cost(
            4 * full * cc * 3 * width + 3 * 10 * full * full * hd * heads,
            8 * full * cc,
            heads * full * full,
        ),
    )(ids, blocks, w3, *qkvl, *douts)


def input_kernel(part, r0, r1, dmid, x, pv, dx, gg):
    cc = x.shape[-1]
    dn = part[...].astype(F32) + r0[part.shape[0] :, :].astype(F32) + r1[...].astype(F32)
    dv, g, _ = crms_back(x[...].astype(F32), pv[3:4, :cc], dn)
    dx[...] = (dmid[...] + dv).astype(BF16)
    gg[...] = jnp.broadcast_to(jnp.sum(g, axis=0, keepdims=True), gg.shape)


def input_grad_of(part, r0, r1, dmid, x, pv):
    return pl.pallas_call(
        input_kernel,
        in_specs=[VMEM] * 6,
        out_specs=[VMEM] * 2,
        out_shape=[
            jax.ShapeDtypeStruct(x.shape, BF16),
            jax.ShapeDtypeStruct((8, x.shape[-1]), F32),
        ],
        compiler_params=params(16),
        cost_estimate=cost(0, x.size * 14),
    )(part, r0, r1, dmid, x, pv)


def both_lengths(t, rows, start):
    @pl.when(t < QUAD - 1)
    def _():
        start(rows)

    @pl.when(t == QUAD - 1)
    def _():
        start(rows - 1)


def place_kernel(places, first, ids, *refs):
    n = len(places)
    srcs = refs[: 4 * n]
    refs = refs[4 * n :]
    outs = refs[:3] if first else refs[3:6]
    x0, x1, od, ou, ow, sem = refs[3:] if first else refs[6:]
    c, s = ids[0], ids[1]
    down, up, wout = outs
    _, rows, _, ff = od.shape
    part = ow.shape[-1]

    def reads(i, j):
        return [
            pltpu.make_async_copy(srcs[4 * i + j], x0.at[i], sem.at[0, i]),
            pltpu.make_async_copy(srcs[4 * i + j + 1], x1.at[i], sem.at[1, i]),
        ]

    for core in range(2):

        @pl.when(c == core)
        def _():
            for i in range(n):
                for m in reads(i, 2 * core):
                    m.start()

    def writes(length, i, side, t):
        o, dst = ((od, down), (ou, up))[side]
        return [
            pltpu.make_async_copy(
                o.at[i, pl.ds(0, length)], dst.at[pl.ds(t * rows, length)], sem.at[2 + side, i]
            ),
            pltpu.make_async_copy(
                ow.at[side, i, pl.ds(0, length)],
                wout.at[pl.ds(t * rows, length), :, pl.ds(side * part, part)],
                sem.at[4 + side, i],
            ),
        ]

    jobs = []
    for i, place in enumerate(places):
        for m in reads(i, 0):
            m.wait()
        swapped = ((place & 1) << 1) | (place >> 1)
        for side, (x, o, k) in enumerate(((x0, od, swapped), (x1, ou, place))):
            t = jnp.bitwise_xor(k, s)
            o[i, :, 0, :] = x[i, :, :ff].astype(F32)
            ow[side, i, :, 0, :] = x[i, :, ff:].astype(F32)
            both_lengths(t, rows, lambda length: [m.start() for m in writes(length, i, side, t)])
            jobs.append((i, side, t))
    for i, side, t in jobs:
        both_lengths(t, rows, lambda length: [m.wait() for m in writes(length, i, side, t)])


def place_rows(places, ids, srcs, outs, cc, ff, model):
    rows, cols = srcs[0].shape
    n = len(places)
    first = outs is None
    operands = [ids, *srcs] + ([] if first else list(outs))
    return pl.pallas_call(
        functools.partial(place_kernel, places, first),
        in_specs=[SMEM] + [HBM] * (len(operands) - 1),
        out_specs=[HBM] * 3,
        out_shape=[jax.ShapeDtypeStruct((cc, 1, m), F32) for m in (ff, ff, model)],
        input_output_aliases={} if first else {4 * n + 1 + i: i for i in range(3)},
        scratch_shapes=[
            pltpu.VMEM((n, rows, cols), BF16),
            pltpu.VMEM((n, rows, cols), BF16),
            pltpu.VMEM((n, rows, 1, ff), F32),
            pltpu.VMEM((n, rows, 1, ff), F32),
            pltpu.VMEM((2, n, rows, 1, cols - ff), F32),
            pltpu.SemaphoreType.DMA((6, n)),
        ],
        compiler_params=params(16),
        cost_estimate=cost(0, 12 * n * rows * cols),
    )(*operands)


def qkv_out_kernel(ids, *refs):
    srcs, out, rows, wide, od, sem = refs[:4], *refs[4:]
    c, s = ids[0], ids[1]
    _, _, half, cols = rows.shape
    width = cols // 3

    def reads(a, b):
        return [
            pltpu.make_async_copy(
                src.at[p, pl.ds(0, half), :],
                rows.at[i, jnp.bitwise_xor(p if i else ((p & 1) << 1) | (p >> 1), s)],
                sem.at[0, i * QUAD + p],
            )
            for i, src in enumerate((a, b))
            for p in range(QUAD)
        ]

    @pl.when(c == 0)
    def _():
        for m in reads(srcs[0], srcs[1]):
            m.start()

    @pl.when(c != 0)
    def _():
        for m in reads(srcs[2], srcs[3]):
            m.start()

    for m in reads(srcs[0], srcs[1]):
        m.wait()
    step = half // 2
    moves = []
    for b in range(4):
        if b >= 2:
            moves[b - 2].wait()
        for t in range(QUAD):
            v = rows[b // 2, t, (b % 2) * step : (b % 2 + 1) * step, :].astype(F32)
            for i in range(3):
                lo = (i * QUAD + t) * width
                wide[:, lo : lo + width] = v[:, i * width : (i + 1) * width]
        od[b % 2, :, 0, :] = wide[...]
        n = step - (b == 3)
        m = pltpu.make_async_copy(
            od.at[b % 2, pl.ds(0, n)], out.at[pl.ds(b * step, n)], sem.at[1, b % 2]
        )
        m.start()
        moves.append(m)
    for m in moves[-2:]:
        m.wait()


def qkv_out(ids, srcs, cc):
    cols = srcs[0].shape[-1]
    half = (cc + 1) // 2
    return pl.pallas_call(
        qkv_out_kernel,
        in_specs=[SMEM] + [HBM] * 4,
        out_specs=HBM,
        out_shape=jax.ShapeDtypeStruct((cc, 1, QUAD * cols), F32),
        scratch_shapes=[
            pltpu.VMEM((2, QUAD, half, cols), BF16),
            pltpu.VMEM((half // 2, QUAD * cols), F32),
            pltpu.VMEM((2, half // 2, 1, QUAD * cols), F32),
            pltpu.SemaphoreType.DMA((2, 2 * QUAD)),
        ],
        compiler_params=params(18),
        cost_estimate=cost(0, 6 * cc * QUAD * cols),
    )(ids, *srcs)


def vectors_kernel(count, ids, *refs):
    srcs, outs, (rows, heads, sem) = refs[:4], refs[4:-3], refs[-3:]
    c, s = ids[0], ids[1]
    _, _, tall, row_len = rows.shape
    top = srcs[0].shape[1] - tall

    def reads(pair):
        return [
            pltpu.make_async_copy(v.at[p, pl.ds(top, tall), :], rows.at[i, p], sem.at[i * QUAD + p])
            for i, v in enumerate(pair)
            for p in range(QUAD)
        ]

    for core in range(2):

        @pl.when(c == core)
        def _():
            for m in reads(srcs[2 * core : 2 * core + 2]):
                m.start()

    for m in reads(srcs[:2]):
        m.wait()
    total = jnp.zeros((tall, row_len), F32)
    for i in range(2):
        for p in range(QUAD):
            total = total + rows[i, p].astype(F32)
    at = 0
    for o in outs[:5]:
        n = o.shape[1]
        for lo in range(0, n, row_len):
            size = min(row_len, n - lo)
            o[0:1, lo : lo + size] = total[at : at + 1, :size]
            at += 1
    heads[...] = jnp.zeros_like(heads)
    for i in range(2):
        for p in range(QUAD):
            k = p if i else ((p & 1) << 1) | (p >> 1)
            heads[jnp.bitwise_xor(k, s)] += rows[i, p, at : at + 8, :].astype(F32)
    width = row_len // 3
    for part in range(2):
        for t in range(QUAD):
            lo = (part * QUAD + t) * width
            outs[5][0:1, lo : lo + width] = heads[t, 0:1, part * width : (part + 1) * width]
    outs[6][0:1, :] = jnp.sqrt(total[at + 1 : at + 2, : outs[6].shape[1]] / count)


def vectors_out(ids, srcs, count, cc, ff, model):
    row_len = srcs[0].shape[-1]
    shapes = [ff, cc, cc, cc, cc, 2 * model, 128]
    return pl.pallas_call(
        functools.partial(vectors_kernel, count),
        in_specs=[SMEM] + [HBM] * 4,
        out_specs=[VMEM] * 7,
        out_shape=[jax.ShapeDtypeStruct((1, n), F32) for n in shapes],
        scratch_shapes=[
            pltpu.VMEM((2, QUAD, 32, row_len), BF16),
            pltpu.VMEM((QUAD, 8, row_len), F32),
            pltpu.SemaphoreType.DMA((2 * QUAD,)),
        ],
        compiler_params=params(8),
        cost_estimate=cost(0, 1 << 19),
    )(ids, *srcs)


def to_first(v):
    pairs = [(i, i ^ 1) for i in range(QUAD)] + [(QUAD + i, QUAD + (i ^ 2)) for i in range(QUAD)]
    return lax.ppermute(v, ("section", "seq"), pairs)


def to_second(v):
    pairs = [(i, i ^ 2) for i in range(QUAD)] + [(QUAD + i, QUAD + (i ^ 1)) for i in range(QUAD)]
    return lax.ppermute(v, ("section", "seq"), pairs)


def to_quad(v, k):
    return lax.ppermute(v, "seq", [(i, i ^ k) for i in range(QUAD)])


def to_core(v):
    return lax.ppermute(v, "section", [(0, 1), (1, 0)])


def dp_partner(v, step):
    n = lax.axis_size("dp")
    return lax.ppermute(v, "dp", [(i, i ^ step) for i in range(n)])


def to_owner(l, v):
    return lax.ppermute(v, "section", [(1 - l, l)])


def tied(*v):
    return lax.optimization_barrier(v)


class Order:
    def __init__(self, token):
        self.token = token

    def wait(self, *v):
        *v, self.token = lax.optimization_barrier((*v, self.token))
        return v

    def run(self, step, *operands):
        out = step(*self.wait(*operands))
        out, self.token = lax.optimization_barrier((out, self.token))
        return out


class DpSum:
    def __init__(self, order_of, make, *operands):
        self.value = None
        self.steps = self.work(order_of, make, operands)

    def go(self):
        next(self.steps, None)

    def finish(self):
        for _ in self.steps:
            pass
        return self.value

    def work(self, order_of, make, operands):
        n = lax.axis_size("dp")
        z = lax.axis_index("dp")

        def split(v, step):
            left = v.shape[0] // n * step if v.ndim == 2 else v.shape[1]
            v = v.reshape(n // (2 * step), 2, left, v.shape[-1])
            low = (z & step) == 0
            return jnp.where(low, v[:, 1], v[:, 0]), jnp.where(low, v[:, 0], v[:, 1])

        def join(v, got, step):
            low = (z & step) == 0
            both = jnp.where(low, jnp.stack([v, got], 1), jnp.stack([got, v], 1))
            return both.reshape(-1, *v.shape[1:])

        away, keep = order_of.run(lambda *v: split(make(*v), 1), *operands)
        step = 1
        while step < n:
            got = dp_partner(away, step)
            yield
            step *= 2
            if step < n:
                away, keep = order_of.run(lambda a, b, s=step: split(add_low(a, b), s), keep, got)
            else:
                v = order_of.run(add_low, keep, got)
        while step > 1:
            step //= 2
            got = dp_partner(v, step)
            yield
            v = order_of.run(functools.partial(join, step=step), v, got)
        self.value = v.reshape(-1, v.shape[-1])


def add_low(a, b):
    return (a.astype(F32) + b.astype(F32)).astype(BF16)


def quad_gather(own):
    one = to_second(own)
    two = to_first(own)
    three = to_first(one)
    return [own, one, two, three]


def on_device(
    layer_in, cotangent, lengths, w_qkv, bias_qv, w_out, bias_out,
    gain_attn, gain_mlp, w_up, bias_up, w_down, bias_down,
):
    micro, _, span, cc = layer_in.shape
    model = w_out.shape[1]
    ff = w_up.shape[-1]
    hd = model // HEADS
    width = model // QUAD
    heads = width // hd
    c = lax.axis_index("section")
    s = lax.axis_index("seq")
    dp_count = lax.axis_size("dp")
    mine = c == 0

    lens = lax.dynamic_index_in_dim(lengths, c, 0, keepdims=False)[0]
    e0 = lens[0]
    e1 = e0 + lens[1]
    e2 = e1 + lens[2]
    e3 = e2 + lens[3]
    ids = jnp.stack([c, s, e0, e1, e2, e3, c, s]).astype(jnp.int32)
    cs = jnp.stack([c, s]).astype(jnp.int32)
    x = rows_in(cs, layer_in)

    def row(v, n=ff):
        return jnp.pad(v, ((0, 0), (0, n - v.shape[-1])))

    qb = lax.dynamic_slice_in_dim(bias_qv, s * width, width, 1)
    vb = lax.dynamic_slice_in_dim(bias_qv, model + s * width, width, 1)
    heads_bias = jnp.concatenate([qb, jnp.zeros((1, width), F32), vb], 1)
    pv_own = jnp.concatenate(
        [row(v) for v in (bias_up, bias_out, bias_down, gain_attn, gain_mlp, heads_bias)]
        + [jnp.zeros((2, ff), F32)]
    )
    w3_own = jnp.concatenate(
        [lax.dynamic_slice_in_dim(w_qkv[0], i * model + s * width, width, 1) for i in range(3)], 1
    )
    pv_got = to_core(pv_own)
    w3_got = to_core(w3_own)
    wo_got = to_core(w_out[0])
    up = (w_up, to_core(w_up))
    dn = (w_down, to_core(w_down))
    pv = [jnp.where(mine, pv_own, pv_got), jnp.where(mine, pv_got, pv_own)]
    w3 = [jnp.where(mine, w3_own, w3_got), jnp.where(mine, w3_got, w3_own)]
    wo = [jnp.where(mine, w_out[0], wo_got), jnp.where(mine, wo_got, w_out[0])]

    normed = x
    saved = []
    squares = []
    for l in range(2):
        blocks = quad_gather(normed)
        if l == 1:
            blocks, df = tied(blocks, rows_in(cs, cotangent))
        qh, kh, vh, lse, blocks, *att = attn_fwd(l == 0, ids, blocks, w3[l], pv[l], heads, hd)
        att = [att[0]] + [to_quad(att[k], k) for k in (1, 2, 3)]
        mid, u, xout, normed, sq, astk = mlp_fwd(
            l, ids, x, att, wo[l], pv[l], pv[min(l + 1, 1)], up, dn
        )
        saved.append((x, blocks, (qh, kh, vh, lse), astk, mid, u))
        squares.append(sq[0, 0])
        x = xout
    outs = [saved[1][0], x]

    order_of = Order(ids)
    run = order_of.run

    def first_part(l, df):
        lr, rr, dmid, g, *douts = run(
            lambda v: mlp_bwd(l, ids, v, saved[l][5], saved[l][4], wo[l], pv[l], up, dn), df
        )
        return lr, rr, dmid, g, [douts[0]] + [to_quad(douts[k], k) for k in (1, 2, 3)]

    def send(l, places, lr, rr):
        return run(lambda a, b: product(True, places, ids, a, b, saved[l][3]), lr, rr)

    def keep(l, places, lr, rr, got):
        return run(lambda a, b, v: product(False, places, ids, a, b, saved[l][3], v), lr, rr, got)

    def attention(l, douts):
        outs = run(lambda *v: attn_bwd(ids, saved[l][1], w3[l], saved[l][2], v), *douts)
        return (*outs, to_first(outs[2]), to_core(outs[3]))

    def input_part(l, p0, pr, q, dmid):
        return run(lambda *v: input_grad_of(*v, saved[l][0], pv[l]), p0, pr, q, dmid)

    def projection(l, gk, gs_got, g, gb, gg):
        heads_sum = jnp.concatenate([gb[0, :width], gb[0, 2 * width :]])
        row_len = 3 * width
        vectors = [
            g[0], g[1, :cc], g[2, :cc], gg[0, :cc], g[4, :cc], heads_sum,
            jnp.broadcast_to(squares[l], (row_len,)),
        ]
        v = [jnp.pad(x, (0, -x.shape[0] % row_len)) for x in vectors]
        v = jnp.concatenate(v).reshape(-1, row_len)
        v = jnp.pad(v, ((0, 32 - v.shape[0]), (0, 0))).astype(BF16)
        return jnp.concatenate([add_low(gk, gs_got), v])

    def wait(*v):
        out = order_of.wait(*v)
        return out[0] if len(out) == 1 else out

    def pair_up(a, b):
        return jnp.stack([a, b])

    def add_first(a, b):
        return add_low(a, b[:span])

    lr1, rr1, dmid1, g1, douts1 = first_part(1, df)

    far1 = to_core(send(1, (3, 2), lr1, rr1))
    douts1 = wait(*douts1)
    near1 = send(1, (1, 0), lr1, rr1)
    far1 = wait(far1)

    far1 = keep(1, (3, 2), lr1, rr1, far1)
    x1a, near1 = to_first(far1[0]), to_core(near1)
    p0, p1, _, _, gk1, gb1, pr, gs_got = attention(1, douts1)
    x1a, near1 = wait(x1a, near1)

    out_got = to_core(run(lambda a, b: jnp.where(mine, a, b), outs[1], outs[0]))
    near1 = keep(1, (1, 0), lr1, rr1, near1)
    half1 = run(add_low, near1[0], x1a)
    pr, gs_got, out_got = wait(pr, gs_got, out_got)

    q = to_second(run(add_first, p1, pr))
    q = wait(q)

    x1b, half1 = wait(far1[1], half1)
    x1b, x2 = to_first(x1b), to_second(half1)
    dx1, gg1 = input_part(1, p0, pr, q, dmid1)
    qkv_sum1 = DpSum(order_of, functools.partial(projection, 1), gk1, gs_got, g1, gb1, gg1)
    lr0, rr0, dmid0, g0, douts0 = first_part(0, dx1)
    far0 = to_core(send(0, (3, 2), lr0, rr0))
    near0 = send(0, (1, 0), lr0, rr0)
    x1b, x2 = wait(x1b, x2)

    sum1 = DpSum(order_of, lambda a, b, d: add_low(add_low(a, b), d), near1[1], x1b, x2)
    sum1.go()
    far0, *douts0 = wait(far0, *douts0)

    far0 = keep(0, (3, 2), lr0, rr0, far0)
    x1a, near0 = to_first(far0[0]), to_core(near0)
    p0, p1, _, _, gk0, gb0, pr, gs_got = attention(0, douts0)
    x1a, near0 = wait(x1a, near0)

    sum1.go()
    near0 = keep(0, (1, 0), lr0, rr0, near0)
    half1 = run(add_low, near0[0], x1a)
    qkv_sum1.go()
    pr, gs_got = wait(pr, gs_got)

    q = to_second(run(add_first, p1, pr))
    q = wait(q)

    x1b = to_first(wait(far0[1]))
    dx0, gg0 = input_part(0, p0, pr, q, dmid0)
    qkv_sum1.go()
    sum1.go()
    x1b, half1 = wait(x1b, half1)

    x2 = to_second(half1)
    sum1.go()
    half0 = run(add_low, near0[1], x1b)
    qkv_sum0 = DpSum(order_of, functools.partial(projection, 0), gk0, gs_got, g0, gb0, gg0)
    qkv_sum0.go()
    qkv_sum1.go()
    x2 = wait(x2)
    own1 = sum1.finish()

    have1 = [own1, to_second(own1), to_first(own1)]
    sum0 = DpSum(order_of, add_low, half0, x2)
    sum0.go()
    qkv_sum1.go()
    qkv_sum0.go()
    sum0.go()
    have1[1], have1[2] = wait(have1[1], have1[2])

    have1.append(to_first(have1[1]))
    qkv_own1 = qkv_sum1.finish()
    qkv_sum0.go()
    got1 = [to_owner(1, own1)]
    sum0.go()
    have1[3], got1[0] = wait(have1[3], got1[0])

    qkv_next1 = to_second(qkv_own1)
    got1.append(to_owner(1, have1[1]))
    qkv_sum0.go()
    qkv_next1, got1[1] = wait(qkv_next1, got1[1])
    qkv_pair1 = run(pair_up, qkv_own1, qkv_next1)
    sum0.go()

    qkv_rest1 = to_first(qkv_pair1)
    got1.append(to_owner(1, have1[2]))
    qkv_own0 = qkv_sum0.finish()
    qkv_next0 = to_second(qkv_own0)
    qkv_rest1, got1[2], qkv_next0 = wait(qkv_rest1, got1[2], qkv_next0)

    own0 = sum0.finish()
    have0 = [own0, to_second(own0), to_first(own0)]
    got1.append(to_owner(1, have1[3]))
    qkv_pair0 = run(pair_up, qkv_own0, qkv_next0)
    qkv_rest0 = to_first(qkv_pair0)
    got1[3] = wait(got1[3])
    got0 = [to_owner(0, own0)]
    in_got = to_core(run(lambda a, b: jnp.where(mine, a, b), dx1, dx0))
    qkv1 = run(lambda a, b: jnp.concatenate([a, b]), qkv_pair1, qkv_rest1)
    layer_out = run(
        lambda a, b, d: rows_out(ids, jnp.where(mine, a, b), d), outs[0], outs[1], out_got
    )
    got0[0], in_got = wait(got0[0], in_got)

    def place(places, outs_w):
        srcs = [v[p] for p in places for v in (have0, got0, got1, have1)]
        n = len(srcs)
        return run(
            lambda *v: place_rows(places, ids, v[:n], v[n:] or None, cc, ff, model), *srcs, *outs_w
        )

    outs_w = place((0,), ())
    input_grad = run(lambda a, b, d: rows_out(ids, jnp.where(mine, a, b), d), dx0, dx1, in_got)
    have0[1], have0[2], qkv_rest0 = wait(have0[1], have0[2], qkv_rest0)

    have0.append(to_first(have0[1]))
    qkv0 = run(lambda a, b: jnp.concatenate([a, b]), qkv_pair0, qkv_rest0)
    have0[1], have0[2] = wait(have0[1], have0[2])
    got0.append(to_owner(0, have0[1]))
    qkv0_got, qkv1_got = to_owner(0, qkv0), to_owner(1, qkv1)
    got0[1] = wait(got0[1])
    outs_w = place((1,), outs_w)
    got0.append(to_owner(0, wait(have0[2])))
    qkv0_got, qkv1_got = wait(qkv0_got, qkv1_got)
    grad_qkv = run(lambda *v: qkv_out(ids, v, cc), qkv0, qkv0_got, qkv1_got, qkv1)
    count = micro * dp_count * span * QUAD
    vectors = run(
        lambda *v: vectors_out(ids, v, count, cc, ff, model), qkv0, qkv0_got, qkv1_got, qkv1
    )
    have0[3], got0[2] = wait(have0[3], got0[2])

    got0.append(to_owner(0, have0[3]))
    outs_w = place((2,), outs_w)
    got0[3] = wait(got0[3])
    grad_down, grad_up, grad_out = place_rows(
        (3,), order_of.token, [v[3] for v in (have0, got0, got1, have1)], outs_w, cc, ff, model
    )

    grad_bup, grad_bout, grad_bdown, grad_ga, grad_gm, grad_bqv, rms = vectors
    return (
        layer_out,
        input_grad,
        jnp.transpose(grad_qkv, (1, 0, 2)),
        grad_bqv,
        jnp.transpose(grad_out, (1, 2, 0)),
        grad_bout,
        grad_ga,
        grad_gm,
        jnp.transpose(grad_up, (1, 0, 2)),
        grad_bup,
        jnp.transpose(grad_down, (1, 2, 0)),
        grad_bdown,
        rms[0, :1],
    )


def solution(mesh):
    two = P("section", None)
    three = P("section", None, None)
    tokens = P(None, "dp", "seq", None)
    stacked = P("section", None, "dp", "seq", None)
    return jax.shard_map(
        on_device,
        mesh=mesh,
        in_specs=(
            tokens, tokens, P(None, "dp", None), three, two, three, two, two, two, three, two, three, two,
        ),
        out_specs=(
            stacked, stacked, three, two, three, two, two, two, three, two, three, two, P("section"),
        ),
        check_vma=False,
    )
```

```python
import functools

import jax
import jax.numpy as jnp
from jax import lax
from jax.experimental import pallas as pl
from jax.experimental.pallas import tpu as pltpu
from jax.sharding import PartitionSpec as P

HEADS = 12
EPS = 1e-6
NEG = -1e30
F32 = jnp.float32
BF16 = jnp.bfloat16
MIB = 1 << 20
QUAD = 4


def nn(a, b):
    return lax.dot_general(a, b, (((1,), (0,)), ((), ())), preferred_element_type=F32)


def nt(a, b):
    return lax.dot_general(a, b, (((1,), (1,)), ((), ())), preferred_element_type=F32)


def tn(a, b):
    return lax.dot_general(a, b, (((0,), (0,)), ((), ())), preferred_element_type=F32)


def order(core, k):
    return jnp.where(core == 1, k, ((k & 1) << 1) | (k >> 1))


def crms_scale(v):
    sq = jnp.sum(v * v, axis=-1, keepdims=True)
    su = jnp.sum(v, axis=-1, keepdims=True)
    full = v.shape[-1] + 1
    return lax.rsqrt((sq + su * su) / full + EPS), su, (sq + su * su) / full


def crms_back(v, gain, grad):
    r, su, _ = crms_scale(v)
    gd = grad * gain
    w = jnp.sum(gd * v, axis=-1, keepdims=True)
    unit = v * r
    dv = gd * r - (w * r * r * r / (v.shape[-1] + 1)) * (v + su)
    return dv, grad * unit, unit * gain


GC = 0.7978845608028654


def gelu_parts(u):
    inner = GC * (u + 0.044715 * (u * u * u))
    th = jnp.tanh(inner)
    return th


def params(mib, **kw):
    return pltpu.CompilerParams(vmem_limit_bytes=mib * MIB, **kw)


def cost(flops, nbytes, trans=0):
    return pl.CostEstimate(
        flops=int(2 * flops), bytes_accessed=int(2 * nbytes), transcendentals=int(2 * trans)
    )


SMEM = pl.BlockSpec(memory_space=pltpu.SMEM)
VMEM = pl.BlockSpec(memory_space=pltpu.VMEM)
HBM = pl.BlockSpec(memory_space=pltpu.HBM)


def rows_in_kernel(ids, v, o):
    @pl.when(ids[0] == 0)
    def _():
        o[...] = v[:, 0, :].T

    @pl.when(ids[0] != 0)
    def _():
        o[...] = v[:, 1, :].T


def rows_in(ids, v):
    micro, _, span, cc = v.shape
    return pl.pallas_call(
        rows_in_kernel,
        in_specs=[SMEM, VMEM],
        out_specs=VMEM,
        out_shape=jax.ShapeDtypeStruct((span, cc), BF16),
        compiler_params=params(16),
        cost_estimate=cost(0, 6 * span * cc),
    )(ids, jnp.transpose(v[:, 0], (2, 0, 1)))


def rows_out_kernel(ids, own, got, o):
    @pl.when(ids[0] == 0)
    def _():
        o[:, 0, :] = own[...].T
        o[:, 1, :] = got[...].T

    @pl.when(ids[0] != 0)
    def _():
        o[:, 0, :] = got[...].T
        o[:, 1, :] = own[...].T


def rows_out(ids, own, got):
    span, cc = own.shape
    o = pl.pallas_call(
        rows_out_kernel,
        in_specs=[SMEM, VMEM, VMEM],
        out_specs=VMEM,
        out_shape=jax.ShapeDtypeStruct((cc, 2, span), BF16),
        compiler_params=params(16),
        cost_estimate=cost(0, 8 * span * cc),
    )(ids, own, got)
    return jnp.transpose(o, (1, 2, 0))[None, :, None]


def visible_bias(ids, n, t, span):
    i = t * span + lax.broadcasted_iota(jnp.int32, (1, span), 1)
    start = jnp.zeros((1, span), jnp.int32)
    for d in range(4):
        end = ids[2 + d]
        start = jnp.maximum(start, jnp.where(i >= end, end, 0))
    j = lax.broadcasted_iota(jnp.int32, (n, span), 0)
    return jnp.where((j >= start) & (j <= i), 0.0, NEG)


def attn_fwd_kernel(
    raw, ids, n0, n1, n2, n3, w_ref, pv_ref, q_hbm, k_hbm, v_hbm, l_hbm, n_hbm,
    a0, a1, a2, a3, qh, kh, vh, lse, nb_scr, at, bias_scr, sem,
):
    c, s = ids[0], ids[1]
    heads, _, hd = qh.shape
    span, cc = n0.shape
    width = heads * hd
    bias = pv_ref[5:6, : 3 * width]
    for p, nb in enumerate((n0, n1, n2, n3)):
        t = jnp.bitwise_xor(order(c, p), s)
        row = pl.multiple_of(t * span, span)
        rows = nb[...]
        if raw:
            v = rows.astype(F32)
            rows = (v * crms_scale(v)[0] * pv_ref[3:4, :cc]).astype(BF16)
            nb_scr[p] = rows
        y = nn(rows, w_ref[...]) + bias
        for h in range(heads):
            lo = h * hd
            qh[h, pl.ds(row, span), :] = (y[:, lo : lo + hd] * (hd**-0.5)).astype(BF16)
            kh[h, pl.ds(row, span), :] = y[:, width + lo : width + lo + hd].astype(BF16)
            vh[h, pl.ds(row, span), :] = y[:, 2 * width + lo : 2 * width + lo + hd].astype(BF16)
    moves = [
        pltpu.make_async_copy(src, dst, sem.at[i])
        for i, (src, dst) in enumerate(
            [(qh, q_hbm), (kh, k_hbm), (vh, v_hbm), (lse, l_hbm)]
            + [(nb_scr.at[p] if raw else nb, n_hbm.at[p]) for p, nb in enumerate((n0, n1, n2, n3))]
        )
    ]
    for i, m in enumerate(moves):
        if i != 3:
            m.start()
    for t in range(QUAD):
        n = span * (t + 1)
        bias_scr[:n, :] = visible_bias(ids, n, t, span)

        def head(h, carry, t=t, n=n):
            q = qh[h, t * span : (t + 1) * span, :]
            sc = nt(kh[h, :n, :], q) + bias_scr[:n, :]
            m = jnp.max(sc, axis=0, keepdims=True)
            e = jnp.exp(sc - m)
            tot = jnp.sum(e, axis=0, keepdims=True)
            pr = (e * (1.0 / tot)).astype(BF16)
            o = tn(vh[h, :n, :], pr)
            at[t, pl.ds(pl.multiple_of(h * hd, hd), hd), :] = o.astype(BF16)
            lse[h, t : t + 1, :] = m + jnp.log(tot)
            return carry

        lax.fori_loop(0, heads, head, 0)
    moves[3].start()
    for k, a in enumerate((a0, a1, a2, a3)):
        a[...] = at[jnp.bitwise_xor(s, k)]
    for m in moves:
        m.wait()


def attn_fwd(raw, ids, blocks, w3, pv, heads, hd):
    span, width = blocks[0].shape
    full = span * QUAD
    hh = jax.ShapeDtypeStruct((heads, full, hd), BF16)
    aa = jax.ShapeDtypeStruct((heads * hd, span), BF16)
    saved = [hh, hh, hh, jax.ShapeDtypeStruct((heads, QUAD, span), F32)]
    nb = jax.ShapeDtypeStruct((QUAD, span, width), BF16)
    return pl.pallas_call(
        functools.partial(attn_fwd_kernel, raw),
        in_specs=[SMEM] + [VMEM] * 6,
        out_specs=[HBM] * 5 + [VMEM] * 4,
        out_shape=[*saved, nb, aa, aa, aa, aa],
        scratch_shapes=[pltpu.VMEM(v.shape, v.dtype) for v in saved]
        + [
            pltpu.VMEM(nb.shape if raw else (1, 8, 128), BF16),
            pltpu.VMEM((QUAD, heads * hd, span), BF16),
            pltpu.VMEM((full, span), F32),
            pltpu.SemaphoreType.DMA((8,)),
        ],
        compiler_params=params(18),
        cost_estimate=cost(
            2 * full * width * 3 * heads * hd + 3 * 4 * full * full * hd * heads,
            4 * full * width,
            heads * full * full,
        ),
    )(ids, *blocks, w3, pv)


def mlp_fwd_kernel(
    layer, ids, x, a0, a1, a2, a3, wo, pv, pvn, pvb, upo, upr, dno, dnr,
    mid, u, xout, nnext, sq, astk, nm, acc,
):
    j = pl.program_id(0)
    c, s = ids[0], ids[1]
    cc = x.shape[-1]
    own = c == layer

    @pl.when(j == 0)
    def _():
        rows = a0.shape[0]
        m = x[...].astype(F32) + pv[1:2, :cc]
        for k, a in enumerate((a0, a1, a2, a3)):
            row = pl.multiple_of(jnp.bitwise_xor(s, k) * rows, rows)
            m = m + tn(a[...], wo[pl.ds(row, rows), :])
            astk[jnp.bitwise_xor(s, k)] = a[...].T
        mid[...] = m
        r, _, _ = crms_scale(m)
        nm[...] = (m * r * pv[4:5, :cc]).astype(BF16)
        acc[...] = m + pv[2:3, :cc]

    wu = lax.select(own, upo[0], upr[0])
    wd = lax.select(own, dno[0], dnr[0])
    ub = nn(nm[...], wu) + pvb[0:1, :]
    u[...] = ub
    act = (0.5 * ub * (1.0 + gelu_parts(ub))).astype(BF16)
    acc[...] += nn(act, wd)

    @pl.when(j == pl.num_programs(0) - 1)
    def _():
        fin = acc[...]
        _, _, ms = crms_scale(fin)
        sq[...] = jnp.broadcast_to(jnp.sum(ms, axis=0, keepdims=True), sq.shape)
        low = fin.astype(BF16)
        xout[...] = low
        lf = low.astype(F32)
        r, _, _ = crms_scale(lf)
        nnext[...] = (lf * r * pvn[3:4, :cc]).astype(BF16)


def mlp_fwd(layer, ids, x, att, wo, pv, pvn, up, dn):
    span, cc = x.shape
    ff = up[0].shape[-1]
    fb = ff // 4
    rows = att[0].shape[0]

    def whole(shape):
        return pl.BlockSpec(shape, lambda j, ids: (0,) * len(shape))

    def pick(mine):
        return lambda j, ids: jnp.where((ids[0] == layer) == mine, j, 0)

    mine, other = pick(True), pick(False)
    grid = pltpu.PrefetchScalarGridSpec(
        num_scalar_prefetch=1,
        grid=(4,),
        in_specs=[whole((span, cc))]
        + [whole((rows, span))] * 4
        + [whole(wo.shape), whole(pv.shape), whole(pvn.shape)]
        + [
            pl.BlockSpec((8, fb), lambda j, ids: (0, j)),
            pl.BlockSpec((1, cc, fb), lambda j, ids: (0, 0, mine(j, ids))),
            pl.BlockSpec((1, cc, fb), lambda j, ids: (0, 0, other(j, ids))),
            pl.BlockSpec((1, fb, cc), lambda j, ids: (0, mine(j, ids), 0)),
            pl.BlockSpec((1, fb, cc), lambda j, ids: (0, other(j, ids), 0)),
        ],
        out_specs=[
            whole((span, cc)),
            pl.BlockSpec((span, fb), lambda j, ids: (0, j)),
            whole((span, cc)),
            whole((span, cc)),
            whole((8, 128)),
            whole((QUAD, span, rows)),
        ],
        scratch_shapes=[pltpu.VMEM((span, cc), BF16), pltpu.VMEM((span, cc), F32)],
    )
    return pl.pallas_call(
        functools.partial(mlp_fwd_kernel, layer),
        grid_spec=grid,
        out_shape=[
            jax.ShapeDtypeStruct((span, cc), F32),
            jax.ShapeDtypeStruct((span, ff), F32),
            jax.ShapeDtypeStruct((span, cc), BF16),
            jax.ShapeDtypeStruct((span, cc), BF16),
            jax.ShapeDtypeStruct((8, 128), F32),
            jax.ShapeDtypeStruct((QUAD, span, rows), BF16),
        ],
        compiler_params=params(26, dimension_semantics=("arbitrary",)),
        cost_estimate=cost(6 * span * cc * ff, 4 * cc * ff + 4 * span * ff, span * ff),
    )(ids, x, *att, wo, pv, pvn, pv, up[0], up[1], dn[0], dn[1])


def mlp_bwd_kernel(
    layer, ids, df, u, mid, wo, pv, upo, upr, dno, dnr,
    lr, rr, dmid, g, d0, d1, d2, d3, acc, wide,
):
    j = pl.program_id(0)
    c, s = ids[0], ids[1]
    cc = df.shape[-1]
    fb = u.shape[-1]
    own = c == layer

    @pl.when(j == 0)
    def _():
        acc[...] = jnp.zeros_like(acc)
        g[...] = jnp.zeros_like(g)

    wu = lax.select(own, upo[0], upr[0])
    wd = lax.select(own, dno[0], dnr[0])
    da = nt(df[...], wd)
    ub = u[...]
    th = gelu_parts(ub)
    half = 0.5 * (1.0 + th)
    lr[0] = (ub * half).astype(BF16)
    slope = half + 0.5 * ub * (1.0 - th * th) * (GC * (1.0 + 3 * 0.044715 * (ub * ub)))
    du = (slope * da).astype(BF16)
    lr[1] = du
    g[0:1, pl.ds(pl.multiple_of(j * fb, 128), fb)] = jnp.sum(du.astype(F32), axis=0, keepdims=True)
    acc[...] += nt(du, wu)

    @pl.when(j == pl.num_programs(0) - 1)
    def _():
        dff = df[...].astype(F32)
        dv, gg, nm = crms_back(mid[...], pv[4:5, :cc], acc[...])
        dm = dff + dv
        low = dm.astype(BF16)
        dmid[...] = dm
        quarter = rr.shape[-1]
        wide[:, cc:] = jnp.zeros((wide.shape[0], wide.shape[1] - cc), BF16)
        for i, v in enumerate((df[...], nm.astype(BF16), low)):
            wide[:, :cc] = v
            for t in range(QUAD):
                rr[i, t] = wide[:, t * quarter : (t + 1) * quarter]
        g[1:2, :cc] = jnp.sum(low.astype(F32), axis=0, keepdims=True)
        g[2:3, :cc] = jnp.sum(dff, axis=0, keepdims=True)
        g[4:5, :cc] = jnp.sum(gg, axis=0, keepdims=True)
        rows = d0.shape[0]
        for k, d in enumerate((d0, d1, d2, d3)):
            row = pl.multiple_of(jnp.bitwise_xor(s, k) * rows, rows)
            d[...] = nt(wo[pl.ds(row, rows), :], low).astype(BF16)


def mlp_bwd(layer, ids, df, u, mid, wo, pv, up, dn):
    span, cc = df.shape
    ff = u.shape[-1]
    fb = ff // 4
    rows = wo.shape[0] // QUAD

    def whole(shape):
        return pl.BlockSpec(shape, lambda j, ids: (0,) * len(shape))

    def pick(mine):
        return lambda j, ids: jnp.where((ids[0] == layer) == mine, j, 0)

    mine, other = pick(True), pick(False)
    grid = pltpu.PrefetchScalarGridSpec(
        num_scalar_prefetch=1,
        grid=(4,),
        in_specs=[
            whole((span, cc)),
            pl.BlockSpec((span, fb), lambda j, ids: (0, j)),
            whole((span, cc)),
            whole(wo.shape),
            whole(pv.shape),
            pl.BlockSpec((1, cc, fb), lambda j, ids: (0, 0, mine(j, ids))),
            pl.BlockSpec((1, cc, fb), lambda j, ids: (0, 0, other(j, ids))),
            pl.BlockSpec((1, fb, cc), lambda j, ids: (0, mine(j, ids), 0)),
            pl.BlockSpec((1, fb, cc), lambda j, ids: (0, other(j, ids), 0)),
        ],
        out_specs=[
            pl.BlockSpec((2, span, fb), lambda j, ids: (0, 0, j)),
            whole((3, QUAD, span, (cc + 1) // QUAD)),
            whole((span, cc)),
            whole((8, ff)),
        ]
        + [whole((rows, span))] * 4,
        scratch_shapes=[pltpu.VMEM((span, cc), F32), pltpu.VMEM((span, cc + 1), BF16)],
    )
    dd = jax.ShapeDtypeStruct((rows, span), BF16)
    return pl.pallas_call(
        functools.partial(mlp_bwd_kernel, layer),
        grid_spec=grid,
        out_shape=[
            jax.ShapeDtypeStruct((2, span, ff), BF16),
            jax.ShapeDtypeStruct((3, QUAD, span, (cc + 1) // QUAD), BF16),
            jax.ShapeDtypeStruct((span, cc), F32),
            jax.ShapeDtypeStruct((8, ff), F32),
            dd, dd, dd, dd,
        ],
        compiler_params=params(26, dimension_semantics=("arbitrary",)),
        cost_estimate=cost(6 * span * cc * ff, 4 * cc * ff + 8 * span * ff, span * ff),
    )(ids, df, u, mid, wo, pv, up[0], up[1], dn[0], dn[1])


def product_kernel(send, places, ids, lr, rr, att, *rest):
    outs = [rest[0].at[i] for i in range(len(places))] if send else rest[1:]
    core = 1 - ids[0] if send else ids[0]
    ff = lr.shape[-1]
    part = att.shape[-1]
    for i, place in enumerate(places):
        t = jnp.bitwise_xor(order(core, place), ids[1])
        out = outs[i]
        main = tn(rr[core, t], lr[core])
        low = rr[2, t]
        sides = [tn(low, att[2 * core + h]) for h in range(2)]
        if not send:
            got = rest[0].at[i]
            main = main + got[:, :ff].astype(F32)
            sides = [v + got[:, ff + h * part : ff + (h + 1) * part].astype(F32) for h, v in enumerate(sides)]
        out[:, :ff] = main.astype(BF16)
        for h, v in enumerate(sides):
            out[:, ff + h * part : ff + (h + 1) * part] = v.astype(BF16)


def product(send, places, ids, lr, rr, att, *got):
    span, quarter = rr.shape[2:]
    cols = lr.shape[-1] + 2 * att.shape[-1]
    return pl.pallas_call(
        functools.partial(product_kernel, send, places),
        in_specs=[SMEM] + [VMEM] * (3 + len(got)),
        out_specs=VMEM if send else [VMEM] * len(places),
        out_shape=jax.ShapeDtypeStruct((len(places), quarter, cols), BF16)
        if send
        else [jax.ShapeDtypeStruct((quarter, cols), BF16)] * len(places),
        compiler_params=params(18),
        cost_estimate=cost(2 * span * quarter * cols * len(places), 2 * 4 * quarter * cols * len(places)),
    )(ids, lr, rr, att, *got)


def attn_bwd_kernel(
    ids, n_hbm, w_hbm, q_hbm, k_hbm, v_hbm, l_hbm, d0, d1, d2, d3,
    p0, p1, far, gs, gk, gb, do, dk, dv, dy, acc, bias_scr,
    nb, w_ref, qh, kh, vh, lse, sem,
):
    c, s = ids[0], ids[1]
    heads, _, hd = qh.shape
    _, span, cc = nb.shape
    width = heads * hd
    moves = [
        pltpu.make_async_copy(src, dst, sem.at[i])
        for i, (src, dst) in enumerate(
            [(q_hbm, qh), (k_hbm, kh), (v_hbm, vh), (l_hbm, lse), (w_hbm, w_ref), (n_hbm, nb)]
        )
    ]
    for m in moves:
        m.start()
    for k, d in enumerate((d0, d1, d2, d3)):
        do[jnp.bitwise_xor(s, k)] = d[...]
    for m in moves[:4]:
        m.wait()
    for t in reversed(range(QUAD)):
        n = span * (t + 1)
        bias_scr[:n, :] = visible_bias(ids, n, t, span)
        for h in range(heads):
            q = qh[h, t * span : (t + 1) * span, :]
            kk = kh[h, :n, :]
            sc = nt(kk, q) + (bias_scr[:n, :] - lse[h, t : t + 1, :])
            pr = jnp.exp(sc)
            dot = do[t, h * hd : (h + 1) * hd, :]
            dp = nn(vh[h, :n, :], dot)
            inner = jnp.sum(pr * dp, axis=0, keepdims=True)
            ds = (pr * (dp - inner)).astype(BF16)
            newk = nn(ds, q)
            newv = nt(pr.astype(BF16), dot)
            if t == QUAD - 1:
                dk[h, :n, :] = newk
                dv[h, :n, :] = newv
            else:
                dk[h, :n, :] += newk
                dv[h, :n, :] += newv
            dq = tn(kk, ds) * (hd**-0.5)
            dy[t * span : (t + 1) * span, h * hd : (h + 1) * hd] = dq.T.astype(BF16)
    for h in range(heads):
        dy[:, width + h * hd : width + (h + 1) * hd] = dk[h].astype(BF16)
        dy[:, 2 * width + h * hd : 2 * width + (h + 1) * hd] = dv[h].astype(BF16)
    for m in moves[4:]:
        m.wait()
    total = jnp.zeros((1, 3 * width), F32)
    for p, out in enumerate((p0, p1, far.at[span:], far.at[:span])):
        row = pl.multiple_of(jnp.bitwise_xor(order(c, p), s) * span, span)
        y = dy[pl.ds(row, span), :]
        out[...] = nt(y, w_ref[...]).astype(BF16)
        total = total + jnp.sum(y.astype(F32), axis=0, keepdims=True)
        g = tn(nb[p], y)
        if p == 0:
            acc[:cc, :] = g
        else:
            acc[:cc, :] += g
    gb[...] = jnp.broadcast_to(total, gb.shape)
    part = gs.shape[0]
    acc[cc:, :] = jnp.zeros((acc.shape[0] - cc, acc.shape[1]), F32)
    gk[...] = acc[pl.ds(pl.multiple_of(c * part, part), part), :].astype(BF16)
    gs[...] = acc[pl.ds(pl.multiple_of((1 - c) * part, part), part), :].astype(BF16)


def attn_bwd(ids, blocks, w3, qkvl, douts):
    _, span, cc = blocks.shape
    heads, full, hd = qkvl[0].shape
    width = heads * hd
    pp = jax.ShapeDtypeStruct((span, cc), BF16)
    gg = jax.ShapeDtypeStruct(((cc + 1) // 2, 3 * width), BF16)
    return pl.pallas_call(
        attn_bwd_kernel,
        in_specs=[SMEM] + [HBM] * 6 + [VMEM] * 4,
        out_specs=[VMEM] * 6,
        out_shape=[pp, pp, jax.ShapeDtypeStruct((2 * span, cc), BF16), gg, gg, jax.ShapeDtypeStruct((8, 3 * width), F32)],
        scratch_shapes=[
            pltpu.VMEM((QUAD, width, span), BF16),
            pltpu.VMEM((heads, full, hd), F32),
            pltpu.VMEM((heads, full, hd), F32),
            pltpu.VMEM((full, 3 * width), BF16),
            pltpu.VMEM((cc + 1, 3 * width), F32),
            pltpu.VMEM((full, span), F32),
            pltpu.VMEM((QUAD, span, cc), BF16),
            pltpu.VMEM(w3.shape, BF16),
            pltpu.VMEM((heads, full, hd), BF16),
            pltpu.VMEM((heads, full, hd), BF16),
            pltpu.VMEM((heads, full, hd), BF16),
            pltpu.VMEM((heads, QUAD, span), F32),
            pltpu.SemaphoreType.DMA((6,)),
        ],
        compiler_params=params(26),
        cost_estimate=cost(
            4 * full * cc * 3 * width + 3 * 10 * full * full * hd * heads,
            8 * full * cc,
            heads * full * full,
        ),
    )(ids, blocks, w3, *qkvl, *douts)


def input_kernel(part, r0, r1, dmid, x, pv, dx, gg):
    cc = x.shape[-1]
    dn = part[...].astype(F32) + r0[part.shape[0] :, :].astype(F32) + r1[...].astype(F32)
    dv, g, _ = crms_back(x[...].astype(F32), pv[3:4, :cc], dn)
    dx[...] = (dmid[...] + dv).astype(BF16)
    gg[...] = jnp.broadcast_to(jnp.sum(g, axis=0, keepdims=True), gg.shape)


def input_grad_of(part, r0, r1, dmid, x, pv):
    return pl.pallas_call(
        input_kernel,
        in_specs=[VMEM] * 6,
        out_specs=[VMEM] * 2,
        out_shape=[
            jax.ShapeDtypeStruct(x.shape, BF16),
            jax.ShapeDtypeStruct((8, x.shape[-1]), F32),
        ],
        compiler_params=params(16),
        cost_estimate=cost(0, x.size * 14),
    )(part, r0, r1, dmid, x, pv)


def both_lengths(t, rows, start):
    @pl.when(t < QUAD - 1)
    def _():
        start(rows)

    @pl.when(t == QUAD - 1)
    def _():
        start(rows - 1)


def place_kernel(places, first, ids, *refs):
    n = len(places)
    srcs = refs[: 4 * n]
    refs = refs[4 * n :]
    outs = refs[:3] if first else refs[3:6]
    x0, x1, od, ou, ow, sem = refs[3:] if first else refs[6:]
    c, s = ids[0], ids[1]
    down, up, wout = outs
    _, rows, _, ff = od.shape
    part = ow.shape[-1]

    def reads(i, j):
        return [
            pltpu.make_async_copy(srcs[4 * i + j], x0.at[i], sem.at[0, i]),
            pltpu.make_async_copy(srcs[4 * i + j + 1], x1.at[i], sem.at[1, i]),
        ]

    for core in range(2):

        @pl.when(c == core)
        def _():
            for i in range(n):
                for m in reads(i, 2 * core):
                    m.start()

    def writes(length, i, side, t):
        o, dst = ((od, down), (ou, up))[side]
        return [
            pltpu.make_async_copy(
                o.at[i, pl.ds(0, length)], dst.at[pl.ds(t * rows, length)], sem.at[2 + side, i]
            ),
            pltpu.make_async_copy(
                ow.at[side, i, pl.ds(0, length)],
                wout.at[pl.ds(t * rows, length), :, pl.ds(side * part, part)],
                sem.at[4 + side, i],
            ),
        ]

    jobs = []
    for i, place in enumerate(places):
        for m in reads(i, 0):
            m.wait()
        swapped = ((place & 1) << 1) | (place >> 1)
        for side, (x, o, k) in enumerate(((x0, od, swapped), (x1, ou, place))):
            t = jnp.bitwise_xor(k, s)
            o[i, :, 0, :] = x[i, :, :ff].astype(F32)
            ow[side, i, :, 0, :] = x[i, :, ff:].astype(F32)
            both_lengths(t, rows, lambda length: [m.start() for m in writes(length, i, side, t)])
            jobs.append((i, side, t))
    for i, side, t in jobs:
        both_lengths(t, rows, lambda length: [m.wait() for m in writes(length, i, side, t)])


def place_rows(places, ids, srcs, outs, cc, ff, model):
    rows, cols = srcs[0].shape
    n = len(places)
    first = outs is None
    operands = [ids, *srcs] + ([] if first else list(outs))
    return pl.pallas_call(
        functools.partial(place_kernel, places, first),
        in_specs=[SMEM] + [HBM] * (len(operands) - 1),
        out_specs=[HBM] * 3,
        out_shape=[jax.ShapeDtypeStruct((cc, 1, m), F32) for m in (ff, ff, model)],
        input_output_aliases={} if first else {4 * n + 1 + i: i for i in range(3)},
        scratch_shapes=[
            pltpu.VMEM((n, rows, cols), BF16),
            pltpu.VMEM((n, rows, cols), BF16),
            pltpu.VMEM((n, rows, 1, ff), F32),
            pltpu.VMEM((n, rows, 1, ff), F32),
            pltpu.VMEM((2, n, rows, 1, cols - ff), F32),
            pltpu.SemaphoreType.DMA((6, n)),
        ],
        compiler_params=params(16),
        cost_estimate=cost(0, 12 * n * rows * cols),
    )(*operands)


def qkv_out_kernel(ids, *refs):
    srcs, out, rows, wide, od, sem = refs[:4], *refs[4:]
    c, s = ids[0], ids[1]
    _, _, half, cols = rows.shape
    width = cols // 3

    def reads(a, b):
        return [
            pltpu.make_async_copy(
                src.at[p, pl.ds(0, half), :],
                rows.at[i, jnp.bitwise_xor(p if i else ((p & 1) << 1) | (p >> 1), s)],
                sem.at[0, i * QUAD + p],
            )
            for i, src in enumerate((a, b))
            for p in range(QUAD)
        ]

    @pl.when(c == 0)
    def _():
        for m in reads(srcs[0], srcs[1]):
            m.start()

    @pl.when(c != 0)
    def _():
        for m in reads(srcs[2], srcs[3]):
            m.start()

    for m in reads(srcs[0], srcs[1]):
        m.wait()
    step = half // 2
    moves = []
    for b in range(4):
        if b >= 2:
            moves[b - 2].wait()
        for t in range(QUAD):
            v = rows[b // 2, t, (b % 2) * step : (b % 2 + 1) * step, :].astype(F32)
            for i in range(3):
                lo = (i * QUAD + t) * width
                wide[:, lo : lo + width] = v[:, i * width : (i + 1) * width]
        od[b % 2, :, 0, :] = wide[...]
        n = step - (b == 3)
        m = pltpu.make_async_copy(
            od.at[b % 2, pl.ds(0, n)], out.at[pl.ds(b * step, n)], sem.at[1, b % 2]
        )
        m.start()
        moves.append(m)
    for m in moves[-2:]:
        m.wait()


def qkv_out(ids, srcs, cc):
    cols = srcs[0].shape[-1]
    half = (cc + 1) // 2
    return pl.pallas_call(
        qkv_out_kernel,
        in_specs=[SMEM] + [HBM] * 4,
        out_specs=HBM,
        out_shape=jax.ShapeDtypeStruct((cc, 1, QUAD * cols), F32),
        scratch_shapes=[
            pltpu.VMEM((2, QUAD, half, cols), BF16),
            pltpu.VMEM((half // 2, QUAD * cols), F32),
            pltpu.VMEM((2, half // 2, 1, QUAD * cols), F32),
            pltpu.SemaphoreType.DMA((2, 2 * QUAD)),
        ],
        compiler_params=params(18),
        cost_estimate=cost(0, 6 * cc * QUAD * cols),
    )(ids, *srcs)


def vectors_kernel(count, ids, *refs):
    srcs, outs, (rows, heads, sem) = refs[:4], refs[4:-3], refs[-3:]
    c, s = ids[0], ids[1]
    _, _, tall, row_len = rows.shape
    top = srcs[0].shape[1] - tall

    def reads(pair):
        return [
            pltpu.make_async_copy(v.at[p, pl.ds(top, tall), :], rows.at[i, p], sem.at[i * QUAD + p])
            for i, v in enumerate(pair)
            for p in range(QUAD)
        ]

    for core in range(2):

        @pl.when(c == core)
        def _():
            for m in reads(srcs[2 * core : 2 * core + 2]):
                m.start()

    for m in reads(srcs[:2]):
        m.wait()
    total = jnp.zeros((tall, row_len), F32)
    for i in range(2):
        for p in range(QUAD):
            total = total + rows[i, p].astype(F32)
    at = 0
    for o in outs[:5]:
        n = o.shape[1]
        for lo in range(0, n, row_len):
            size = min(row_len, n - lo)
            o[0:1, lo : lo + size] = total[at : at + 1, :size]
            at += 1
    heads[...] = jnp.zeros_like(heads)
    for i in range(2):
        for p in range(QUAD):
            k = p if i else ((p & 1) << 1) | (p >> 1)
            heads[jnp.bitwise_xor(k, s)] += rows[i, p, at : at + 8, :].astype(F32)
    width = row_len // 3
    for part in range(2):
        for t in range(QUAD):
            lo = (part * QUAD + t) * width
            outs[5][0:1, lo : lo + width] = heads[t, 0:1, part * width : (part + 1) * width]
    outs[6][0:1, :] = jnp.sqrt(total[at + 1 : at + 2, : outs[6].shape[1]] / count)


def vectors_out(ids, srcs, count, cc, ff, model):
    row_len = srcs[0].shape[-1]
    shapes = [ff, cc, cc, cc, cc, 2 * model, 128]
    return pl.pallas_call(
        functools.partial(vectors_kernel, count),
        in_specs=[SMEM] + [HBM] * 4,
        out_specs=[VMEM] * 7,
        out_shape=[jax.ShapeDtypeStruct((1, n), F32) for n in shapes],
        scratch_shapes=[
            pltpu.VMEM((2, QUAD, 32, row_len), BF16),
            pltpu.VMEM((QUAD, 8, row_len), F32),
            pltpu.SemaphoreType.DMA((2 * QUAD,)),
        ],
        compiler_params=params(8),
        cost_estimate=cost(0, 1 << 19),
    )(ids, *srcs)


def to_first(v):
    pairs = [(i, i ^ 1) for i in range(QUAD)] + [(QUAD + i, QUAD + (i ^ 2)) for i in range(QUAD)]
    return lax.ppermute(v, ("section", "seq"), pairs)


def to_second(v):
    pairs = [(i, i ^ 2) for i in range(QUAD)] + [(QUAD + i, QUAD + (i ^ 1)) for i in range(QUAD)]
    return lax.ppermute(v, ("section", "seq"), pairs)


def to_quad(v, k):
    return lax.ppermute(v, "seq", [(i, i ^ k) for i in range(QUAD)])


def to_core(v):
    return lax.ppermute(v, "section", [(0, 1), (1, 0)])


def dp_partner(v, step):
    n = lax.axis_size("dp")
    return lax.ppermute(v, "dp", [(i, i ^ step) for i in range(n)])


def to_owner(l, v):
    return lax.ppermute(v, "section", [(1 - l, l)])


def tied(*v):
    return lax.optimization_barrier(v)


class Order:
    def __init__(self, token):
        self.token = token

    def wait(self, *v):
        *v, self.token = lax.optimization_barrier((*v, self.token))
        return v

    def run(self, step, *operands):
        out = step(*self.wait(*operands))
        out, self.token = lax.optimization_barrier((out, self.token))
        return out


class DpSum:
    def __init__(self, order_of, make, *operands):
        self.value = None
        self.steps = self.work(order_of, make, operands)

    def go(self):
        next(self.steps, None)

    def finish(self):
        for _ in self.steps:
            pass
        return self.value

    def work(self, order_of, make, operands):
        n = lax.axis_size("dp")
        z = lax.axis_index("dp")

        def split(v, step):
            left = v.shape[0] // n * step if v.ndim == 2 else v.shape[1]
            v = v.reshape(n // (2 * step), 2, left, v.shape[-1])
            low = (z & step) == 0
            return jnp.where(low, v[:, 1], v[:, 0]), jnp.where(low, v[:, 0], v[:, 1])

        def join(v, got, step):
            low = (z & step) == 0
            both = jnp.where(low, jnp.stack([v, got], 1), jnp.stack([got, v], 1))
            return both.reshape(-1, *v.shape[1:])

        away, keep = order_of.run(lambda *v: split(make(*v), 1), *operands)
        step = 1
        while step < n:
            got = dp_partner(away, step)
            yield
            step *= 2
            if step < n:
                away, keep = order_of.run(lambda a, b, s=step: split(add_low(a, b), s), keep, got)
            else:
                v = order_of.run(add_low, keep, got)
        while step > 1:
            step //= 2
            got = dp_partner(v, step)
            yield
            v = order_of.run(functools.partial(join, step=step), v, got)
        self.value = v.reshape(-1, v.shape[-1])


def add_low(a, b):
    return (a.astype(F32) + b.astype(F32)).astype(BF16)


def quad_gather(own):
    one = to_second(own)
    two = to_first(own)
    three = to_first(one)
    return [own, one, two, three]


def on_device(
    layer_in, cotangent, lengths, w_qkv, bias_qv, w_out, bias_out,
    gain_attn, gain_mlp, w_up, bias_up, w_down, bias_down,
):
    micro, _, span, cc = layer_in.shape
    model = w_out.shape[1]
    ff = w_up.shape[-1]
    hd = model // HEADS
    width = model // QUAD
    heads = width // hd
    c = lax.axis_index("section")
    s = lax.axis_index("seq")
    dp_count = lax.axis_size("dp")
    mine = c == 0

    lens = lax.dynamic_index_in_dim(lengths, c, 0, keepdims=False)[0]
    e0 = lens[0]
    e1 = e0 + lens[1]
    e2 = e1 + lens[2]
    e3 = e2 + lens[3]
    ids = jnp.stack([c, s, e0, e1, e2, e3, c, s]).astype(jnp.int32)
    cs = jnp.stack([c, s]).astype(jnp.int32)
    x = rows_in(cs, layer_in)

    def row(v, n=ff):
        return jnp.pad(v, ((0, 0), (0, n - v.shape[-1])))

    qb = lax.dynamic_slice_in_dim(bias_qv, s * width, width, 1)
    vb = lax.dynamic_slice_in_dim(bias_qv, model + s * width, width, 1)
    heads_bias = jnp.concatenate([qb, jnp.zeros((1, width), F32), vb], 1)
    pv_own = jnp.concatenate(
        [row(v) for v in (bias_up, bias_out, bias_down, gain_attn, gain_mlp, heads_bias)]
        + [jnp.zeros((2, ff), F32)]
    )
    w3_own = jnp.concatenate(
        [lax.dynamic_slice_in_dim(w_qkv[0], i * model + s * width, width, 1) for i in range(3)], 1
    )
    pv_got = to_core(pv_own)
    w3_got = to_core(w3_own)
    wo_got = to_core(w_out[0])
    up = (w_up, to_core(w_up))
    dn = (w_down, to_core(w_down))
    pv = [jnp.where(mine, pv_own, pv_got), jnp.where(mine, pv_got, pv_own)]
    w3 = [jnp.where(mine, w3_own, w3_got), jnp.where(mine, w3_got, w3_own)]
    wo = [jnp.where(mine, w_out[0], wo_got), jnp.where(mine, wo_got, w_out[0])]

    normed = x
    saved = []
    squares = []
    for l in range(2):
        blocks = quad_gather(normed)
        if l == 1:
            blocks, df = tied(blocks, rows_in(cs, cotangent))
        qh, kh, vh, lse, blocks, *att = attn_fwd(l == 0, ids, blocks, w3[l], pv[l], heads, hd)
        att = [att[0]] + [to_quad(att[k], k) for k in (1, 2, 3)]
        mid, u, xout, normed, sq, astk = mlp_fwd(
            l, ids, x, att, wo[l], pv[l], pv[min(l + 1, 1)], up, dn
        )
        saved.append((x, blocks, (qh, kh, vh, lse), astk, mid, u))
        squares.append(sq[0, 0])
        x = xout
    outs = [saved[1][0], x]

    order_of = Order(ids)
    run = order_of.run

    def first_part(l, df):
        lr, rr, dmid, g, *douts = run(
            lambda v: mlp_bwd(l, ids, v, saved[l][5], saved[l][4], wo[l], pv[l], up, dn), df
        )
        return lr, rr, dmid, g, [douts[0]] + [to_quad(douts[k], k) for k in (1, 2, 3)]

    def send(l, places, lr, rr):
        return run(lambda a, b: product(True, places, ids, a, b, saved[l][3]), lr, rr)

    def keep(l, places, lr, rr, got):
        return run(lambda a, b, v: product(False, places, ids, a, b, saved[l][3], v), lr, rr, got)

    def attention(l, douts):
        outs = run(lambda *v: attn_bwd(ids, saved[l][1], w3[l], saved[l][2], v), *douts)
        return (*outs, to_first(outs[2]), to_core(outs[3]))

    def input_part(l, p0, pr, q, dmid):
        return run(lambda *v: input_grad_of(*v, saved[l][0], pv[l]), p0, pr, q, dmid)

    def projection(l, gk, gs_got, g, gb, gg):
        heads_sum = jnp.concatenate([gb[0, :width], gb[0, 2 * width :]])
        row_len = 3 * width
        vectors = [
            g[0], g[1, :cc], g[2, :cc], gg[0, :cc], g[4, :cc], heads_sum,
            jnp.broadcast_to(squares[l], (row_len,)),
        ]
        v = [jnp.pad(x, (0, -x.shape[0] % row_len)) for x in vectors]
        v = jnp.concatenate(v).reshape(-1, row_len)
        v = jnp.pad(v, ((0, 32 - v.shape[0]), (0, 0))).astype(BF16)
        return jnp.concatenate([add_low(gk, gs_got), v])

    def wait(*v):
        out = order_of.wait(*v)
        return out[0] if len(out) == 1 else out

    def pair_up(a, b):
        return jnp.stack([a, b])

    def add_first(a, b):
        return add_low(a, b[:span])

    lr1, rr1, dmid1, g1, douts1 = first_part(1, df)

    far1 = to_core(send(1, (3, 2), lr1, rr1))
    douts1 = wait(*douts1)
    near1 = send(1, (1, 0), lr1, rr1)
    far1 = wait(far1)

    far1 = keep(1, (3, 2), lr1, rr1, far1)
    x1a, near1 = to_first(far1[0]), to_core(near1)
    p0, p1, _, _, gk1, gb1, pr, gs_got = attention(1, douts1)
    x1a, near1 = wait(x1a, near1)

    out_got = to_core(run(lambda a, b: jnp.where(mine, a, b), outs[1], outs[0]))
    near1 = keep(1, (1, 0), lr1, rr1, near1)
    half1 = run(add_low, near1[0], x1a)
    pr, gs_got, out_got = wait(pr, gs_got, out_got)

    q = to_second(run(add_first, p1, pr))
    q = wait(q)

    x1b, half1 = wait(far1[1], half1)
    x1b, x2 = to_first(x1b), to_second(half1)
    dx1, gg1 = input_part(1, p0, pr, q, dmid1)
    qkv_sum1 = DpSum(order_of, functools.partial(projection, 1), gk1, gs_got, g1, gb1, gg1)
    lr0, rr0, dmid0, g0, douts0 = first_part(0, dx1)
    far0 = to_core(send(0, (3, 2), lr0, rr0))
    near0 = send(0, (1, 0), lr0, rr0)
    x1b, x2 = wait(x1b, x2)

    sum1 = DpSum(order_of, lambda a, b, d: add_low(add_low(a, b), d), near1[1], x1b, x2)
    sum1.go()
    far0, *douts0 = wait(far0, *douts0)

    far0 = keep(0, (3, 2), lr0, rr0, far0)
    x1a, near0 = to_first(far0[0]), to_core(near0)
    p0, p1, _, _, gk0, gb0, pr, gs_got = attention(0, douts0)
    x1a, near0 = wait(x1a, near0)

    sum1.go()
    near0 = keep(0, (1, 0), lr0, rr0, near0)
    half1 = run(add_low, near0[0], x1a)
    qkv_sum1.go()
    pr, gs_got = wait(pr, gs_got)

    q = to_second(run(add_first, p1, pr))
    q = wait(q)

    x1b = to_first(wait(far0[1]))
    dx0, gg0 = input_part(0, p0, pr, q, dmid0)
    qkv_sum1.go()
    sum1.go()
    x1b, half1 = wait(x1b, half1)

    x2 = to_second(half1)
    sum1.go()
    half0 = run(add_low, near0[1], x1b)
    qkv_sum0 = DpSum(order_of, functools.partial(projection, 0), gk0, gs_got, g0, gb0, gg0)
    qkv_sum0.go()
    qkv_sum1.go()
    x2 = wait(x2)
    own1 = sum1.finish()

    have1 = [own1, to_second(own1), to_first(own1)]
    sum0 = DpSum(order_of, add_low, half0, x2)
    sum0.go()
    qkv_sum1.go()
    qkv_sum0.go()
    sum0.go()
    have1[1], have1[2] = wait(have1[1], have1[2])

    have1.append(to_first(have1[1]))
    qkv_own1 = qkv_sum1.finish()
    qkv_sum0.go()
    got1 = [to_owner(1, own1)]
    sum0.go()
    have1[3], got1[0] = wait(have1[3], got1[0])

    qkv_next1 = to_second(qkv_own1)
    got1.append(to_owner(1, have1[1]))
    qkv_sum0.go()
    qkv_next1, got1[1] = wait(qkv_next1, got1[1])
    qkv_pair1 = run(pair_up, qkv_own1, qkv_next1)
    sum0.go()

    qkv_rest1 = to_first(qkv_pair1)
    got1.append(to_owner(1, have1[2]))
    qkv_own0 = qkv_sum0.finish()
    qkv_next0 = to_second(qkv_own0)
    qkv_rest1, got1[2], qkv_next0 = wait(qkv_rest1, got1[2], qkv_next0)

    own0 = sum0.finish()
    have0 = [own0, to_second(own0), to_first(own0)]
    got1.append(to_owner(1, have1[3]))
    qkv_pair0 = run(pair_up, qkv_own0, qkv_next0)
    qkv_rest0 = to_first(qkv_pair0)
    got1[3] = wait(got1[3])
    got0 = [to_owner(0, own0)]
    in_got = to_core(run(lambda a, b: jnp.where(mine, a, b), dx1, dx0))
    qkv1 = run(lambda a, b: jnp.concatenate([a, b]), qkv_pair1, qkv_rest1)
    layer_out = run(
        lambda a, b, d: rows_out(ids, jnp.where(mine, a, b), d), outs[0], outs[1], out_got
    )
    got0[0], in_got = wait(got0[0], in_got)

    def place(places, outs_w):
        srcs = [v[p] for p in places for v in (have0, got0, got1, have1)]
        n = len(srcs)
        return run(
            lambda *v: place_rows(places, ids, v[:n], v[n:] or None, cc, ff, model), *srcs, *outs_w
        )

    outs_w = place((0,), ())
    input_grad = run(lambda a, b, d: rows_out(ids, jnp.where(mine, a, b), d), dx0, dx1, in_got)
    have0[1], have0[2], qkv_rest0 = wait(have0[1], have0[2], qkv_rest0)

    have0.append(to_first(have0[1]))
    qkv0 = run(lambda a, b: jnp.concatenate([a, b]), qkv_pair0, qkv_rest0)
    have0[1], have0[2] = wait(have0[1], have0[2])
    got0.append(to_owner(0, have0[1]))
    qkv0_got, qkv1_got = to_owner(0, qkv0), to_owner(1, qkv1)
    got0[1] = wait(got0[1])
    outs_w = place((1,), outs_w)
    got0.append(to_owner(0, wait(have0[2])))
    qkv0_got, qkv1_got = wait(qkv0_got, qkv1_got)
    grad_qkv = run(lambda *v: qkv_out(ids, v, cc), qkv0, qkv0_got, qkv1_got, qkv1)
    count = micro * dp_count * span * QUAD
    vectors = run(
        lambda *v: vectors_out(ids, v, count, cc, ff, model), qkv0, qkv0_got, qkv1_got, qkv1
    )
    have0[3], got0[2] = wait(have0[3], got0[2])

    got0.append(to_owner(0, have0[3]))
    outs_w = place((2,), outs_w)
    got0[3] = wait(got0[3])
    grad_down, grad_up, grad_out = place_rows(
        (3,), order_of.token, [v[3] for v in (have0, got0, got1, have1)], outs_w, cc, ff, model
    )

    grad_bup, grad_bout, grad_bdown, grad_ga, grad_gm, grad_bqv, rms = vectors
    return (
        layer_out,
        input_grad,
        jnp.transpose(grad_qkv, (1, 0, 2)),
        grad_bqv,
        jnp.transpose(grad_out, (1, 2, 0)),
        grad_bout,
        grad_ga,
        grad_gm,
        jnp.transpose(grad_up, (1, 0, 2)),
        grad_bup,
        jnp.transpose(grad_down, (1, 2, 0)),
        grad_bdown,
        rms[0, :1],
    )


def solution(mesh):
    two = P("section", None)
    three = P("section", None, None)
    tokens = P(None, "dp", "seq", None)
    stacked = P("section", None, "dp", "seq", None)
    return jax.shard_map(
        on_device,
        mesh=mesh,
        in_specs=(
            tokens, tokens, P(None, "dp", None), three, two, three, two, two, two, three, two, three, two,
        ),
        out_specs=(
            stacked, stacked, three, two, three, two, two, two, three, two, three, two, P("section"),
        ),
        check_vma=False,
    )
```

```python
import functools

import jax
import jax.numpy as jnp
from jax import lax
from jax.experimental import pallas as pl
from jax.experimental.pallas import tpu as pltpu
from jax.sharding import PartitionSpec as P

HEADS = 12
EPS = 1e-6
NEG = -1e30
F32 = jnp.float32
BF16 = jnp.bfloat16
MIB = 1 << 20
QUAD = 4


def nn(a, b):
    return lax.dot_general(a, b, (((1,), (0,)), ((), ())), preferred_element_type=F32)


def nt(a, b):
    return lax.dot_general(a, b, (((1,), (1,)), ((), ())), preferred_element_type=F32)


def tn(a, b):
    return lax.dot_general(a, b, (((0,), (0,)), ((), ())), preferred_element_type=F32)


def order(core, k):
    return jnp.where(core == 1, k, ((k & 1) << 1) | (k >> 1))


def crms_scale(v):
    sq = jnp.sum(v * v, axis=-1, keepdims=True)
    su = jnp.sum(v, axis=-1, keepdims=True)
    full = v.shape[-1] + 1
    return lax.rsqrt((sq + su * su) / full + EPS), su, (sq + su * su) / full


def crms_back(v, gain, grad):
    r, su, _ = crms_scale(v)
    gd = grad * gain
    w = jnp.sum(gd * v, axis=-1, keepdims=True)
    unit = v * r
    dv = gd * r - (w * r * r * r / (v.shape[-1] + 1)) * (v + su)
    return dv, grad * unit, unit * gain


GC = 0.7978845608028654


def gelu_parts(u):
    inner = GC * (u + 0.044715 * (u * u * u))
    th = jnp.tanh(inner)
    return th


def params(mib, **kw):
    return pltpu.CompilerParams(vmem_limit_bytes=mib * MIB, **kw)


def cost(flops, nbytes, trans=0):
    return pl.CostEstimate(
        flops=int(2 * flops), bytes_accessed=int(2 * nbytes), transcendentals=int(2 * trans)
    )


SMEM = pl.BlockSpec(memory_space=pltpu.SMEM)
VMEM = pl.BlockSpec(memory_space=pltpu.VMEM)
HBM = pl.BlockSpec(memory_space=pltpu.HBM)


def rows_in_kernel(ids, v, o):
    @pl.when(ids[0] == 0)
    def _():
        o[...] = v[:, 0, :].T

    @pl.when(ids[0] != 0)
    def _():
        o[...] = v[:, 1, :].T


def rows_in(ids, v):
    micro, _, span, cc = v.shape
    return pl.pallas_call(
        rows_in_kernel,
        in_specs=[SMEM, VMEM],
        out_specs=VMEM,
        out_shape=jax.ShapeDtypeStruct((span, cc), BF16),
        compiler_params=params(16),
        cost_estimate=cost(0, 6 * span * cc),
    )(ids, jnp.transpose(v[:, 0], (2, 0, 1)))


def rows_out_kernel(ids, own, got, o):
    @pl.when(ids[0] == 0)
    def _():
        o[:, 0, :] = own[...].T
        o[:, 1, :] = got[...].T

    @pl.when(ids[0] != 0)
    def _():
        o[:, 0, :] = got[...].T
        o[:, 1, :] = own[...].T


def rows_out(ids, own, got):
    span, cc = own.shape
    o = pl.pallas_call(
        rows_out_kernel,
        in_specs=[SMEM, VMEM, VMEM],
        out_specs=VMEM,
        out_shape=jax.ShapeDtypeStruct((cc, 2, span), BF16),
        compiler_params=params(16),
        cost_estimate=cost(0, 8 * span * cc),
    )(ids, own, got)
    return jnp.transpose(o, (1, 2, 0))[None, :, None]


def visible_bias(ids, n, t, span):
    i = t * span + lax.broadcasted_iota(jnp.int32, (1, span), 1)
    start = jnp.zeros((1, span), jnp.int32)
    for d in range(4):
        end = ids[2 + d]
        start = jnp.maximum(start, jnp.where(i >= end, end, 0))
    j = lax.broadcasted_iota(jnp.int32, (n, span), 0)
    return jnp.where((j >= start) & (j <= i), 0.0, NEG)


def attn_fwd_kernel(
    raw, ids, n0, n1, n2, n3, w_ref, pv_ref, q_hbm, k_hbm, v_hbm, l_hbm, n_hbm,
    a0, a1, a2, a3, qh, kh, vh, lse, nb_scr, at, bias_scr, sem,
):
    c, s = ids[0], ids[1]
    heads, _, hd = qh.shape
    span, cc = n0.shape
    width = heads * hd
    bias = pv_ref[5:6, : 3 * width]
    for p, nb in enumerate((n0, n1, n2, n3)):
        t = jnp.bitwise_xor(order(c, p), s)
        row = pl.multiple_of(t * span, span)
        rows = nb[...]
        if raw:
            v = rows.astype(F32)
            rows = (v * crms_scale(v)[0] * pv_ref[3:4, :cc]).astype(BF16)
            nb_scr[p] = rows
        y = nn(rows, w_ref[...]) + bias
        for h in range(heads):
            lo = h * hd
            qh[h, pl.ds(row, span), :] = (y[:, lo : lo + hd] * (hd**-0.5)).astype(BF16)
            kh[h, pl.ds(row, span), :] = y[:, width + lo : width + lo + hd].astype(BF16)
            vh[h, pl.ds(row, span), :] = y[:, 2 * width + lo : 2 * width + lo + hd].astype(BF16)
    moves = [
        pltpu.make_async_copy(src, dst, sem.at[i])
        for i, (src, dst) in enumerate(
            [(qh, q_hbm), (kh, k_hbm), (vh, v_hbm), (lse, l_hbm)]
            + [(nb_scr.at[p] if raw else nb, n_hbm.at[p]) for p, nb in enumerate((n0, n1, n2, n3))]
        )
    ]
    for i, m in enumerate(moves):
        if i != 3:
            m.start()
    for t in range(QUAD):
        n = span * (t + 1)
        bias_scr[:n, :] = visible_bias(ids, n, t, span)

        def head(h, carry, t=t, n=n):
            q = qh[h, t * span : (t + 1) * span, :]
            sc = nt(kh[h, :n, :], q) + bias_scr[:n, :]
            m = jnp.max(sc, axis=0, keepdims=True)
            e = jnp.exp(sc - m)
            tot = jnp.sum(e, axis=0, keepdims=True)
            pr = (e * (1.0 / tot)).astype(BF16)
            o = tn(vh[h, :n, :], pr)
            at[t, pl.ds(pl.multiple_of(h * hd, hd), hd), :] = o.astype(BF16)
            lse[h, t : t + 1, :] = m + jnp.log(tot)
            return carry

        lax.fori_loop(0, heads, head, 0)
    moves[3].start()
    for k, a in enumerate((a0, a1, a2, a3)):
        a[...] = at[jnp.bitwise_xor(s, k)]
    for m in moves:
        m.wait()


def attn_fwd(raw, ids, blocks, w3, pv, heads, hd):
    span, width = blocks[0].shape
    full = span * QUAD
    hh = jax.ShapeDtypeStruct((heads, full, hd), BF16)
    aa = jax.ShapeDtypeStruct((heads * hd, span), BF16)
    saved = [hh, hh, hh, jax.ShapeDtypeStruct((heads, QUAD, span), F32)]
    nb = jax.ShapeDtypeStruct((QUAD, span, width), BF16)
    return pl.pallas_call(
        functools.partial(attn_fwd_kernel, raw),
        in_specs=[SMEM] + [VMEM] * 6,
        out_specs=[HBM] * 5 + [VMEM] * 4,
        out_shape=[*saved, nb, aa, aa, aa, aa],
        scratch_shapes=[pltpu.VMEM(v.shape, v.dtype) for v in saved]
        + [
            pltpu.VMEM(nb.shape if raw else (1, 8, 128), BF16),
            pltpu.VMEM((QUAD, heads * hd, span), BF16),
            pltpu.VMEM((full, span), F32),
            pltpu.SemaphoreType.DMA((8,)),
        ],
        compiler_params=params(15),
        cost_estimate=cost(
            2 * full * width * 3 * heads * hd + 3 * 4 * full * full * hd * heads,
            4 * full * width,
            heads * full * full,
        ),
    )(ids, *blocks, w3, pv)


def mlp_fwd_kernel(
    layer, ids, x, a0, a1, a2, a3, wo, pv, pvn, pvb, upo, upr, dno, dnr,
    mid, u, xout, nnext, sq, astk, nm, acc,
):
    j = pl.program_id(0)
    c, s = ids[0], ids[1]
    cc = x.shape[-1]
    own = c == layer

    @pl.when(j == 0)
    def _():
        rows = a0.shape[0]
        m = x[...].astype(F32) + pv[1:2, :cc]
        for k, a in enumerate((a0, a1, a2, a3)):
            row = pl.multiple_of(jnp.bitwise_xor(s, k) * rows, rows)
            m = m + tn(a[...], wo[pl.ds(row, rows), :])
            astk[jnp.bitwise_xor(s, k)] = a[...].T
        mid[...] = m
        r, _, _ = crms_scale(m)
        nm[...] = (m * r * pv[4:5, :cc]).astype(BF16)
        acc[...] = m + pv[2:3, :cc]

    wu = lax.select(own, upo[0], upr[0])
    wd = lax.select(own, dno[0], dnr[0])
    ub = nn(nm[...], wu) + pvb[0:1, :]
    u[...] = ub
    act = (0.5 * ub * (1.0 + gelu_parts(ub))).astype(BF16)
    acc[...] += nn(act, wd)

    @pl.when(j == pl.num_programs(0) - 1)
    def _():
        fin = acc[...]
        _, _, ms = crms_scale(fin)
        sq[...] = jnp.broadcast_to(jnp.sum(ms, axis=0, keepdims=True), sq.shape)
        low = fin.astype(BF16)
        xout[...] = low
        lf = low.astype(F32)
        r, _, _ = crms_scale(lf)
        nnext[...] = (lf * r * pvn[3:4, :cc]).astype(BF16)


def mlp_fwd(layer, ids, x, att, wo, pv, pvn, up, dn):
    span, cc = x.shape
    ff = up[0].shape[-1]
    fb = ff // 4
    rows = att[0].shape[0]

    def whole(shape):
        return pl.BlockSpec(shape, lambda j, ids: (0,) * len(shape))

    def pick(mine):
        return lambda j, ids: jnp.where((ids[0] == layer) == mine, j, 0)

    mine, other = pick(True), pick(False)
    grid = pltpu.PrefetchScalarGridSpec(
        num_scalar_prefetch=1,
        grid=(4,),
        in_specs=[whole((span, cc))]
        + [whole((rows, span))] * 4
        + [whole(wo.shape), whole(pv.shape), whole(pvn.shape)]
        + [
            pl.BlockSpec((8, fb), lambda j, ids: (0, j)),
            pl.BlockSpec((1, cc, fb), lambda j, ids: (0, 0, mine(j, ids))),
            pl.BlockSpec((1, cc, fb), lambda j, ids: (0, 0, other(j, ids))),
            pl.BlockSpec((1, fb, cc), lambda j, ids: (0, mine(j, ids), 0)),
            pl.BlockSpec((1, fb, cc), lambda j, ids: (0, other(j, ids), 0)),
        ],
        out_specs=[
            whole((span, cc)),
            pl.BlockSpec((span, fb), lambda j, ids: (0, j)),
            whole((span, cc)),
            whole((span, cc)),
            whole((8, 128)),
            whole((QUAD, span, rows)),
        ],
        scratch_shapes=[pltpu.VMEM((span, cc), BF16), pltpu.VMEM((span, cc), F32)],
    )
    return pl.pallas_call(
        functools.partial(mlp_fwd_kernel, layer),
        grid_spec=grid,
        out_shape=[
            jax.ShapeDtypeStruct((span, cc), F32),
            jax.ShapeDtypeStruct((span, ff), F32),
            jax.ShapeDtypeStruct((span, cc), BF16),
            jax.ShapeDtypeStruct((span, cc), BF16),
            jax.ShapeDtypeStruct((8, 128), F32),
            jax.ShapeDtypeStruct((QUAD, span, rows), BF16),
        ],
        compiler_params=params(23, dimension_semantics=("arbitrary",)),
        cost_estimate=cost(6 * span * cc * ff, 4 * cc * ff + 4 * span * ff, span * ff),
    )(ids, x, *att, wo, pv, pvn, pv, up[0], up[1], dn[0], dn[1])


def mlp_bwd_kernel(
    layer, ids, df, u, mid, wo, pv, upo, upr, dno, dnr,
    lr, rr, dmid, g, d0, d1, d2, d3, acc, wide,
):
    j = pl.program_id(0)
    c, s = ids[0], ids[1]
    cc = df.shape[-1]
    fb = u.shape[-1]
    own = c == layer

    @pl.when(j == 0)
    def _():
        acc[...] = jnp.zeros_like(acc)
        g[...] = jnp.zeros_like(g)

    wu = lax.select(own, upo[0], upr[0])
    wd = lax.select(own, dno[0], dnr[0])
    da = nt(df[...], wd)
    ub = u[...]
    th = gelu_parts(ub)
    half = 0.5 * (1.0 + th)
    lr[0] = (ub * half).astype(BF16)
    slope = half + 0.5 * ub * (1.0 - th * th) * (GC * (1.0 + 3 * 0.044715 * (ub * ub)))
    du = (slope * da).astype(BF16)
    lr[1] = du
    g[0:1, pl.ds(pl.multiple_of(j * fb, 128), fb)] = jnp.sum(du.astype(F32), axis=0, keepdims=True)
    acc[...] += nt(du, wu)

    @pl.when(j == pl.num_programs(0) - 1)
    def _():
        dff = df[...].astype(F32)
        dv, gg, nm = crms_back(mid[...], pv[4:5, :cc], acc[...])
        dm = dff + dv
        low = dm.astype(BF16)
        dmid[...] = dm
        quarter = rr.shape[-1]
        wide[:, cc:] = jnp.zeros((wide.shape[0], wide.shape[1] - cc), BF16)
        for i, v in enumerate((df[...], nm.astype(BF16), low)):
            wide[:, :cc] = v
            for t in range(QUAD):
                rr[i, t] = wide[:, t * quarter : (t + 1) * quarter]
        g[1:2, :cc] = jnp.sum(low.astype(F32), axis=0, keepdims=True)
        g[2:3, :cc] = jnp.sum(dff, axis=0, keepdims=True)
        g[4:5, :cc] = jnp.sum(gg, axis=0, keepdims=True)
        rows = d0.shape[0]
        for k, d in enumerate((d0, d1, d2, d3)):
            row = pl.multiple_of(jnp.bitwise_xor(s, k) * rows, rows)
            d[...] = nt(wo[pl.ds(row, rows), :], low).astype(BF16)


def mlp_bwd(layer, ids, df, u, mid, wo, pv, up, dn):
    span, cc = df.shape
    ff = u.shape[-1]
    fb = ff // 4
    rows = wo.shape[0] // QUAD

    def whole(shape):
        return pl.BlockSpec(shape, lambda j, ids: (0,) * len(shape))

    def pick(mine):
        return lambda j, ids: jnp.where((ids[0] == layer) == mine, j, 0)

    mine, other = pick(True), pick(False)
    grid = pltpu.PrefetchScalarGridSpec(
        num_scalar_prefetch=1,
        grid=(4,),
        in_specs=[
            whole((span, cc)),
            pl.BlockSpec((span, fb), lambda j, ids: (0, j)),
            whole((span, cc)),
            whole(wo.shape),
            whole(pv.shape),
            pl.BlockSpec((1, cc, fb), lambda j, ids: (0, 0, mine(j, ids))),
            pl.BlockSpec((1, cc, fb), lambda j, ids: (0, 0, other(j, ids))),
            pl.BlockSpec((1, fb, cc), lambda j, ids: (0, mine(j, ids), 0)),
            pl.BlockSpec((1, fb, cc), lambda j, ids: (0, other(j, ids), 0)),
        ],
        out_specs=[
            pl.BlockSpec((2, span, fb), lambda j, ids: (0, 0, j)),
            whole((3, QUAD, span, (cc + 1) // QUAD)),
            whole((span, cc)),
            whole((8, ff)),
        ]
        + [whole((rows, span))] * 4,
        scratch_shapes=[pltpu.VMEM((span, cc), F32), pltpu.VMEM((span, cc + 1), BF16)],
    )
    dd = jax.ShapeDtypeStruct((rows, span), BF16)
    return pl.pallas_call(
        functools.partial(mlp_bwd_kernel, layer),
        grid_spec=grid,
        out_shape=[
            jax.ShapeDtypeStruct((2, span, ff), BF16),
            jax.ShapeDtypeStruct((3, QUAD, span, (cc + 1) // QUAD), BF16),
            jax.ShapeDtypeStruct((span, cc), F32),
            jax.ShapeDtypeStruct((8, ff), F32),
            dd, dd, dd, dd,
        ],
        compiler_params=params(23, dimension_semantics=("arbitrary",)),
        cost_estimate=cost(6 * span * cc * ff, 4 * cc * ff + 8 * span * ff, span * ff),
    )(ids, df, u, mid, wo, pv, up[0], up[1], dn[0], dn[1])


def product_kernel(send, places, ids, lr, rr, att, *rest):
    outs = [rest[0].at[i] for i in range(len(places))] if send else rest[1:]
    core = 1 - ids[0] if send else ids[0]
    ff = lr.shape[-1]
    part = att.shape[-1]
    for i, place in enumerate(places):
        t = jnp.bitwise_xor(order(core, place), ids[1])
        out = outs[i]
        main = tn(rr[core, t], lr[core])
        low = rr[2, t]
        sides = [tn(low, att[2 * core + h]) for h in range(2)]
        if not send:
            got = rest[0].at[i]
            main = main + got[:, :ff].astype(F32)
            sides = [v + got[:, ff + h * part : ff + (h + 1) * part].astype(F32) for h, v in enumerate(sides)]
        out[:, :ff] = main.astype(BF16)
        for h, v in enumerate(sides):
            out[:, ff + h * part : ff + (h + 1) * part] = v.astype(BF16)


def product(send, places, ids, lr, rr, att, *got):
    span, quarter = rr.shape[2:]
    cols = lr.shape[-1] + 2 * att.shape[-1]
    return pl.pallas_call(
        functools.partial(product_kernel, send, places),
        in_specs=[SMEM] + [VMEM] * (3 + len(got)),
        out_specs=VMEM if send else [VMEM] * len(places),
        out_shape=jax.ShapeDtypeStruct((len(places), quarter, cols), BF16)
        if send
        else [jax.ShapeDtypeStruct((quarter, cols), BF16)] * len(places),
        compiler_params=params(15),
        cost_estimate=cost(2 * span * quarter * cols * len(places), 2 * 4 * quarter * cols * len(places)),
    )(ids, lr, rr, att, *got)


def attn_bwd_kernel(
    ids, n_hbm, w_hbm, q_hbm, k_hbm, v_hbm, l_hbm, d0, d1, d2, d3,
    p0, p1, far, gs, gk, gb, do, dk, dv, dy, acc, bias_scr,
    nb, w_ref, qh, kh, vh, lse, sem,
):
    c, s = ids[0], ids[1]
    heads, _, hd = qh.shape
    _, span, cc = nb.shape
    width = heads * hd
    moves = [
        pltpu.make_async_copy(src, dst, sem.at[i])
        for i, (src, dst) in enumerate(
            [(q_hbm, qh), (k_hbm, kh), (v_hbm, vh), (l_hbm, lse), (w_hbm, w_ref), (n_hbm, nb)]
        )
    ]
    for m in moves:
        m.start()
    for k, d in enumerate((d0, d1, d2, d3)):
        do[jnp.bitwise_xor(s, k)] = d[...]
    for m in moves[:4]:
        m.wait()
    for t in reversed(range(QUAD)):
        n = span * (t + 1)
        bias_scr[:n, :] = visible_bias(ids, n, t, span)
        for h in range(heads):
            q = qh[h, t * span : (t + 1) * span, :]
            kk = kh[h, :n, :]
            sc = nt(kk, q) + (bias_scr[:n, :] - lse[h, t : t + 1, :])
            pr = jnp.exp(sc)
            dot = do[t, h * hd : (h + 1) * hd, :]
            dp = nn(vh[h, :n, :], dot)
            inner = jnp.sum(pr * dp, axis=0, keepdims=True)
            ds = (pr * (dp - inner)).astype(BF16)
            newk = nn(ds, q)
            newv = nt(pr.astype(BF16), dot)
            if t == QUAD - 1:
                dk[h, :n, :] = newk
                dv[h, :n, :] = newv
            else:
                dk[h, :n, :] += newk
                dv[h, :n, :] += newv
            dq = tn(kk, ds) * (hd**-0.5)
            dy[t * span : (t + 1) * span, h * hd : (h + 1) * hd] = dq.T.astype(BF16)
    for h in range(heads):
        dy[:, width + h * hd : width + (h + 1) * hd] = dk[h].astype(BF16)
        dy[:, 2 * width + h * hd : 2 * width + (h + 1) * hd] = dv[h].astype(BF16)
    for m in moves[4:]:
        m.wait()
    total = jnp.zeros((1, 3 * width), F32)
    for p, out in enumerate((p0, p1, far.at[span:], far.at[:span])):
        row = pl.multiple_of(jnp.bitwise_xor(order(c, p), s) * span, span)
        y = dy[pl.ds(row, span), :]
        out[...] = nt(y, w_ref[...]).astype(BF16)
        total = total + jnp.sum(y.astype(F32), axis=0, keepdims=True)
        g = tn(nb[p], y)
        if p == 0:
            acc[:cc, :] = g
        else:
            acc[:cc, :] += g
    gb[...] = jnp.broadcast_to(total, gb.shape)
    part = gs.shape[0]
    acc[cc:, :] = jnp.zeros((acc.shape[0] - cc, acc.shape[1]), F32)
    gk[...] = acc[pl.ds(pl.multiple_of(c * part, part), part), :].astype(BF16)
    gs[...] = acc[pl.ds(pl.multiple_of((1 - c) * part, part), part), :].astype(BF16)


def attn_bwd(ids, blocks, w3, qkvl, douts):
    _, span, cc = blocks.shape
    heads, full, hd = qkvl[0].shape
    width = heads * hd
    pp = jax.ShapeDtypeStruct((span, cc), BF16)
    gg = jax.ShapeDtypeStruct(((cc + 1) // 2, 3 * width), BF16)
    return pl.pallas_call(
        attn_bwd_kernel,
        in_specs=[SMEM] + [HBM] * 6 + [VMEM] * 4,
        out_specs=[VMEM] * 6,
        out_shape=[pp, pp, jax.ShapeDtypeStruct((2 * span, cc), BF16), gg, gg, jax.ShapeDtypeStruct((8, 3 * width), F32)],
        scratch_shapes=[
            pltpu.VMEM((QUAD, width, span), BF16),
            pltpu.VMEM((heads, full, hd), F32),
            pltpu.VMEM((heads, full, hd), F32),
            pltpu.VMEM((full, 3 * width), BF16),
            pltpu.VMEM((cc + 1, 3 * width), F32),
            pltpu.VMEM((full, span), F32),
            pltpu.VMEM((QUAD, span, cc), BF16),
            pltpu.VMEM(w3.shape, BF16),
            pltpu.VMEM((heads, full, hd), BF16),
            pltpu.VMEM((heads, full, hd), BF16),
            pltpu.VMEM((heads, full, hd), BF16),
            pltpu.VMEM((heads, QUAD, span), F32),
            pltpu.SemaphoreType.DMA((6,)),
        ],
        compiler_params=params(24),
        cost_estimate=cost(
            4 * full * cc * 3 * width + 3 * 10 * full * full * hd * heads,
            8 * full * cc,
            heads * full * full,
        ),
    )(ids, blocks, w3, *qkvl, *douts)


def input_kernel(part, r0, r1, dmid, x, pv, dx, gg):
    cc = x.shape[-1]
    dn = part[...].astype(F32) + r0[part.shape[0] :, :].astype(F32) + r1[...].astype(F32)
    dv, g, _ = crms_back(x[...].astype(F32), pv[3:4, :cc], dn)
    dx[...] = (dmid[...] + dv).astype(BF16)
    gg[...] = jnp.broadcast_to(jnp.sum(g, axis=0, keepdims=True), gg.shape)


def input_grad_of(part, r0, r1, dmid, x, pv):
    return pl.pallas_call(
        input_kernel,
        in_specs=[VMEM] * 6,
        out_specs=[VMEM] * 2,
        out_shape=[
            jax.ShapeDtypeStruct(x.shape, BF16),
            jax.ShapeDtypeStruct((8, x.shape[-1]), F32),
        ],
        compiler_params=params(16),
        cost_estimate=cost(0, x.size * 14),
    )(part, r0, r1, dmid, x, pv)


def both_lengths(t, rows, start):
    @pl.when(t < QUAD - 1)
    def _():
        start(rows)

    @pl.when(t == QUAD - 1)
    def _():
        start(rows - 1)


def place_kernel(places, first, ids, *refs):
    n = len(places)
    srcs = refs[: 4 * n]
    refs = refs[4 * n :]
    outs = refs[:3] if first else refs[3:6]
    x0, x1, od, ou, ow, sem = refs[3:] if first else refs[6:]
    c, s = ids[0], ids[1]
    down, up, wout = outs
    _, rows, _, ff = od.shape
    part = ow.shape[-1]

    def reads(i, j):
        return [
            pltpu.make_async_copy(srcs[4 * i + j], x0.at[i], sem.at[0, i]),
            pltpu.make_async_copy(srcs[4 * i + j + 1], x1.at[i], sem.at[1, i]),
        ]

    for core in range(2):

        @pl.when(c == core)
        def _():
            for i in range(n):
                for m in reads(i, 2 * core):
                    m.start()

    def writes(length, i, side, t):
        o, dst = ((od, down), (ou, up))[side]
        return [
            pltpu.make_async_copy(
                o.at[i, pl.ds(0, length)], dst.at[pl.ds(t * rows, length)], sem.at[2 + side, i]
            ),
            pltpu.make_async_copy(
                ow.at[side, i, pl.ds(0, length)],
                wout.at[pl.ds(t * rows, length), :, pl.ds(side * part, part)],
                sem.at[4 + side, i],
            ),
        ]

    jobs = []
    for i, place in enumerate(places):
        for m in reads(i, 0):
            m.wait()
        swapped = ((place & 1) << 1) | (place >> 1)
        for side, (x, o, k) in enumerate(((x0, od, swapped), (x1, ou, place))):
            t = jnp.bitwise_xor(k, s)
            o[i, :, 0, :] = x[i, :, :ff].astype(F32)
            ow[side, i, :, 0, :] = x[i, :, ff:].astype(F32)
            both_lengths(t, rows, lambda length: [m.start() for m in writes(length, i, side, t)])
            jobs.append((i, side, t))
    for i, side, t in jobs:
        both_lengths(t, rows, lambda length: [m.wait() for m in writes(length, i, side, t)])


def place_rows(places, ids, srcs, outs, cc, ff, model):
    rows, cols = srcs[0].shape
    n = len(places)
    first = outs is None
    operands = [ids, *srcs] + ([] if first else list(outs))
    return pl.pallas_call(
        functools.partial(place_kernel, places, first),
        in_specs=[SMEM] + [HBM] * (len(operands) - 1),
        out_specs=[HBM] * 3,
        out_shape=[jax.ShapeDtypeStruct((cc, 1, m), F32) for m in (ff, ff, model)],
        input_output_aliases={} if first else {4 * n + 1 + i: i for i in range(3)},
        scratch_shapes=[
            pltpu.VMEM((n, rows, cols), BF16),
            pltpu.VMEM((n, rows, cols), BF16),
            pltpu.VMEM((n, rows, 1, ff), F32),
            pltpu.VMEM((n, rows, 1, ff), F32),
            pltpu.VMEM((2, n, rows, 1, cols - ff), F32),
            pltpu.SemaphoreType.DMA((6, n)),
        ],
        compiler_params=params(16),
        cost_estimate=cost(0, 12 * n * rows * cols),
    )(*operands)


def qkv_out_kernel(ids, *refs):
    srcs, out, rows, wide, od, sem = refs[:4], *refs[4:]
    c, s = ids[0], ids[1]
    _, _, half, cols = rows.shape
    width = cols // 3

    def reads(a, b):
        return [
            pltpu.make_async_copy(
                src.at[p, pl.ds(0, half), :],
                rows.at[i, jnp.bitwise_xor(p if i else ((p & 1) << 1) | (p >> 1), s)],
                sem.at[0, i * QUAD + p],
            )
            for i, src in enumerate((a, b))
            for p in range(QUAD)
        ]

    @pl.when(c == 0)
    def _():
        for m in reads(srcs[0], srcs[1]):
            m.start()

    @pl.when(c != 0)
    def _():
        for m in reads(srcs[2], srcs[3]):
            m.start()

    for m in reads(srcs[0], srcs[1]):
        m.wait()
    step = half // 2
    moves = []
    for b in range(4):
        if b >= 2:
            moves[b - 2].wait()
        for t in range(QUAD):
            v = rows[b // 2, t, (b % 2) * step : (b % 2 + 1) * step, :].astype(F32)
            for i in range(3):
                lo = (i * QUAD + t) * width
                wide[:, lo : lo + width] = v[:, i * width : (i + 1) * width]
        od[b % 2, :, 0, :] = wide[...]
        n = step - (b == 3)
        m = pltpu.make_async_copy(
            od.at[b % 2, pl.ds(0, n)], out.at[pl.ds(b * step, n)], sem.at[1, b % 2]
        )
        m.start()
        moves.append(m)
    for m in moves[-2:]:
        m.wait()


def qkv_out(ids, srcs, cc):
    cols = srcs[0].shape[-1]
    half = (cc + 1) // 2
    return pl.pallas_call(
        qkv_out_kernel,
        in_specs=[SMEM] + [HBM] * 4,
        out_specs=HBM,
        out_shape=jax.ShapeDtypeStruct((cc, 1, QUAD * cols), F32),
        scratch_shapes=[
            pltpu.VMEM((2, QUAD, half, cols), BF16),
            pltpu.VMEM((half // 2, QUAD * cols), F32),
            pltpu.VMEM((2, half // 2, 1, QUAD * cols), F32),
            pltpu.SemaphoreType.DMA((2, 2 * QUAD)),
        ],
        compiler_params=params(15),
        cost_estimate=cost(0, 6 * cc * QUAD * cols),
    )(ids, *srcs)


def vectors_kernel(count, ids, *refs):
    srcs, outs, (rows, heads, sem) = refs[:4], refs[4:-3], refs[-3:]
    c, s = ids[0], ids[1]
    _, _, tall, row_len = rows.shape
    top = srcs[0].shape[1] - tall

    def reads(pair):
        return [
            pltpu.make_async_copy(v.at[p, pl.ds(top, tall), :], rows.at[i, p], sem.at[i * QUAD + p])
            for i, v in enumerate(pair)
            for p in range(QUAD)
        ]

    for core in range(2):

        @pl.when(c == core)
        def _():
            for m in reads(srcs[2 * core : 2 * core + 2]):
                m.start()

    for m in reads(srcs[:2]):
        m.wait()
    total = jnp.zeros((tall, row_len), F32)
    for i in range(2):
        for p in range(QUAD):
            total = total + rows[i, p].astype(F32)
    at = 0
    for o in outs[:5]:
        n = o.shape[1]
        for lo in range(0, n, row_len):
            size = min(row_len, n - lo)
            o[0:1, lo : lo + size] = total[at : at + 1, :size]
            at += 1
    heads[...] = jnp.zeros_like(heads)
    for i in range(2):
        for p in range(QUAD):
            k = p if i else ((p & 1) << 1) | (p >> 1)
            heads[jnp.bitwise_xor(k, s)] += rows[i, p, at : at + 8, :].astype(F32)
    width = row_len // 3
    for part in range(2):
        for t in range(QUAD):
            lo = (part * QUAD + t) * width
            outs[5][0:1, lo : lo + width] = heads[t, 0:1, part * width : (part + 1) * width]
    outs[6][0:1, :] = jnp.sqrt(total[at + 1 : at + 2, : outs[6].shape[1]] / count)


def vectors_out(ids, srcs, count, cc, ff, model):
    row_len = srcs[0].shape[-1]
    shapes = [ff, cc, cc, cc, cc, 2 * model, 128]
    return pl.pallas_call(
        functools.partial(vectors_kernel, count),
        in_specs=[SMEM] + [HBM] * 4,
        out_specs=[VMEM] * 7,
        out_shape=[jax.ShapeDtypeStruct((1, n), F32) for n in shapes],
        scratch_shapes=[
            pltpu.VMEM((2, QUAD, 32, row_len), BF16),
            pltpu.VMEM((QUAD, 8, row_len), F32),
            pltpu.SemaphoreType.DMA((2 * QUAD,)),
        ],
        compiler_params=params(8),
        cost_estimate=cost(0, 1 << 19),
    )(ids, *srcs)


def to_first(v):
    pairs = [(i, i ^ 1) for i in range(QUAD)] + [(QUAD + i, QUAD + (i ^ 2)) for i in range(QUAD)]
    return lax.ppermute(v, ("section", "seq"), pairs)


def to_second(v):
    pairs = [(i, i ^ 2) for i in range(QUAD)] + [(QUAD + i, QUAD + (i ^ 1)) for i in range(QUAD)]
    return lax.ppermute(v, ("section", "seq"), pairs)


def to_quad(v, k):
    return lax.ppermute(v, "seq", [(i, i ^ k) for i in range(QUAD)])


def to_core(v):
    return lax.ppermute(v, "section", [(0, 1), (1, 0)])


def dp_partner(v, step):
    n = lax.axis_size("dp")
    return lax.ppermute(v, "dp", [(i, i ^ step) for i in range(n)])


def to_owner(l, v):
    return lax.ppermute(v, "section", [(1 - l, l)])


def tied(*v):
    return lax.optimization_barrier(v)


class Order:
    def __init__(self, token):
        self.token = token

    def wait(self, *v):
        *v, self.token = lax.optimization_barrier((*v, self.token))
        return v

    def run(self, step, *operands):
        out = step(*self.wait(*operands))
        out, self.token = lax.optimization_barrier((out, self.token))
        return out


class DpSum:
    def __init__(self, order_of, make, *operands):
        self.value = None
        self.steps = self.work(order_of, make, operands)

    def go(self):
        next(self.steps, None)

    def finish(self):
        for _ in self.steps:
            pass
        return self.value

    def work(self, order_of, make, operands):
        n = lax.axis_size("dp")
        z = lax.axis_index("dp")

        def split(v, step):
            left = v.shape[0] // n * step if v.ndim == 2 else v.shape[1]
            v = v.reshape(n // (2 * step), 2, left, v.shape[-1])
            low = (z & step) == 0
            return jnp.where(low, v[:, 1], v[:, 0]), jnp.where(low, v[:, 0], v[:, 1])

        def join(v, got, step):
            low = (z & step) == 0
            both = jnp.where(low, jnp.stack([v, got], 1), jnp.stack([got, v], 1))
            return both.reshape(-1, *v.shape[1:])

        away, keep = order_of.run(lambda *v: split(make(*v), 1), *operands)
        step = 1
        while step < n:
            got = dp_partner(away, step)
            yield
            step *= 2
            if step < n:
                away, keep = order_of.run(lambda a, b, s=step: split(add_low(a, b), s), keep, got)
            else:
                v = order_of.run(add_low, keep, got)
        while step > 1:
            step //= 2
            got = dp_partner(v, step)
            yield
            v = order_of.run(functools.partial(join, step=step), v, got)
        self.value = v.reshape(-1, v.shape[-1])


def add_low(a, b):
    return (a.astype(F32) + b.astype(F32)).astype(BF16)


def quad_gather(own):
    one = to_second(own)
    two = to_first(own)
    three = to_first(one)
    return [own, one, two, three]


def on_device(
    layer_in, cotangent, lengths, w_qkv, bias_qv, w_out, bias_out,
    gain_attn, gain_mlp, w_up, bias_up, w_down, bias_down,
):
    micro, _, span, cc = layer_in.shape
    model = w_out.shape[1]
    ff = w_up.shape[-1]
    hd = model // HEADS
    width = model // QUAD
    heads = width // hd
    c = lax.axis_index("section")
    s = lax.axis_index("seq")
    dp_count = lax.axis_size("dp")
    mine = c == 0

    lens = lax.dynamic_index_in_dim(lengths, c, 0, keepdims=False)[0]
    e0 = lens[0]
    e1 = e0 + lens[1]
    e2 = e1 + lens[2]
    e3 = e2 + lens[3]
    ids = jnp.stack([c, s, e0, e1, e2, e3, c, s]).astype(jnp.int32)
    cs = jnp.stack([c, s]).astype(jnp.int32)
    x = rows_in(cs, layer_in)

    def row(v, n=ff):
        return jnp.pad(v, ((0, 0), (0, n - v.shape[-1])))

    qb = lax.dynamic_slice_in_dim(bias_qv, s * width, width, 1)
    vb = lax.dynamic_slice_in_dim(bias_qv, model + s * width, width, 1)
    heads_bias = jnp.concatenate([qb, jnp.zeros((1, width), F32), vb], 1)
    pv_own = jnp.concatenate(
        [row(v) for v in (bias_up, bias_out, bias_down, gain_attn, gain_mlp, heads_bias)]
        + [jnp.zeros((2, ff), F32)]
    )
    w3_own = jnp.concatenate(
        [lax.dynamic_slice_in_dim(w_qkv[0], i * model + s * width, width, 1) for i in range(3)], 1
    )
    pv_got = to_core(pv_own)
    w3_got = to_core(w3_own)
    wo_got = to_core(w_out[0])
    up = (w_up, to_core(w_up))
    dn = (w_down, to_core(w_down))
    pv = [jnp.where(mine, pv_own, pv_got), jnp.where(mine, pv_got, pv_own)]
    w3 = [jnp.where(mine, w3_own, w3_got), jnp.where(mine, w3_got, w3_own)]
    wo = [jnp.where(mine, w_out[0], wo_got), jnp.where(mine, wo_got, w_out[0])]

    normed = x
    saved = []
    squares = []
    for l in range(2):
        blocks = quad_gather(normed)
        if l == 1:
            blocks, df = tied(blocks, rows_in(cs, cotangent))
        qh, kh, vh, lse, blocks, *att = attn_fwd(l == 0, ids, blocks, w3[l], pv[l], heads, hd)
        att = [att[0]] + [to_quad(att[k], k) for k in (1, 2, 3)]
        mid, u, xout, normed, sq, astk = mlp_fwd(
            l, ids, x, att, wo[l], pv[l], pv[min(l + 1, 1)], up, dn
        )
        saved.append((x, blocks, (qh, kh, vh, lse), astk, mid, u))
        squares.append(sq[0, 0])
        x = xout
    outs = [saved[1][0], x]

    order_of = Order(ids)
    run = order_of.run

    def first_part(l, df):
        lr, rr, dmid, g, *douts = run(
            lambda v: mlp_bwd(l, ids, v, saved[l][5], saved[l][4], wo[l], pv[l], up, dn), df
        )
        return lr, rr, dmid, g, [douts[0]] + [to_quad(douts[k], k) for k in (1, 2, 3)]

    def send(l, places, lr, rr):
        return run(lambda a, b: product(True, places, ids, a, b, saved[l][3]), lr, rr)

    def keep(l, places, lr, rr, got):
        return run(lambda a, b, v: product(False, places, ids, a, b, saved[l][3], v), lr, rr, got)

    def attention(l, douts):
        outs = run(lambda *v: attn_bwd(ids, saved[l][1], w3[l], saved[l][2], v), *douts)
        return (*outs, to_first(outs[2]), to_core(outs[3]))

    def input_part(l, p0, pr, q, dmid):
        return run(lambda *v: input_grad_of(*v, saved[l][0], pv[l]), p0, pr, q, dmid)

    def projection(l, gk, gs_got, g, gb, gg):
        heads_sum = jnp.concatenate([gb[0, :width], gb[0, 2 * width :]])
        row_len = 3 * width
        vectors = [
            g[0], g[1, :cc], g[2, :cc], gg[0, :cc], g[4, :cc], heads_sum,
            jnp.broadcast_to(squares[l], (row_len,)),
        ]
        v = [jnp.pad(x, (0, -x.shape[0] % row_len)) for x in vectors]
        v = jnp.concatenate(v).reshape(-1, row_len)
        v = jnp.pad(v, ((0, 32 - v.shape[0]), (0, 0))).astype(BF16)
        return jnp.concatenate([add_low(gk, gs_got), v])

    def wait(*v):
        out = order_of.wait(*v)
        return out[0] if len(out) == 1 else out

    def pair_up(a, b):
        return jnp.stack([a, b])

    def add_first(a, b):
        return add_low(a, b[:span])

    lr1, rr1, dmid1, g1, douts1 = first_part(1, df)

    far1 = to_core(send(1, (3, 2), lr1, rr1))
    douts1 = wait(*douts1)
    near1 = send(1, (1, 0), lr1, rr1)
    far1 = wait(far1)

    far1 = keep(1, (3, 2), lr1, rr1, far1)
    x1a, near1 = to_first(far1[0]), to_core(near1)
    p0, p1, _, _, gk1, gb1, pr, gs_got = attention(1, douts1)
    x1a, near1 = wait(x1a, near1)

    out_got = to_core(run(lambda a, b: jnp.where(mine, a, b), outs[1], outs[0]))
    near1 = keep(1, (1, 0), lr1, rr1, near1)
    half1 = run(add_low, near1[0], x1a)
    pr, gs_got, out_got = wait(pr, gs_got, out_got)

    q = to_second(run(add_first, p1, pr))
    q = wait(q)

    x1b, half1 = wait(far1[1], half1)
    x1b, x2 = to_first(x1b), to_second(half1)
    dx1, gg1 = input_part(1, p0, pr, q, dmid1)
    qkv_sum1 = DpSum(order_of, functools.partial(projection, 1), gk1, gs_got, g1, gb1, gg1)
    lr0, rr0, dmid0, g0, douts0 = first_part(0, dx1)
    far0 = to_core(send(0, (3, 2), lr0, rr0))
    near0 = send(0, (1, 0), lr0, rr0)
    x1b, x2 = wait(x1b, x2)

    sum1 = DpSum(order_of, lambda a, b, d: add_low(add_low(a, b), d), near1[1], x1b, x2)
    sum1.go()
    far0, *douts0 = wait(far0, *douts0)

    far0 = keep(0, (3, 2), lr0, rr0, far0)
    x1a, near0 = to_first(far0[0]), to_core(near0)
    p0, p1, _, _, gk0, gb0, pr, gs_got = attention(0, douts0)
    x1a, near0 = wait(x1a, near0)

    sum1.go()
    near0 = keep(0, (1, 0), lr0, rr0, near0)
    half1 = run(add_low, near0[0], x1a)
    qkv_sum1.go()
    pr, gs_got = wait(pr, gs_got)

    q = to_second(run(add_first, p1, pr))
    q = wait(q)

    x1b = to_first(wait(far0[1]))
    dx0, gg0 = input_part(0, p0, pr, q, dmid0)
    qkv_sum1.go()
    sum1.go()
    x1b, half1 = wait(x1b, half1)

    x2 = to_second(half1)
    sum1.go()
    half0 = run(add_low, near0[1], x1b)
    qkv_sum0 = DpSum(order_of, functools.partial(projection, 0), gk0, gs_got, g0, gb0, gg0)
    qkv_sum0.go()
    qkv_sum1.go()
    x2 = wait(x2)
    own1 = sum1.finish()

    have1 = [own1, to_second(own1), to_first(own1)]
    sum0 = DpSum(order_of, add_low, half0, x2)
    sum0.go()
    qkv_sum1.go()
    qkv_sum0.go()
    sum0.go()
    have1[1], have1[2] = wait(have1[1], have1[2])

    have1.append(to_first(have1[1]))
    qkv_own1 = qkv_sum1.finish()
    qkv_sum0.go()
    got1 = [to_owner(1, own1)]
    sum0.go()
    have1[3], got1[0] = wait(have1[3], got1[0])

    qkv_next1 = to_second(qkv_own1)
    got1.append(to_owner(1, have1[1]))
    qkv_sum0.go()
    qkv_next1, got1[1] = wait(qkv_next1, got1[1])
    qkv_pair1 = run(pair_up, qkv_own1, qkv_next1)
    sum0.go()

    qkv_rest1 = to_first(qkv_pair1)
    got1.append(to_owner(1, have1[2]))
    qkv_own0 = qkv_sum0.finish()
    qkv_next0 = to_second(qkv_own0)
    qkv_rest1, got1[2], qkv_next0 = wait(qkv_rest1, got1[2], qkv_next0)

    own0 = sum0.finish()
    have0 = [own0, to_second(own0), to_first(own0)]
    got1.append(to_owner(1, have1[3]))
    qkv_pair0 = run(pair_up, qkv_own0, qkv_next0)
    qkv_rest0 = to_first(qkv_pair0)
    got1[3] = wait(got1[3])
    got0 = [to_owner(0, own0)]
    in_got = to_core(run(lambda a, b: jnp.where(mine, a, b), dx1, dx0))
    qkv1 = run(lambda a, b: jnp.concatenate([a, b]), qkv_pair1, qkv_rest1)
    layer_out = run(
        lambda a, b, d: rows_out(ids, jnp.where(mine, a, b), d), outs[0], outs[1], out_got
    )
    got0[0], in_got = wait(got0[0], in_got)

    def place(places, outs_w):
        srcs = [v[p] for p in places for v in (have0, got0, got1, have1)]
        n = len(srcs)
        return run(
            lambda *v: place_rows(places, ids, v[:n], v[n:] or None, cc, ff, model), *srcs, *outs_w
        )

    outs_w = place((0,), ())
    input_grad = run(lambda a, b, d: rows_out(ids, jnp.where(mine, a, b), d), dx0, dx1, in_got)
    have0[1], have0[2], qkv_rest0 = wait(have0[1], have0[2], qkv_rest0)

    have0.append(to_first(have0[1]))
    qkv0 = run(lambda a, b: jnp.concatenate([a, b]), qkv_pair0, qkv_rest0)
    have0[1], have0[2] = wait(have0[1], have0[2])
    got0.append(to_owner(0, have0[1]))
    qkv0_got, qkv1_got = to_owner(0, qkv0), to_owner(1, qkv1)
    got0[1] = wait(got0[1])
    outs_w = place((1,), outs_w)
    got0.append(to_owner(0, wait(have0[2])))
    qkv0_got, qkv1_got = wait(qkv0_got, qkv1_got)
    grad_qkv = run(lambda *v: qkv_out(ids, v, cc), qkv0, qkv0_got, qkv1_got, qkv1)
    count = micro * dp_count * span * QUAD
    vectors = run(
        lambda *v: vectors_out(ids, v, count, cc, ff, model), qkv0, qkv0_got, qkv1_got, qkv1
    )
    have0[3], got0[2] = wait(have0[3], got0[2])

    got0.append(to_owner(0, have0[3]))
    outs_w = place((2,), outs_w)
    got0[3] = wait(got0[3])
    grad_down, grad_up, grad_out = place_rows(
        (3,), order_of.token, [v[3] for v in (have0, got0, got1, have1)], outs_w, cc, ff, model
    )

    grad_bup, grad_bout, grad_bdown, grad_ga, grad_gm, grad_bqv, rms = vectors
    return (
        layer_out,
        input_grad,
        jnp.transpose(grad_qkv, (1, 0, 2)),
        grad_bqv,
        jnp.transpose(grad_out, (1, 2, 0)),
        grad_bout,
        grad_ga,
        grad_gm,
        jnp.transpose(grad_up, (1, 0, 2)),
        grad_bup,
        jnp.transpose(grad_down, (1, 2, 0)),
        grad_bdown,
        rms[0, :1],
    )


def solution(mesh):
    two = P("section", None)
    three = P("section", None, None)
    tokens = P(None, "dp", "seq", None)
    stacked = P("section", None, "dp", "seq", None)
    return jax.shard_map(
        on_device,
        mesh=mesh,
        in_specs=(
            tokens, tokens, P(None, "dp", None), three, two, three, two, two, two, three, two, three, two,
        ),
        out_specs=(
            stacked, stacked, three, two, three, two, two, two, three, two, three, two, P("section"),
        ),
        check_vma=False,
    )
```
